32 devices in a mesh: dp: 8 (over z, y), section: 4 (over x, core).
Axes of the slice: x: 2, y: 2, z: 4, core: 2. Of those that a mesh axis runs over, the one named last changes fastest.
Arguments:
- global_crops: bfloat16 [64, 197, 384], P(('dp', 'section')), may hold values from -6 to 6
- local_crops: bfloat16 [320, 37, 384], P(('dp', 'section')), may hold values from -6 to 6
- local_count: int32 [32], P('dp'), may hold values from 2 to 10, as said below
- global_cotangent: bfloat16 [64, 197, 384], P(('dp', 'section')), may hold values from -6 to 6
- local_cotangent: bfloat16 [320, 37, 384], P(('dp', 'section')), may hold values from -6 to 6
- attend_gain: bfloat16 [2, 384], replicated, may hold values from 0.5 to 1.5
- attend_shift: bfloat16 [2, 384], replicated, may hold values from -3 to 3
- mixer_weight: bfloat16 [2, 384, 1152], replicated, may hold values from -0.3125 to 0.3125
- mixer_bias: bfloat16 [2, 768], replicated, may hold values from -3 to 3
- output_weight: bfloat16 [2, 384, 384], replicated, may hold values from -2.5 to 2.5
- output_bias: bfloat16 [2, 384], replicated, may hold values from -3 to 3
- feed_gain: bfloat16 [2, 384], replicated, may hold values from 0.5 to 1.5
- feed_shift: bfloat16 [2, 384], replicated, may hold values from -3 to 3
- expand_weight: bfloat16 [2, 384, 1536], replicated, may hold values from -0.3125 to 0.3125
- expand_bias: bfloat16 [2, 1536], replicated, may hold values from -3 to 3
- reduce_weight: bfloat16 [2, 1536, 384], replicated, may hold values from -0.15625 to 0.15625
- reduce_bias: bfloat16 [2, 384], replicated, may hold values from -3 to 3
Outputs:
- global_output: bfloat16 [64, 197, 384], P(('dp', 'section'))
- local_output: bfloat16 [320, 37, 384], P(('dp', 'section'))
- global_input_grad: bfloat16 [64, 197, 384], P(('dp', 'section'))
- local_input_grad: bfloat16 [320, 37, 384], P(('dp', 'section'))
- attend_gain_grad: float32 [2, 384], replicated
- attend_shift_grad: float32 [2, 384], replicated
- mixer_weight_grad: float32 [2, 384, 1152], replicated
- mixer_bias_grad: float32 [2, 768], replicated
- output_weight_grad: float32 [2, 384, 384], replicated
- output_bias_grad: float32 [2, 384], replicated
- feed_gain_grad: float32 [2, 384], replicated
- feed_shift_grad: float32 [2, 384], replicated
- expand_weight_grad: float32 [2, 384, 1536], replicated
- expand_bias_grad: float32 [2, 1536], replicated
- reduce_weight_grad: float32 [2, 1536, 384], replicated
- reduce_bias_grad: float32 [2, 384], replicated
The draws below stay inside these ranges and needn't reach their ends.
Inputs may be any that keep to these rules, and one draw needn't show every extreme that they name: `local_count`: small counts are far more common than large ones; at least one image has 10 live local crops in every draw.
All inputs are finite; a program needn't handle non-finite values.
Results may differ from the reference program's by a relative error of at most 0.015.
Values may be sent and summed in bfloat16 or wider, within the bound.
A program may use at most 128 MiB of HBM per device.

```python
import jax
import jax.numpy as jnp
from jax import lax

D = 384
HEADS = 6
HEAD = 64
FF = 1536
LAYERS = 2
GLOBAL_LEN = 197
LOCAL_LEN = 37
LOC_MAX = 10
IMAGES = 32


def draw_local_count(key, part):
    key = jax.random.fold_in(key, 11)
    first, second, third = jax.random.split(key, 3)
    left = jax.random.randint(first, (IMAGES,), 0, 10)
    right = jax.random.randint(second, (IMAGES,), 0, 10)
    counts = jnp.minimum(2 + left * right // 6, LOC_MAX)
    chosen = jax.random.randint(third, (), 0, IMAGES)
    return jnp.where(jnp.arange(IMAGES) == chosen, LOC_MAX, counts).astype(jnp.int32)


def level_of(own_key, dims, cuts, smallest, top_value):
    def one(axis_at, shards_of):
        steps = jax.random.uniform(jax.random.fold_in(jax.random.fold_in(own_key, 6), axis_at), (shards_of,), jnp.float32, smallest / len(cuts), top_value / len(cuts))
        return jnp.repeat(jnp.exp(steps), dims[axis_at] // shards_of).reshape((-1,) + (1,) * (len(dims) - axis_at - 1))

    level = one(*cuts[0])
    for cut in cuts[1:]:
        level = level * one(*cut)
    return level


def noise(key, shape, scale, limit, cuts=(), held_as=jnp.bfloat16):
    array = scale * jax.random.normal(key, shape, jnp.float32)
    if cuts:
        array = array * level_of(key, shape, cuts, -0.22, 0.18)
    return jnp.clip(array, -limit, limit).astype(held_as)


def setup_inputs(seed: int = 0) -> dict:
    keys = jax.random.split(jax.random.key(seed), 18)
    return {
        "global_crops": noise(keys[0], (IMAGES * 2, GLOBAL_LEN, D), 1.0, 6.0, ((0, 32),)),
        "local_crops": noise(keys[1], (IMAGES * LOC_MAX, LOCAL_LEN, D), 1.0, 6.0, ((0, 32),)),
        "local_count": draw_local_count(jax.random.fold_in(keys[17], 71), 0),
        "global_cotangent": noise(keys[3], (IMAGES * 2, GLOBAL_LEN, D), 1.0, 6.0, ((0, 32),)),
        "local_cotangent": noise(keys[4], (IMAGES * LOC_MAX, LOCAL_LEN, D), 1.0, 6.0, ((0, 32),)),
        "attend_gain": jnp.clip(1.0 + 0.1 * jax.random.normal(keys[5], (LAYERS, D), jnp.float32), 0.5, 1.5).astype(jnp.bfloat16),
        "attend_shift": noise(keys[6], (LAYERS, D), 0.3, 3.0),
        "mixer_weight": noise(keys[7], (LAYERS, D, 3 * D), D ** -0.5, 0.3125),
        "mixer_bias": noise(keys[8], (LAYERS, 2 * D), 0.3, 3.0),
        "output_weight": noise(keys[9], (LAYERS, D, D), (max(D // 64, 1)) ** -0.5, 2.5),
        "output_bias": noise(keys[10], (LAYERS, D), 0.3, 3.0),
        "feed_gain": jnp.clip(1.0 + 0.1 * jax.random.normal(keys[11], (LAYERS, D), jnp.float32), 0.5, 1.5).astype(jnp.bfloat16),
        "feed_shift": noise(keys[12], (LAYERS, D), 0.3, 3.0),
        "expand_weight": noise(keys[13], (LAYERS, D, FF), D ** -0.5, 0.3125),
        "expand_bias": noise(keys[14], (LAYERS, FF), 0.3, 3.0),
        "reduce_weight": noise(keys[15], (LAYERS, FF, D), FF ** -0.5, 0.15625),
        "reduce_bias": noise(keys[16], (LAYERS, D), 0.3, 3.0),
    }


@jax.custom_vjp
def low(v):
    return lax.optimization_barrier(v.astype(jnp.bfloat16)).astype(jnp.float32)

@jax.custom_vjp
def low_back(v):
    return v

def low_keep(v):
    return (low(v), None)

def low_pass(kept, grad):
    return (grad,)

def back_keep(v):
    return (v, None)

def back_low(kept, grad):
    return (low(grad),)
low.defvjp(low_keep, low_pass)
low_back.defvjp(back_keep, back_low)
EPS = 1e-06
HIGH = lax.Precision.HIGHEST

def layer_norm(rows, gain, shift):
    row_mean = lax.optimization_barrier(jnp.mean(rows, -1, keepdims=True))
    centred = rows - row_mean
    variance = lax.optimization_barrier(jnp.mean(centred * centred, -1, keepdims=True))
    return centred * lax.rsqrt(variance + EPS) * gain + shift

def both_low(value):
    return low_back(low(value))

def attention_branch(rows, gain, shift, mixer_weight, mixer_bias, output_weight, output_bias):
    crops, length, width = rows.shape
    normed = low(layer_norm(rows, gain, shift))
    bias = jnp.concatenate([mixer_bias[:width], jnp.zeros((width,), jnp.float32), mixer_bias[width:]])
    packed = jnp.einsum('csd,de->cse', normed, mixer_weight, precision=HIGH) + bias
    packed = both_low(packed).reshape(crops, length, 3, HEADS, HEAD)
    query, key, value = (packed[:, :, 0], packed[:, :, 1], packed[:, :, 2])
    scores = low_back(jnp.einsum('cqhe,ckhe->chqk', query, key, precision=HIGH) * HEAD ** (-0.5))
    shares = low(jax.nn.softmax(scores, axis=-1))
    mixed = jnp.einsum('chqk,ckhe->cqhe', shares, value, precision=HIGH).reshape(crops, length, width)
    mixed = both_low(mixed)
    return jnp.einsum('csd,de->cse', mixed, output_weight, precision=HIGH) + output_bias

def feed_branch(rows, gain, shift, expand_weight, expand_bias, reduce_weight, reduce_bias):
    normed = low(layer_norm(rows, gain, shift))
    up_value = low_back(jnp.einsum('csd,df->csf', normed, expand_weight, precision=HIGH) + expand_bias)
    hidden = low(jax.nn.gelu(up_value, approximate=False))
    return jnp.einsum('csf,fd->csd', hidden, reduce_weight, precision=HIGH) + reduce_bias

def layers_forward(params, global_rows, local_rows, live):
    attend_gain, attend_shift, mixer_weight, mixer_bias, output_weight, output_bias, feed_gain, feed_shift, expand_weight, expand_bias, reduce_weight, reduce_bias = params
    streams = [global_rows, local_rows]
    for layer in range(LAYERS):
        streams = [both_low(rows + attention_branch(rows, attend_gain[layer], attend_shift[layer], mixer_weight[layer], mixer_bias[layer], output_weight[layer], output_bias[layer])) for rows in streams]
        streams = [both_low(rows + feed_branch(rows, feed_gain[layer], feed_shift[layer], expand_weight[layer], expand_bias[layer], reduce_weight[layer], reduce_bias[layer])) for rows in streams]
    return (streams[0], streams[1] * live[:, None, None])

def reference(global_crops, local_crops, local_count, global_cotangent, local_cotangent, attend_gain, attend_shift, mixer_weight, mixer_bias, output_weight, output_bias, feed_gain, feed_shift, expand_weight, expand_bias, reduce_weight, reduce_bias):
    params = tuple((weight.astype(jnp.float32) for weight in (attend_gain, attend_shift, mixer_weight, mixer_bias, output_weight, output_bias, feed_gain, feed_shift, expand_weight, expand_bias, reduce_weight, reduce_bias)))
    global_all = global_crops.astype(jnp.float32).reshape(IMAGES, 2, GLOBAL_LEN, D)
    local_all = local_crops.astype(jnp.float32).reshape(IMAGES, LOC_MAX, LOCAL_LEN, D)
    global_cot = global_cotangent.astype(jnp.float32).reshape(IMAGES, 2, GLOBAL_LEN, D)
    local_cot = local_cotangent.astype(jnp.float32).reshape(IMAGES, LOC_MAX, LOCAL_LEN, D)
    live_all = (jnp.arange(LOC_MAX)[None, :] < local_count[:, None]).astype(jnp.float32)

    def one_image(totals, inputs):
        global_rows, local_rows, live, global_grad, local_grad = inputs

        def forward(weights, global_in, local_in):
            return layers_forward(weights, global_in, local_in, live)
        outputs, backward = jax.vjp(forward, params, global_rows, local_rows)
        weight_grads, global_back, local_back = backward((global_grad, local_grad))
        totals = jax.tree.map(lambda left, right: left + right, totals, weight_grads)
        return (totals, (outputs[0].astype(jnp.bfloat16), outputs[1].astype(jnp.bfloat16), global_back.astype(jnp.bfloat16), local_back.astype(jnp.bfloat16)))
    zeros = jax.tree.map(jnp.zeros_like, params)
    totals, results = lax.scan(one_image, zeros, (global_all, local_all, live_all, global_cot, local_cot))
    global_output = results[0].reshape(IMAGES * 2, GLOBAL_LEN, D)
    local_output = results[1].reshape(IMAGES * LOC_MAX, LOCAL_LEN, D)
    global_input_grad = results[2].reshape(IMAGES * 2, GLOBAL_LEN, D)
    local_input_grad = results[3].reshape(IMAGES * LOC_MAX, LOCAL_LEN, D)
    return (global_output, local_output, global_input_grad, local_input_grad, totals[0], totals[1], totals[2], totals[3], totals[4], totals[5], totals[6], totals[7], totals[8], totals[9], totals[10], totals[11])
```

```python
import jax
import jax.numpy as jnp
from jax import lax
from jax.sharding import PartitionSpec as P

HEADS = 6
HEAD = 64


EPS = 1e-06


def layer_norm(rows, gain, shift):
    row_mean = jnp.mean(rows, -1, keepdims=True)
    centred = rows - row_mean
    variance = jnp.mean(centred * centred, -1, keepdims=True)
    return centred * lax.rsqrt(variance + EPS) * gain + shift


def gelu_exact(values):
    return jax.nn.gelu(values, approximate=False)


def attention_forward(rows, weights):
    gain, shift, mixer_weight, mixer_bias, output_weight, output_bias = weights
    crops, length, width = rows.shape
    normed_low = layer_norm(rows, gain, shift).astype(jnp.bfloat16)
    bias = jnp.concatenate(
        [mixer_bias[:width], jnp.zeros((width,), jnp.float32), mixer_bias[width:]]
    )
    packed = (
        jnp.einsum("csd,de->cse", normed_low, mixer_weight, preferred_element_type=jnp.float32)
        + bias
    ).astype(jnp.bfloat16)
    split = packed.reshape(crops, length, 3, HEADS, HEAD)
    query, key, value = (split[:, :, 0], split[:, :, 1], split[:, :, 2])
    scores = jnp.einsum(
        "cqhe,ckhe->chqk", query, key, preferred_element_type=jnp.float32
    ) * HEAD ** (-0.5)
    shares = jax.nn.softmax(scores, axis=-1)
    shares_low = shares.astype(jnp.bfloat16)
    mixed = jnp.einsum("chqk,ckhe->cqhe", shares_low, value, preferred_element_type=jnp.float32)
    mixed_low = mixed.reshape(crops, length, width).astype(jnp.bfloat16)
    result = (
        rows
        + jnp.einsum("csd,de->cse", mixed_low, output_weight, preferred_element_type=jnp.float32)
        + output_bias
    )
    return (result, (normed_low, query, key, value, shares, shares_low, mixed_low))


def attention_backward(rows, weights, grad_low):
    gain, shift, mixer_weight, mixer_bias, output_weight, output_bias = weights
    crops, length, width = rows.shape
    result, kept = attention_forward(rows, weights)
    normed_low, query, key, value, shares, shares_low, mixed_low = kept
    output_grad = jnp.einsum("csd,cse->de", mixed_low, grad_low, preferred_element_type=jnp.float32)
    output_bias_grad = jnp.sum(grad_low, (0, 1), dtype=jnp.float32)
    mixed_grad = jnp.einsum(
        "cse,de->csd", grad_low, output_weight, preferred_element_type=jnp.float32
    )
    mixed_grad = mixed_grad.astype(jnp.bfloat16).reshape(crops, length, HEADS, HEAD)
    share_grad = jnp.einsum(
        "cqhe,ckhe->chqk", mixed_grad, value, preferred_element_type=jnp.float32
    )
    inner = jnp.sum(share_grad * shares, -1, keepdims=True)
    score_grad = (shares * (share_grad - inner)).astype(jnp.bfloat16)
    scale = HEAD ** (-0.5)
    query_grad = (
        jnp.einsum("chqk,ckhe->cqhe", score_grad, key, preferred_element_type=jnp.float32) * scale
    )
    key_grad = (
        jnp.einsum("chqk,cqhe->ckhe", score_grad, query, preferred_element_type=jnp.float32) * scale
    )
    value_grad = jnp.einsum(
        "chqk,cqhe->ckhe", shares_low, mixed_grad, preferred_element_type=jnp.float32
    )
    packed_grad = (
        jnp.stack([query_grad, key_grad, value_grad], 2)
        .reshape(crops, length, 3 * width)
        .astype(jnp.bfloat16)
    )
    mixer_grad = jnp.einsum(
        "csd,cse->de", normed_low, packed_grad, preferred_element_type=jnp.float32
    )
    bias_sums = jnp.sum(packed_grad, (0, 1), dtype=jnp.float32)
    normed_grad = jnp.einsum(
        "cse,de->csd", packed_grad, mixer_weight, preferred_element_type=jnp.float32
    )
    unused, norm_back = jax.vjp(layer_norm, rows, gain, shift)
    rows_grad, gain_grad, shift_grad = norm_back(normed_grad)
    input_grad = grad_low.astype(jnp.float32) + rows_grad
    wide = jnp.concatenate(
        [bias_sums[:width], bias_sums[2 * width :], jnp.zeros((2 * width,), jnp.float32)]
    )
    first = jnp.concatenate([mixer_grad, output_grad], 1)
    second = jnp.zeros((first.shape[1], width), jnp.float32)
    return (input_grad, (first, second, gain_grad, shift_grad, wide, output_bias_grad))


def feed_forward(rows, weights):
    gain, shift, expand_weight, expand_bias, reduce_weight, reduce_bias = weights
    normed_low = layer_norm(rows, gain, shift).astype(jnp.bfloat16)
    up_value = (
        jnp.einsum("csd,df->csf", normed_low, expand_weight, preferred_element_type=jnp.float32)
        + expand_bias
    )
    hidden_low = gelu_exact(up_value).astype(jnp.bfloat16)
    result = (
        rows
        + jnp.einsum("csf,fd->csd", hidden_low, reduce_weight, preferred_element_type=jnp.float32)
        + reduce_bias
    )
    return (result, (normed_low, up_value, hidden_low))


def feed_backward(rows, weights, grad_low):
    gain, shift, expand_weight, expand_bias, reduce_weight, reduce_bias = weights
    result, kept = feed_forward(rows, weights)
    normed_low, up_value, hidden_low = kept
    reduce_grad = jnp.einsum(
        "csf,csd->fd", hidden_low, grad_low, preferred_element_type=jnp.float32
    )
    reduce_bias_grad = jnp.sum(grad_low, (0, 1), dtype=jnp.float32)
    hidden_grad = jnp.einsum(
        "csd,fd->csf", grad_low, reduce_weight, preferred_element_type=jnp.float32
    )
    unused, gelu_back = jax.vjp(gelu_exact, up_value)
    up_grad = gelu_back(hidden_grad)[0].astype(jnp.bfloat16)
    expand_grad = jnp.einsum("csd,csf->df", normed_low, up_grad, preferred_element_type=jnp.float32)
    expand_bias_grad = jnp.sum(up_grad, (0, 1), dtype=jnp.float32)
    normed_grad = jnp.einsum(
        "csf,df->csd", up_grad, expand_weight, preferred_element_type=jnp.float32
    )
    unused_norm, norm_back = jax.vjp(layer_norm, rows, gain, shift)
    rows_grad, gain_grad, shift_grad = norm_back(normed_grad)
    input_grad = grad_low.astype(jnp.float32) + rows_grad
    return (
        input_grad,
        (expand_grad, reduce_grad, gain_grad, shift_grad, expand_bias_grad, reduce_bias_grad),
    )


def shards(
    global_crops,
    local_crops,
    local_count,
    global_cotangent,
    local_cotangent,
    attend_gain,
    attend_shift,
    mixer_weight,
    mixer_bias,
    output_weight,
    output_bias,
    feed_gain,
    feed_shift,
    expand_weight,
    expand_bias,
    reduce_weight,
    reduce_bias,
):
    images = local_count.shape[0]
    sections = lax.axis_size("section")
    own = images // sections
    slots = local_crops.shape[0] // own
    width = global_crops.shape[2]
    first = lax.axis_index("section") * own
    counts = lax.dynamic_slice_in_dim(local_count, first, own, 0)
    live = (jnp.arange(slots)[None, :] < counts[:, None]).astype(jnp.bfloat16).reshape(-1, 1, 1)

    def attend_weights(layer):
        return (
            attend_gain[layer].astype(jnp.float32),
            attend_shift[layer].astype(jnp.float32),
            mixer_weight[layer],
            mixer_bias[layer].astype(jnp.float32),
            output_weight[layer],
            output_bias[layer].astype(jnp.float32),
        )

    def feed_weights(layer):
        return (
            feed_gain[layer].astype(jnp.float32),
            feed_shift[layer].astype(jnp.float32),
            expand_weight[layer],
            expand_bias[layer].astype(jnp.float32),
            reduce_weight[layer],
            reduce_bias[layer].astype(jnp.float32),
        )

    streams = (global_crops, local_crops)
    kept = []
    for layer in range(2):
        kept.append(streams)
        streams = tuple(
            attention_forward(rows.astype(jnp.float32), attend_weights(layer))[0].astype(jnp.bfloat16)
            for rows in streams
        )
        kept.append(streams)
        streams = tuple(
            feed_forward(rows.astype(jnp.float32), feed_weights(layer))[0].astype(jnp.bfloat16)
            for rows in streams
        )
    global_output, local_output = streams[0], streams[1] * live
    grads = (global_cotangent, local_cotangent * live)
    sums = [None] * 4
    for layer in (1, 0):
        for kind, fn, weights in ((1, feed_backward, feed_weights), (0, attention_backward, attend_weights)):
            rows = kept[2 * layer + kind]
            parts = [fn(r.astype(jnp.float32), weights(layer), g) for r, g in zip(rows, grads)]
            grads = tuple(p[0].astype(jnp.bfloat16) for p in parts)
            terms = jax.tree.map(jnp.add, parts[0][1], parts[1][1])
            first, second = terms[0].astype(jnp.bfloat16), terms[1].astype(jnp.bfloat16)
            both = ("dp", "section")
            if kind == 0:
                sums[2 * layer] = lax.psum((first,) + terms[2:], both)
            else:
                sums[2 * layer + 1] = lax.psum((first, second) + terms[2:], both)
    a0, f0, a1, f1 = sums

    def pair(x, y):
        return jnp.stack([x, y]).astype(jnp.float32)

    return (
        global_output,
        local_output,
        grads[0],
        grads[1],
        pair(a0[1], a1[1]),
        pair(a0[2], a1[2]),
        pair(a0[0][:, : 3 * width], a1[0][:, : 3 * width]),
        pair(a0[3][: 2 * width], a1[3][: 2 * width]),
        pair(a0[0][:, 3 * width :], a1[0][:, 3 * width :]),
        pair(a0[4], a1[4]),
        pair(f0[2], f1[2]),
        pair(f0[3], f1[3]),
        pair(f0[0], f1[0]),
        pair(f0[4], f1[4]),
        pair(f0[1], f1[1]),
        pair(f0[5], f1[5]),
    )


def solution(mesh):
    in_specs = (
        P(("dp", "section"), None, None),
        P(("dp", "section"), None, None),
        P("dp"),
        P(("dp", "section"), None, None),
        P(("dp", "section"), None, None),
        P(),
        P(),
        P(),
        P(),
        P(),
        P(),
        P(),
        P(),
        P(),
        P(),
        P(),
        P(),
    )
    out_specs = (
        P(("dp", "section"), None, None),
        P(("dp", "section"), None, None),
        P(("dp", "section"), None, None),
        P(("dp", "section"), None, None),
        P(),
        P(),
        P(),
        P(),
        P(),
        P(),
        P(),
        P(),
        P(),
        P(),
        P(),
        P(),
    )
    return jax.shard_map(shards, mesh=mesh, in_specs=in_specs, out_specs=out_specs, check_vma=False)
```

```python
import functools

import jax
import jax.numpy as jnp
from jax import lax
from jax.experimental import pallas as pl
from jax.experimental.pallas import tpu as pltpu
from jax.sharding import PartitionSpec as P

HEADS = 6
HEAD = 64
EPS = 1e-06
TILE = 16
LANES = 128
BLOCK = 256
LOG2E = 1.4426950408889634
F32 = jnp.float32
BF16 = jnp.bfloat16


def up_to(value, step):
    return -(-value // step) * step


def mm(left, right):
    return lax.dot_general(left, right, (((1,), (0,)), ((), ())), preferred_element_type=F32)


def mm_nt(left, right):
    return lax.dot_general(left, right, (((1,), (1,)), ((), ())), preferred_element_type=F32)


def mm_tn(left, right):
    return lax.dot_general(left, right, (((0,), (0,)), ((), ())), preferred_element_type=F32)


def norm(rows):
    centred = rows - jnp.mean(rows, -1, keepdims=True)
    scale = lax.rsqrt(jnp.mean(centred * centred, -1, keepdims=True) + EPS)
    return centred * scale, scale


def norm_back(grad, unit, scale, gain):
    slope = grad * gain
    first = jnp.mean(slope, -1, keepdims=True)
    second = jnp.mean(slope * unit, -1, keepdims=True)
    return scale * (slope - first - unit * second)


def gelu_parts(u):
    size = jnp.abs(u)
    d = 1.0 + (0.3275911 * 0.7071067811865476) * size
    t = pl.reciprocal(d, approx=True)
    t = t * (2.0 - d * t)
    poly = 0.5 * 1.061405429
    for a in (-1.453152027, 1.421413741, -0.284496736, 0.254829592):
        poly = poly * t + 0.5 * a
    bell = jnp.exp2((u * u) * (-0.5 * LOG2E))
    tail = poly * t * bell
    phi = jnp.where(u < 0.0, tail, 1.0 - tail)
    return u * phi, phi + (u * bell) * 0.3989422804014327


def fold8(value):
    rows, width = value.shape
    return jnp.sum(value.reshape(rows // 8, 8, width), 0)


def kernel(
    dims,
    counts,
    global_in,
    local_in,
    global_cot,
    local_cot,
    attend_gain,
    attend_shift,
    mixer_weight,
    mixer_bias,
    output_weight,
    output_bias,
    feed_gain,
    feed_shift,
    expand_weight,
    expand_bias,
    reduce_weight,
    reduce_bias,
    global_out,
    local_out,
    global_back,
    local_back,
    feed_sum,
    attend_sum,
    x_s,
    unit_s,
    scale_s,
    norm_t,
    packed_s,
    power_s,
    inverse_s,
    mixed_s,
    mixed_t,
    act_s,
    slope_s,
    grad_s,
    grad_low,
    grad_t,
    dup_s,
    mask_s,
    vec_s,
    acc_s,
):
    seq, group, width = dims.seq, dims.group, dims.width
    glen, llen = dims.glen, dims.llen
    n_global, n_local, n_seq = dims.n_global, dims.n_local, dims.n_seq
    hidden = dims.hidden
    count = counts[lax.axis_index("section")]
    pairs = HEADS // 2
    lane = lax.broadcasted_iota(jnp.int32, (1, LANES), 1)
    low_half = (lane < HEAD).astype(F32).astype(BF16)
    high_half = (lane >= HEAD).astype(F32).astype(BF16)
    score_scale = HEAD ** (-0.5)

    for s in range(n_seq):
        x_s[0, s, seq - 32 :, :] = jnp.zeros((32, width), F32)
        grad_s[s, seq - 32 :, :] = jnp.zeros((32, width), F32)
    row_id = lax.broadcasted_iota(jnp.int32, (seq, seq), 0)
    col_id = lax.broadcasted_iota(jnp.int32, (seq, seq), 1)
    row_crop = sum((row_id >= llen * j).astype(jnp.int32) for j in range(1, group + 1))
    col_crop = sum((col_id >= llen * j).astype(jnp.int32) for j in range(1, group + 1))
    far = jnp.float32(-1e30)
    mask_s[0] = jnp.where(col_id < glen, jnp.float32(0), far)
    mask_s[1] = jnp.where(row_crop == col_crop, jnp.float32(0), far)
    one_row = (lax.broadcasted_iota(jnp.int32, (TILE, seq), 0) == 0).astype(F32).astype(BF16)
    for s in range(n_seq):
        for i in range(4):
            norm_t[i, s, width:, :] = one_row
        for i in range(2):
            mixed_t[i, s, width:, :] = one_row

    def live_rows(g):
        rows = lax.broadcasted_iota(jnp.int32, (seq, 1), 0)
        return (rows < llen * jnp.clip(count - g * group, 0, group)).astype(F32)

    for s in range(n_global):
        x_s[0, s, 0:glen, :] = global_in[s].astype(F32)
        grad_s[s, 0:glen, :] = global_cot[s].astype(F32)
    for j in range(n_local):
        s, at = n_global + j // group, llen * (j % group)
        x_s[0, s, at : at + llen, :] = local_in[j].astype(F32)
        grad_s[s, at : at + llen, :] = local_cot[j].astype(F32)
    for s in range(n_global, n_seq):
        grad_s[s] = grad_s[s] * live_rows(s - n_global)

    def row(ref, layer):
        return ref[...].astype(F32)[layer : layer + 1]

    for layer in range(2):
        gain, shift = row(attend_gain, layer), row(attend_shift, layer)
        bias = row(mixer_bias, layer)
        bias = jnp.concatenate([bias[:, :width], jnp.zeros((1, width), F32), bias[:, width:]], 1)
        out_bias = row(output_bias, layer)
        gain2, shift2 = row(feed_gain, layer), row(feed_shift, layer)
        bias_up, bias_down = row(expand_bias, layer), row(reduce_bias, layer)

        def attend(s, _):
            x = x_s[2 * layer, s]
            unit, scale = norm(x)
            unit_s[2 * layer, s] = unit
            scale_s[2 * layer, s] = scale
            normed = (unit * gain + shift).astype(BF16)
            norm_t[2 * layer, s, 0:width, :] = normed.T
            packed = (mm(normed, mixer_weight[layer]) + bias).astype(BF16)
            packed_s[layer, s] = packed
            mask = mask_s[jnp.where(s < n_global, 0, 1)]
            mixed = []
            for p in range(pairs):
                at = p * LANES
                query = packed[:, at : at + LANES]
                key = packed[:, width + at : width + at + LANES]
                value = packed[:, 2 * width + at : 2 * width + at + LANES]
                total = None
                for h, half in enumerate((low_half, high_half)):
                    scores = mm_nt(query * half, key) * (score_scale * LOG2E) + mask
                    power = jnp.exp2(scores - jnp.max(scores, -1, keepdims=True)).astype(BF16)
                    power_s[layer, s, 2 * p + h] = power
                    spread = jnp.broadcast_to(half, (seq, LANES))
                    term = mm(power, jnp.concatenate([value * half, spread], 1))
                    total = term if total is None else total + term
                inverse = 1.0 / total[:, LANES:]
                inverse_s[layer, s, :, at : at + LANES] = inverse
                mixed.append((total[:, :LANES] * inverse).astype(BF16))
            mixed = jnp.concatenate(mixed, 1)
            mixed_s[layer, s] = mixed
            mixed_t[layer, s, 0:width, :] = mixed.T
            x = x + mm(mixed, output_weight[layer]) + out_bias
            x_s[2 * layer + 1, s] = x.astype(BF16).astype(F32)
            return 0

        lax.fori_loop(0, n_seq, attend, 0)

        def feed(s, _):
            x = x_s[2 * layer + 1, s]
            unit, scale = norm(x)
            unit_s[2 * layer + 1, s] = unit
            scale_s[2 * layer + 1, s] = scale
            normed = (unit * gain2 + shift2).astype(BF16)
            norm_t[2 * layer + 1, s, 0:width, :] = normed.T
            for c in range(hidden // BLOCK):
                cols = slice(c * BLOCK, (c + 1) * BLOCK)
                up = mm(normed, expand_weight[layer, :, cols]) + bias_up[:, cols]
                act, slope = gelu_parts(up)
                act_s[layer, s, :, cols] = act.astype(BF16)
                slope_s[layer, s, :, cols] = slope.astype(BF16)
            x = x + mm(act_s[layer, s], reduce_weight[layer]) + bias_down
            x_s[2 * layer + 2, s] = x.astype(BF16).astype(F32)
            return 0

        lax.fori_loop(0, n_seq, feed, 0)

    for s in range(n_global):
        global_out[s] = x_s[4, s, 0:glen, :].astype(BF16)
    for j in range(n_local):
        s, at = n_global + j // group, llen * (j % group)
        alive = (count > j).astype(F32)
        local_out[j] = (x_s[4, s, at : at + llen, :] * alive).astype(BF16)

    def put_vector(at, value):
        for c in range(0, value.shape[1], BLOCK):
            piece = value[:, c : c + BLOCK]
            vec_s[at + c // BLOCK : at + c // BLOCK + 1, 0 : piece.shape[1]] = piece

    for layer in (1, 0):
        vec_s[...] = jnp.zeros_like(vec_s)
        gain2, gain = row(feed_gain, layer), row(attend_gain, layer)
        acc_s[...] = jnp.zeros_like(acc_s)

        def feed_back(s, _):
            grad = grad_s[s]
            grad_in = grad.astype(BF16)
            grad_low[s] = grad_in
            grad_t[s] = grad_in.T
            acc_s[2] = acc_s[2] + fold8(grad)
            for c in range(hidden // BLOCK):
                cols = slice(c * BLOCK, (c + 1) * BLOCK)
                dact = mm_nt(grad_in, reduce_weight[layer, cols, :])
                dup_s[s, :, cols] = (dact * slope_s[layer, s, :, cols].astype(F32)).astype(BF16)
            dh = mm_nt(dup_s[s], expand_weight[layer])
            unit, scale = unit_s[2 * layer + 1, s], scale_s[2 * layer + 1, s]
            acc_s[0] = acc_s[0] + fold8(dh * unit)
            acc_s[1] = acc_s[1] + fold8(dh)
            grad = grad + norm_back(dh, unit, scale, gain2)
            grad_s[s] = grad.astype(BF16).astype(F32)
            return 0

        lax.fori_loop(0, n_seq, feed_back, 0)
        put_vector(dims.at["feed_gain"], jnp.sum(acc_s[0], 0, keepdims=True))
        put_vector(dims.at["feed_shift"], jnp.sum(acc_s[1], 0, keepdims=True))
        put_vector(dims.at["reduce_bias"], jnp.sum(acc_s[2], 0, keepdims=True))

        blocks = hidden // BLOCK
        for c in range(blocks):
            cols = slice(c * BLOCK, (c + 1) * BLOCK)
            total = mm(norm_t[2 * layer + 1, 0], dup_s[0, :, cols])
            for s in range(1, n_seq):
                total = total + mm(norm_t[2 * layer + 1, s], dup_s[s, :, cols])
            feed_sum[layer, c * width : (c + 1) * width, :] = total[:width].astype(BF16)
            at = dims.at["expand_bias"] + c
            vec_s[at : at + 1, :] = total[width : width + 1]
            total = mm(grad_t[0], act_s[layer, 0, :, cols])
            for s in range(1, n_seq):
                total = total + mm(grad_t[s], act_s[layer, s, :, cols])
            at = (blocks + c) * width
            feed_sum[layer, at : at + width, :] = total.astype(BF16)

        acc_s[...] = jnp.zeros_like(acc_s)

        def attend_back(s, _):
            grad = grad_s[s]
            grad_in = grad.astype(BF16)
            grad_low[s] = grad_in
            dmixed = mm_nt(grad_in, output_weight[layer])
            parts = [None] * (3 * pairs)
            for p in range(pairs):
                at = p * LANES
                query = packed_s[layer, s, :, at : at + LANES]
                key = packed_s[layer, s, :, width + at : width + at + LANES]
                value = packed_s[layer, s, :, 2 * width + at : 2 * width + at + LANES]
                dm = dmixed[:, at : at + LANES] * inverse_s[layer, s, :, at : at + LANES]
                inner = -(dm * mixed_s[layer, s, :, at : at + LANES].astype(F32)).astype(BF16)
                dm = dm.astype(BF16)
                wide_value = jnp.concatenate([value, jnp.ones_like(value)], 1)
                dq = dk = dv = None
                for h, half in enumerate((low_half, high_half)):
                    power = power_s[layer, s, 2 * p + h]
                    dm_half = dm * half
                    left = jnp.concatenate([dm_half, inner * half], 1)
                    ds = (power.astype(F32) * mm_nt(left, wide_value)).astype(BF16)
                    terms = (mm(ds, key * half), mm_tn(ds, query * half), mm_tn(power, dm_half))
                    dq = terms[0] if dq is None else dq + terms[0]
                    dk = terms[1] if dk is None else dk + terms[1]
                    dv = terms[2] if dv is None else dv + terms[2]
                parts[p] = (dq * score_scale).astype(BF16)
                parts[pairs + p] = (dk * score_scale).astype(BF16)
                parts[2 * pairs + p] = dv.astype(BF16)
            dpacked = jnp.concatenate(parts, 1)
            dup_s[s, :, 0 : 3 * width] = dpacked
            dh = mm_nt(dpacked, mixer_weight[layer])
            unit, scale = unit_s[2 * layer, s], scale_s[2 * layer, s]
            acc_s[0] = acc_s[0] + fold8(dh * unit)
            acc_s[1] = acc_s[1] + fold8(dh)
            grad = grad + norm_back(dh, unit, scale, gain)
            grad_s[s] = grad.astype(BF16).astype(F32)
            return 0

        lax.fori_loop(0, n_seq, attend_back, 0)
        put_vector(dims.at["attend_gain"], jnp.sum(acc_s[0], 0, keepdims=True))
        put_vector(dims.at["attend_shift"], jnp.sum(acc_s[1], 0, keepdims=True))

        bias_parts = []
        for c in range(0, 4 * width, LANES):
            if c < 3 * width:
                left, right, at = norm_t.at[2 * layer], dup_s, c
            else:
                left, right, at = mixed_t.at[layer], grad_low, c - 3 * width
            total = mm(left[0], right[0, :, at : at + LANES])
            for s in range(1, n_seq):
                total = total + mm(left[s], right[s, :, at : at + LANES])
            top = (c // BLOCK) * width
            side = c % BLOCK
            attend_sum[layer, top : top + width, side : side + LANES] = total[:width].astype(BF16)
            bias_parts.append(total[width : width + 1])
        each = width // LANES
        put_vector(
            dims.at["mixer_bias"],
            jnp.concatenate(bias_parts[:each] + bias_parts[2 * each : 3 * each], 1),
        )
        put_vector(dims.at["output_bias"], jnp.concatenate(bias_parts[3 * each :], 1))
        top = 4 * width * width // BLOCK
        attend_sum[layer, top : top + dims.vec_rows, :] = vec_s[...].astype(BF16)

    for s in range(n_global):
        global_back[s] = grad_s[s, 0:glen, :].astype(BF16)
    for j in range(n_local):
        s, at = n_global + j // group, llen * (j % group)
        local_back[j] = grad_s[s, at : at + llen, :].astype(BF16)


class Dims:
    def __init__(self, global_crops, local_crops, hidden):
        self.n_global, self.glen, self.width = global_crops.shape
        self.n_local, self.llen, _ = local_crops.shape
        self.hidden = hidden
        self.seq = up_to(self.glen, TILE)
        self.group = self.seq // self.llen
        while self.n_local % self.group:
            self.group -= 1
        self.n_seq = self.n_global + self.n_local // self.group
        sizes = (
            ("attend_gain", self.width),
            ("attend_shift", self.width),
            ("mixer_bias", 2 * self.width),
            ("output_bias", self.width),
            ("feed_gain", self.width),
            ("feed_shift", self.width),
            ("expand_bias", hidden),
            ("reduce_bias", self.width),
        )
        self.at, row = {}, 0
        for name, size in sizes:
            self.at[name] = row
            row += -(-size // BLOCK)
        self.vec_rows = up_to(row, TILE)
        self.feed_rows = 2 * self.width * hidden // BLOCK
        self.attend_rows = 4 * self.width * self.width // BLOCK + self.vec_rows


def run_kernel(counts, arrays, dims):
    d = dims
    n, seq, width, hidden = d.n_seq, d.seq, d.width, d.hidden
    crops = [jax.ShapeDtypeStruct(a.shape, BF16) for a in arrays[:2]]
    outs = crops + crops
    outs += [
        jax.ShapeDtypeStruct((2, d.feed_rows, BLOCK), BF16),
        jax.ShapeDtypeStruct((2, d.attend_rows, BLOCK), BF16),
    ]
    scratch = [
        pltpu.VMEM((5, n, seq, width), F32),
        pltpu.VMEM((4, n, seq, width), F32),
        pltpu.VMEM((4, n, seq, 1), F32),
        pltpu.VMEM((4, n, width + TILE, seq), BF16),
        pltpu.VMEM((2, n, seq, 3 * width), BF16),
        pltpu.VMEM((2, n, HEADS, seq, seq), BF16),
        pltpu.VMEM((2, n, seq, width), F32),
        pltpu.VMEM((2, n, seq, width), BF16),
        pltpu.VMEM((2, n, width + TILE, seq), BF16),
        pltpu.VMEM((2, n, seq, hidden), BF16),
        pltpu.VMEM((2, n, seq, hidden), BF16),
        pltpu.VMEM((n, seq, width), F32),
        pltpu.VMEM((n, seq, width), BF16),
        pltpu.VMEM((n, width, seq), BF16),
        pltpu.VMEM((n, seq, hidden), BF16),
        pltpu.VMEM((2, seq, seq), F32),
        pltpu.VMEM((d.vec_rows, BLOCK), F32),
        pltpu.VMEM((3, 8, width), F32),
    ]
    vmem = pl.BlockSpec(memory_space=pltpu.VMEM)
    return pl.pallas_call(
        functools.partial(kernel, d),
        out_shape=outs,
        in_specs=[pl.BlockSpec(memory_space=pltpu.SMEM)] + [vmem] * len(arrays),
        out_specs=[vmem] * len(outs),
        scratch_shapes=scratch,
        compiler_params=pltpu.CompilerParams(vmem_limit_bytes=62 * 1024 * 1024),
    )(counts, *arrays)


def shards(
    global_crops,
    local_crops,
    local_count,
    global_cotangent,
    local_cotangent,
    *weights,
):
    dims = Dims(global_crops, local_crops, weights[8].shape[2])
    width, hidden = dims.width, dims.hidden
    outs = run_kernel(
        local_count, (global_crops, local_crops, global_cotangent, local_cotangent) + weights, dims
    )
    feed, attend = lax.psum((outs[4], outs[5]), ("dp", "section"))
    feed, attend = feed.astype(F32), attend.astype(F32)

    def blocks(array, first, count):
        part = array[:, first * width : (first + count) * width]
        return part.reshape(2, count, width, BLOCK).transpose(0, 2, 1, 3).reshape(2, width, -1)

    count = hidden // BLOCK
    expand_grad = blocks(feed, 0, count)
    reduce_grad = blocks(feed, count, count).transpose(0, 2, 1)
    both = blocks(attend, 0, 4 * width // BLOCK)
    top = 4 * width * width // BLOCK

    def vector(name, size):
        at = top + dims.at[name]
        return attend[:, at : at + -(-size // BLOCK)].reshape(2, -1)[:, :size]

    return (
        outs[0],
        outs[1],
        outs[2],
        outs[3],
        vector("attend_gain", width),
        vector("attend_shift", width),
        both[:, :, : 3 * width],
        vector("mixer_bias", 2 * width),
        both[:, :, 3 * width :],
        vector("output_bias", width),
        vector("feed_gain", width),
        vector("feed_shift", width),
        expand_grad,
        vector("expand_bias", hidden),
        reduce_grad,
        vector("reduce_bias", width),
    )


def solution(mesh):
    crops = P(("dp", "section"), None, None)
    return jax.shard_map(
        shards,
        mesh=mesh,
        in_specs=(crops, crops, P("dp"), crops, crops) + (P(),) * 12,
        out_specs=(crops,) * 4 + (P(),) * 12,
        check_vma=False,
    )
```

```python
import functools

import jax
import jax.numpy as jnp
from jax import lax
from jax.experimental import pallas as pl
from jax.experimental.pallas import tpu as pltpu
from jax.sharding import PartitionSpec as P

HEADS = 6
HEAD = 64
EPS = 1e-06
TILE = 16
LANES = 128
BLOCK = 256
LOG2E = 1.4426950408889634
F32 = jnp.float32
BF16 = jnp.bfloat16


def up_to(value, step):
    return -(-value // step) * step


def mm(left, right):
    return lax.dot_general(left, right, (((1,), (0,)), ((), ())), preferred_element_type=F32)


def mm_nt(left, right):
    return lax.dot_general(left, right, (((1,), (1,)), ((), ())), preferred_element_type=F32)


def mm_tn(left, right):
    return lax.dot_general(left, right, (((0,), (0,)), ((), ())), preferred_element_type=F32)


def norm(rows):
    centred = rows - jnp.mean(rows, -1, keepdims=True)
    scale = lax.rsqrt(jnp.mean(centred * centred, -1, keepdims=True) + EPS)
    return centred * scale, scale


def norm_back(grad, unit, scale, gain):
    slope = grad * gain
    first = jnp.mean(slope, -1, keepdims=True)
    second = jnp.mean(slope * unit, -1, keepdims=True)
    return scale * (slope - first - unit * second)


def gelu_parts(u):
    size = jnp.abs(u)
    d = 1.0 + (0.3275911 * 0.7071067811865476) * size
    t = pl.reciprocal(d, approx=True)
    t = t * (2.0 - d * t)
    poly = 0.5 * 1.061405429
    for a in (-1.453152027, 1.421413741, -0.284496736, 0.254829592):
        poly = poly * t + 0.5 * a
    bell = jnp.exp2((u * u) * (-0.5 * LOG2E))
    tail = poly * t * bell
    phi = jnp.where(u < 0.0, tail, 1.0 - tail)
    return u * phi, phi + (u * bell) * 0.3989422804014327


def fold8(value):
    rows, width = value.shape
    return jnp.sum(value.reshape(rows // 8, 8, width), 0)


def kernel(
    dims,
    counts,
    global_in,
    local_in,
    global_cot,
    local_cot,
    attend_gain,
    attend_shift,
    mixer_weight,
    mixer_bias,
    output_weight,
    output_bias,
    feed_gain,
    feed_shift,
    expand_weight,
    expand_bias,
    reduce_weight,
    reduce_bias,
    global_out,
    local_out,
    global_back,
    local_back,
    feed_all,
    attend_all,
    feed_sum,
    attend_sum,
    x_s,
    unit_s,
    scale_s,
    norm_t,
    packed_s,
    power_s,
    inverse_s,
    mixed_s,
    mixed_t,
    act_s,
    slope_s,
    grad_s,
    grad_low,
    grad_t,
    dup_s,
    mask_s,
    vec_s,
    acc_s,
    *wires,
):
    seq, group, width = dims.seq, dims.group, dims.width
    glen, llen = dims.glen, dims.llen
    n_global, n_local, n_seq = dims.n_global, dims.n_local, dims.n_seq
    hidden = dims.hidden
    count = counts[lax.axis_index("section")]
    pairs = HEADS // 2
    lane = lax.broadcasted_iota(jnp.int32, (1, LANES), 1)
    low_half = (lane < HEAD).astype(F32).astype(BF16)
    high_half = (lane >= HEAD).astype(F32).astype(BF16)
    score_scale = HEAD ** (-0.5)

    net = Net(dims.wires)
    net.greet()
    n_stage = len(dims.wires)
    chunks = []
    for i, (sums, alls, layer) in enumerate(
        ((feed_sum, feed_all, 1), (attend_sum, attend_all, 1), (feed_sum, feed_all, 0), (attend_sum, attend_all, 0))
    ):
        kind = i % 2
        landing = wires[kind * n_stage : (kind + 1) * n_stage]
        sems = [w.at[i] for w in wires[2 * n_stage : 2 * n_stage + 3]]
        sems.append(wires[2 * n_stage + 3].at[kind])
        chunks.append(Chunk(net, sums.at[layer], alls.at[layer], landing, sems, i // 2))
    feed_1, attend_1, feed_0, attend_0 = chunks

    def after(s, plan):
        for i, steps in plan.items():

            @pl.when(s == i)
            def _():
                for chunk in steps:
                    chunk.advance()

    for s in range(n_seq):
        x_s[s, seq - 32 :, :] = jnp.zeros((32, width), F32)
        grad_s[s, seq - 32 :, :] = jnp.zeros((32, width), F32)
    row_id = lax.broadcasted_iota(jnp.int32, (seq, seq), 0)
    col_id = lax.broadcasted_iota(jnp.int32, (seq, seq), 1)
    row_crop = sum((row_id >= llen * j).astype(jnp.int32) for j in range(1, group + 1))
    col_crop = sum((col_id >= llen * j).astype(jnp.int32) for j in range(1, group + 1))
    far = jnp.float32(-1e30)
    mask_s[0] = jnp.where(col_id < glen, jnp.float32(0), far).astype(BF16)
    mask_s[1] = jnp.where(row_crop == col_crop, jnp.float32(0), far).astype(BF16)
    one_row = (lax.broadcasted_iota(jnp.int32, (TILE, seq), 0) == 0).astype(F32).astype(BF16)
    for s in range(n_seq):
        for i in range(4):
            norm_t[i, s, width:, :] = one_row
        for i in range(2):
            mixed_t[i, s, width:, :] = one_row

    def live_rows(g):
        rows = lax.broadcasted_iota(jnp.int32, (seq, 1), 0)
        return (rows < llen * jnp.clip(count - g * group, 0, group)).astype(F32)

    for s in range(n_global):
        x_s[s, 0:glen, :] = global_in[s].astype(F32)
        grad_s[s, 0:glen, :] = global_cot[s].astype(F32)
    for j in range(n_local):
        s, at = n_global + j // group, llen * (j % group)
        x_s[s, at : at + llen, :] = local_in[j].astype(F32)
        grad_s[s, at : at + llen, :] = local_cot[j].astype(F32)
    for s in range(n_global, n_seq):
        grad_s[s] = grad_s[s] * live_rows(s - n_global)

    def row(ref, layer):
        return ref[...].astype(F32)[layer : layer + 1]

    def start_back(s, grad):
        grad_in = grad.astype(BF16)
        grad_t[s] = grad_in.T
        acc_s[2] = acc_s[2] + fold8(grad)
        return grad_in

    def end_back(s, grad, unit, scale, gain, dh):
        unit = unit.astype(F32)
        acc_s[0] = acc_s[0] + fold8(dh * unit)
        acc_s[1] = acc_s[1] + fold8(dh)
        grad = grad + norm_back(dh, unit, scale, gain)
        grad_s[s] = grad.astype(BF16).astype(F32)

    for layer in range(2):
        gain, shift = row(attend_gain, layer), row(attend_shift, layer)
        bias = row(mixer_bias, layer)
        bias = jnp.concatenate([bias[:, :width], jnp.zeros((1, width), F32), bias[:, width:]], 1)
        out_bias = row(output_bias, layer)
        gain2, shift2 = row(feed_gain, layer), row(feed_shift, layer)
        bias_up, bias_down = row(expand_bias, layer), row(reduce_bias, layer)

        def attend(s, _):
            x = x_s[s]
            unit, scale = norm(x)
            unit_s[2 * layer, s] = unit.astype(BF16)
            scale_s[2 * layer, s] = scale
            normed = (unit * gain + shift).astype(BF16)
            norm_t[2 * layer, s, 0:width, :] = normed.T
            packed = (mm(normed, mixer_weight[layer]) + bias).astype(BF16)
            packed_s[layer, s] = packed
            mask = mask_s[jnp.where(s < n_global, 0, 1)].astype(F32)
            mixed = []
            for p in range(pairs):
                at = p * LANES
                query = packed[:, at : at + LANES]
                key = packed[:, width + at : width + at + LANES]
                value = packed[:, 2 * width + at : 2 * width + at + LANES]
                total = None
                for h, half in enumerate((low_half, high_half)):
                    scores = mm_nt(query * half, key) * (score_scale * LOG2E) + mask
                    power = jnp.exp2(scores - jnp.max(scores, -1, keepdims=True)).astype(BF16)
                    power_s[layer, s, 2 * p + h] = power
                    spread = jnp.broadcast_to(half, (seq, LANES))
                    term = mm(power, jnp.concatenate([value * half, spread], 1))
                    total = term if total is None else total + term
                inverse = 1.0 / total[:, LANES:]
                inverse_s[layer, s, :, at : at + LANES] = inverse
                mixed.append((total[:, :LANES] * inverse).astype(BF16))
            mixed = jnp.concatenate(mixed, 1)
            mixed_s[layer, s] = mixed
            mixed_t[layer, s, 0:width, :] = mixed.T
            x = x + mm(mixed, output_weight[layer]) + out_bias
            x_s[s] = x.astype(BF16).astype(F32)
            return 0

        lax.fori_loop(0, n_seq, attend, 0)

        def feed(s, _):
            x = x_s[s]
            unit, scale = norm(x)
            normed = (unit * gain2 + shift2).astype(BF16)
            norm_t[2 * layer + 1, s, 0:width, :] = normed.T
            if layer == 0:
                unit_s[1, s] = unit.astype(BF16)
                scale_s[1, s] = scale
            else:
                grad = grad_s[s]
                grad_in = start_back(s, grad)
            for c in range(hidden // BLOCK):
                cols = slice(c * BLOCK, (c + 1) * BLOCK)
                up = mm(normed, expand_weight[layer, :, cols]) + bias_up[:, cols]
                act, slope = gelu_parts(up)
                act_s[layer, s, :, cols] = act.astype(BF16)
                if layer == 0:
                    slope_s[s, :, cols] = slope.astype(BF16)
                else:
                    dact = mm_nt(grad_in, reduce_weight[layer, cols, :])
                    dup_s[s, :, cols] = (dact * slope).astype(BF16)
            x = x + mm(act_s[layer, s], reduce_weight[layer]) + bias_down
            x_s[s] = x.astype(BF16).astype(F32)
            if layer == 1:
                end_back(s, grad, unit, scale, gain2, mm_nt(dup_s[s], expand_weight[layer]))
            return 0

        if layer == 1:
            acc_s[...] = jnp.zeros_like(acc_s)
        lax.fori_loop(0, n_seq, feed, 0)

    for s in range(n_global):
        global_out[s] = x_s[s, 0:glen, :].astype(BF16)
    for j in range(n_local):
        s, at = n_global + j // group, llen * (j % group)
        alive = (count > j).astype(F32)
        local_out[j] = (x_s[s, at : at + llen, :] * alive).astype(BF16)

    def put_vector(at, value):
        for c in range(0, value.shape[1], BLOCK):
            piece = value[:, c : c + BLOCK]
            vec_s[at + c // BLOCK : at + c // BLOCK + 1, 0 : piece.shape[1]] = piece

    for layer in (1, 0):
        vec_s[...] = jnp.zeros_like(vec_s)
        gain2, gain = row(feed_gain, layer), row(attend_gain, layer)

        def feed_back(s, _):
            grad = grad_s[s]
            grad_in = start_back(s, grad)
            for c in range(hidden // BLOCK):
                cols = slice(c * BLOCK, (c + 1) * BLOCK)
                dact = mm_nt(grad_in, reduce_weight[layer, cols, :])
                dup_s[s, :, cols] = (dact * slope_s[s, :, cols].astype(F32)).astype(BF16)
            dh = mm_nt(dup_s[s], expand_weight[layer])
            end_back(s, grad, unit_s[1, s], scale_s[1, s], gain2, dh)
            after(s, {0: [feed_1], 1: [attend_1, feed_1], 2: [feed_1], 3: [attend_1]})
            return 0

        if layer == 0:
            acc_s[...] = jnp.zeros_like(acc_s)
            lax.fori_loop(0, n_seq, feed_back, 0)
        put_vector(dims.at["feed_gain"], jnp.sum(acc_s[0], 0, keepdims=True))
        put_vector(dims.at["feed_shift"], jnp.sum(acc_s[1], 0, keepdims=True))
        put_vector(dims.at["reduce_bias"], jnp.sum(acc_s[2], 0, keepdims=True))

        blocks = hidden // BLOCK
        for c in range(blocks):
            cols = slice(c * BLOCK, (c + 1) * BLOCK)
            total = mm(norm_t[2 * layer + 1, 0], dup_s[0, :, cols])
            for s in range(1, n_seq):
                total = total + mm(norm_t[2 * layer + 1, s], dup_s[s, :, cols])
            feed_sum[layer, c * width : (c + 1) * width, :] = total[:width].astype(BF16)
            at = dims.at["expand_bias"] + c
            vec_s[at : at + 1, :] = total[width : width + 1]
            total = mm(grad_t[0], act_s[layer, 0, :, cols])
            for s in range(1, n_seq):
                total = total + mm(grad_t[s], act_s[layer, s, :, cols])
            at = (blocks + c) * width
            feed_sum[layer, at : at + width, :] = total.astype(BF16)
            if layer == 0 and c == 2:
                feed_1.advance()
                attend_1.advance()
        if layer == 1:
            net.wait_greeting()
            feed_1.begin()
        else:
            feed_0.begin()

        acc_s[...] = jnp.zeros_like(acc_s)

        def attend_back(s, _):
            grad = grad_s[s]
            grad_in = grad.astype(BF16)
            grad_low[s] = grad_in
            dmixed = mm_nt(grad_in, output_weight[layer])
            parts = [None] * (3 * pairs)
            for p in range(pairs):
                at = p * LANES
                query = packed_s[layer, s, :, at : at + LANES]
                key = packed_s[layer, s, :, width + at : width + at + LANES]
                value = packed_s[layer, s, :, 2 * width + at : 2 * width + at + LANES]
                dm = dmixed[:, at : at + LANES] * inverse_s[layer, s, :, at : at + LANES]
                inner = -(dm * mixed_s[layer, s, :, at : at + LANES].astype(F32)).astype(BF16)
                dm = dm.astype(BF16)
                wide_value = jnp.concatenate([value, jnp.ones_like(value)], 1)
                dq = dk = dv = None
                for h, half in enumerate((low_half, high_half)):
                    power = power_s[layer, s, 2 * p + h]
                    dm_half = dm * half
                    left = jnp.concatenate([dm_half, inner * half], 1)
                    ds = (power.astype(F32) * mm_nt(left, wide_value)).astype(BF16)
                    terms = (mm(ds, key * half), mm_tn(ds, query * half), mm_tn(power, dm_half))
                    dq = terms[0] if dq is None else dq + terms[0]
                    dk = terms[1] if dk is None else dk + terms[1]
                    dv = terms[2] if dv is None else dv + terms[2]
                parts[p] = (dq * score_scale).astype(BF16)
                parts[pairs + p] = (dk * score_scale).astype(BF16)
                parts[2 * pairs + p] = dv.astype(BF16)
            dpacked = jnp.concatenate(parts, 1)
            dup_s[s, :, 0 : 3 * width] = dpacked
            dh = mm_nt(dpacked, mixer_weight[layer])
            end_back(s, grad, unit_s[2 * layer, s], scale_s[2 * layer, s], gain, dh)
            if layer == 1:
                after(s, {0: [feed_1], 3: [feed_1]})
            else:
                after(s, {0: [feed_0, feed_1], 1: [attend_1], 2: [feed_0, feed_1], 3: [attend_1]})
            return 0

        lax.fori_loop(0, n_seq, attend_back, 0)
        put_vector(dims.at["attend_gain"], jnp.sum(acc_s[0], 0, keepdims=True))
        put_vector(dims.at["attend_shift"], jnp.sum(acc_s[1], 0, keepdims=True))

        bias_parts = []
        for columns, left, right in (
            (3 * width, norm_t.at[2 * layer], dup_s),
            (width, mixed_t.at[layer], grad_low),
        ):
            for c in range(0, columns, BLOCK):
                size = min(BLOCK, columns - c)
                total = mm(left[0], right[0, :, c : c + size])
                for s in range(1, n_seq):
                    total = total + mm(left[s], right[s, :, c : c + size])
                for k in range(0, size, LANES):
                    m = (c + k) // LANES
                    if columns == width:
                        block, side = 2 * m + 1, LANES
                    else:
                        block, side = 2 * (m // 3) + (m % 3) // 2, (m % 3 % 2) * LANES
                    part = total[:, k : k + LANES]
                    attend_sum[layer, block * width : (block + 1) * width, side : side + LANES] = part[:width].astype(BF16)
                    bias_parts.append(part[width : width + 1])
            if layer == 0 and columns > width:
                feed_0.advance()
                attend_1.advance()
        each = width // LANES
        put_vector(
            dims.at["mixer_bias"],
            jnp.concatenate(bias_parts[:each] + bias_parts[2 * each : 3 * each], 1),
        )
        put_vector(dims.at["output_bias"], jnp.concatenate(bias_parts[3 * each :], 1))
        top = dims.vec_top
        attend_sum[layer, top : top + dims.vec_rows, :] = vec_s[...].astype(BF16)
        if dims.attend_rows > top + dims.vec_rows:
            rest = dims.attend_rows - top - dims.vec_rows
            attend_sum[layer, top + dims.vec_rows :, :] = jnp.zeros((rest, BLOCK), BF16)
        if dims.feed_rows > 2 * hidden * width // BLOCK:
            rest = dims.feed_rows - 2 * hidden * width // BLOCK
            feed_sum[layer, dims.feed_rows - rest :, :] = jnp.zeros((rest, BLOCK), BF16)
        (attend_1 if layer == 1 else attend_0).begin()

    left = True
    while left:
        left = False
        for chunk in (attend_1, feed_0, attend_0):
            if chunk.step < 2 * n_stage:
                chunk.advance()
                left = True
    for chunk in chunks:
        chunk.finish()
    for s in range(n_global):
        global_back[s] = grad_s[s, 0:glen, :].astype(BF16)
    for j in range(n_local):
        s, at = n_global + j // group, llen * (j % group)
        local_back[j] = grad_s[s, at : at + llen, :].astype(BF16)


class Wire:
    def __init__(self, size, first, second):
        self.size, self.first, self.second = size, first, second


def wires_of(mesh):
    names = mesh.axis_names
    places = {}
    for axis, name in enumerate(names):
        line = [mesh.devices[tuple(i if a == axis else 0 for a in range(2))] for i in range(mesh.devices.shape[axis])]
        spots = [(d.core_on_chip,) + tuple(d.coords) for d in line]
        found, total = [], 1
        for k in range(4):
            values = sorted({p[k] for p in spots})
            if len(values) > 1:
                stride = next(i for i, p in enumerate(spots) if p[k] != spots[0][k])
                found.append((k, axis, stride, len(values)))
                total *= len(values)
        good = total == len(line)
        for k, _, stride, size in found:
            values = [p[k] for p in spots]
            good = good and all(v == values[i // stride % size * stride] for i, v in enumerate(values))
        if not good:
            found = [(4 + axis, axis, 1, len(line))]
        for k, axis, stride, size in found:
            places[k] = (axis, stride, size)
    wires = []
    if 0 in places:
        wires.append(Wire(places[0][2], places[0], places[0]))
    if 0 in places and 1 in places and 2 in places and places[1][2] == places[2][2]:
        wires.append(Wire(places[1][2], places[1], places[2]))
        wires.append(Wire(places[1][2], places[2], places[1]))
        order = [3, 4, 5]
    else:
        order = [1, 2, 3, 4, 5]
    for k in order:
        if k in places:
            wires.append(Wire(places[k][2], places[k], places[k]))
    return wires


class Net:
    def __init__(self, wires):
        self.axes = ("dp", "section")
        self.here = [lax.axis_index(a) for a in self.axes]
        self.wires = wires
        first = wires[0]
        odd = self.spot(first.first) % 2 if first.size == 2 else 0
        self.odd = odd
        self.at = []
        for w in wires:
            a, b = self.spot(w.first), self.spot(w.second)
            self.at.append(a if w.first == w.second else a + odd * (b - a))

    def spot(self, place):
        axis, stride, size = place
        return self.here[axis] // stride % size

    def peer(self, stage, k):
        w = self.wires[stage]
        place = (self.at[stage] + k) % w.size
        move = place - self.at[stage]
        target = list(self.here)
        if w.first == w.second:
            target[w.first[0]] = target[w.first[0]] + move * w.first[1]
        else:
            target[w.first[0]] = target[w.first[0]] + move * w.first[1] * (1 - self.odd)
            target[w.second[0]] = target[w.second[0]] + move * w.second[1] * self.odd
        return tuple(target), place

    def greet(self):
        barrier = pltpu.get_barrier_semaphore()
        for stage, w in enumerate(self.wires):
            for k in range(1, w.size):
                pl.semaphore_signal(barrier, inc=1, device_id=self.peer(stage, k)[0], device_id_type=pl.DeviceIdType.MESH)

    def wait_greeting(self):
        pl.semaphore_wait(pltpu.get_barrier_semaphore(), sum(w.size - 1 for w in self.wires))


class Chunk:
    def __init__(self, net, sums, alls, landing, sems, turn):
        self.net, self.sums, self.alls, self.landing = net, sums, alls, landing
        self.send, self.recv, self.local, self.free = sems
        self.turn = turn
        size, start = sums.shape[0], 0
        self.unit = size
        for w in net.wires:
            self.unit //= w.size
        self.size, self.start = [], []
        for stage, w in enumerate(net.wires):
            size //= w.size
            self.size.append(size)
            self.start.append((start, size))
            start = start + net.at[stage] * size
        self.own = start
        self.stages = len(net.wires)
        self.step = 0
        self.sem_at, at = {}, 0
        for phase in range(2):
            for stage, w in enumerate(net.wires):
                for k in range(1, w.size):
                    self.sem_at[phase, stage, k] = at
                    at += 1

    def rows(self, stage, place):
        start, size = self.start[stage]
        return pl.ds(pl.multiple_of(start + place * size, TILE), size)

    def copy(self, phase, stage, k):
        target, place = self.net.peer(stage, k)
        at = self.sem_at[phase, stage, k]
        if phase == 0:
            source, to = self.sums.at[self.rows(stage, place)], self.landing[stage].at[k - 1]
        else:
            rows = self.rows(stage, self.net.at[stage])
            source = (self.sums if stage == self.stages - 1 else self.alls).at[rows]
            to = self.alls.at[rows]
        return pltpu.make_async_remote_copy(
            src_ref=source,
            dst_ref=to,
            send_sem=self.send.at[at],
            recv_sem=self.recv.at[at],
            device_id=target,
            device_id_type=pl.DeviceIdType.MESH,
        )

    def arrival(self, stage, k):
        target, place = self.net.peer(stage, self.net.wires[stage].size - k)
        at = self.sem_at[1, stage, k]
        landed = self.alls.at[self.rows(stage, place)]
        return pltpu.make_async_remote_copy(
            src_ref=landed,
            dst_ref=landed,
            send_sem=self.send.at[at],
            recv_sem=self.recv.at[at],
            device_id=target,
            device_id_type=pl.DeviceIdType.MESH,
        )

    def start_stage(self, phase, stage):
        if phase == 0 and self.turn == 1:
            pl.semaphore_wait(self.free.at[stage], self.net.wires[stage].size - 1)
        for k in range(1, self.net.wires[stage].size):
            self.copy(phase, stage, k).start()

    def begin(self):
        self.start_stage(0, 0)

    def own_copy(self):
        rows = self.rows(self.stages - 1, self.net.at[-1])
        return pltpu.make_async_copy(self.sums.at[rows], self.alls.at[rows], self.local.at[0])

    def advance(self):
        step = self.step
        if step == 2 * self.stages:
            return
        self.step += 1
        if step < self.stages:
            peers = range(1, self.net.wires[step].size)
            for k in peers:
                self.copy(0, step, k).wait_recv()
            base = self.start[step][0] + self.net.at[step] * self.size[step]
            landing = self.landing[step]

            def add(i, _):
                at = pl.ds(pl.multiple_of(base + i * self.unit, TILE), self.unit)
                total = self.sums[at, :].astype(F32)
                for k in peers:
                    total = total + landing[k - 1, pl.ds(pl.multiple_of(i * self.unit, TILE), self.unit), :].astype(F32)
                self.sums[at, :] = total.astype(BF16)
                return 0

            lax.fori_loop(0, self.size[step] // self.unit, add, 0)
            if self.turn == 0:
                for k in peers:
                    target = self.net.peer(step, k)[0]
                    pl.semaphore_signal(self.free.at[step], inc=1, device_id=target, device_id_type=pl.DeviceIdType.MESH)
            if step + 1 < self.stages:
                self.start_stage(0, step + 1)
            else:
                self.own_copy().start()
                self.start_stage(1, step)
        else:
            stage = 2 * self.stages - 1 - step
            for k in range(1, self.net.wires[stage].size):
                self.arrival(stage, k).wait_recv()
            if stage == self.stages - 1:
                self.own_copy().wait()
            if stage > 0:
                self.start_stage(1, stage - 1)

    def finish(self):
        assert self.step == 2 * self.stages
        for phase, stage, k in self.sem_at:
            self.copy(phase, stage, k).wait_send()


class Dims:
    def __init__(self, global_crops, local_crops, hidden, wires):
        self.wires = wires
        self.n_global, self.glen, self.width = global_crops.shape
        self.n_local, self.llen, _ = local_crops.shape
        self.hidden = hidden
        self.seq = up_to(self.glen, TILE)
        self.group = self.seq // self.llen
        while self.n_local % self.group:
            self.group -= 1
        self.n_seq = self.n_global + self.n_local // self.group
        sizes = (
            ("attend_gain", self.width),
            ("attend_shift", self.width),
            ("mixer_bias", 2 * self.width),
            ("output_bias", self.width),
            ("feed_gain", self.width),
            ("feed_shift", self.width),
            ("expand_bias", hidden),
            ("reduce_bias", self.width),
        )
        self.names, self.sizes = [name for name, _ in sizes], dict(sizes)
        self.at, row = {}, 0
        for name, size in sizes:
            self.at[name] = row
            row += -(-size // BLOCK)
        self.vec_rows = 2 * TILE
        assert row <= self.vec_rows and self.width * hidden % self.vec_rows == 0
        step = TILE
        for w in wires:
            step *= w.size
        self.vec_top = 4 * self.width * self.width // BLOCK
        self.feed_rows = up_to(2 * self.width * hidden // BLOCK, step)
        self.attend_rows = up_to(self.vec_top + self.vec_rows, step)


def run_kernel(counts, arrays, dims):
    d = dims
    n, seq, width, hidden = d.n_seq, d.seq, d.width, d.hidden
    crops = [jax.ShapeDtypeStruct(a.shape, BF16) for a in arrays[:2]]
    outs = crops + crops
    outs += [
        jax.ShapeDtypeStruct((2, d.feed_rows, BLOCK), BF16),
        jax.ShapeDtypeStruct((2, d.attend_rows, BLOCK), BF16),
    ]
    scratch = [
        pltpu.VMEM((2, d.feed_rows, BLOCK), BF16),
        pltpu.VMEM((2, d.attend_rows, BLOCK), BF16),
        pltpu.VMEM((n, seq, width), F32),
        pltpu.VMEM((3, n, seq, width), BF16),
        pltpu.VMEM((3, n, seq, 1), F32),
        pltpu.VMEM((4, n, width + TILE, seq), BF16),
        pltpu.VMEM((2, n, seq, 3 * width), BF16),
        pltpu.VMEM((2, n, HEADS, seq, seq), BF16),
        pltpu.VMEM((2, n, seq, width), F32),
        pltpu.VMEM((2, n, seq, width), BF16),
        pltpu.VMEM((2, n, width + TILE, seq), BF16),
        pltpu.VMEM((2, n, seq, hidden), BF16),
        pltpu.VMEM((n, seq, hidden), BF16),
        pltpu.VMEM((n, seq, width), F32),
        pltpu.VMEM((n, seq, width), BF16),
        pltpu.VMEM((n, width, seq), BF16),
        pltpu.VMEM((n, seq, hidden), BF16),
        pltpu.VMEM((2, seq, seq), BF16),
        pltpu.VMEM((d.vec_rows, BLOCK), F32),
        pltpu.VMEM((3, 8, width), F32),
    ]
    for rows in (d.feed_rows, d.attend_rows):
        for w in d.wires:
            rows //= w.size
            scratch.append(pltpu.VMEM((w.size - 1, rows, BLOCK), BF16))
    peers = 2 * sum(w.size - 1 for w in d.wires)
    scratch += [
        pltpu.SemaphoreType.DMA((4, peers)),
        pltpu.SemaphoreType.DMA((4, peers)),
        pltpu.SemaphoreType.DMA((4, 1)),
        pltpu.SemaphoreType.REGULAR((2, len(d.wires))),
    ]
    vmem = pl.BlockSpec(memory_space=pltpu.VMEM)
    anywhere = pl.BlockSpec(memory_space=pl.ANY)
    return pl.pallas_call(
        functools.partial(kernel, d),
        out_shape=outs,
        in_specs=[pl.BlockSpec(memory_space=pltpu.SMEM)] + [vmem] * len(arrays),
        out_specs=[vmem] * 4 + [anywhere] * 2,
        scratch_shapes=scratch,
        compiler_params=pltpu.CompilerParams(
            vmem_limit_bytes=63 * 1024 * 1024, collective_id=0, has_side_effects=True
        ),
    )(counts, *arrays)


THIRDS = 3


def cast_kernel(dims, expand, reduce, attend, vectors, *outs):
    mixer_grad, output_grad, expand_grad, reduce_grad = outs[:4]
    width = dims.width
    for b in range(2):
        rows = slice(b * width, (b + 1) * width)
        cols = slice(b * BLOCK, (b + 1) * BLOCK)
        expand_grad[0, :, cols] = expand[0, rows, :].astype(F32)
        reduce_grad[0, cols, :] = reduce[0, rows, :].T.astype(F32)
    mixer_grad[0, :, 0:BLOCK] = attend[0, 0:width, :].astype(F32)
    mixer_grad[0, :, BLOCK:] = attend[0, width:, 0:LANES].astype(F32)
    output_grad[0] = attend[0, width:, LANES:].astype(F32)

    @pl.when((pl.program_id(0) == 0) & (pl.program_id(1) == 0))
    def _():
        for ref, name in zip(outs[4:], dims.names, strict=True):
            size = ref.shape[1]
            for c in range(0, size, BLOCK):
                at = dims.at[name] + c // BLOCK
                piece = min(BLOCK, size - c)
                for layer in range(2):
                    ref[layer : layer + 1, c : c + piece] = vectors[layer].astype(F32)[at : at + 1, 0:piece]


def run_cast(feed, attend, dims):
    d = dims
    width, hidden = d.width, d.hidden
    part = (1, 2 * width, BLOCK)
    grads = [(width, 3 * width), (width, width), (width, hidden), (hidden, width)]
    shapes = [jax.ShapeDtypeStruct((2,) + g, F32) for g in grads]
    specs = [
        pl.BlockSpec((1, width, 3 * width // THIRDS), lambda l, t: (l, 0, t)),
        pl.BlockSpec((1, width, width // THIRDS), lambda l, t: (l, 0, t)),
        pl.BlockSpec((1, width, hidden // THIRDS), lambda l, t: (l, 0, t)),
        pl.BlockSpec((1, hidden // THIRDS, width), lambda l, t: (l, t, 0)),
    ]
    for name in d.names:
        shapes.append(jax.ShapeDtypeStruct((2, d.sizes[name]), F32))
        specs.append(pl.BlockSpec((2, d.sizes[name]), lambda l, t: (0, 0)))
    return pl.pallas_call(
        functools.partial(cast_kernel, d),
        grid=(2, THIRDS),
        out_shape=shapes,
        in_specs=[
            pl.BlockSpec(part, lambda l, t: (l, t, 0)),
            pl.BlockSpec(part, lambda l, t: (l, THIRDS + t, 0)),
            pl.BlockSpec(part, lambda l, t: (l, t, 0)),
            pl.BlockSpec((2, d.vec_rows, BLOCK), lambda l, t: (0, d.vec_top // d.vec_rows, 0)),
        ],
        out_specs=specs,
        compiler_params=pltpu.CompilerParams(vmem_limit_bytes=32 * 1024 * 1024),
    )(feed, feed, attend, attend)


def shards(wires, global_crops, local_crops, local_count, global_cotangent, local_cotangent, *weights):
    dims = Dims(global_crops, local_crops, weights[8].shape[2], wires)
    outs = run_kernel(
        local_count, (global_crops, local_crops, global_cotangent, local_cotangent) + weights, dims
    )
    mixer, output, expand, reduce, *vectors = run_cast(outs[4], outs[5], dims)
    v = dict(zip(dims.names, vectors, strict=True))
    return (
        outs[0],
        outs[1],
        outs[2],
        outs[3],
        v["attend_gain"],
        v["attend_shift"],
        mixer,
        v["mixer_bias"],
        output,
        v["output_bias"],
        v["feed_gain"],
        v["feed_shift"],
        expand,
        v["expand_bias"],
        reduce,
        v["reduce_bias"],
    )


def solution(mesh):
    crops = P(("dp", "section"), None, None)
    return jax.shard_map(
        functools.partial(shards, wires_of(mesh)),
        mesh=mesh,
        in_specs=(crops, crops, P("dp"), crops, crops) + (P(),) * 12,
        out_specs=(crops,) * 4 + (P(),) * 12,
        check_vma=False,
    )
```

```python
import functools

import jax
import jax.numpy as jnp
from jax import lax
from jax.experimental import pallas as pl
from jax.experimental.pallas import tpu as pltpu
from jax.sharding import PartitionSpec as P

HEADS = 6
HEAD = 64
EPS = 1e-06
TILE = 16
LANES = 128
BLOCK = 256
LOG2E = 1.4426950408889634
F32 = jnp.float32
BF16 = jnp.bfloat16


def up_to(value, step):
    return -(-value // step) * step


def mm(left, right):
    return lax.dot_general(left, right, (((1,), (0,)), ((), ())), preferred_element_type=F32)


def mm_nt(left, right):
    return lax.dot_general(left, right, (((1,), (1,)), ((), ())), preferred_element_type=F32)


def mm_tn(left, right):
    return lax.dot_general(left, right, (((0,), (0,)), ((), ())), preferred_element_type=F32)


def norm(rows):
    centred = rows - jnp.mean(rows, -1, keepdims=True)
    scale = lax.rsqrt(jnp.mean(centred * centred, -1, keepdims=True) + EPS)
    return centred * scale, scale


def norm_back(grad, unit, scale, gain):
    slope = grad * gain
    first = jnp.mean(slope, -1, keepdims=True)
    second = jnp.mean(slope * unit, -1, keepdims=True)
    return scale * (slope - first - unit * second)


def gelu_parts(u):
    size = jnp.abs(u)
    d = 1.0 + (0.3275911 * 0.7071067811865476) * size
    t = pl.reciprocal(d, approx=True)
    t = t * (2.0 - d * t)
    poly = 0.5 * 1.061405429
    for a in (-1.453152027, 1.421413741, -0.284496736, 0.254829592):
        poly = poly * t + 0.5 * a
    bell = jnp.exp2((u * u) * (-0.5 * LOG2E))
    tail = poly * t * bell
    phi = jnp.where(u < 0.0, tail, 1.0 - tail)
    return u * phi, phi + (u * bell) * 0.3989422804014327


def fold8(value):
    rows, width = value.shape
    return jnp.sum(value.reshape(rows // 8, 8, width), 0)


def kernel(
    dims,
    counts,
    global_in,
    local_in,
    global_cot,
    local_cot,
    attend_gain,
    attend_shift,
    mixer_weight,
    mixer_bias,
    output_weight,
    output_bias,
    feed_gain,
    feed_shift,
    expand_weight,
    expand_bias,
    reduce_weight,
    reduce_bias,
    global_out,
    local_out,
    global_back,
    local_back,
    sums_out,
    sums,
    x_s,
    unit_s,
    scale_s,
    norm_t,
    packed_s,
    power_s,
    inverse_s,
    mixed_s,
    mixed_t,
    act_s,
    slope_s,
    grad_s,
    grad_low,
    grad_t,
    dup_s,
    mask_s,
    vec_s,
    acc_s,
    *wires,
):
    seq, group, width = dims.seq, dims.group, dims.width
    glen, llen = dims.glen, dims.llen
    n_global, n_local, n_seq = dims.n_global, dims.n_local, dims.n_seq
    hidden = dims.hidden
    count = counts[lax.axis_index("section")]
    pairs = HEADS // 2
    lane = lax.broadcasted_iota(jnp.int32, (1, LANES), 1)
    low_half = (lane < HEAD).astype(F32).astype(BF16)
    high_half = (lane >= HEAD).astype(F32).astype(BF16)
    score_scale = HEAD ** (-0.5)

    net = Net(dims.wires)
    net.greet()
    n_stage = len(dims.wires)
    landings, sems = wires[: n_stage * dims.n_chunk], wires[n_stage * dims.n_chunk :]
    flow = Flow(net)
    for layer in (1, 0):
        for i in range(dims.n_chunk):
            landing = landings[i * n_stage : (i + 1) * n_stage]
            number = (1 - layer) * dims.n_chunk + i
            own = [w.at[number] for w in sems[:4]] + [sems[4].at[i]]
            rows = pl.ds(dims.bounds[i], dims.bounds[i + 1] - dims.bounds[i])
            flow.chunks.append(
                Chunk(net, sums.at[layer, rows], sums_out.at[layer, rows], landing, own, (1 - layer), layer, dims.bounds[i : i + 2])
            )

    for s in range(n_seq):
        x_s[s, seq - 32 :, :] = jnp.zeros((32, width), F32)
        grad_s[s, seq - 32 :, :] = jnp.zeros((32, width), F32)
    row_id = lax.broadcasted_iota(jnp.int32, (seq, seq), 0)
    col_id = lax.broadcasted_iota(jnp.int32, (seq, seq), 1)
    row_crop = sum((row_id >= llen * j).astype(jnp.int32) for j in range(1, group + 1))
    col_crop = sum((col_id >= llen * j).astype(jnp.int32) for j in range(1, group + 1))
    far = jnp.float32(-1e30)
    mask_s[0] = jnp.where(col_id < glen, jnp.float32(0), far).astype(BF16)
    mask_s[1] = jnp.where(row_crop == col_crop, jnp.float32(0), far).astype(BF16)
    one_row = (lax.broadcasted_iota(jnp.int32, (TILE, seq), 0) == 0).astype(F32).astype(BF16)
    for s in range(n_seq):
        for i in range(4):
            norm_t[i, s, width:, :] = one_row
        for i in range(2):
            mixed_t[i, s, width:, :] = one_row

    def live_rows(g):
        rows = lax.broadcasted_iota(jnp.int32, (seq, 1), 0)
        return (rows < llen * jnp.clip(count - g * group, 0, group)).astype(F32)

    for s in range(n_global):
        x_s[s, 0:glen, :] = global_in[s].astype(F32)
        grad_s[s, 0:glen, :] = global_cot[s].astype(F32)
    for j in range(n_local):
        s, at = n_global + j // group, llen * (j % group)
        x_s[s, at : at + llen, :] = local_in[j].astype(F32)
        grad_s[s, at : at + llen, :] = local_cot[j].astype(F32)
    for s in range(n_global, n_seq):
        grad_s[s] = grad_s[s] * live_rows(s - n_global)

    def row(ref, layer):
        return ref[...].astype(F32)[layer : layer + 1]

    slopes = (slope_s, dup_s)

    def start_back(s, grad):
        grad_t[s] = grad.astype(BF16).T
        acc_s[2] = acc_s[2] + fold8(grad)

    def end_back(s, grad, unit, scale, gain, dh):
        unit = unit.astype(F32)
        acc_s[0] = acc_s[0] + fold8(dh * unit)
        acc_s[1] = acc_s[1] + fold8(dh)
        grad = (grad + norm_back(dh, unit, scale, gain)).astype(BF16)
        grad_low[s] = grad
        grad_s[s] = grad.astype(F32)

    def product(left, right, cols):
        total = mm(left[0], right[0, :, cols])
        for s in range(1, n_seq):
            total = total + mm(left[s], right[s, :, cols])
        return total

    for layer in range(2):
        gain, shift = row(attend_gain, layer), row(attend_shift, layer)
        bias = row(mixer_bias, layer)
        bias = jnp.concatenate([bias[:, :width], jnp.zeros((1, width), F32), bias[:, width:]], 1)
        out_bias = row(output_bias, layer)
        gain2, shift2 = row(feed_gain, layer), row(feed_shift, layer)
        bias_up, bias_down = row(expand_bias, layer), row(reduce_bias, layer)

        def attend(s, _):
            x = x_s[s]
            unit, scale = norm(x)
            unit_s[2 * layer, s] = unit.astype(BF16)
            scale_s[2 * layer, s] = scale
            normed = (unit * gain + shift).astype(BF16)
            norm_t[2 * layer, s, 0:width, :] = normed.T
            packed = (mm(normed, mixer_weight[layer]) + bias).astype(BF16)
            packed_s[layer, s] = packed
            mask = mask_s[jnp.where(s < n_global, 0, 1)].astype(F32)
            mixed = []
            for p in range(pairs):
                at = p * LANES
                query = packed[:, at : at + LANES]
                key = packed[:, width + at : width + at + LANES]
                value = packed[:, 2 * width + at : 2 * width + at + LANES]
                total = None
                for h, half in enumerate((low_half, high_half)):
                    scores = mm_nt(query * half, key) * (score_scale * LOG2E) + mask
                    power = jnp.exp2(scores - jnp.max(scores, -1, keepdims=True)).astype(BF16)
                    power_s[layer, s, 2 * p + h] = power
                    spread = jnp.broadcast_to(half, (seq, LANES))
                    term = mm(power, jnp.concatenate([value * half, spread], 1))
                    total = term if total is None else total + term
                inverse = 1.0 / total[:, LANES:]
                inverse_s[layer, s, :, at : at + LANES] = inverse
                mixed.append((total[:, :LANES] * inverse).astype(BF16))
            mixed = jnp.concatenate(mixed, 1)
            mixed_s[layer, s] = mixed
            mixed_t[layer, s, 0:width, :] = mixed.T
            x = x + mm(mixed, output_weight[layer]) + out_bias
            x_s[s] = x.astype(BF16).astype(F32)
            return 0

        lax.fori_loop(0, n_seq, attend, 0)

        def feed(s, _):
            x = x_s[s]
            unit, scale = norm(x)
            normed = (unit * gain2 + shift2).astype(BF16)
            norm_t[2 * layer + 1, s, 0:width, :] = normed.T
            unit_s[2 * layer + 1, s] = unit.astype(BF16)
            scale_s[2 * layer + 1, s] = scale
            if layer == 1:
                start_back(s, grad_s[s])
            for c in range(hidden // BLOCK):
                cols = slice(c * BLOCK, (c + 1) * BLOCK)
                up = mm(normed, expand_weight[layer, :, cols]) + bias_up[:, cols]
                act, slope = gelu_parts(up)
                act_s[layer, s, :, cols] = act.astype(BF16)
                slopes[layer][s, :, cols] = slope.astype(BF16)
            x = x + mm(act_s[layer, s], reduce_weight[layer]) + bias_down
            x_s[s] = x.astype(BF16).astype(F32)
            return 0

        if layer == 1:
            acc_s[...] = jnp.zeros_like(acc_s)
        lax.fori_loop(0, n_seq, feed, 0)

    for s in range(n_global):
        global_out[s] = x_s[s, 0:glen, :].astype(BF16)
    for j in range(n_local):
        s, at = n_global + j // group, llen * (j % group)
        alive = (count > j).astype(F32)
        local_out[j] = (x_s[s, at : at + llen, :] * alive).astype(BF16)

    def put_vector(at, value):
        for c in range(0, value.shape[1], BLOCK):
            piece = value[:, c : c + BLOCK]
            vec_s[at + c // BLOCK : at + c // BLOCK + 1, 0 : piece.shape[1]] = piece

    def put_tile(layer, top, m, part):
        at = top + (m // 3) * (width + fold)
        side = m % 3 * LANES
        part = part.astype(BF16)
        if m % 3 < 2:
            sums[layer, at : at + width, side : side + LANES] = part
        else:
            at = at + width
            sums[layer, at : at + fold, 0:LANES] = part[:fold]
            sums[layer, at : at + fold, LANES:] = part[fold:]

    blocks = hidden // BLOCK
    fold = width // 2
    tops = dims.tops
    net.wait_greeting()
    for layer in (1, 0):
        vec_s[...] = jnp.zeros_like(vec_s)
        gain2, gain = row(feed_gain, layer), row(attend_gain, layer)
        put_vector(dims.at["reduce_bias"], jnp.sum(acc_s[2], 0, keepdims=True))

        for c in range(blocks):
            total = product(grad_t, act_s.at[layer], slice(c * BLOCK, (c + 1) * BLOCK))
            at = tops[0] + c * width
            sums[layer, at : at + width, :] = total.astype(BF16)
            flow.ready(layer, at + width)
            flow.tick(0.45)

        def feed_back(s, _):
            grad = grad_s[s]
            grad_in = grad.astype(BF16)
            for c in range(blocks):
                cols = slice(c * BLOCK, (c + 1) * BLOCK)
                dact = mm_nt(grad_in, reduce_weight[layer, cols, :])
                dup_s[s, :, cols] = (dact * slopes[layer][s, :, cols].astype(F32)).astype(BF16)
            dh = mm_nt(dup_s[s], expand_weight[layer])
            end_back(s, grad, unit_s[2 * layer + 1, s], scale_s[2 * layer + 1, s], gain2, dh)
            flow.ticks(s, n_seq, 1.3)
            return 0

        acc_s[0:2] = jnp.zeros((2, 8, width), F32)
        lax.fori_loop(0, n_seq, feed_back, 0)
        put_vector(dims.at["feed_gain"], jnp.sum(acc_s[0], 0, keepdims=True))
        put_vector(dims.at["feed_shift"], jnp.sum(acc_s[1], 0, keepdims=True))

        for c in range(blocks):
            total = product(norm_t.at[2 * layer + 1], dup_s, slice(c * BLOCK, (c + 1) * BLOCK))
            at = tops[1] + c * width
            sums[layer, at : at + width, :] = total[:width].astype(BF16)
            at_bias = dims.at["expand_bias"] + c
            vec_s[at_bias : at_bias + 1, :] = total[width : width + 1]
            flow.ready(layer, at + width)
            flow.tick(0.45)

        bias_parts = []
        for c in range(0, width, BLOCK):
            size = min(BLOCK, width - c)
            total = product(mixed_t.at[layer], grad_low, slice(c, c + size))
            for k in range(0, size, LANES):
                put_tile(layer, tops[2], (c + k) // LANES, total[:width, k : k + LANES])
                bias_parts.append(total[width : width + 1, k : k + LANES])
        put_vector(dims.at["output_bias"], jnp.concatenate(bias_parts, 1))
        flow.ready(layer, tops[3])
        flow.tick(0.8)

        def attend_back(s, _):
            grad = grad_s[s]
            dmixed = mm_nt(grad_low[s], output_weight[layer])
            parts = [None] * (3 * pairs)
            for p in range(pairs):
                at = p * LANES
                query = packed_s[layer, s, :, at : at + LANES]
                key = packed_s[layer, s, :, width + at : width + at + LANES]
                value = packed_s[layer, s, :, 2 * width + at : 2 * width + at + LANES]
                dm = dmixed[:, at : at + LANES] * inverse_s[layer, s, :, at : at + LANES]
                inner = -(dm * mixed_s[layer, s, :, at : at + LANES].astype(F32)).astype(BF16)
                dm = dm.astype(BF16)
                wide_value = jnp.concatenate([value, jnp.ones_like(value)], 1)
                dq = dk = dv = None
                for h, half in enumerate((low_half, high_half)):
                    power = power_s[layer, s, 2 * p + h]
                    dm_half = dm * half
                    left = jnp.concatenate([dm_half, inner * half], 1)
                    ds = (power.astype(F32) * mm_nt(left, wide_value)).astype(BF16)
                    terms = (mm(ds, key * half), mm_tn(ds, query * half), mm_tn(power, dm_half))
                    dq = terms[0] if dq is None else dq + terms[0]
                    dk = terms[1] if dk is None else dk + terms[1]
                    dv = terms[2] if dv is None else dv + terms[2]
                parts[p] = (dq * score_scale).astype(BF16)
                parts[pairs + p] = (dk * score_scale).astype(BF16)
                parts[2 * pairs + p] = dv.astype(BF16)
            dpacked = jnp.concatenate(parts, 1)
            dup_s[s, :, 0 : 3 * width] = dpacked
            dh = mm_nt(dpacked, mixer_weight[layer])
            end_back(s, grad, unit_s[2 * layer, s], scale_s[2 * layer, s], gain, dh)
            if layer == 1:
                start_back(s, grad_s[s])
            flow.ticks(s, n_seq, 2.3)
            return 0

        acc_s[...] = jnp.zeros_like(acc_s)
        lax.fori_loop(0, n_seq, attend_back, 0)
        put_vector(dims.at["attend_gain"], jnp.sum(acc_s[0], 0, keepdims=True))
        put_vector(dims.at["attend_shift"], jnp.sum(acc_s[1], 0, keepdims=True))

        bias_parts = []
        for c in range(0, 3 * width, BLOCK):
            size = min(BLOCK, 3 * width - c)
            total = product(norm_t.at[2 * layer], dup_s, slice(c, c + size))
            for k in range(0, size, LANES):
                put_tile(layer, tops[3], (c + k) // LANES, total[:width, k : k + LANES])
                bias_parts.append(total[width : width + 1, k : k + LANES])
            flow.tick(0.5)
        each = width // LANES
        put_vector(
            dims.at["mixer_bias"],
            jnp.concatenate(bias_parts[:each] + bias_parts[2 * each :], 1),
        )
        sums[layer, tops[4] : tops[4] + dims.vec_rows, :] = vec_s[...].astype(BF16)
        rest = dims.rows - tops[4] - dims.vec_rows
        if rest:
            sums[layer, dims.rows - rest :, :] = jnp.zeros((rest, BLOCK), BF16)
        flow.ready(layer, dims.rows)

    for s in range(n_global):
        global_back[s] = grad_s[s, 0:glen, :].astype(BF16)
    for j in range(n_local):
        s, at = n_global + j // group, llen * (j % group)
        local_back[j] = grad_s[s, at : at + llen, :].astype(BF16)
    flow.drain()


class Wire:
    def __init__(self, size, first, second):
        self.size, self.first, self.second = size, first, second


def wires_of(mesh):
    names = mesh.axis_names
    places = {}
    for axis, name in enumerate(names):
        line = [mesh.devices[tuple(i if a == axis else 0 for a in range(2))] for i in range(mesh.devices.shape[axis])]
        spots = [(d.core_on_chip,) + tuple(d.coords) for d in line]
        found, total = [], 1
        for k in range(4):
            values = sorted({p[k] for p in spots})
            if len(values) > 1:
                stride = next(i for i, p in enumerate(spots) if p[k] != spots[0][k])
                found.append((k, axis, stride, len(values)))
                total *= len(values)
        good = total == len(line)
        for k, _, stride, size in found:
            values = [p[k] for p in spots]
            good = good and all(v == values[i // stride % size * stride] for i, v in enumerate(values))
        if not good:
            found = [(4 + axis, axis, 1, len(line))]
        for k, axis, stride, size in found:
            places[k] = (axis, stride, size)
    wires = []
    if 0 in places:
        wires.append(Wire(places[0][2], places[0], places[0]))
    if 0 in places and 1 in places and 2 in places and places[1][2] == places[2][2]:
        wires.append(Wire(places[1][2], places[1], places[2]))
        wires.append(Wire(places[1][2], places[2], places[1]))
        order = [3, 4, 5]
    else:
        order = [1, 2, 3, 4, 5]
    for k in order:
        if k in places:
            wires.append(Wire(places[k][2], places[k], places[k]))
    return wires


class Net:
    def __init__(self, wires):
        self.axes = ("dp", "section")
        self.here = [lax.axis_index(a) for a in self.axes]
        self.wires = wires
        first = wires[0]
        odd = self.spot(first.first) % 2 if first.size == 2 else 0
        self.odd = odd
        self.at = []
        for w in wires:
            a, b = self.spot(w.first), self.spot(w.second)
            self.at.append(a if w.first == w.second else a + odd * (b - a))

    def spot(self, place):
        axis, stride, size = place
        return self.here[axis] // stride % size

    def peer(self, stage, k):
        w = self.wires[stage]
        place = (self.at[stage] + k) % w.size
        move = place - self.at[stage]
        target = list(self.here)
        if w.first == w.second:
            target[w.first[0]] = target[w.first[0]] + move * w.first[1]
        else:
            target[w.first[0]] = target[w.first[0]] + move * w.first[1] * (1 - self.odd)
            target[w.second[0]] = target[w.second[0]] + move * w.second[1] * self.odd
        return tuple(target), place

    def greet(self):
        barrier = pltpu.get_barrier_semaphore()
        for stage, w in enumerate(self.wires):
            for k in range(1, w.size):
                pl.semaphore_signal(barrier, inc=1, device_id=self.peer(stage, k)[0], device_id_type=pl.DeviceIdType.MESH)

    def wait_greeting(self):
        pl.semaphore_wait(pltpu.get_barrier_semaphore(), sum(w.size - 1 for w in self.wires))


class Chunk:
    def __init__(self, net, sums, out, landing, sems, turn, layer, bounds):
        self.net, self.sums, self.out, self.landing = net, sums, out, landing
        self.send, self.recv, self.local, self.sent, self.free = sems
        self.turn = turn
        self.layer, self.end = layer, bounds[1]
        self.due = None
        size, start = sums.shape[0], 0
        self.unit = size
        for w in net.wires:
            self.unit //= w.size
        self.size, self.start = [], []
        for stage, w in enumerate(net.wires):
            size //= w.size
            self.size.append(size)
            self.start.append((start, size))
            start = start + net.at[stage] * size
        self.own = start
        self.stages = len(net.wires)
        self.step = 0
        self.sem_at, at = {}, 0
        for phase in range(2):
            for stage, w in enumerate(net.wires):
                for k in range(1, w.size):
                    self.sem_at[phase, stage, k] = at
                    at += 1

    def rows(self, stage, place):
        start, size = self.start[stage]
        return pl.ds(pl.multiple_of(start + place * size, TILE), size)

    def copy(self, phase, stage, k):
        target, place = self.net.peer(stage, k)
        at = self.sem_at[phase, stage, k]
        if phase == 0:
            source, to = self.sums.at[self.rows(stage, place)], self.landing[stage].at[k - 1]
        else:
            rows = self.rows(stage, self.net.at[stage])
            source = to = self.sums.at[rows]
        return pltpu.make_async_remote_copy(
            src_ref=source,
            dst_ref=to,
            send_sem=self.send.at[at],
            recv_sem=self.recv.at[at],
            device_id=target,
            device_id_type=pl.DeviceIdType.MESH,
        )

    def arrival(self, stage, k):
        target, place = self.net.peer(stage, self.net.wires[stage].size - k)
        at = self.sem_at[1, stage, k]
        landed = self.sums.at[self.rows(stage, place)]
        return pltpu.make_async_remote_copy(
            src_ref=landed,
            dst_ref=landed,
            send_sem=self.send.at[at],
            recv_sem=self.recv.at[at],
            device_id=target,
            device_id_type=pl.DeviceIdType.MESH,
        )

    def start_stage(self, phase, stage):
        if phase == 0 and self.turn == 1:
            pl.semaphore_wait(self.free.at[stage], self.net.wires[stage].size - 1)
        if phase == 1:
            pl.semaphore_wait(self.sent.at[stage], self.net.wires[stage].size - 1)
        for k in range(1, self.net.wires[stage].size):
            self.copy(phase, stage, k).start()

    def span(self, step):
        last = self.stages - 1
        stage = step if step <= last else 2 * self.stages - 1 - step
        row = BLOCK * 2 / 1e5 * SLOW
        if stage == 0:
            return LATENCY + self.size[0] * row / 3
        if stage == last:
            return LATENCY + self.size[stage] * self.net.wires[stage].size ** 2 / 2 * row
        return LATENCY + self.size[stage] * (self.net.wires[stage].size - 1) * row

    def begin(self, now):
        self.start_stage(0, 0)
        self.due = now + self.span(0)

    def out_copy(self):
        return pltpu.make_async_copy(self.sums, self.out, self.local.at[0])

    def advance(self, now):
        step = self.step
        self.step += 1
        self.due = now + self.span(self.step) if self.step < 2 * self.stages else None
        if step < self.stages:
            peers = range(1, self.net.wires[step].size)
            for k in peers:
                self.copy(0, step, k).wait_recv()
            base = self.start[step][0] + self.net.at[step] * self.size[step]
            landing = self.landing[step]

            def add(i, _):
                at = pl.ds(pl.multiple_of(base + i * self.unit, TILE), self.unit)
                total = self.sums[at, :].astype(F32)
                for k in peers:
                    total = total + landing[k - 1, pl.ds(pl.multiple_of(i * self.unit, TILE), self.unit), :].astype(F32)
                self.sums[at, :] = total.astype(BF16)
                return 0

            lax.fori_loop(0, self.size[step] // self.unit, add, 0)
            for k in peers:
                self.copy(0, step, k).wait_send()
                target = self.net.peer(step, k)[0]
                pl.semaphore_signal(self.sent.at[step], inc=1, device_id=target, device_id_type=pl.DeviceIdType.MESH)
                if self.turn == 0:
                    pl.semaphore_signal(self.free.at[step], inc=1, device_id=target, device_id_type=pl.DeviceIdType.MESH)
            if step + 1 < self.stages:
                self.start_stage(0, step + 1)
            else:
                self.start_stage(1, step)
        else:
            stage = 2 * self.stages - 1 - step
            for k in range(1, self.net.wires[stage].size):
                self.arrival(stage, k).wait_recv()
            if stage > 0:
                self.start_stage(1, stage - 1)
            else:
                self.out_copy().start()

    def finish(self):
        for phase, stage, k in self.sem_at:
            if phase == 1:
                self.copy(phase, stage, k).wait_send()
        self.out_copy().wait()


LATENCY = 2.0
SLOW = 1.2


class Flow:
    def __init__(self, net):
        self.chunks, self.now, self.waiting = [], 0.0, 0

    def ready(self, layer, rows):
        while self.waiting < len(self.chunks):
            chunk = self.chunks[self.waiting]
            if chunk.layer != layer or chunk.end > rows:
                return
            chunk.begin(self.now)
            self.waiting += 1

    def take(self):
        while True:
            due = [c for c in self.chunks if c.due is not None and c.due <= self.now]
            if not due:
                return
            min(due, key=lambda c: c.due).advance(self.now)

    def tick(self, time):
        self.now += time
        self.take()

    def ticks(self, s, count, time):
        for i in range(count):
            self.now += time
            if any(c.due is not None and c.due <= self.now for c in self.chunks):
                pl.when(s == i)(self.take)

    def drain(self):
        while any(c.due is not None for c in self.chunks):
            self.now = max(self.now, min(c.due for c in self.chunks if c.due is not None))
            self.take()
        for chunk in self.chunks:
            chunk.finish()


class Dims:
    def __init__(self, global_crops, local_crops, hidden, wires):
        self.wires = wires
        self.n_global, self.glen, self.width = global_crops.shape
        self.n_local, self.llen, _ = local_crops.shape
        self.hidden = hidden
        self.seq = up_to(self.glen, TILE)
        self.group = self.seq // self.llen
        while self.n_local % self.group:
            self.group -= 1
        self.n_seq = self.n_global + self.n_local // self.group
        sizes = (
            ("attend_gain", self.width),
            ("attend_shift", self.width),
            ("mixer_bias", 2 * self.width),
            ("output_bias", self.width),
            ("feed_gain", self.width),
            ("feed_shift", self.width),
            ("expand_bias", hidden),
            ("reduce_bias", self.width),
        )
        self.names, self.sizes = [name for name, _ in sizes], dict(sizes)
        self.at, row = {}, 0
        for name, size in sizes:
            self.at[name] = row
            row += -(-size // BLOCK)
        self.vec_rows = 2 * TILE
        assert row <= self.vec_rows and self.width * hidden % self.vec_rows == 0
        step = TILE
        for w in wires:
            step *= w.size
        ff = self.width * hidden // BLOCK
        square = self.width * self.width // BLOCK
        self.tops = (0, ff, 2 * ff, 2 * ff + square, 2 * ff + 4 * square)
        self.rows = up_to(self.tops[4] + self.vec_rows, step)
        parts = self.rows // step
        cuts = sorted({0, parts * 4 // 14, parts * 7 // 14, parts * 10 // 14, parts})
        self.bounds = [c * step for c in cuts]
        self.n_chunk = len(cuts) - 1


def run_kernel(counts, arrays, dims):
    d = dims
    n, seq, width, hidden = d.n_seq, d.seq, d.width, d.hidden
    crops = [jax.ShapeDtypeStruct(a.shape, BF16) for a in arrays[:2]]
    outs = crops + crops
    outs += [jax.ShapeDtypeStruct((2, d.rows, BLOCK), BF16)]
    scratch = [
        pltpu.VMEM((2, d.rows, BLOCK), BF16),
        pltpu.VMEM((n, seq, width), F32),
        pltpu.VMEM((4, n, seq, width), BF16),
        pltpu.VMEM((4, n, seq, 1), F32),
        pltpu.VMEM((4, n, width + TILE, seq), BF16),
        pltpu.VMEM((2, n, seq, 3 * width), BF16),
        pltpu.VMEM((2, n, HEADS, seq, seq), BF16),
        pltpu.VMEM((2, n, seq, width), F32),
        pltpu.VMEM((2, n, seq, width), BF16),
        pltpu.VMEM((2, n, width + TILE, seq), BF16),
        pltpu.VMEM((2, n, seq, hidden), BF16),
        pltpu.VMEM((n, seq, hidden), BF16),
        pltpu.VMEM((n, seq, width), F32),
        pltpu.VMEM((n, seq, width), BF16),
        pltpu.VMEM((n, width, seq), BF16),
        pltpu.VMEM((n, seq, hidden), BF16),
        pltpu.VMEM((2, seq, seq), BF16),
        pltpu.VMEM((d.vec_rows, BLOCK), F32),
        pltpu.VMEM((3, 8, width), F32),
    ]
    for i in range(d.n_chunk):
        rows = d.bounds[i + 1] - d.bounds[i]
        for w in d.wires:
            rows //= w.size
            scratch.append(pltpu.VMEM((w.size - 1, rows, BLOCK), BF16))
    peers = 2 * sum(w.size - 1 for w in d.wires)
    scratch += [
        pltpu.SemaphoreType.DMA((2 * d.n_chunk, peers)),
        pltpu.SemaphoreType.DMA((2 * d.n_chunk, peers)),
        pltpu.SemaphoreType.DMA((2 * d.n_chunk, 1)),
        pltpu.SemaphoreType.REGULAR((2 * d.n_chunk, len(d.wires))),
        pltpu.SemaphoreType.REGULAR((d.n_chunk, len(d.wires))),
    ]
    vmem = pl.BlockSpec(memory_space=pltpu.VMEM)
    anywhere = pl.BlockSpec(memory_space=pl.ANY)
    return pl.pallas_call(
        functools.partial(kernel, d),
        out_shape=outs,
        in_specs=[pl.BlockSpec(memory_space=pltpu.SMEM)] + [vmem] * len(arrays),
        out_specs=[vmem] * 4 + [anywhere],
        scratch_shapes=scratch,
        compiler_params=pltpu.CompilerParams(
            vmem_limit_bytes=63 * 1024 * 1024, collective_id=0, has_side_effects=True
        ),
    )(counts, *arrays)


THIRDS = 3


def cast_kernel(dims, reduce, expand, output, mixer, vectors, *outs):
    mixer_grad, output_grad, expand_grad, reduce_grad = outs[:4]
    width = dims.width
    fold = width // 2
    for b in range(2):
        rows = slice(b * width, (b + 1) * width)
        cols = slice(b * BLOCK, (b + 1) * BLOCK)
        expand_grad[0, :, cols] = expand[0, rows, :].astype(F32)
        reduce_grad[0, cols, :] = reduce[0, rows, :].T.astype(F32)
    for source, target in ((mixer, mixer_grad), (output, output_grad)):
        target[0, :, 0:BLOCK] = source[0, 0:width, :].astype(F32)
        target[0, 0:fold, BLOCK:] = source[0, width:, 0:LANES].astype(F32)
        target[0, fold:, BLOCK:] = source[0, width:, LANES:].astype(F32)

    @pl.when((pl.program_id(0) == 0) & (pl.program_id(1) == 0))
    def _():
        for ref, name in zip(outs[4:], dims.names, strict=True):
            size = ref.shape[1]
            for c in range(0, size, BLOCK):
                at = dims.at[name] + c // BLOCK
                piece = min(BLOCK, size - c)
                for layer in range(2):
                    ref[layer : layer + 1, c : c + piece] = vectors[layer].astype(F32)[at : at + 1, 0:piece]


def run_cast(sums, dims):
    d = dims
    width, hidden = d.width, d.hidden
    part = (1, 2 * width, BLOCK)
    square = (1, width * width // BLOCK, BLOCK)
    grads = [(width, 3 * width), (width, width), (width, hidden), (hidden, width)]
    shapes = [jax.ShapeDtypeStruct((2,) + g, F32) for g in grads]
    specs = [
        pl.BlockSpec((1, width, 3 * width // THIRDS), lambda l, t: (l, 0, t)),
        pl.BlockSpec((1, width, width), lambda l, t: (l, 0, 0)),
        pl.BlockSpec((1, width, hidden // THIRDS), lambda l, t: (l, 0, t)),
        pl.BlockSpec((1, hidden // THIRDS, width), lambda l, t: (l, t, 0)),
    ]
    for name in d.names:
        shapes.append(jax.ShapeDtypeStruct((2, d.sizes[name]), F32))
        specs.append(pl.BlockSpec((2, d.sizes[name]), lambda l, t: (0, 0)))
    return pl.pallas_call(
        functools.partial(cast_kernel, d),
        grid=(2, THIRDS),
        out_shape=shapes,
        in_specs=[
            pl.BlockSpec(part, lambda l, t: (l, t, 0)),
            pl.BlockSpec(part, lambda l, t: (l, THIRDS + t, 0)),
            pl.BlockSpec(square, lambda l, t: (l, d.tops[2] // square[1], 0)),
            pl.BlockSpec(square, lambda l, t: (l, d.tops[3] // square[1] + t, 0)),
            pl.BlockSpec((2, d.vec_rows, BLOCK), lambda l, t: (0, d.tops[4] // d.vec_rows, 0)),
        ],
        out_specs=specs,
        compiler_params=pltpu.CompilerParams(vmem_limit_bytes=32 * 1024 * 1024),
    )(sums, sums, sums, sums, sums)


def shards(wires, global_crops, local_crops, local_count, global_cotangent, local_cotangent, *weights):
    dims = Dims(global_crops, local_crops, weights[8].shape[2], wires)
    outs = run_kernel(
        local_count, (global_crops, local_crops, global_cotangent, local_cotangent) + weights, dims
    )
    mixer, output, expand, reduce, *vectors = run_cast(outs[4], dims)
    v = dict(zip(dims.names, vectors, strict=True))
    return (
        outs[0],
        outs[1],
        outs[2],
        outs[3],
        v["attend_gain"],
        v["attend_shift"],
        mixer,
        v["mixer_bias"],
        output,
        v["output_bias"],
        v["feed_gain"],
        v["feed_shift"],
        expand,
        v["expand_bias"],
        reduce,
        v["reduce_bias"],
    )


def solution(mesh):
    crops = P(("dp", "section"), None, None)
    return jax.shard_map(
        functools.partial(shards, wires_of(mesh)),
        mesh=mesh,
        in_specs=(crops, crops, P("dp"), crops, crops) + (P(),) * 12,
        out_specs=(crops,) * 4 + (P(),) * 12,
        check_vma=False,
    )
```

```python
import functools

import jax
import jax.numpy as jnp
from jax import lax
from jax.experimental import pallas as pl
from jax.experimental.pallas import tpu as pltpu
from jax.sharding import PartitionSpec as P

HEADS = 6
HEAD = 64
EPS = 1e-06
TILE = 16
LANES = 128
BLOCK = 256
LOG2E = 1.4426950408889634
F32 = jnp.float32
BF16 = jnp.bfloat16


def up_to(value, step):
    return -(-value // step) * step


def mm(left, right):
    return lax.dot_general(left, right, (((1,), (0,)), ((), ())), preferred_element_type=F32)


def mm_nt(left, right):
    return lax.dot_general(left, right, (((1,), (1,)), ((), ())), preferred_element_type=F32)


def mm_tn(left, right):
    return lax.dot_general(left, right, (((0,), (0,)), ((), ())), preferred_element_type=F32)


def norm(rows):
    centred = rows - jnp.mean(rows, -1, keepdims=True)
    scale = lax.rsqrt(jnp.mean(centred * centred, -1, keepdims=True) + EPS)
    return centred * scale, scale


def norm_back(grad, unit, scale, gain):
    slope = grad * gain
    first = jnp.mean(slope, -1, keepdims=True)
    second = jnp.mean(slope * unit, -1, keepdims=True)
    return scale * (slope - first - unit * second)


def gelu_parts(u):
    size = jnp.abs(u)
    d = 1.0 + (0.3275911 * 0.7071067811865476) * size
    t = pl.reciprocal(d, approx=True)
    t = t * (2.0 - d * t)
    poly = 0.5 * 1.061405429
    for a in (-1.453152027, 1.421413741, -0.284496736, 0.254829592):
        poly = poly * t + 0.5 * a
    bell = jnp.exp2((u * u) * (-0.5 * LOG2E))
    tail = poly * t * bell
    phi = jnp.where(u < 0.0, tail, 1.0 - tail)
    return u * phi, phi + (u * bell) * 0.3989422804014327


def fold8(value):
    rows, width = value.shape
    return jnp.sum(value.reshape(rows // 8, 8, width), 0)


def kernel(
    dims,
    counts,
    global_in,
    local_in,
    global_cot,
    local_cot,
    attend_gain,
    attend_shift,
    mixer_weight,
    mixer_bias,
    output_weight,
    output_bias,
    feed_gain,
    feed_shift,
    expand_weight,
    expand_bias,
    reduce_weight,
    reduce_bias,
    global_out,
    local_out,
    global_back,
    local_back,
    sums_out,
    sums,
    crop_s,
    x_s,
    unit_s,
    scale_s,
    norm_t,
    packed_s,
    power_s,
    inverse_s,
    mixed_s,
    mixed_t,
    act_s,
    slope_s,
    grad_s,
    grad_low,
    grad_t,
    dup_s,
    mask_s,
    vec_s,
    acc_s,
    *wires,
):
    seq, group, width = dims.seq, dims.group, dims.width
    glen, llen = dims.glen, dims.llen
    n_global, n_local, n_seq = dims.n_global, dims.n_local, dims.n_seq
    hidden = dims.hidden
    count = counts[lax.axis_index("section")]
    pairs = HEADS // 2
    lane = lax.broadcasted_iota(jnp.int32, (1, LANES), 1)
    low_half = (lane < HEAD).astype(F32).astype(BF16)
    high_half = (lane >= HEAD).astype(F32).astype(BF16)
    score_scale = HEAD ** (-0.5)

    net = Net(dims.wires)
    net.greet()
    n_stage = len(dims.wires)
    sets = dims.landing_sets
    landings, sems = wires[: n_stage * sum(sets)], wires[n_stage * sum(sets) :]
    flow = Flow(net)
    number = 0
    for layer in (1, 0):
        bounds = dims.bounds[layer]
        for i in range(len(bounds) - 1):
            shared = len(sets) == 1
            at = (i if shared else number) * n_stage
            own = [w.at[number] for w in sems[:4]] + [sems[4].at[i]]
            rows = pl.ds(bounds[i], bounds[i + 1] - bounds[i])
            turn = (1 - layer) if shared else None
            flow.chunks.append(
                Chunk(net, sums.at[layer, rows], sums_out.at[layer, rows], landings[at : at + n_stage], own, turn, layer, bounds[i + 1])
            )
            number += 1

    for s in range(n_seq):
        x_s[s, seq - 32 :, :] = jnp.zeros((32, width), F32)
        grad_s[s, seq - 32 :, :] = jnp.zeros((32, width), F32)
    row_id = lax.broadcasted_iota(jnp.int32, (seq, seq), 0)
    col_id = lax.broadcasted_iota(jnp.int32, (seq, seq), 1)
    row_crop = sum((row_id >= llen * j).astype(jnp.int32) for j in range(1, group + 1))
    col_crop = sum((col_id >= llen * j).astype(jnp.int32) for j in range(1, group + 1))
    far = jnp.float32(-1e30)
    mask_s[0] = jnp.where(col_id < glen, jnp.float32(0), far).astype(BF16)
    mask_s[1] = jnp.where(row_crop == col_crop, jnp.float32(0), far).astype(BF16)
    one_row = (lax.broadcasted_iota(jnp.int32, (TILE, seq), 0) == 0).astype(F32).astype(BF16)
    for s in range(n_seq):
        for i in range(4):
            norm_t[i, s, width:, :] = one_row
        for i in range(2):
            mixed_t[i, s, width:, :] = one_row

    def live_rows(g):
        rows = lax.broadcasted_iota(jnp.int32, (seq, 1), 0)
        return (rows < llen * jnp.clip(count - g * group, 0, group)).astype(F32)

    for source, target in ((global_in, x_s), (global_cot, grad_s)):
        crop_s[...] = source[...].astype(F32)
        for s in range(n_global):
            target[s, 0:glen, :] = crop_s[:, s, :]
    for j in range(n_local):
        s, at = n_global + j // group, llen * (j % group)
        x_s[s, at : at + llen, :] = local_in[j].astype(F32)
        grad_s[s, at : at + llen, :] = local_cot[j].astype(F32)
    for s in range(n_global, n_seq):
        grad_s[s] = grad_s[s] * live_rows(s - n_global)

    def row(ref, layer):
        return ref[...].astype(F32)[layer : layer + 1]

    slopes = (slope_s, dup_s)

    def start_back(s, grad):
        grad_t[s] = grad.astype(BF16).T
        acc_s[2] = acc_s[2] + fold8(grad)

    def end_back(s, grad, unit, scale, gain, dh):
        unit = unit.astype(F32)
        acc_s[0] = acc_s[0] + fold8(dh * unit)
        acc_s[1] = acc_s[1] + fold8(dh)
        grad = (grad + norm_back(dh, unit, scale, gain)).astype(BF16)
        grad_low[s] = grad
        grad_s[s] = grad.astype(F32)

    def product(left, right, cols):
        total = mm(left[0], right[0, :, cols])
        for s in range(1, n_seq):
            total = total + mm(left[s], right[s, :, cols])
        return total

    for layer in range(2):
        gain, shift = row(attend_gain, layer), row(attend_shift, layer)
        bias = row(mixer_bias, layer)
        bias = jnp.concatenate([bias[:, :width], jnp.zeros((1, width), F32), bias[:, width:]], 1)
        out_bias = row(output_bias, layer)
        gain2, shift2 = row(feed_gain, layer), row(feed_shift, layer)
        bias_up, bias_down = row(expand_bias, layer), row(reduce_bias, layer)

        def attend(s, _):
            x = x_s[s]
            unit, scale = norm(x)
            unit_s[2 * layer, s] = unit.astype(BF16)
            scale_s[2 * layer, s] = scale
            normed = (unit * gain + shift).astype(BF16)
            norm_t[2 * layer, s, 0:width, :] = normed.T
            packed = (mm(normed, mixer_weight[layer]) + bias).astype(BF16)
            packed_s[layer, s] = packed
            mask = mask_s[jnp.where(s < n_global, 0, 1)].astype(F32)
            mixed = []
            for p in range(pairs):
                at = p * LANES
                query = packed[:, at : at + LANES]
                key = packed[:, width + at : width + at + LANES]
                value = packed[:, 2 * width + at : 2 * width + at + LANES]
                total = None
                for h, half in enumerate((low_half, high_half)):
                    scores = mm_nt(query * half, key) * (score_scale * LOG2E) + mask
                    power = jnp.exp2(scores - jnp.max(scores, -1, keepdims=True)).astype(BF16)
                    power_s[layer, s, 2 * p + h] = power
                    spread = jnp.broadcast_to(half, (seq, LANES))
                    term = mm(power, jnp.concatenate([value * half, spread], 1))
                    total = term if total is None else total + term
                inverse = 1.0 / total[:, LANES:]
                inverse_s[layer, s, :, at : at + LANES] = inverse
                mixed.append((total[:, :LANES] * inverse).astype(BF16))
            mixed = jnp.concatenate(mixed, 1)
            mixed_s[layer, s] = mixed
            mixed_t[layer, s, 0:width, :] = mixed.T
            x = x + mm(mixed, output_weight[layer]) + out_bias
            x_s[s] = x.astype(BF16).astype(F32)
            return 0

        lax.fori_loop(0, n_seq, attend, 0)

        def feed(s, _):
            x = x_s[s]
            unit, scale = norm(x)
            normed = (unit * gain2 + shift2).astype(BF16)
            norm_t[2 * layer + 1, s, 0:width, :] = normed.T
            unit_s[2 * layer + 1, s] = unit.astype(BF16)
            scale_s[2 * layer + 1, s] = scale
            if layer == 1:
                start_back(s, grad_s[s])
            for c in range(hidden // BLOCK):
                cols = slice(c * BLOCK, (c + 1) * BLOCK)
                up = mm(normed, expand_weight[layer, :, cols]) + bias_up[:, cols]
                act, slope = gelu_parts(up)
                act_s[layer, s, :, cols] = act.astype(BF16)
                slopes[layer][s, :, cols] = slope.astype(BF16)
            x = x + mm(act_s[layer, s], reduce_weight[layer]) + bias_down
            x_s[s] = x.astype(BF16).astype(F32)
            return 0

        if layer == 1:
            acc_s[...] = jnp.zeros_like(acc_s)
        lax.fori_loop(0, n_seq, feed, 0)

    for s in range(n_global):
        crop_s[:, s, :] = x_s[s, 0:glen, :]
    global_out[...] = crop_s[...].astype(BF16)
    for j in range(n_local):
        s, at = n_global + j // group, llen * (j % group)
        alive = (count > j).astype(F32)
        local_out[j] = (x_s[s, at : at + llen, :] * alive).astype(BF16)

    def put_vector(at, value):
        for c in range(0, value.shape[1], BLOCK):
            piece = value[:, c : c + BLOCK]
            vec_s[at + c // BLOCK : at + c // BLOCK + 1, 0 : piece.shape[1]] = piece

    def put_tile(layer, top, m, part):
        at = top + (m // 3) * (width + fold)
        side = m % 3 * LANES
        part = part.astype(BF16)
        if m % 3 < 2:
            sums[layer, at : at + width, side : side + LANES] = part
        else:
            at = at + width
            sums[layer, at : at + fold, 0:LANES] = part[:fold]
            sums[layer, at : at + fold, LANES:] = part[fold:]

    blocks = hidden // BLOCK
    fold = width // 2
    tops = dims.tops
    net.wait_greeting()
    for layer in (1, 0):
        vec_s[...] = jnp.zeros_like(vec_s)
        gain2, gain = row(feed_gain, layer), row(attend_gain, layer)
        put_vector(dims.at["reduce_bias"], jnp.sum(acc_s[2], 0, keepdims=True))

        for c in range(blocks):
            total = product(grad_t, act_s.at[layer], slice(c * BLOCK, (c + 1) * BLOCK))
            at = tops[0] + c * width
            sums[layer, at : at + width, :] = total.astype(BF16)
            flow.ready(layer, at + width)
            flow.tick(0.45)

        def feed_back(s, _):
            grad = grad_s[s]
            grad_in = grad.astype(BF16)
            for c in range(blocks):
                cols = slice(c * BLOCK, (c + 1) * BLOCK)
                dact = mm_nt(grad_in, reduce_weight[layer, cols, :])
                dup_s[s, :, cols] = (dact * slopes[layer][s, :, cols].astype(F32)).astype(BF16)
            dh = mm_nt(dup_s[s], expand_weight[layer])
            end_back(s, grad, unit_s[2 * layer + 1, s], scale_s[2 * layer + 1, s], gain2, dh)
            flow.ticks(s, n_seq, 1.3)
            return 0

        acc_s[0:2] = jnp.zeros((2, 8, width), F32)
        lax.fori_loop(0, n_seq, feed_back, 0)
        put_vector(dims.at["feed_gain"], jnp.sum(acc_s[0], 0, keepdims=True))
        put_vector(dims.at["feed_shift"], jnp.sum(acc_s[1], 0, keepdims=True))

        for c in range(blocks):
            total = product(norm_t.at[2 * layer + 1], dup_s, slice(c * BLOCK, (c + 1) * BLOCK))
            at = tops[1] + c * width
            sums[layer, at : at + width, :] = total[:width].astype(BF16)
            at_bias = dims.at["expand_bias"] + c
            vec_s[at_bias : at_bias + 1, :] = total[width : width + 1]
            flow.ready(layer, at + width)
            flow.tick(0.45)

        bias_parts = []
        for c in range(0, width, BLOCK):
            size = min(BLOCK, width - c)
            total = product(mixed_t.at[layer], grad_low, slice(c, c + size))
            for k in range(0, size, LANES):
                put_tile(layer, tops[2], (c + k) // LANES, total[:width, k : k + LANES])
                bias_parts.append(total[width : width + 1, k : k + LANES])
        put_vector(dims.at["output_bias"], jnp.concatenate(bias_parts, 1))
        flow.ready(layer, tops[3])
        flow.tick(0.8)

        def attend_back(s, _):
            grad = grad_s[s]
            dmixed = mm_nt(grad_low[s], output_weight[layer])
            parts = [None] * (3 * pairs)
            for p in range(pairs):
                at = p * LANES
                query = packed_s[layer, s, :, at : at + LANES]
                key = packed_s[layer, s, :, width + at : width + at + LANES]
                value = packed_s[layer, s, :, 2 * width + at : 2 * width + at + LANES]
                dm = dmixed[:, at : at + LANES] * inverse_s[layer, s, :, at : at + LANES]
                inner = -(dm * mixed_s[layer, s, :, at : at + LANES].astype(F32)).astype(BF16)
                dm = dm.astype(BF16)
                wide_value = jnp.concatenate([value, jnp.ones_like(value)], 1)
                dq = dk = dv = None
                for h, half in enumerate((low_half, high_half)):
                    power = power_s[layer, s, 2 * p + h]
                    dm_half = dm * half
                    left = jnp.concatenate([dm_half, inner * half], 1)
                    ds = (power.astype(F32) * mm_nt(left, wide_value)).astype(BF16)
                    terms = (mm(ds, key * half), mm_tn(ds, query * half), mm_tn(power, dm_half))
                    dq = terms[0] if dq is None else dq + terms[0]
                    dk = terms[1] if dk is None else dk + terms[1]
                    dv = terms[2] if dv is None else dv + terms[2]
                parts[p] = (dq * score_scale).astype(BF16)
                parts[pairs + p] = (dk * score_scale).astype(BF16)
                parts[2 * pairs + p] = dv.astype(BF16)
            dpacked = jnp.concatenate(parts, 1)
            dup_s[s, :, 0 : 3 * width] = dpacked
            dh = mm_nt(dpacked, mixer_weight[layer])
            end_back(s, grad, unit_s[2 * layer, s], scale_s[2 * layer, s], gain, dh)
            if layer == 1:
                start_back(s, grad_s[s])
            flow.ticks(s, n_seq, 2.3)
            return 0

        acc_s[...] = jnp.zeros_like(acc_s)
        lax.fori_loop(0, n_seq, attend_back, 0)
        put_vector(dims.at["attend_gain"], jnp.sum(acc_s[0], 0, keepdims=True))
        put_vector(dims.at["attend_shift"], jnp.sum(acc_s[1], 0, keepdims=True))

        bias_parts = []
        for c in range(0, 3 * width, BLOCK):
            size = min(BLOCK, 3 * width - c)
            total = product(norm_t.at[2 * layer], dup_s, slice(c, c + size))
            for k in range(0, size, LANES):
                put_tile(layer, tops[3], (c + k) // LANES, total[:width, k : k + LANES])
                bias_parts.append(total[width : width + 1, k : k + LANES])
            flow.tick(0.5)
        each = width // LANES
        put_vector(
            dims.at["mixer_bias"],
            jnp.concatenate(bias_parts[:each] + bias_parts[2 * each :], 1),
        )
        sums[layer, tops[4] : tops[4] + dims.vec_rows, :] = vec_s[...].astype(BF16)
        rest = dims.rows - tops[4] - dims.vec_rows
        if rest:
            sums[layer, dims.rows - rest :, :] = jnp.zeros((rest, BLOCK), BF16)
        flow.ready(layer, dims.rows)

    for s in range(n_global):
        crop_s[:, s, :] = grad_s[s, 0:glen, :]
    global_back[...] = crop_s[...].astype(BF16)
    for j in range(n_local):
        s, at = n_global + j // group, llen * (j % group)
        local_back[j] = grad_s[s, at : at + llen, :].astype(BF16)
    flow.drain()


class Wire:
    def __init__(self, size, first, second):
        self.size, self.first, self.second = size, first, second


def wires_of(mesh):
    names = mesh.axis_names
    places = {}
    for axis, name in enumerate(names):
        line = [mesh.devices[tuple(i if a == axis else 0 for a in range(2))] for i in range(mesh.devices.shape[axis])]
        spots = [(d.core_on_chip,) + tuple(d.coords) for d in line]
        found, total = [], 1
        for k in range(4):
            values = sorted({p[k] for p in spots})
            if len(values) > 1:
                stride = next(i for i, p in enumerate(spots) if p[k] != spots[0][k])
                found.append((k, axis, stride, len(values)))
                total *= len(values)
        good = total == len(line)
        for k, _, stride, size in found:
            values = [p[k] for p in spots]
            good = good and all(v == values[i // stride % size * stride] for i, v in enumerate(values))
        if not good:
            found = [(4 + axis, axis, 1, len(line))]
        for k, axis, stride, size in found:
            places[k] = (axis, stride, size)
    wires = []
    if 0 in places:
        wires.append(Wire(places[0][2], places[0], places[0]))
    if 0 in places and 1 in places and 2 in places and places[1][2] == places[2][2]:
        wires.append(Wire(places[1][2], places[1], places[2]))
        wires.append(Wire(places[1][2], places[2], places[1]))
        order = [3, 4, 5]
    else:
        order = [1, 2, 3, 4, 5]
    for k in order:
        if k in places:
            wires.append(Wire(places[k][2], places[k], places[k]))
    return wires


class Net:
    def __init__(self, wires):
        self.axes = ("dp", "section")
        self.here = [lax.axis_index(a) for a in self.axes]
        self.wires = wires
        first = wires[0]
        odd = self.spot(first.first) % 2 if first.size == 2 else 0
        self.odd = odd
        self.at = []
        for w in wires:
            a, b = self.spot(w.first), self.spot(w.second)
            self.at.append(a if w.first == w.second else a + odd * (b - a))

    def spot(self, place):
        axis, stride, size = place
        return self.here[axis] // stride % size

    def peer(self, stage, k):
        w = self.wires[stage]
        place = (self.at[stage] + k) % w.size
        move = place - self.at[stage]
        target = list(self.here)
        if w.first == w.second:
            target[w.first[0]] = target[w.first[0]] + move * w.first[1]
        else:
            target[w.first[0]] = target[w.first[0]] + move * w.first[1] * (1 - self.odd)
            target[w.second[0]] = target[w.second[0]] + move * w.second[1] * self.odd
        return tuple(target), place

    def greet(self):
        barrier = pltpu.get_barrier_semaphore()
        for stage, w in enumerate(self.wires):
            for k in range(1, w.size):
                pl.semaphore_signal(barrier, inc=1, device_id=self.peer(stage, k)[0], device_id_type=pl.DeviceIdType.MESH)

    def wait_greeting(self):
        pl.semaphore_wait(pltpu.get_barrier_semaphore(), sum(w.size - 1 for w in self.wires))


class Chunk:
    def __init__(self, net, sums, out, landing, sems, turn, layer, end):
        self.net, self.sums, self.out, self.landing = net, sums, out, landing
        self.send, self.recv, self.local, self.sent, self.free = sems
        self.turn = turn
        self.layer, self.end = layer, end
        self.due = None
        size, start = sums.shape[0], 0
        self.unit = size
        for w in net.wires:
            self.unit //= w.size
        self.size, self.start = [], []
        for stage, w in enumerate(net.wires):
            size //= w.size
            self.size.append(size)
            self.start.append((start, size))
            start = start + net.at[stage] * size
        self.own = start
        self.stages = len(net.wires)
        self.step = 0
        self.sem_at, at = {}, 0
        for phase in range(2):
            for stage, w in enumerate(net.wires):
                for k in range(1, w.size):
                    self.sem_at[phase, stage, k] = at
                    at += 1

    def rows(self, stage, place):
        start, size = self.start[stage]
        return pl.ds(pl.multiple_of(start + place * size, TILE), size)

    def copy(self, phase, stage, k):
        target, place = self.net.peer(stage, k)
        at = self.sem_at[phase, stage, k]
        if phase == 0:
            source, to = self.sums.at[self.rows(stage, place)], self.landing[stage].at[k - 1]
        else:
            rows = self.rows(stage, self.net.at[stage])
            source = to = self.sums.at[rows]
        return pltpu.make_async_remote_copy(
            src_ref=source,
            dst_ref=to,
            send_sem=self.send.at[at],
            recv_sem=self.recv.at[at],
            device_id=target,
            device_id_type=pl.DeviceIdType.MESH,
        )

    def arrival(self, stage, k):
        target, place = self.net.peer(stage, self.net.wires[stage].size - k)
        at = self.sem_at[1, stage, k]
        landed = self.sums.at[self.rows(stage, place)]
        return pltpu.make_async_remote_copy(
            src_ref=landed,
            dst_ref=landed,
            send_sem=self.send.at[at],
            recv_sem=self.recv.at[at],
            device_id=target,
            device_id_type=pl.DeviceIdType.MESH,
        )

    def start_stage(self, phase, stage):
        if phase == 0 and self.turn == 1:
            pl.semaphore_wait(self.free.at[stage], self.net.wires[stage].size - 1)
        if phase == 1:
            pl.semaphore_wait(self.sent.at[stage], self.net.wires[stage].size - 1)
        for k in range(1, self.net.wires[stage].size):
            self.copy(phase, stage, k).start()

    def load(self):
        last = self.stages - 1
        stage = self.step if self.step <= last else 2 * self.stages - 1 - self.step
        peers = self.net.wires[stage].size - 1
        row = BLOCK * 2
        if stage == 0:
            return 0, self.size[0] * row / 4
        if stage == last:
            return 2, self.size[stage] * (peers + 1) ** 2 / 2 * row
        return 1, self.size[stage] * peers * row

    def begin(self):
        self.start_stage(0, 0)

    def out_copy(self):
        return pltpu.make_async_copy(self.sums, self.out, self.local.at[0])

    def advance(self):
        step = self.step
        self.step += 1
        if step < self.stages:
            peers = range(1, self.net.wires[step].size)
            for k in peers:
                self.copy(0, step, k).wait_recv()
            base = self.start[step][0] + self.net.at[step] * self.size[step]
            landing = self.landing[step]

            def add(i, _):
                at = pl.ds(pl.multiple_of(base + i * self.unit, TILE), self.unit)
                total = self.sums[at, :].astype(F32)
                for k in peers:
                    total = total + landing[k - 1, pl.ds(pl.multiple_of(i * self.unit, TILE), self.unit), :].astype(F32)
                self.sums[at, :] = total.astype(BF16)
                return 0

            lax.fori_loop(0, self.size[step] // self.unit, add, 0)
            for k in peers:
                self.copy(0, step, k).wait_send()
                target = self.net.peer(step, k)[0]
                pl.semaphore_signal(self.sent.at[step], inc=1, device_id=target, device_id_type=pl.DeviceIdType.MESH)
                if self.turn == 0:
                    pl.semaphore_signal(self.free.at[step], inc=1, device_id=target, device_id_type=pl.DeviceIdType.MESH)
            if step + 1 < self.stages:
                self.start_stage(0, step + 1)
            else:
                self.start_stage(1, step)
        else:
            stage = 2 * self.stages - 1 - step
            for k in range(1, self.net.wires[stage].size):
                self.arrival(stage, k).wait_recv()
            if stage > 0:
                self.start_stage(1, stage - 1)
            else:
                self.out_copy().start()

    def finish(self):
        for phase, stage, k in self.sem_at:
            if phase == 1:
                self.copy(phase, stage, k).wait_send()
        self.out_copy().wait()


LATENCY = 2.0
RATE = 80e3
STEP = 0.4


class Flow:
    def __init__(self, net):
        self.chunks, self.now, self.waiting, self.free = [], 0.0, 0, [0.0] * 3

    def book(self, chunk):
        kind, size = chunk.load()
        self.free[kind] = max(self.now, self.free[kind]) + size / RATE
        chunk.due = self.free[kind] + LATENCY

    def ready(self, layer, rows):
        while self.waiting < len(self.chunks):
            chunk = self.chunks[self.waiting]
            if chunk.layer != layer or chunk.end > rows:
                return
            chunk.begin()
            self.book(chunk)
            self.waiting += 1

    def due(self):
        return sorted((c for c in self.chunks if c.due is not None and c.due <= self.now), key=lambda c: c.due)

    def take(self):
        while self.due():
            chunk = self.due()[0]
            chunk.advance()
            self.now += STEP
            if chunk.step < 2 * chunk.stages:
                self.book(chunk)
            else:
                chunk.due = None

    def tick(self, time):
        self.now += time
        self.take()

    def ticks(self, s, count, time):
        for i in range(count):
            self.now += time
            if self.due():
                pl.when(s == i)(self.take)

    def drain(self):
        while any(c.due is not None for c in self.chunks):
            self.now = max(self.now, min(c.due for c in self.chunks if c.due is not None))
            self.take()
        for chunk in self.chunks:
            chunk.finish()


class Dims:
    def __init__(self, global_crops, local_crops, hidden, wires):
        self.wires = wires
        self.glen, self.n_global, self.width = global_crops.shape
        self.n_local, self.llen, _ = local_crops.shape
        self.hidden = hidden
        self.seq = up_to(self.glen, TILE)
        self.group = self.seq // self.llen
        while self.n_local % self.group:
            self.group -= 1
        self.n_seq = self.n_global + self.n_local // self.group
        sizes = (
            ("attend_gain", self.width),
            ("attend_shift", self.width),
            ("mixer_bias", 2 * self.width),
            ("output_bias", self.width),
            ("feed_gain", self.width),
            ("feed_shift", self.width),
            ("expand_bias", hidden),
            ("reduce_bias", self.width),
        )
        self.names, self.sizes = [name for name, _ in sizes], dict(sizes)
        self.at, row = {}, 0
        for name, size in sizes:
            self.at[name] = row
            row += -(-size // BLOCK)
        self.vec_rows = 2 * TILE
        assert row <= self.vec_rows and self.width * hidden % self.vec_rows == 0
        step = TILE
        for w in wires:
            step *= w.size
        ff = self.width * hidden // BLOCK
        square = self.width * self.width // BLOCK
        self.tops = (0, ff, 2 * ff, 2 * ff + square, 2 * ff + 4 * square)
        self.rows = up_to(self.tops[4] + self.vec_rows, step)
        parts = self.rows // step
        cuts = ((0, 4, 7, 10, 12, 14), (0, 4, 10, 14))
        self.bounds = [[c * step for c in sorted({parts * k // 14 for k in layer})] for layer in cuts]
        self.landing_sets = [len(b) - 1 for b in self.bounds[::-1]]
        if self.bounds[0] == self.bounds[1]:
            self.landing_sets = self.landing_sets[:1]
        self.n_chunk = sum(len(b) - 1 for b in self.bounds)


def run_kernel(counts, arrays, dims):
    d = dims
    n, seq, width, hidden = d.n_seq, d.seq, d.width, d.hidden
    crops = [jax.ShapeDtypeStruct(a.shape, BF16) for a in arrays[:2]]
    outs = crops + crops
    outs += [jax.ShapeDtypeStruct((2, d.rows, BLOCK), BF16)]
    scratch = [
        pltpu.VMEM((2, d.rows, BLOCK), BF16),
        pltpu.VMEM((d.glen, d.n_global, width), F32),
        pltpu.VMEM((n, seq, width), F32),
        pltpu.VMEM((4, n, seq, width), BF16),
        pltpu.VMEM((4, n, seq, 1), F32),
        pltpu.VMEM((4, n, width + TILE, seq), BF16),
        pltpu.VMEM((2, n, seq, 3 * width), BF16),
        pltpu.VMEM((2, n, HEADS, seq, seq), BF16),
        pltpu.VMEM((2, n, seq, width), F32),
        pltpu.VMEM((2, n, seq, width), BF16),
        pltpu.VMEM((2, n, width + TILE, seq), BF16),
        pltpu.VMEM((2, n, seq, hidden), BF16),
        pltpu.VMEM((n, seq, hidden), BF16),
        pltpu.VMEM((n, seq, width), F32),
        pltpu.VMEM((n, seq, width), BF16),
        pltpu.VMEM((n, width, seq), BF16),
        pltpu.VMEM((n, seq, hidden), BF16),
        pltpu.VMEM((2, seq, seq), BF16),
        pltpu.VMEM((d.vec_rows, BLOCK), F32),
        pltpu.VMEM((3, 8, width), F32),
    ]
    for layer in (1, 0)[: len(d.landing_sets)]:
        for first, end in zip(d.bounds[layer], d.bounds[layer][1:]):
            rows = end - first
            for w in d.wires:
                rows //= w.size
                scratch.append(pltpu.VMEM((w.size - 1, rows, BLOCK), BF16))
    peers = 2 * sum(w.size - 1 for w in d.wires)
    scratch += [
        pltpu.SemaphoreType.DMA((d.n_chunk, peers)),
        pltpu.SemaphoreType.DMA((d.n_chunk, peers)),
        pltpu.SemaphoreType.DMA((d.n_chunk, 1)),
        pltpu.SemaphoreType.REGULAR((d.n_chunk, len(d.wires))),
        pltpu.SemaphoreType.REGULAR((d.n_chunk, len(d.wires))),
    ]
    vmem = pl.BlockSpec(memory_space=pltpu.VMEM)
    anywhere = pl.BlockSpec(memory_space=pl.ANY)
    return pl.pallas_call(
        functools.partial(kernel, d),
        out_shape=outs,
        in_specs=[pl.BlockSpec(memory_space=pltpu.SMEM)] + [vmem] * len(arrays),
        out_specs=[vmem] * 4 + [anywhere],
        scratch_shapes=scratch,
        compiler_params=pltpu.CompilerParams(
            vmem_limit_bytes=63 * 1024 * 1024, collective_id=0, has_side_effects=True
        ),
    )(counts, *arrays)


THIRDS = 3


def cast_kernel(dims, reduce, expand, output, mixer, vectors, *rest):
    crops, outs, sems = rest[:4], rest[4:-5], rest[-1]
    copies = [pltpu.make_async_copy(a, b, sems.at[i]) for i, (a, b) in enumerate(zip(crops, rest[-5:-1], strict=True))]

    @pl.when((pl.program_id(0) == 0) & (pl.program_id(1) == 0))
    def _():
        for copy in copies:
            copy.start()

    mixer_grad, output_grad, expand_grad, reduce_grad = outs[:4]
    width = dims.width
    fold = width // 2
    for b in range(2):
        rows = slice(b * width, (b + 1) * width)
        cols = slice(b * BLOCK, (b + 1) * BLOCK)
        expand_grad[0, :, cols] = expand[0, rows, :].astype(F32)
        reduce_grad[0, cols, :] = reduce[0, rows, :].T.astype(F32)
    for source, target in ((mixer, mixer_grad), (output, output_grad)):
        target[0, :, 0:BLOCK] = source[0, 0:width, :].astype(F32)
        target[0, 0:fold, BLOCK:] = source[0, width:, 0:LANES].astype(F32)
        target[0, fold:, BLOCK:] = source[0, width:, LANES:].astype(F32)

    @pl.when((pl.program_id(0) == 1) & (pl.program_id(1) == THIRDS - 1))
    def _():
        for ref, name in zip(outs[4:], dims.names, strict=True):
            size = ref.shape[1]
            for c in range(0, size, BLOCK):
                at = dims.at[name] + c // BLOCK
                piece = min(BLOCK, size - c)
                for layer in range(2):
                    ref[layer : layer + 1, c : c + piece] = vectors[layer].astype(F32)[at : at + 1, 0:piece]
        for copy in copies:
            copy.wait()


def run_cast(sums, crops, dims):
    d = dims
    width, hidden = d.width, d.hidden
    part = (1, 2 * width, BLOCK)
    square = (1, width * width // BLOCK, BLOCK)
    grads = [(width, 3 * width), (width, width), (width, hidden), (hidden, width)]
    shapes = [jax.ShapeDtypeStruct((2,) + g, F32) for g in grads]
    specs = [
        pl.BlockSpec((1, width, 3 * width // THIRDS), lambda l, t: (l, 0, t)),
        pl.BlockSpec((1, width, width), lambda l, t: (l, 0, 0)),
        pl.BlockSpec((1, width, hidden // THIRDS), lambda l, t: (l, 0, t)),
        pl.BlockSpec((1, hidden // THIRDS, width), lambda l, t: (l, t, 0)),
    ]
    for name in d.names:
        shapes.append(jax.ShapeDtypeStruct((2, d.sizes[name]), F32))
        specs.append(pl.BlockSpec((2, d.sizes[name]), lambda l, t: (0, 0)))
    for crop in crops:
        shapes.append(jax.ShapeDtypeStruct(crop.shape, crop.dtype))
        specs.append(pl.BlockSpec(memory_space=pl.ANY))
    return pl.pallas_call(
        functools.partial(cast_kernel, d),
        grid=(2, THIRDS),
        out_shape=shapes,
        in_specs=[
            pl.BlockSpec(part, lambda l, t: (l, t, 0)),
            pl.BlockSpec(part, lambda l, t: (l, THIRDS + t, 0)),
            pl.BlockSpec(square, lambda l, t: (l, d.tops[2] // square[1], 0)),
            pl.BlockSpec(square, lambda l, t: (l, d.tops[3] // square[1] + t, 0)),
            pl.BlockSpec((2, d.vec_rows, BLOCK), lambda l, t: (0, d.tops[4] // d.vec_rows, 0)),
        ]
        + [pl.BlockSpec(memory_space=pl.ANY)] * 4,
        out_specs=specs,
        scratch_shapes=[pltpu.SemaphoreType.DMA((4,))],
        compiler_params=pltpu.CompilerParams(vmem_limit_bytes=62 * 1024 * 1024),
    )(sums, sums, sums, sums, sums, *crops)


def shards(wires, global_crops, local_crops, local_count, global_cotangent, local_cotangent, *weights):
    global_crops, global_cotangent = global_crops.transpose(1, 0, 2), global_cotangent.transpose(1, 0, 2)
    dims = Dims(global_crops, local_crops, weights[8].shape[2], wires)
    outs = run_kernel(
        local_count, (global_crops, local_crops, global_cotangent, local_cotangent) + weights, dims
    )
    mixer, output, expand, reduce, *rest = run_cast(outs[4], outs[:4], dims)
    vectors, crops = rest[:-4], rest[-4:]
    v = dict(zip(dims.names, vectors, strict=True))
    return (
        crops[0].transpose(1, 0, 2),
        crops[1],
        crops[2].transpose(1, 0, 2),
        crops[3],
        v["attend_gain"],
        v["attend_shift"],
        mixer,
        v["mixer_bias"],
        output,
        v["output_bias"],
        v["feed_gain"],
        v["feed_shift"],
        expand,
        v["expand_bias"],
        reduce,
        v["reduce_bias"],
    )


def solution(mesh):
    crops = P(("dp", "section"), None, None)
    return jax.shard_map(
        functools.partial(shards, wires_of(mesh)),
        mesh=mesh,
        in_specs=(crops, crops, P("dp"), crops, crops) + (P(),) * 12,
        out_specs=(crops,) * 4 + (P(),) * 12,
        check_vma=False,
    )
```

```python
import functools

import jax
import jax.numpy as jnp
from jax import lax
from jax.experimental import pallas as pl
from jax.experimental.pallas import tpu as pltpu
from jax.sharding import PartitionSpec as P

HEADS = 6
HEAD = 64
EPS = 1e-06
TILE = 16
LANES = 128
BLOCK = 256
LOG2E = 1.4426950408889634
F32 = jnp.float32
BF16 = jnp.bfloat16


def up_to(value, step):
    return -(-value // step) * step


def mm(left, right):
    return lax.dot_general(left, right, (((1,), (0,)), ((), ())), preferred_element_type=F32)


def mm_nt(left, right):
    return lax.dot_general(left, right, (((1,), (1,)), ((), ())), preferred_element_type=F32)


def mm_tn(left, right):
    return lax.dot_general(left, right, (((0,), (0,)), ((), ())), preferred_element_type=F32)


def norm(rows):
    centred = rows - jnp.mean(rows, -1, keepdims=True)
    scale = lax.rsqrt(jnp.mean(centred * centred, -1, keepdims=True) + EPS)
    return centred * scale, scale


def norm_back(grad, unit, scale, gain):
    slope = grad * gain
    first = jnp.mean(slope, -1, keepdims=True)
    second = jnp.mean(slope * unit, -1, keepdims=True)
    return scale * (slope - first - unit * second)


def gelu_parts(u):
    size = jnp.abs(u)
    d = 1.0 + (0.3275911 * 0.7071067811865476) * size
    t = pl.reciprocal(d, approx=True)
    t = t * (2.0 - d * t)
    poly = 0.5 * 1.061405429
    for a in (-1.453152027, 1.421413741, -0.284496736, 0.254829592):
        poly = poly * t + 0.5 * a
    bell = jnp.exp2((u * u) * (-0.5 * LOG2E))
    tail = poly * t * bell
    phi = jnp.where(u < 0.0, tail, 1.0 - tail)
    return u * phi, phi + (u * bell) * 0.3989422804014327


def fold8(value):
    rows, width = value.shape
    return jnp.sum(value.reshape(rows // 8, 8, width), 0)


def kernel(
    dims,
    counts,
    global_in,
    local_in,
    global_cot,
    local_cot,
    attend_gain,
    attend_shift,
    mixer_weight,
    mixer_bias,
    output_weight,
    output_bias,
    feed_gain,
    feed_shift,
    expand_weight,
    expand_bias,
    reduce_weight,
    reduce_bias,
    global_out,
    local_out,
    global_back,
    local_back,
    sums_out,
    sums,
    crop_s,
    x_s,
    unit_s,
    scale_s,
    norm_t,
    packed_s,
    power_s,
    inverse_s,
    mixed_s,
    mixed_t,
    act_s,
    slope_s,
    grad_s,
    grad_low,
    grad_t,
    dup_s,
    mask_s,
    vec_s,
    acc_s,
    *wires,
):
    seq, group, width = dims.seq, dims.group, dims.width
    glen, llen = dims.glen, dims.llen
    n_global, n_local, n_seq = dims.n_global, dims.n_local, dims.n_seq
    hidden = dims.hidden
    count = counts[lax.axis_index("section")]
    pairs = HEADS // 2
    lane = lax.broadcasted_iota(jnp.int32, (1, LANES), 1)
    low_half = (lane < HEAD).astype(F32).astype(BF16)
    high_half = (lane >= HEAD).astype(F32).astype(BF16)
    score_scale = HEAD ** (-0.5)

    net = Net(dims.wires)
    net.greet()
    n_stage = len(dims.wires)
    sets = dims.landing_sets
    landings, sems = wires[: n_stage * sum(sets)], wires[n_stage * sum(sets) :]
    flow = Flow(net)
    number = 0
    for layer in (1, 0):
        bounds = dims.bounds[layer]
        for i in range(len(bounds) - 1):
            shared = len(sets) == 1
            at = (i if shared else number) * n_stage
            own = [w.at[number] for w in sems[:4]] + [sems[4].at[i]]
            rows = pl.ds(bounds[i], bounds[i + 1] - bounds[i])
            turn = (1 - layer) if shared else None
            flow.chunks.append(
                Chunk(net, sums.at[layer, rows], sums_out.at[layer, rows], landings[at : at + n_stage], own, turn, layer, bounds[i + 1])
            )
            number += 1

    for s in range(n_seq):
        x_s[s, seq - 32 :, :] = jnp.zeros((32, width), F32)
        grad_s[s, seq - 32 :, :] = jnp.zeros((32, width), F32)
    row_id = lax.broadcasted_iota(jnp.int32, (seq, seq), 0)
    col_id = lax.broadcasted_iota(jnp.int32, (seq, seq), 1)
    row_crop = sum((row_id >= llen * j).astype(jnp.int32) for j in range(1, group + 1))
    col_crop = sum((col_id >= llen * j).astype(jnp.int32) for j in range(1, group + 1))
    far = jnp.float32(-1e30)
    mask_s[0] = jnp.where(col_id < glen, jnp.float32(0), far).astype(BF16)
    mask_s[1] = jnp.where(row_crop == col_crop, jnp.float32(0), far).astype(BF16)
    one_row = (lax.broadcasted_iota(jnp.int32, (TILE, seq), 0) == 0).astype(F32).astype(BF16)
    for s in range(n_seq):
        for i in range(4):
            norm_t[i, s, width:, :] = one_row
        for i in range(2):
            mixed_t[i, s, width:, :] = one_row

    def live_rows(g):
        rows = lax.broadcasted_iota(jnp.int32, (seq, 1), 0)
        return (rows < llen * jnp.clip(count - g * group, 0, group)).astype(F32)

    for source, target in ((global_in, x_s), (global_cot, grad_s)):
        crop_s[...] = source[...].astype(F32)
        for s in range(n_global):
            target[s, 0:glen, :] = crop_s[:, s, :]
    for j in range(n_local):
        s, at = n_global + j // group, llen * (j % group)
        x_s[s, at : at + llen, :] = local_in[j].astype(F32)
        grad_s[s, at : at + llen, :] = local_cot[j].astype(F32)
    for s in range(n_global, n_seq):
        grad_s[s] = grad_s[s] * live_rows(s - n_global)

    def row(ref, layer):
        return ref[...].astype(F32)[layer : layer + 1]

    slopes = (slope_s, dup_s)

    def start_back(s, grad):
        grad_t[s] = grad.astype(BF16).T
        acc_s[2] = acc_s[2] + fold8(grad)

    def end_back(s, grad, unit, scale, gain, dh):
        unit = unit.astype(F32)
        acc_s[0] = acc_s[0] + fold8(dh * unit)
        acc_s[1] = acc_s[1] + fold8(dh)
        grad = (grad + norm_back(dh, unit, scale, gain)).astype(BF16)
        grad_low[s] = grad
        grad_s[s] = grad.astype(F32)

    def product(left, right, cols):
        total = mm(left[0], right[0, :, cols])
        for s in range(1, n_seq):
            total = total + mm(left[s], right[s, :, cols])
        return total

    for layer in range(2):
        gain, shift = row(attend_gain, layer), row(attend_shift, layer)
        bias = row(mixer_bias, layer)
        bias = jnp.concatenate([bias[:, :width], jnp.zeros((1, width), F32), bias[:, width:]], 1)
        out_bias = row(output_bias, layer)
        gain2, shift2 = row(feed_gain, layer), row(feed_shift, layer)
        bias_up, bias_down = row(expand_bias, layer), row(reduce_bias, layer)

        def attend(s, _):
            x = x_s[s]
            unit, scale = norm(x)
            unit_s[2 * layer, s] = unit.astype(BF16)
            scale_s[2 * layer, s] = scale
            normed = (unit * gain + shift).astype(BF16)
            norm_t[2 * layer, s, 0:width, :] = normed.T
            packed = (mm(normed, mixer_weight[layer]) + bias).astype(BF16)
            packed_s[layer, s] = packed
            mask = mask_s[jnp.where(s < n_global, 0, 1)].astype(F32)
            mixed = []
            for p in range(pairs):
                at = p * LANES
                query = packed[:, at : at + LANES]
                key = packed[:, width + at : width + at + LANES]
                value = packed[:, 2 * width + at : 2 * width + at + LANES]
                total = None
                for h, half in enumerate((low_half, high_half)):
                    scores = mm_nt(query * half, key) * (score_scale * LOG2E) + mask
                    power = jnp.exp2(scores - jnp.max(scores, -1, keepdims=True)).astype(BF16)
                    power_s[layer, s, 2 * p + h] = power
                    spread = jnp.broadcast_to(half, (seq, LANES))
                    term = mm(power, jnp.concatenate([value * half, spread], 1))
                    total = term if total is None else total + term
                inverse = 1.0 / total[:, LANES:]
                inverse_s[layer, s, :, at : at + LANES] = inverse
                mixed.append((total[:, :LANES] * inverse).astype(BF16))
            mixed = jnp.concatenate(mixed, 1)
            mixed_s[layer, s] = mixed
            mixed_t[layer, s, 0:width, :] = mixed.T
            x = x + mm(mixed, output_weight[layer]) + out_bias
            x_s[s] = x.astype(BF16).astype(F32)
            return 0

        lax.fori_loop(0, n_seq, attend, 0)

        def feed(s, _):
            x = x_s[s]
            unit, scale = norm(x)
            normed = (unit * gain2 + shift2).astype(BF16)
            norm_t[2 * layer + 1, s, 0:width, :] = normed.T
            unit_s[2 * layer + 1, s] = unit.astype(BF16)
            scale_s[2 * layer + 1, s] = scale
            if layer == 1:
                start_back(s, grad_s[s])
            for c in range(hidden // BLOCK):
                cols = slice(c * BLOCK, (c + 1) * BLOCK)
                up = mm(normed, expand_weight[layer, :, cols]) + bias_up[:, cols]
                act, slope = gelu_parts(up)
                act_s[layer, s, :, cols] = act.astype(BF16)
                slopes[layer][s, :, cols] = slope.astype(BF16)
            x = x + mm(act_s[layer, s], reduce_weight[layer]) + bias_down
            x_s[s] = x.astype(BF16).astype(F32)
            return 0

        if layer == 1:
            acc_s[...] = jnp.zeros_like(acc_s)
        lax.fori_loop(0, n_seq, feed, 0)

    for s in range(n_global):
        crop_s[:, s, :] = x_s[s, 0:glen, :]
    global_out[...] = crop_s[...].astype(BF16)
    for j in range(n_local):
        s, at = n_global + j // group, llen * (j % group)
        alive = (count > j).astype(F32)
        local_out[j] = (x_s[s, at : at + llen, :] * alive).astype(BF16)

    def put_vector(at, value):
        for c in range(0, value.shape[1], BLOCK):
            piece = value[:, c : c + BLOCK]
            vec_s[at + c // BLOCK : at + c // BLOCK + 1, 0 : piece.shape[1]] = piece

    def put_tile(layer, top, m, part):
        at = top + (m // 3) * (width + fold)
        side = m % 3 * LANES
        part = part.astype(BF16)
        if m % 3 < 2:
            sums[layer, at : at + width, side : side + LANES] = part
        else:
            at = at + width
            sums[layer, at : at + fold, 0:LANES] = part[:fold]
            sums[layer, at : at + fold, LANES:] = part[fold:]

    blocks = hidden // BLOCK
    fold = width // 2
    tops = dims.tops
    net.wait_greeting()
    for layer in (1, 0):
        vec_s[...] = jnp.zeros_like(vec_s)
        gain2, gain = row(feed_gain, layer), row(attend_gain, layer)
        put_vector(dims.at["reduce_bias"], jnp.sum(acc_s[2], 0, keepdims=True))

        for c in range(blocks):
            total = product(grad_t, act_s.at[layer], slice(c * BLOCK, (c + 1) * BLOCK))
            at = tops[0] + c * width
            sums[layer, at : at + width, :] = total.astype(BF16)
            flow.ready(layer, at + width)
            flow.tick(0.45)

        def feed_back(s, _):
            grad = grad_s[s]
            grad_in = grad.astype(BF16)
            for c in range(blocks):
                cols = slice(c * BLOCK, (c + 1) * BLOCK)
                dact = mm_nt(grad_in, reduce_weight[layer, cols, :])
                dup_s[s, :, cols] = (dact * slopes[layer][s, :, cols].astype(F32)).astype(BF16)
            dh = mm_nt(dup_s[s], expand_weight[layer])
            end_back(s, grad, unit_s[2 * layer + 1, s], scale_s[2 * layer + 1, s], gain2, dh)
            flow.ticks(s, n_seq, 1.3)
            return 0

        acc_s[0:2] = jnp.zeros((2, 8, width), F32)
        lax.fori_loop(0, n_seq, feed_back, 0)
        put_vector(dims.at["feed_gain"], jnp.sum(acc_s[0], 0, keepdims=True))
        put_vector(dims.at["feed_shift"], jnp.sum(acc_s[1], 0, keepdims=True))

        for c in range(blocks):
            total = product(norm_t.at[2 * layer + 1], dup_s, slice(c * BLOCK, (c + 1) * BLOCK))
            at = tops[1] + c * width
            sums[layer, at : at + width, :] = total[:width].astype(BF16)
            at_bias = dims.at["expand_bias"] + c
            vec_s[at_bias : at_bias + 1, :] = total[width : width + 1]
            flow.ready(layer, at + width)
            flow.tick(0.45)

        bias_parts = []
        for c in range(0, width, BLOCK):
            size = min(BLOCK, width - c)
            total = product(mixed_t.at[layer], grad_low, slice(c, c + size))
            for k in range(0, size, LANES):
                put_tile(layer, tops[2], (c + k) // LANES, total[:width, k : k + LANES])
                bias_parts.append(total[width : width + 1, k : k + LANES])
        put_vector(dims.at["output_bias"], jnp.concatenate(bias_parts, 1))
        flow.ready(layer, tops[3])
        flow.tick(0.8)

        def attend_back(s, _):
            grad = grad_s[s]
            dmixed = mm_nt(grad_low[s], output_weight[layer])
            parts = [None] * (3 * pairs)
            for p in range(pairs):
                at = p * LANES
                query = packed_s[layer, s, :, at : at + LANES]
                key = packed_s[layer, s, :, width + at : width + at + LANES]
                value = packed_s[layer, s, :, 2 * width + at : 2 * width + at + LANES]
                dm = dmixed[:, at : at + LANES] * inverse_s[layer, s, :, at : at + LANES]
                inner = -(dm * mixed_s[layer, s, :, at : at + LANES].astype(F32)).astype(BF16)
                dm = dm.astype(BF16)
                wide_value = jnp.concatenate([value, jnp.ones_like(value)], 1)
                dq = dk = dv = None
                for h, half in enumerate((low_half, high_half)):
                    power = power_s[layer, s, 2 * p + h]
                    dm_half = dm * half
                    left = jnp.concatenate([dm_half, inner * half], 1)
                    ds = (power.astype(F32) * mm_nt(left, wide_value)).astype(BF16)
                    terms = (mm(ds, key * half), mm_tn(ds, query * half), mm_tn(power, dm_half))
                    dq = terms[0] if dq is None else dq + terms[0]
                    dk = terms[1] if dk is None else dk + terms[1]
                    dv = terms[2] if dv is None else dv + terms[2]
                parts[p] = (dq * score_scale).astype(BF16)
                parts[pairs + p] = (dk * score_scale).astype(BF16)
                parts[2 * pairs + p] = dv.astype(BF16)
            dpacked = jnp.concatenate(parts, 1)
            dup_s[s, :, 0 : 3 * width] = dpacked
            dh = mm_nt(dpacked, mixer_weight[layer])
            end_back(s, grad, unit_s[2 * layer, s], scale_s[2 * layer, s], gain, dh)
            if layer == 1:
                start_back(s, grad_s[s])
            flow.ticks(s, n_seq, 2.3)
            return 0

        acc_s[...] = jnp.zeros_like(acc_s)
        lax.fori_loop(0, n_seq, attend_back, 0)
        put_vector(dims.at["attend_gain"], jnp.sum(acc_s[0], 0, keepdims=True))
        put_vector(dims.at["attend_shift"], jnp.sum(acc_s[1], 0, keepdims=True))

        bias_parts = []
        for c in range(0, 3 * width, BLOCK):
            size = min(BLOCK, 3 * width - c)
            total = product(norm_t.at[2 * layer], dup_s, slice(c, c + size))
            for k in range(0, size, LANES):
                put_tile(layer, tops[3], (c + k) // LANES, total[:width, k : k + LANES])
                bias_parts.append(total[width : width + 1, k : k + LANES])
            flow.tick(0.5)
        each = width // LANES
        put_vector(
            dims.at["mixer_bias"],
            jnp.concatenate(bias_parts[:each] + bias_parts[2 * each :], 1),
        )
        sums[layer, tops[4] : tops[4] + dims.vec_rows, :] = vec_s[...].astype(BF16)
        rest = dims.rows - tops[4] - dims.vec_rows
        if rest:
            sums[layer, dims.rows - rest :, :] = jnp.zeros((rest, BLOCK), BF16)
        flow.ready(layer, dims.rows)

    for s in range(n_global):
        crop_s[:, s, :] = grad_s[s, 0:glen, :]
    global_back[...] = crop_s[...].astype(BF16)
    for j in range(n_local):
        s, at = n_global + j // group, llen * (j % group)
        local_back[j] = grad_s[s, at : at + llen, :].astype(BF16)
    flow.drain()


class Wire:
    def __init__(self, size, first, second):
        self.size, self.first, self.second = size, first, second


def wires_of(mesh):
    names = mesh.axis_names
    places = {}
    for axis, name in enumerate(names):
        line = [mesh.devices[tuple(i if a == axis else 0 for a in range(2))] for i in range(mesh.devices.shape[axis])]
        spots = [(d.core_on_chip,) + tuple(d.coords) for d in line]
        found, total = [], 1
        for k in range(4):
            values = sorted({p[k] for p in spots})
            if len(values) > 1:
                stride = next(i for i, p in enumerate(spots) if p[k] != spots[0][k])
                found.append((k, axis, stride, len(values)))
                total *= len(values)
        good = total == len(line)
        for k, _, stride, size in found:
            values = [p[k] for p in spots]
            good = good and all(v == values[i // stride % size * stride] for i, v in enumerate(values))
        if not good:
            found = [(4 + axis, axis, 1, len(line))]
        for k, axis, stride, size in found:
            places[k] = (axis, stride, size)
    wires = []
    if 0 in places:
        wires.append(Wire(places[0][2], places[0], places[0]))
    if 0 in places and 1 in places and 2 in places and places[1][2] == places[2][2]:
        wires.append(Wire(places[1][2], places[1], places[2]))
        wires.append(Wire(places[1][2], places[2], places[1]))
        order = [3, 4, 5]
    else:
        order = [1, 2, 3, 4, 5]
    for k in order:
        if k in places:
            wires.append(Wire(places[k][2], places[k], places[k]))
    return wires


class Net:
    def __init__(self, wires):
        self.axes = ("dp", "section")
        self.here = [lax.axis_index(a) for a in self.axes]
        self.wires = wires
        first = wires[0]
        odd = self.spot(first.first) % 2 if first.size == 2 else 0
        self.odd = odd
        self.at = []
        for w in wires:
            a, b = self.spot(w.first), self.spot(w.second)
            self.at.append(a if w.first == w.second else a + odd * (b - a))

    def spot(self, place):
        axis, stride, size = place
        return self.here[axis] // stride % size

    def peer(self, stage, k):
        w = self.wires[stage]
        place = (self.at[stage] + k) % w.size
        move = place - self.at[stage]
        target = list(self.here)
        if w.first == w.second:
            target[w.first[0]] = target[w.first[0]] + move * w.first[1]
        else:
            target[w.first[0]] = target[w.first[0]] + move * w.first[1] * (1 - self.odd)
            target[w.second[0]] = target[w.second[0]] + move * w.second[1] * self.odd
        return tuple(target), place

    def greet(self):
        barrier = pltpu.get_barrier_semaphore()
        for stage, w in enumerate(self.wires):
            for k in range(1, w.size):
                pl.semaphore_signal(barrier, inc=1, device_id=self.peer(stage, k)[0], device_id_type=pl.DeviceIdType.MESH)

    def wait_greeting(self):
        pl.semaphore_wait(pltpu.get_barrier_semaphore(), sum(w.size - 1 for w in self.wires))


class Chunk:
    def __init__(self, net, sums, out, landing, sems, turn, layer, end):
        self.net, self.sums, self.out, self.landing = net, sums, out, landing
        self.send, self.recv, self.local, self.sent, self.free = sems
        self.turn = turn
        self.layer, self.end = layer, end
        self.due = None
        size, start = sums.shape[0], 0
        self.unit = size
        for w in net.wires:
            self.unit //= w.size
        self.size, self.start = [], []
        for stage, w in enumerate(net.wires):
            size //= w.size
            self.size.append(size)
            self.start.append((start, size))
            start = start + net.at[stage] * size
        self.own = start
        self.stages = len(net.wires)
        self.step = 0
        self.sem_at, at = {}, 0
        for phase in range(2):
            for stage, w in enumerate(net.wires):
                for k in range(1, w.size):
                    self.sem_at[phase, stage, k] = at
                    at += 1

    def rows(self, stage, place):
        start, size = self.start[stage]
        return pl.ds(pl.multiple_of(start + place * size, TILE), size)

    def copy(self, phase, stage, k):
        target, place = self.net.peer(stage, k)
        at = self.sem_at[phase, stage, k]
        if phase == 0:
            source, to = self.sums.at[self.rows(stage, place)], self.landing[stage].at[k - 1]
        else:
            rows = self.rows(stage, self.net.at[stage])
            source = to = self.sums.at[rows]
        return pltpu.make_async_remote_copy(
            src_ref=source,
            dst_ref=to,
            send_sem=self.send.at[at],
            recv_sem=self.recv.at[at],
            device_id=target,
            device_id_type=pl.DeviceIdType.MESH,
        )

    def arrival(self, stage, k):
        target, place = self.net.peer(stage, self.net.wires[stage].size - k)
        at = self.sem_at[1, stage, k]
        landed = self.sums.at[self.rows(stage, place)]
        return pltpu.make_async_remote_copy(
            src_ref=landed,
            dst_ref=landed,
            send_sem=self.send.at[at],
            recv_sem=self.recv.at[at],
            device_id=target,
            device_id_type=pl.DeviceIdType.MESH,
        )

    def start_stage(self, phase, stage):
        if phase == 0 and self.turn == 1:
            pl.semaphore_wait(self.free.at[stage], self.net.wires[stage].size - 1)
        if phase == 1:
            pl.semaphore_wait(self.sent.at[stage], self.net.wires[stage].size - 1)
        for k in range(1, self.net.wires[stage].size):
            self.copy(phase, stage, k).start()

    def load(self):
        last = self.stages - 1
        stage = self.step if self.step <= last else 2 * self.stages - 1 - self.step
        peers = self.net.wires[stage].size - 1
        row = BLOCK * 2
        if stage == 0:
            return 0, self.size[0] * row / 4
        if stage == last:
            return 2, self.size[stage] * (peers + 1) ** 2 / 2 * row
        return 1, self.size[stage] * peers * row

    def begin(self):
        self.start_stage(0, 0)

    def out_copy(self):
        return pltpu.make_async_copy(self.sums, self.out, self.local.at[0])

    def advance(self):
        step = self.step
        self.step += 1
        if step < self.stages:
            peers = range(1, self.net.wires[step].size)
            for k in peers:
                self.copy(0, step, k).wait_recv()
            base = self.start[step][0] + self.net.at[step] * self.size[step]
            landing = self.landing[step]

            def add(i, _):
                at = pl.ds(pl.multiple_of(base + i * self.unit, TILE), self.unit)
                total = self.sums[at, :].astype(F32)
                for k in peers:
                    total = total + landing[k - 1, pl.ds(pl.multiple_of(i * self.unit, TILE), self.unit), :].astype(F32)
                self.sums[at, :] = total.astype(BF16)
                return 0

            lax.fori_loop(0, self.size[step] // self.unit, add, 0)
            for k in peers:
                self.copy(0, step, k).wait_send()
                target = self.net.peer(step, k)[0]
                pl.semaphore_signal(self.sent.at[step], inc=1, device_id=target, device_id_type=pl.DeviceIdType.MESH)
                if self.turn == 0:
                    pl.semaphore_signal(self.free.at[step], inc=1, device_id=target, device_id_type=pl.DeviceIdType.MESH)
            if step + 1 < self.stages:
                self.start_stage(0, step + 1)
            else:
                self.start_stage(1, step)
        else:
            stage = 2 * self.stages - 1 - step
            for k in range(1, self.net.wires[stage].size):
                self.arrival(stage, k).wait_recv()
            if stage > 0:
                self.start_stage(1, stage - 1)
            else:
                self.out_copy().start()

    def finish(self):
        for phase, stage, k in self.sem_at:
            if phase == 1:
                self.copy(phase, stage, k).wait_send()
        self.out_copy().wait()


LATENCY = 2.0
RATE = 80e3
STEP = 0.4


class Flow:
    def __init__(self, net):
        self.chunks, self.now, self.waiting, self.free = [], 0.0, 0, [0.0] * 3

    def book(self, chunk):
        kind, size = chunk.load()
        self.free[kind] = max(self.now, self.free[kind]) + size / RATE
        chunk.due = self.free[kind] + LATENCY

    def ready(self, layer, rows):
        while self.waiting < len(self.chunks):
            chunk = self.chunks[self.waiting]
            if chunk.layer != layer or chunk.end > rows:
                return
            chunk.begin()
            self.book(chunk)
            self.waiting += 1

    def due(self):
        return sorted((c for c in self.chunks if c.due is not None and c.due <= self.now), key=lambda c: c.due)

    def take(self):
        while self.due():
            chunk = self.due()[0]
            chunk.advance()
            self.now += STEP
            if chunk.step < 2 * chunk.stages:
                self.book(chunk)
            else:
                chunk.due = None

    def tick(self, time):
        self.now += time
        self.take()

    def ticks(self, s, count, time):
        for i in range(count):
            self.now += time
            if self.due():
                pl.when(s == i)(self.take)

    def drain(self):
        while any(c.due is not None for c in self.chunks):
            self.now = max(self.now, min(c.due for c in self.chunks if c.due is not None))
            self.take()
        for chunk in self.chunks:
            chunk.finish()


class Dims:
    def __init__(self, global_crops, local_crops, hidden, wires):
        self.wires = wires
        self.glen, self.n_global, self.width = global_crops.shape
        self.n_local, self.llen, _ = local_crops.shape
        self.hidden = hidden
        self.seq = up_to(self.glen, TILE)
        self.group = self.seq // self.llen
        while self.n_local % self.group:
            self.group -= 1
        self.n_seq = self.n_global + self.n_local // self.group
        sizes = (
            ("attend_gain", self.width),
            ("attend_shift", self.width),
            ("mixer_bias", 2 * self.width),
            ("output_bias", self.width),
            ("feed_gain", self.width),
            ("feed_shift", self.width),
            ("expand_bias", hidden),
            ("reduce_bias", self.width),
        )
        self.names, self.sizes = [name for name, _ in sizes], dict(sizes)
        self.at, row = {}, 0
        for name, size in sizes:
            self.at[name] = row
            row += -(-size // BLOCK)
        self.vec_rows = 2 * TILE
        assert row <= self.vec_rows and self.width * hidden % self.vec_rows == 0
        step = TILE
        for w in wires:
            step *= w.size
        ff = self.width * hidden // BLOCK
        square = self.width * self.width // BLOCK
        self.tops = (0, ff, 2 * ff, 2 * ff + square, 2 * ff + 4 * square)
        self.rows = up_to(self.tops[4] + self.vec_rows, step)
        parts = self.rows // step
        cuts = ((0, 4, 7, 10, 12, 14), (0, 4, 10, 14))
        self.bounds = [[c * step for c in sorted({parts * k // 14 for k in layer})] for layer in cuts]
        self.landing_sets = [len(b) - 1 for b in self.bounds[::-1]]
        if self.bounds[0] == self.bounds[1]:
            self.landing_sets = self.landing_sets[:1]
        self.n_chunk = sum(len(b) - 1 for b in self.bounds)


def run_kernel(counts, arrays, dims):
    d = dims
    n, seq, width, hidden = d.n_seq, d.seq, d.width, d.hidden
    crops = [jax.ShapeDtypeStruct(a.shape, BF16) for a in arrays[:2]]
    outs = crops + crops
    outs += [jax.ShapeDtypeStruct((2, d.rows, BLOCK), BF16)]
    scratch = [
        pltpu.VMEM((2, d.rows, BLOCK), BF16),
        pltpu.VMEM((d.glen, d.n_global, width), F32),
        pltpu.VMEM((n, seq, width), F32),
        pltpu.VMEM((4, n, seq, width), BF16),
        pltpu.VMEM((4, n, seq, 1), F32),
        pltpu.VMEM((4, n, width + TILE, seq), BF16),
        pltpu.VMEM((2, n, seq, 3 * width), BF16),
        pltpu.VMEM((2, n, HEADS, seq, seq), BF16),
        pltpu.VMEM((2, n, seq, width), F32),
        pltpu.VMEM((2, n, seq, width), BF16),
        pltpu.VMEM((2, n, width + TILE, seq), BF16),
        pltpu.VMEM((2, n, seq, hidden), BF16),
        pltpu.VMEM((n, seq, hidden), BF16),
        pltpu.VMEM((n, seq, width), F32),
        pltpu.VMEM((n, seq, width), BF16),
        pltpu.VMEM((n, width, seq), BF16),
        pltpu.VMEM((n, seq, hidden), BF16),
        pltpu.VMEM((2, seq, seq), BF16),
        pltpu.VMEM((d.vec_rows, BLOCK), F32),
        pltpu.VMEM((3, 8, width), F32),
    ]
    for layer in (1, 0)[: len(d.landing_sets)]:
        for first, end in zip(d.bounds[layer], d.bounds[layer][1:]):
            rows = end - first
            for w in d.wires:
                rows //= w.size
                scratch.append(pltpu.VMEM((w.size - 1, rows, BLOCK), BF16))
    peers = 2 * sum(w.size - 1 for w in d.wires)
    scratch += [
        pltpu.SemaphoreType.DMA((d.n_chunk, peers)),
        pltpu.SemaphoreType.DMA((d.n_chunk, peers)),
        pltpu.SemaphoreType.DMA((d.n_chunk, 1)),
        pltpu.SemaphoreType.REGULAR((d.n_chunk, len(d.wires))),
        pltpu.SemaphoreType.REGULAR((d.n_chunk, len(d.wires))),
    ]
    vmem = pl.BlockSpec(memory_space=pltpu.VMEM)
    anywhere = pl.BlockSpec(memory_space=pl.ANY)
    return pl.pallas_call(
        functools.partial(kernel, d),
        out_shape=outs,
        in_specs=[pl.BlockSpec(memory_space=pltpu.SMEM)] + [vmem] * len(arrays),
        out_specs=[vmem] * 4 + [anywhere],
        scratch_shapes=scratch,
        compiler_params=pltpu.CompilerParams(
            vmem_limit_bytes=63 * 1024 * 1024, collective_id=0, has_side_effects=True
        ),
    )(counts, *arrays)


THIRDS = 3


def cast_kernel(dims, reduce, expand, output, mixer, vectors, *rest):
    crops, outs, held, sems = rest[:4], rest[4:-9], rest[-5:-1], rest[-1]
    step = pl.program_id(0) * THIRDS + pl.program_id(1)
    loads = [pltpu.make_async_copy(a, b, sems.at[0, i]) for i, (a, b) in enumerate(zip(crops, held, strict=True))]
    stores = [pltpu.make_async_copy(a, b, sems.at[1, i]) for i, (a, b) in enumerate(zip(held, rest[-9:-5], strict=True))]

    @pl.when(step == 0)
    def _():
        for copy in loads:
            copy.start()

    @pl.when(step == 1)
    def _():
        for load, store in zip(loads, stores, strict=True):
            load.wait()
            store.start()

    mixer_grad, output_grad, expand_grad, reduce_grad = outs[:4]
    width = dims.width
    fold = width // 2
    for b in range(2):
        rows = slice(b * width, (b + 1) * width)
        cols = slice(b * BLOCK, (b + 1) * BLOCK)
        expand_grad[0, :, cols] = expand[0, rows, :].astype(F32)
        reduce_grad[0, cols, :] = reduce[0, rows, :].T.astype(F32)
    for source, target in ((mixer, mixer_grad), (output, output_grad)):
        target[0, :, 0:BLOCK] = source[0, 0:width, :].astype(F32)
        target[0, 0:fold, BLOCK:] = source[0, width:, 0:LANES].astype(F32)
        target[0, fold:, BLOCK:] = source[0, width:, LANES:].astype(F32)

    @pl.when(step == 2 * THIRDS - 1)
    def _():
        for ref, name in zip(outs[4:], dims.names, strict=True):
            size = ref.shape[1]
            for c in range(0, size, BLOCK):
                at = dims.at[name] + c // BLOCK
                piece = min(BLOCK, size - c)
                for layer in range(2):
                    ref[layer : layer + 1, c : c + piece] = vectors[layer].astype(F32)[at : at + 1, 0:piece]
        for store in stores:
            store.wait()


def run_cast(sums, crops, dims):
    d = dims
    width, hidden = d.width, d.hidden
    part = (1, 2 * width, BLOCK)
    square = (1, width * width // BLOCK, BLOCK)
    grads = [(width, 3 * width), (width, width), (width, hidden), (hidden, width)]
    shapes = [jax.ShapeDtypeStruct((2,) + g, F32) for g in grads]
    specs = [
        pl.BlockSpec((1, width, 3 * width // THIRDS), lambda l, t: (l, 0, t)),
        pl.BlockSpec((1, width, width), lambda l, t: (l, 0, 0)),
        pl.BlockSpec((1, width, hidden // THIRDS), lambda l, t: (l, 0, t)),
        pl.BlockSpec((1, hidden // THIRDS, width), lambda l, t: (l, t, 0)),
    ]
    for name in d.names:
        shapes.append(jax.ShapeDtypeStruct((2, d.sizes[name]), F32))
        specs.append(pl.BlockSpec((2, d.sizes[name]), lambda l, t: (0, 0)))
    for crop in crops:
        shapes.append(jax.ShapeDtypeStruct(crop.shape, crop.dtype))
        specs.append(pl.BlockSpec(memory_space=pl.ANY))
    return pl.pallas_call(
        functools.partial(cast_kernel, d),
        grid=(2, THIRDS),
        out_shape=shapes,
        in_specs=[
            pl.BlockSpec(part, lambda l, t: (l, t, 0)),
            pl.BlockSpec(part, lambda l, t: (l, THIRDS + t, 0)),
            pl.BlockSpec(square, lambda l, t: (l, d.tops[2] // square[1], 0)),
            pl.BlockSpec(square, lambda l, t: (l, d.tops[3] // square[1] + t, 0)),
            pl.BlockSpec((2, d.vec_rows, BLOCK), lambda l, t: (0, d.tops[4] // d.vec_rows, 0)),
        ]
        + [pl.BlockSpec(memory_space=pl.ANY)] * 4,
        out_specs=specs,
        scratch_shapes=[pltpu.VMEM(c.shape, c.dtype) for c in crops] + [pltpu.SemaphoreType.DMA((2, 4))],
        compiler_params=pltpu.CompilerParams(vmem_limit_bytes=62 * 1024 * 1024),
    )(sums, sums, sums, sums, sums, *crops)


def shards(wires, global_crops, local_crops, local_count, global_cotangent, local_cotangent, *weights):
    global_crops, global_cotangent = global_crops.transpose(1, 0, 2), global_cotangent.transpose(1, 0, 2)
    dims = Dims(global_crops, local_crops, weights[8].shape[2], wires)
    outs = run_kernel(
        local_count, (global_crops, local_crops, global_cotangent, local_cotangent) + weights, dims
    )
    mixer, output, expand, reduce, *rest = run_cast(outs[4], outs[:4], dims)
    vectors, crops = rest[:-4], rest[-4:]
    v = dict(zip(dims.names, vectors, strict=True))
    return (
        crops[0].transpose(1, 0, 2),
        crops[1],
        crops[2].transpose(1, 0, 2),
        crops[3],
        v["attend_gain"],
        v["attend_shift"],
        mixer,
        v["mixer_bias"],
        output,
        v["output_bias"],
        v["feed_gain"],
        v["feed_shift"],
        expand,
        v["expand_bias"],
        reduce,
        v["reduce_bias"],
    )


def solution(mesh):
    crops = P(("dp", "section"), None, None)
    return jax.shard_map(
        functools.partial(shards, wires_of(mesh)),
        mesh=mesh,
        in_specs=(crops, crops, P("dp"), crops, crops) + (P(),) * 12,
        out_specs=(crops,) * 4 + (P(),) * 12,
        check_vma=False,
    )
```

```python
import functools

import jax
import jax.numpy as jnp
from jax import lax
from jax.experimental import pallas as pl
from jax.experimental.pallas import tpu as pltpu
from jax.sharding import PartitionSpec as P

HEADS = 6
HEAD = 64
EPS = 1e-06
TILE = 16
LANES = 128
BLOCK = 256
ROWS = 32
LOG2E = 1.4426950408889634
F32 = jnp.float32
BF16 = jnp.bfloat16


def up_to(value, step):
    return -(-value // step) * step


def mm(left, right):
    return lax.dot_general(left, right, (((1,), (0,)), ((), ())), preferred_element_type=F32)


def mm_nt(left, right):
    return lax.dot_general(left, right, (((1,), (1,)), ((), ())), preferred_element_type=F32)


def norm(rows):
    centred = rows - jnp.mean(rows, -1, keepdims=True)
    scale = lax.rsqrt(jnp.mean(centred * centred, -1, keepdims=True) + EPS)
    return centred * scale, scale


def norm_back(grad, unit, scale, gain):
    slope = grad * gain
    first = jnp.mean(slope, -1, keepdims=True)
    second = jnp.mean(slope * unit, -1, keepdims=True)
    return scale * (slope - first - unit * second)


def gelu_parts(u):
    size = jnp.abs(u)
    d = 1.0 + (0.3275911 * 0.7071067811865476) * size
    t = pl.reciprocal(d, approx=True)
    t = t * (2.0 - d * t)
    poly = 0.5 * 1.061405429
    for a in (-1.453152027, 1.421413741, -0.284496736, 0.254829592):
        poly = poly * t + 0.5 * a
    bell = jnp.exp2((u * u) * (-0.5 * LOG2E))
    tail = poly * t * bell
    phi = jnp.where(u < 0.0, tail, 1.0 - tail)
    return u * phi, phi + (u * bell) * 0.3989422804014327


def add_to(total, value):
    return value if total is None else total + value


def fold8(value):
    rows, width = value.shape
    return jnp.sum(value.reshape(rows // 8, 8, width), 0)


def kernel(
    dims,
    counts,
    global_in,
    local_in,
    global_cot,
    local_cot,
    attend_gain,
    attend_shift,
    mixer_weight,
    mixer_bias,
    output_weight,
    output_bias,
    feed_gain,
    feed_shift,
    expand_weight,
    expand_bias,
    reduce_weight,
    reduce_bias,
    global_out,
    local_out,
    global_back,
    local_back,
    sums_out,
    sums,
    crop_s,
    x_s,
    unit_s,
    scale_s,
    norm_t,
    packed_s,
    power_s,
    mixed_s,
    mixed_t,
    act_s,
    slope_s,
    grad_s,
    grad_low,
    grad_t,
    dup_s,
    mask_s,
    normed_s,
    dm_s,
    inner_s,
    dqt_s,
    vec_s,
    acc_s,
    *wires,
):
    seq, group, width = dims.seq, dims.group, dims.width
    glen, llen = dims.glen, dims.llen
    n_global, n_local, n_seq = dims.n_global, dims.n_local, dims.n_seq
    hidden = dims.hidden
    count = counts[lax.axis_index("section")]
    pairs = HEADS // 2
    lane = lax.broadcasted_iota(jnp.int32, (1, LANES), 1)
    low_half = (lane < HEAD).astype(F32).astype(BF16)
    high_half = (lane >= HEAD).astype(F32).astype(BF16)
    score_scale = HEAD ** (-0.5)
    row_blocks = [slice(a, min(a + ROWS, seq)) for a in range(0, seq, ROWS)]

    net = Net(dims.wires)
    net.greet()
    n_stage = len(dims.wires)
    sets = dims.landing_sets
    landings, sems = wires[: n_stage * sum(sets)], wires[n_stage * sum(sets) :]
    flow = Flow(net)
    number = 0
    for layer in (1, 0):
        bounds = dims.bounds[layer]
        for i in range(len(bounds) - 1):
            shared = len(sets) == 1
            at = (i if shared else number) * n_stage
            own = [w.at[number] for w in sems[:4]] + [sems[4].at[i]]
            rows = pl.ds(bounds[i], bounds[i + 1] - bounds[i])
            turn = (1 - layer) if shared else None
            flow.chunks.append(
                Chunk(net, sums.at[layer, rows], sums_out.at[layer, rows], landings[at : at + n_stage], own, turn, layer, bounds[i + 1])
            )
            number += 1

    for s in range(n_seq):
        x_s[s, seq - 32 :, :] = jnp.zeros((32, width), F32)
        grad_s[s, seq - 32 :, :] = jnp.zeros((32, width), F32)
    row_id = lax.broadcasted_iota(jnp.int32, (seq, seq), 0)
    col_id = lax.broadcasted_iota(jnp.int32, (seq, seq), 1)
    row_crop = sum((row_id >= llen * j).astype(jnp.int32) for j in range(1, group + 1))
    col_crop = sum((col_id >= llen * j).astype(jnp.int32) for j in range(1, group + 1))
    far = jnp.float32(-1e30)
    mask_s[0] = jnp.where(row_id < glen, jnp.float32(0), far)
    mask_s[1] = jnp.where(row_crop == col_crop, jnp.float32(0), far)
    one_row = (lax.broadcasted_iota(jnp.int32, (TILE, seq), 0) == 0).astype(F32).astype(BF16)
    for s in range(n_seq):
        for i in range(4):
            norm_t[i, s, width:, :] = one_row
        for i in range(2):
            mixed_t[i, s, width:, :] = one_row

    def live_rows(g):
        rows = lax.broadcasted_iota(jnp.int32, (seq, 1), 0)
        return (rows < llen * jnp.clip(count - g * group, 0, group)).astype(F32)

    for source, target in ((global_in, x_s), (global_cot, grad_s)):
        crop_s[...] = source[...].astype(F32)
        for s in range(n_global):
            target[s, 0:glen, :] = crop_s[:, s, :]
    for j in range(n_local):
        s, at = n_global + j // group, llen * (j % group)
        x_s[s, at : at + llen, :] = local_in[j].astype(F32)
        grad_s[s, at : at + llen, :] = local_cot[j].astype(F32)
    for s in range(n_global, n_seq):
        grad_s[s] = grad_s[s] * live_rows(s - n_global)

    def row(ref, layer):
        return ref[...].astype(F32)[layer : layer + 1]

    slopes = (slope_s, dup_s)

    def start_back(s):
        total = None
        for rows in row_blocks:
            grad = grad_s[s, rows, :]
            grad_low[s, rows, :] = grad.astype(BF16)
            total = add_to(total, fold8(grad))
        acc_s[2] = acc_s[2] + total
        grad_t[s] = grad_low[s].T

    def end_back(s, place, gain, dh):
        first = second = None
        for rows in row_blocks:
            unit, scale = unit_s[place, s, rows, :].astype(F32), scale_s[place, s, rows, :]
            part = dh[rows]
            first, second = add_to(first, fold8(part * unit)), add_to(second, fold8(part))
            grad = (grad_s[s, rows, :] + norm_back(part, unit, scale, gain)).astype(BF16)
            grad_low[s, rows, :] = grad
            grad_s[s, rows, :] = grad.astype(F32)
        acc_s[0] = acc_s[0] + first
        acc_s[1] = acc_s[1] + second

    def start_norm(s, place, gain, shift):
        for rows in row_blocks:
            unit, scale = norm(x_s[s, rows, :])
            unit_s[place, s, rows, :] = unit.astype(BF16)
            scale_s[place, s, rows, :] = scale
            normed_s[rows, :] = (unit * gain + shift).astype(BF16)
        norm_t[place, s, 0:width, :] = normed_s[...].T

    def end_forward(s, branch, bias):
        for rows in row_blocks:
            x_s[s, rows, :] = (x_s[s, rows, :] + (branch[rows] + bias)).astype(BF16).astype(F32)

    def product(left, right, cols):
        total = mm(left[0], right[0, :, cols])
        for s in range(1, n_seq):
            total = total + mm(left[s], right[s, :, cols])
        return total

    for layer in range(2):
        gain, shift = row(attend_gain, layer), row(attend_shift, layer)
        bias = row(mixer_bias, layer)
        bias = jnp.concatenate([bias[:, :width], jnp.zeros((1, width), F32), bias[:, width:]], 1)
        out_bias = row(output_bias, layer)
        gain2, shift2 = row(feed_gain, layer), row(feed_shift, layer)
        bias_up, bias_down = row(expand_bias, layer), row(reduce_bias, layer)

        def attend(s, _):
            start_norm(s, 2 * layer, gain, shift)
            for c in range(0, 3 * width, BLOCK):
                cols = slice(c, min(c + BLOCK, 3 * width))
                packed = mm(normed_s[...], mixer_weight[layer, :, cols])
                for rows in row_blocks:
                    packed_s[layer, s, rows, cols] = (packed[rows] + bias[:, cols]).astype(BF16)
            mask = mask_s.at[jnp.where(s < n_global, 0, 1)]
            value_t = packed_s[layer, s, :, 2 * width :].T
            for p in range(pairs):
                at = p * LANES
                query = packed_s[layer, s, :, at : at + LANES]
                key = packed_s[layer, s, :, width + at : width + at + LANES]
                for h, half in enumerate((low_half, high_half)):
                    scores = mm_nt(key * half, query)
                    shares = []
                    for a in range(0, seq, LANES):
                        cols = slice(a, min(a + LANES, seq))
                        part = scores[:, cols] * (score_scale * LOG2E) + mask[:, cols]
                        power = jnp.exp2(part - jnp.max(part, 0, keepdims=True))
                        shares.append((power * (1.0 / jnp.sum(power, 0, keepdims=True))).astype(BF16))
                    shares = jnp.concatenate(shares, 1)
                    power_s[layer, s, 2 * p + h] = shares
                    head = slice(at + h * HEAD, at + (h + 1) * HEAD)
                    mixed_t[layer, s, head, :] = mm(value_t[head], shares).astype(BF16)
            mixed_s[layer, s] = mixed_t[layer, s, 0:width, :].T
            end_forward(s, mm(mixed_s[layer, s], output_weight[layer]), out_bias)
            return 0

        lax.fori_loop(0, n_seq, attend, 0)

        def feed(s, _):
            start_norm(s, 2 * layer + 1, gain2, shift2)
            if layer == 1:
                start_back(s)
            for c in range(hidden // BLOCK):
                cols = slice(c * BLOCK, (c + 1) * BLOCK)
                up = mm(normed_s[...], expand_weight[layer, :, cols])
                for rows in row_blocks:
                    act, slope = gelu_parts(up[rows] + bias_up[:, cols])
                    act_s[layer, s, rows, cols] = act.astype(BF16)
                    slopes[layer][s, rows, cols] = slope.astype(BF16)
            end_forward(s, mm(act_s[layer, s], reduce_weight[layer]), bias_down)
            return 0

        if layer == 1:
            acc_s[...] = jnp.zeros_like(acc_s)
        lax.fori_loop(0, n_seq, feed, 0)

    for s in range(n_global):
        crop_s[:, s, :] = x_s[s, 0:glen, :]
    global_out[...] = crop_s[...].astype(BF16)
    for j in range(n_local):
        s, at = n_global + j // group, llen * (j % group)
        alive = (count > j).astype(F32)
        local_out[j] = (x_s[s, at : at + llen, :] * alive).astype(BF16)

    def put_vector(at, value):
        for c in range(0, value.shape[1], BLOCK):
            piece = value[:, c : c + BLOCK]
            vec_s[at + c // BLOCK : at + c // BLOCK + 1, 0 : piece.shape[1]] = piece

    def put_tile(layer, top, m, part):
        at = top + (m // 3) * (width + fold)
        side = m % 3 * LANES
        part = part.astype(BF16)
        if m % 3 < 2:
            sums[layer, at : at + width, side : side + LANES] = part
        else:
            at = at + width
            sums[layer, at : at + fold, 0:LANES] = part[:fold]
            sums[layer, at : at + fold, LANES:] = part[fold:]

    blocks = hidden // BLOCK
    fold = width // 2
    tops = dims.tops
    net.wait_greeting()
    for layer in (1, 0):
        vec_s[...] = jnp.zeros_like(vec_s)
        gain2, gain = row(feed_gain, layer), row(attend_gain, layer)
        put_vector(dims.at["reduce_bias"], jnp.sum(acc_s[2], 0, keepdims=True))

        for c in range(blocks):
            total = product(grad_t, act_s.at[layer], slice(c * BLOCK, (c + 1) * BLOCK))
            at = tops[0] + c * width
            sums[layer, at : at + width, :] = total.astype(BF16)
            flow.ready(layer, at + width)
            flow.tick(0.45)

        def feed_back(s, _):
            for c in range(blocks):
                cols = slice(c * BLOCK, (c + 1) * BLOCK)
                dact = mm_nt(grad_low[s], reduce_weight[layer, cols, :])
                for rows in row_blocks:
                    dup_s[s, rows, cols] = (dact[rows] * slopes[layer][s, rows, cols].astype(F32)).astype(BF16)
            end_back(s, 2 * layer + 1, gain2, mm_nt(dup_s[s], expand_weight[layer]))
            flow.ticks(s, n_seq, 1.3)
            return 0

        acc_s[0:2] = jnp.zeros((2, 8, width), F32)
        lax.fori_loop(0, n_seq, feed_back, 0)
        put_vector(dims.at["feed_gain"], jnp.sum(acc_s[0], 0, keepdims=True))
        put_vector(dims.at["feed_shift"], jnp.sum(acc_s[1], 0, keepdims=True))

        for c in range(blocks):
            total = product(norm_t.at[2 * layer + 1], dup_s, slice(c * BLOCK, (c + 1) * BLOCK))
            at = tops[1] + c * width
            sums[layer, at : at + width, :] = total[:width].astype(BF16)
            at_bias = dims.at["expand_bias"] + c
            vec_s[at_bias : at_bias + 1, :] = total[width : width + 1]
            flow.ready(layer, at + width)
            flow.tick(0.45)

        bias_parts = []
        for c in range(0, width, BLOCK):
            size = min(BLOCK, width - c)
            total = product(mixed_t.at[layer], grad_low, slice(c, c + size))
            for k in range(0, size, LANES):
                put_tile(layer, tops[2], (c + k) // LANES, total[:width, k : k + LANES])
                bias_parts.append(total[width : width + 1, k : k + LANES])
        put_vector(dims.at["output_bias"], jnp.concatenate(bias_parts, 1))
        flow.ready(layer, tops[3])
        flow.tick(0.8)

        def attend_back(s, _):
            dmixed = mm_nt(grad_low[s], output_weight[layer])
            for rows in row_blocks:
                dm_s[rows, :] = dmixed[rows].astype(BF16)
                inner_s[rows, :] = -(dmixed[rows] * mixed_s[layer, s, rows, :].astype(F32)).astype(BF16)
            key_t = packed_s[layer, s, :, width : 2 * width].T
            for p in range(pairs):
                at = p * LANES
                query = packed_s[layer, s, :, at : at + LANES]
                value = packed_s[layer, s, :, 2 * width + at : 2 * width + at + LANES]
                dm, inner = dm_s[:, at : at + LANES], inner_s[:, at : at + LANES]
                wide_value = jnp.concatenate([value, jnp.ones_like(value)], 1)
                dk = dv = None
                for h, half in enumerate((low_half, high_half)):
                    dm_half = dm * half
                    slope = mm_nt(wide_value, jnp.concatenate([dm_half, inner * half], 1))
                    ds = []
                    for rows in row_blocks:
                        ds.append((power_s[layer, s, 2 * p + h, rows, :].astype(F32) * slope[rows]).astype(BF16))
                    ds = jnp.concatenate(ds, 0)
                    head = slice(at + h * HEAD, at + (h + 1) * HEAD)
                    dqt_s[head, :] = (mm(key_t[head], ds) * score_scale).astype(BF16)
                    dk = add_to(dk, mm(ds, query * half))
                    dv = add_to(dv, mm(power_s[layer, s, 2 * p + h], dm_half))
                dup_s[s, :, width + at : width + at + LANES] = (dk * score_scale).astype(BF16)
                dup_s[s, :, 2 * width + at : 2 * width + at + LANES] = dv.astype(BF16)
            dup_s[s, :, 0:width] = dqt_s[...].T
            end_back(s, 2 * layer, gain, mm_nt(dup_s[s, :, 0 : 3 * width], mixer_weight[layer]))
            if layer == 1:
                start_back(s)
            flow.ticks(s, n_seq, 2.3)
            return 0

        acc_s[...] = jnp.zeros_like(acc_s)
        lax.fori_loop(0, n_seq, attend_back, 0)
        put_vector(dims.at["attend_gain"], jnp.sum(acc_s[0], 0, keepdims=True))
        put_vector(dims.at["attend_shift"], jnp.sum(acc_s[1], 0, keepdims=True))

        bias_parts = []
        for c in range(0, 3 * width, BLOCK):
            size = min(BLOCK, 3 * width - c)
            total = product(norm_t.at[2 * layer], dup_s, slice(c, c + size))
            for k in range(0, size, LANES):
                put_tile(layer, tops[3], (c + k) // LANES, total[:width, k : k + LANES])
                bias_parts.append(total[width : width + 1, k : k + LANES])
            flow.tick(0.5)
        each = width // LANES
        put_vector(
            dims.at["mixer_bias"],
            jnp.concatenate(bias_parts[:each] + bias_parts[2 * each :], 1),
        )
        sums[layer, tops[4] : tops[4] + dims.vec_rows, :] = vec_s[...].astype(BF16)
        rest = dims.rows - tops[4] - dims.vec_rows
        if rest:
            sums[layer, dims.rows - rest :, :] = jnp.zeros((rest, BLOCK), BF16)
        flow.ready(layer, dims.rows)

    for s in range(n_global):
        crop_s[:, s, :] = grad_s[s, 0:glen, :]
    global_back[...] = crop_s[...].astype(BF16)
    for j in range(n_local):
        s, at = n_global + j // group, llen * (j % group)
        local_back[j] = grad_s[s, at : at + llen, :].astype(BF16)
    flow.drain()


class Wire:
    def __init__(self, size, first, second):
        self.size, self.first, self.second = size, first, second


def wires_of(mesh):
    names = mesh.axis_names
    places = {}
    for axis, name in enumerate(names):
        line = [mesh.devices[tuple(i if a == axis else 0 for a in range(2))] for i in range(mesh.devices.shape[axis])]
        spots = [(d.core_on_chip,) + tuple(d.coords) for d in line]
        found, total = [], 1
        for k in range(4):
            values = sorted({p[k] for p in spots})
            if len(values) > 1:
                stride = next(i for i, p in enumerate(spots) if p[k] != spots[0][k])
                found.append((k, axis, stride, len(values)))
                total *= len(values)
        good = total == len(line)
        for k, _, stride, size in found:
            values = [p[k] for p in spots]
            good = good and all(v == values[i // stride % size * stride] for i, v in enumerate(values))
        if not good:
            found = [(4 + axis, axis, 1, len(line))]
        for k, axis, stride, size in found:
            places[k] = (axis, stride, size)
    wires = []
    if 0 in places:
        wires.append(Wire(places[0][2], places[0], places[0]))
    if 0 in places and 1 in places and 2 in places and places[1][2] == places[2][2]:
        wires.append(Wire(places[1][2], places[1], places[2]))
        wires.append(Wire(places[1][2], places[2], places[1]))
        order = [3, 4, 5]
    else:
        order = [1, 2, 3, 4, 5]
    for k in order:
        if k in places:
            wires.append(Wire(places[k][2], places[k], places[k]))
    return wires


class Net:
    def __init__(self, wires):
        self.axes = ("dp", "section")
        self.here = [lax.axis_index(a) for a in self.axes]
        self.wires = wires
        first = wires[0]
        odd = self.spot(first.first) % 2 if first.size == 2 else 0
        self.odd = odd
        self.at = []
        for w in wires:
            a, b = self.spot(w.first), self.spot(w.second)
            self.at.append(a if w.first == w.second else a + odd * (b - a))

    def spot(self, place):
        axis, stride, size = place
        return self.here[axis] // stride % size

    def peer(self, stage, k):
        w = self.wires[stage]
        place = (self.at[stage] + k) % w.size
        move = place - self.at[stage]
        target = list(self.here)
        if w.first == w.second:
            target[w.first[0]] = target[w.first[0]] + move * w.first[1]
        else:
            target[w.first[0]] = target[w.first[0]] + move * w.first[1] * (1 - self.odd)
            target[w.second[0]] = target[w.second[0]] + move * w.second[1] * self.odd
        return tuple(target), place

    def greet(self):
        barrier = pltpu.get_barrier_semaphore()
        for stage, w in enumerate(self.wires):
            for k in range(1, w.size):
                pl.semaphore_signal(barrier, inc=1, device_id=self.peer(stage, k)[0], device_id_type=pl.DeviceIdType.MESH)

    def wait_greeting(self):
        pl.semaphore_wait(pltpu.get_barrier_semaphore(), sum(w.size - 1 for w in self.wires))


class Chunk:
    def __init__(self, net, sums, out, landing, sems, turn, layer, end):
        self.net, self.sums, self.out, self.landing = net, sums, out, landing
        self.send, self.recv, self.local, self.sent, self.free = sems
        self.turn = turn
        self.layer, self.end = layer, end
        self.due = None
        size, start = sums.shape[0], 0
        self.unit = size
        for w in net.wires:
            self.unit //= w.size
        self.size, self.start = [], []
        for stage, w in enumerate(net.wires):
            size //= w.size
            self.size.append(size)
            self.start.append((start, size))
            start = start + net.at[stage] * size
        self.own = start
        self.stages = len(net.wires)
        self.step = 0
        self.sem_at, at = {}, 0
        for phase in range(2):
            for stage, w in enumerate(net.wires):
                for k in range(1, w.size):
                    self.sem_at[phase, stage, k] = at
                    at += 1

    def rows(self, stage, place):
        start, size = self.start[stage]
        return pl.ds(pl.multiple_of(start + place * size, TILE), size)

    def copy(self, phase, stage, k):
        target, place = self.net.peer(stage, k)
        at = self.sem_at[phase, stage, k]
        if phase == 0:
            source, to = self.sums.at[self.rows(stage, place)], self.landing[stage].at[k - 1]
        else:
            rows = self.rows(stage, self.net.at[stage])
            source = to = self.sums.at[rows]
        return pltpu.make_async_remote_copy(
            src_ref=source,
            dst_ref=to,
            send_sem=self.send.at[at],
            recv_sem=self.recv.at[at],
            device_id=target,
            device_id_type=pl.DeviceIdType.MESH,
        )

    def arrival(self, stage, k):
        target, place = self.net.peer(stage, self.net.wires[stage].size - k)
        at = self.sem_at[1, stage, k]
        landed = self.sums.at[self.rows(stage, place)]
        return pltpu.make_async_remote_copy(
            src_ref=landed,
            dst_ref=landed,
            send_sem=self.send.at[at],
            recv_sem=self.recv.at[at],
            device_id=target,
            device_id_type=pl.DeviceIdType.MESH,
        )

    def start_stage(self, phase, stage):
        if phase == 0 and self.turn == 1:
            pl.semaphore_wait(self.free.at[stage], self.net.wires[stage].size - 1)
        if phase == 1:
            pl.semaphore_wait(self.sent.at[stage], self.net.wires[stage].size - 1)
        for k in range(1, self.net.wires[stage].size):
            self.copy(phase, stage, k).start()

    def load(self):
        last = self.stages - 1
        stage = self.step if self.step <= last else 2 * self.stages - 1 - self.step
        peers = self.net.wires[stage].size - 1
        row = BLOCK * 2
        if stage == 0:
            return 0, self.size[0] * row / 4
        if stage == last:
            return 2, self.size[stage] * (peers + 1) ** 2 / 2 * row
        return 1, self.size[stage] * peers * row

    def begin(self):
        self.start_stage(0, 0)

    def out_copy(self):
        return pltpu.make_async_copy(self.sums, self.out, self.local.at[0])

    def advance(self):
        step = self.step
        self.step += 1
        if step < self.stages:
            peers = range(1, self.net.wires[step].size)
            for k in peers:
                self.copy(0, step, k).wait_recv()
            base = self.start[step][0] + self.net.at[step] * self.size[step]
            landing = self.landing[step]

            def add(i, _):
                at = pl.ds(pl.multiple_of(base + i * self.unit, TILE), self.unit)
                total = self.sums[at, :].astype(F32)
                for k in peers:
                    total = total + landing[k - 1, pl.ds(pl.multiple_of(i * self.unit, TILE), self.unit), :].astype(F32)
                self.sums[at, :] = total.astype(BF16)
                return 0

            lax.fori_loop(0, self.size[step] // self.unit, add, 0)
            for k in peers:
                self.copy(0, step, k).wait_send()
                target = self.net.peer(step, k)[0]
                pl.semaphore_signal(self.sent.at[step], inc=1, device_id=target, device_id_type=pl.DeviceIdType.MESH)
                if self.turn == 0:
                    pl.semaphore_signal(self.free.at[step], inc=1, device_id=target, device_id_type=pl.DeviceIdType.MESH)
            if step + 1 < self.stages:
                self.start_stage(0, step + 1)
            else:
                self.start_stage(1, step)
        else:
            stage = 2 * self.stages - 1 - step
            for k in range(1, self.net.wires[stage].size):
                self.arrival(stage, k).wait_recv()
            if stage > 0:
                self.start_stage(1, stage - 1)
            else:
                self.out_copy().start()

    def finish(self):
        for phase, stage, k in self.sem_at:
            if phase == 1:
                self.copy(phase, stage, k).wait_send()
        self.out_copy().wait()


LATENCY = 2.0
RATE = 80e3
STEP = 0.4


class Flow:
    def __init__(self, net):
        self.chunks, self.now, self.waiting, self.free = [], 0.0, 0, [0.0] * 3

    def book(self, chunk):
        kind, size = chunk.load()
        self.free[kind] = max(self.now, self.free[kind]) + size / RATE
        chunk.due = self.free[kind] + LATENCY

    def ready(self, layer, rows):
        while self.waiting < len(self.chunks):
            chunk = self.chunks[self.waiting]
            if chunk.layer != layer or chunk.end > rows:
                return
            chunk.begin()
            self.book(chunk)
            self.waiting += 1

    def due(self):
        return sorted((c for c in self.chunks if c.due is not None and c.due <= self.now), key=lambda c: c.due)

    def take(self):
        while self.due():
            chunk = self.due()[0]
            chunk.advance()
            self.now += STEP
            if chunk.step < 2 * chunk.stages:
                self.book(chunk)
            else:
                chunk.due = None

    def tick(self, time):
        self.now += time
        self.take()

    def ticks(self, s, count, time):
        for i in range(count):
            self.now += time
            if self.due():
                pl.when(s == i)(self.take)

    def drain(self):
        while any(c.due is not None for c in self.chunks):
            self.now = max(self.now, min(c.due for c in self.chunks if c.due is not None))
            self.take()
        for chunk in self.chunks:
            chunk.finish()


class Dims:
    def __init__(self, global_crops, local_crops, hidden, wires):
        self.wires = wires
        self.glen, self.n_global, self.width = global_crops.shape
        self.n_local, self.llen, _ = local_crops.shape
        self.hidden = hidden
        self.seq = up_to(self.glen, TILE)
        self.group = self.seq // self.llen
        while self.n_local % self.group:
            self.group -= 1
        self.n_seq = self.n_global + self.n_local // self.group
        sizes = (
            ("attend_gain", self.width),
            ("attend_shift", self.width),
            ("mixer_bias", 2 * self.width),
            ("output_bias", self.width),
            ("feed_gain", self.width),
            ("feed_shift", self.width),
            ("expand_bias", hidden),
            ("reduce_bias", self.width),
        )
        self.names, self.sizes = [name for name, _ in sizes], dict(sizes)
        self.at, row = {}, 0
        for name, size in sizes:
            self.at[name] = row
            row += -(-size // BLOCK)
        self.vec_rows = 2 * TILE
        assert row <= self.vec_rows and self.width * hidden % self.vec_rows == 0
        step = TILE
        for w in wires:
            step *= w.size
        ff = self.width * hidden // BLOCK
        square = self.width * self.width // BLOCK
        self.tops = (0, ff, 2 * ff, 2 * ff + square, 2 * ff + 4 * square)
        self.rows = up_to(self.tops[4] + self.vec_rows, step)
        parts = self.rows // step
        cuts = ((0, 4, 7, 10, 12, 14), (0, 4, 10, 14))
        self.bounds = [[c * step for c in sorted({parts * k // 14 for k in layer})] for layer in cuts]
        self.landing_sets = [len(b) - 1 for b in self.bounds[::-1]]
        if self.bounds[0] == self.bounds[1]:
            self.landing_sets = self.landing_sets[:1]
        self.n_chunk = sum(len(b) - 1 for b in self.bounds)


def run_kernel(counts, arrays, dims):
    d = dims
    n, seq, width, hidden = d.n_seq, d.seq, d.width, d.hidden
    crops = [jax.ShapeDtypeStruct(a.shape, BF16) for a in arrays[:2]]
    outs = crops + crops
    outs += [jax.ShapeDtypeStruct((2, d.rows, BLOCK), BF16)]
    scratch = [
        pltpu.VMEM((2, d.rows, BLOCK), BF16),
        pltpu.VMEM((d.glen, d.n_global, width), F32),
        pltpu.VMEM((n, seq, width), F32),
        pltpu.VMEM((4, n, seq, width), BF16),
        pltpu.VMEM((4, n, seq, 1), F32),
        pltpu.VMEM((4, n, width + TILE, seq), BF16),
        pltpu.VMEM((2, n, seq, 3 * width), BF16),
        pltpu.VMEM((2, n, HEADS, seq, seq), BF16),
        pltpu.VMEM((2, n, seq, width), BF16),
        pltpu.VMEM((2, n, width + TILE, seq), BF16),
        pltpu.VMEM((2, n, seq, hidden), BF16),
        pltpu.VMEM((n, seq, hidden), BF16),
        pltpu.VMEM((n, seq, width), F32),
        pltpu.VMEM((n, seq, width), BF16),
        pltpu.VMEM((n, width, seq), BF16),
        pltpu.VMEM((n, seq, hidden), BF16),
        pltpu.VMEM((2, seq, seq), F32),
        pltpu.VMEM((seq, width), BF16),
        pltpu.VMEM((seq, width), BF16),
        pltpu.VMEM((seq, width), BF16),
        pltpu.VMEM((width, seq), BF16),
        pltpu.VMEM((d.vec_rows, BLOCK), F32),
        pltpu.VMEM((3, 8, width), F32),
    ]
    for layer in (1, 0)[: len(d.landing_sets)]:
        for first, end in zip(d.bounds[layer], d.bounds[layer][1:]):
            rows = end - first
            for w in d.wires:
                rows //= w.size
                scratch.append(pltpu.VMEM((w.size - 1, rows, BLOCK), BF16))
    peers = 2 * sum(w.size - 1 for w in d.wires)
    scratch += [
        pltpu.SemaphoreType.DMA((d.n_chunk, peers)),
        pltpu.SemaphoreType.DMA((d.n_chunk, peers)),
        pltpu.SemaphoreType.DMA((d.n_chunk, 1)),
        pltpu.SemaphoreType.REGULAR((d.n_chunk, len(d.wires))),
        pltpu.SemaphoreType.REGULAR((d.n_chunk, len(d.wires))),
    ]
    vmem = pl.BlockSpec(memory_space=pltpu.VMEM)
    anywhere = pl.BlockSpec(memory_space=pl.ANY)
    return pl.pallas_call(
        functools.partial(kernel, d),
        out_shape=outs,
        in_specs=[pl.BlockSpec(memory_space=pltpu.SMEM)] + [vmem] * len(arrays),
        out_specs=[vmem] * 4 + [anywhere],
        scratch_shapes=scratch,
        compiler_params=pltpu.CompilerParams(
            vmem_limit_bytes=63 * 1024 * 1024, collective_id=0, has_side_effects=True
        ),
    )(counts, *arrays)


THIRDS = 3


def cast_kernel(dims, reduce, expand, output, mixer, vectors, *rest):
    crops, outs, held, sems = rest[:4], rest[4:-9], rest[-5:-1], rest[-1]
    step = pl.program_id(0) * THIRDS + pl.program_id(1)
    loads = [pltpu.make_async_copy(a, b, sems.at[0, i]) for i, (a, b) in enumerate(zip(crops, held, strict=True))]
    stores = [pltpu.make_async_copy(a, b, sems.at[1, i]) for i, (a, b) in enumerate(zip(held, rest[-9:-5], strict=True))]

    @pl.when(step == 0)
    def _():
        for copy in loads:
            copy.start()

    @pl.when(step == 1)
    def _():
        for load, store in zip(loads, stores, strict=True):
            load.wait()
            store.start()

    mixer_grad, output_grad, expand_grad, reduce_grad = outs[:4]
    width = dims.width
    fold = width // 2
    for b in range(2):
        rows = slice(b * width, (b + 1) * width)
        cols = slice(b * BLOCK, (b + 1) * BLOCK)
        expand_grad[0, :, cols] = expand[0, rows, :].astype(F32)
        reduce_grad[0, cols, :] = reduce[0, rows, :].T.astype(F32)
    for source, target in ((mixer, mixer_grad), (output, output_grad)):
        target[0, :, 0:BLOCK] = source[0, 0:width, :].astype(F32)
        target[0, 0:fold, BLOCK:] = source[0, width:, 0:LANES].astype(F32)
        target[0, fold:, BLOCK:] = source[0, width:, LANES:].astype(F32)

    @pl.when(step == 2 * THIRDS - 1)
    def _():
        for ref, name in zip(outs[4:], dims.names, strict=True):
            size = ref.shape[1]
            for c in range(0, size, BLOCK):
                at = dims.at[name] + c // BLOCK
                piece = min(BLOCK, size - c)
                for layer in range(2):
                    ref[layer : layer + 1, c : c + piece] = vectors[layer].astype(F32)[at : at + 1, 0:piece]
        for store in stores:
            store.wait()


def run_cast(sums, crops, dims):
    d = dims
    width, hidden = d.width, d.hidden
    part = (1, 2 * width, BLOCK)
    square = (1, width * width // BLOCK, BLOCK)
    grads = [(width, 3 * width), (width, width), (width, hidden), (hidden, width)]
    shapes = [jax.ShapeDtypeStruct((2,) + g, F32) for g in grads]
    specs = [
        pl.BlockSpec((1, width, 3 * width // THIRDS), lambda l, t: (l, 0, t)),
        pl.BlockSpec((1, width, width), lambda l, t: (l, 0, 0)),
        pl.BlockSpec((1, width, hidden // THIRDS), lambda l, t: (l, 0, t)),
        pl.BlockSpec((1, hidden // THIRDS, width), lambda l, t: (l, t, 0)),
    ]
    for name in d.names:
        shapes.append(jax.ShapeDtypeStruct((2, d.sizes[name]), F32))
        specs.append(pl.BlockSpec((2, d.sizes[name]), lambda l, t: (0, 0)))
    for crop in crops:
        shapes.append(jax.ShapeDtypeStruct(crop.shape, crop.dtype))
        specs.append(pl.BlockSpec(memory_space=pl.ANY))
    return pl.pallas_call(
        functools.partial(cast_kernel, d),
        grid=(2, THIRDS),
        out_shape=shapes,
        in_specs=[
            pl.BlockSpec(part, lambda l, t: (l, t, 0)),
            pl.BlockSpec(part, lambda l, t: (l, THIRDS + t, 0)),
            pl.BlockSpec(square, lambda l, t: (l, d.tops[2] // square[1], 0)),
            pl.BlockSpec(square, lambda l, t: (l, d.tops[3] // square[1] + t, 0)),
            pl.BlockSpec((2, d.vec_rows, BLOCK), lambda l, t: (0, d.tops[4] // d.vec_rows, 0)),
        ]
        + [pl.BlockSpec(memory_space=pl.ANY)] * 4,
        out_specs=specs,
        scratch_shapes=[pltpu.VMEM(c.shape, c.dtype) for c in crops] + [pltpu.SemaphoreType.DMA((2, 4))],
        compiler_params=pltpu.CompilerParams(vmem_limit_bytes=62 * 1024 * 1024),
    )(sums, sums, sums, sums, sums, *crops)


def shards(wires, global_crops, local_crops, local_count, global_cotangent, local_cotangent, *weights):
    global_crops, global_cotangent = global_crops.transpose(1, 0, 2), global_cotangent.transpose(1, 0, 2)
    dims = Dims(global_crops, local_crops, weights[8].shape[2], wires)
    outs = run_kernel(
        local_count, (global_crops, local_crops, global_cotangent, local_cotangent) + weights, dims
    )
    mixer, output, expand, reduce, *rest = run_cast(outs[4], outs[:4], dims)
    vectors, crops = rest[:-4], rest[-4:]
    v = dict(zip(dims.names, vectors, strict=True))
    return (
        crops[0].transpose(1, 0, 2),
        crops[1],
        crops[2].transpose(1, 0, 2),
        crops[3],
        v["attend_gain"],
        v["attend_shift"],
        mixer,
        v["mixer_bias"],
        output,
        v["output_bias"],
        v["feed_gain"],
        v["feed_shift"],
        expand,
        v["expand_bias"],
        reduce,
        v["reduce_bias"],
    )


def solution(mesh):
    crops = P(("dp", "section"), None, None)
    return jax.shard_map(
        functools.partial(shards, wires_of(mesh)),
        mesh=mesh,
        in_specs=(crops, crops, P("dp"), crops, crops) + (P(),) * 12,
        out_specs=(crops,) * 4 + (P(),) * 12,
        check_vma=False,
    )
```

```python
import functools

import jax
import jax.numpy as jnp
from jax import lax
from jax.experimental import pallas as pl
from jax.experimental.pallas import tpu as pltpu
from jax.sharding import PartitionSpec as P

HEADS = 6
HEAD = 64
EPS = 1e-06
TILE = 16
LANES = 128
BLOCK = 256
ROWS = 32
LOG2E = 1.4426950408889634
F32 = jnp.float32
BF16 = jnp.bfloat16


def up_to(value, step):
    return -(-value // step) * step


def mm(left, right):
    return lax.dot_general(left, right, (((1,), (0,)), ((), ())), preferred_element_type=F32)


def mm_nt(left, right):
    return lax.dot_general(left, right, (((1,), (1,)), ((), ())), preferred_element_type=F32)


def norm(rows):
    centred = rows - jnp.mean(rows, -1, keepdims=True)
    scale = lax.rsqrt(jnp.mean(centred * centred, -1, keepdims=True) + EPS)
    return centred * scale, scale


def norm_back(grad, unit, scale, gain):
    slope = grad * gain
    first = jnp.mean(slope, -1, keepdims=True)
    second = jnp.mean(slope * unit, -1, keepdims=True)
    return scale * (slope - first - unit * second)


def gelu_parts(u):
    size = jnp.abs(u)
    d = 1.0 + (0.3275911 * 0.7071067811865476) * size
    t = pl.reciprocal(d, approx=True)
    t = t * (2.0 - d * t)
    poly = 0.5 * 1.061405429
    for a in (-1.453152027, 1.421413741, -0.284496736, 0.254829592):
        poly = poly * t + 0.5 * a
    bell = jnp.exp2((u * u) * (-0.5 * LOG2E))
    tail = poly * t * bell
    phi = jnp.where(u < 0.0, tail, 1.0 - tail)
    return u * phi, phi + (u * bell) * 0.3989422804014327


def add_to(total, value):
    return value if total is None else total + value


def fold8(value):
    rows, width = value.shape
    return jnp.sum(value.reshape(rows // 8, 8, width), 0)


def kernel(
    dims,
    counts,
    global_in,
    local_in,
    global_cot,
    local_cot,
    attend_gain,
    attend_shift,
    mixer_weight,
    mixer_bias,
    output_weight,
    output_bias,
    feed_gain,
    feed_shift,
    expand_weight,
    expand_bias,
    reduce_weight,
    reduce_bias,
    global_out,
    local_out,
    global_back,
    local_back,
    sums_out,
    sums,
    crop_s,
    x_s,
    unit_s,
    scale_s,
    norm_t,
    packed_s,
    power_s,
    mixed_s,
    mixed_t,
    act_s,
    slope_s,
    grad_s,
    grad_low,
    grad_t,
    dup_s,
    mask_s,
    normed_s,
    dm_s,
    inner_s,
    dqt_s,
    vec_s,
    acc_s,
    *wires,
):
    seq, group, width = dims.seq, dims.group, dims.width
    glen, llen = dims.glen, dims.llen
    n_global, n_local, n_seq = dims.n_global, dims.n_local, dims.n_seq
    hidden = dims.hidden
    count = counts[lax.axis_index("section")]
    pairs = HEADS // 2
    lane = lax.broadcasted_iota(jnp.int32, (1, LANES), 1)
    low_half = (lane < HEAD).astype(F32).astype(BF16)
    high_half = (lane >= HEAD).astype(F32).astype(BF16)
    score_scale = HEAD ** (-0.5)
    row_blocks = [slice(a, min(a + ROWS, seq)) for a in range(0, seq, ROWS)]

    net = Net(dims.wires)
    net.greet()
    n_stage = len(dims.wires)
    sets = dims.landing_sets
    landings, sems = wires[: n_stage * sum(sets)], wires[n_stage * sum(sets) :]
    flow = Flow(net)
    number = 0
    for layer in (1, 0):
        bounds = dims.bounds[layer]
        for i in range(len(bounds) - 1):
            shared = len(sets) == 1
            at = (i if shared else number) * n_stage
            own = [w.at[number] for w in sems[:4]] + [sems[4].at[i]]
            rows = pl.ds(bounds[i], bounds[i + 1] - bounds[i])
            turn = (1 - layer) if shared else None
            flow.chunks.append(
                Chunk(net, sums.at[layer, rows], sums_out.at[layer, rows], landings[at : at + n_stage], own, turn, layer, bounds[i + 1])
            )
            number += 1

    for s in range(n_seq):
        x_s[s, seq - 32 :, :] = jnp.zeros((32, width), F32)
        grad_s[s, seq - 32 :, :] = jnp.zeros((32, width), F32)
    row_id = lax.broadcasted_iota(jnp.int32, (seq, seq), 0)
    col_id = lax.broadcasted_iota(jnp.int32, (seq, seq), 1)
    row_crop = sum((row_id >= llen * j).astype(jnp.int32) for j in range(1, group + 1))
    col_crop = sum((col_id >= llen * j).astype(jnp.int32) for j in range(1, group + 1))
    far = jnp.float32(-1e30)
    mask_s[0] = jnp.where(row_id < glen, jnp.float32(0), far)
    mask_s[1] = jnp.where(row_crop == col_crop, jnp.float32(0), far)
    one_row = (lax.broadcasted_iota(jnp.int32, (TILE, seq), 0) == 0).astype(F32).astype(BF16)
    for s in range(n_seq):
        for i in range(4):
            norm_t[i, s, width:, :] = one_row
        for i in range(2):
            mixed_t[i, s, width:, :] = one_row

    def live_rows(g):
        rows = lax.broadcasted_iota(jnp.int32, (seq, 1), 0)
        return (rows < llen * jnp.clip(count - g * group, 0, group)).astype(F32)

    for source, target in ((global_in, x_s), (global_cot, grad_s)):
        crop_s[...] = source[...].astype(F32)
        for s in range(n_global):
            target[s, 0:glen, :] = crop_s[:, s, :]
    for j in range(n_local):
        s, at = n_global + j // group, llen * (j % group)
        x_s[s, at : at + llen, :] = local_in[j].astype(F32)
        grad_s[s, at : at + llen, :] = local_cot[j].astype(F32)
    for s in range(n_global, n_seq):
        grad_s[s] = grad_s[s] * live_rows(s - n_global)

    def row(ref, layer):
        return ref[...].astype(F32)[layer : layer + 1]

    slopes = (slope_s.at[0], slope_s.at[1])

    def start_back(s):
        grad = grad_s[s]
        acc_s[2] = acc_s[2] + fold8(grad)
        grad = grad.astype(BF16)
        grad_low[s] = grad
        grad_t[s] = grad.T

    def end_back(s, place, gain, dh):
        first = second = None
        units, scales, grads, news = unit_s[place, s], scale_s[place, s], grad_s[s], []
        for rows in row_blocks:
            unit, part = units[rows].astype(F32), dh[rows]
            first, second = add_to(first, fold8(part * unit)), add_to(second, fold8(part))
            news.append((grads[rows] + norm_back(part, unit, scales[rows], gain)).astype(BF16))
        for rows, new in zip(row_blocks, news, strict=True):
            grad_low[s, rows, :] = new
            grad_s[s, rows, :] = new.astype(F32)
        acc_s[0] = acc_s[0] + first
        acc_s[1] = acc_s[1] + second

    def start_norm(s, place, gain, shift):
        x, normed = x_s[s], []
        for rows in row_blocks:
            unit, scale = norm(x[rows])
            unit_s[place, s, rows, :] = unit.astype(BF16)
            scale_s[place, s, rows, :] = scale
            normed.append((unit * gain + shift).astype(BF16))
        normed = jnp.concatenate(normed, 0)
        normed_s[...] = normed
        norm_t[place, s, 0:width, :] = normed.T

    def end_forward(s, branch, bias):
        x_s[s] = (x_s[s] + (branch + bias)).astype(BF16).astype(F32)

    def product(left, right, cols):
        total = mm(left[0], right[0, :, cols])
        for s in range(1, n_seq):
            total = total + mm(left[s], right[s, :, cols])
        return total

    for layer in range(2):
        gain, shift = row(attend_gain, layer), row(attend_shift, layer)
        bias = row(mixer_bias, layer)
        bias = jnp.concatenate([bias[:, :width], jnp.zeros((1, width), F32), bias[:, width:]], 1)
        out_bias = row(output_bias, layer)
        gain2, shift2 = row(feed_gain, layer), row(feed_shift, layer)
        bias_up, bias_down = row(expand_bias, layer), row(reduce_bias, layer)

        def attend(s, _):
            start_norm(s, 2 * layer, gain, shift)
            for c in range(0, 3 * width, BLOCK):
                cols = slice(c, min(c + BLOCK, 3 * width))
                packed = mm(normed_s[...], mixer_weight[layer, :, cols])
                for rows in row_blocks:
                    packed_s[layer, s, rows, cols] = (packed[rows] + bias[:, cols]).astype(BF16)
            mask = mask_s.at[jnp.where(s < n_global, 0, 1)]
            value_t = packed_s[layer, s, :, 2 * width :].T
            for p in range(pairs):
                at = p * LANES
                query = packed_s[layer, s, :, at : at + LANES]
                key = packed_s[layer, s, :, width + at : width + at + LANES]
                for h, half in enumerate((low_half, high_half)):
                    scores = mm_nt(key * half, query)
                    shares = []
                    for a in range(0, seq, LANES):
                        cols = slice(a, min(a + LANES, seq))
                        part = scores[:, cols] * (score_scale * LOG2E) + mask[:, cols]
                        power = jnp.exp2(part - jnp.max(part, 0, keepdims=True))
                        shares.append((power * (1.0 / jnp.sum(power, 0, keepdims=True))).astype(BF16))
                    shares = jnp.concatenate(shares, 1)
                    power_s[layer, s, 2 * p + h] = shares
                    head = slice(at + h * HEAD, at + (h + 1) * HEAD)
                    mixed_t[layer, s, head, :] = mm(value_t[head], shares).astype(BF16)
            mixed_s[layer, s] = mixed_t[layer, s, 0:width, :].T
            end_forward(s, mm(mixed_s[layer, s], output_weight[layer]), out_bias)
            return 0

        lax.fori_loop(0, n_seq, attend, 0)

        def feed(s, _):
            start_norm(s, 2 * layer + 1, gain2, shift2)
            if layer == 1:
                start_back(s)
            for c in range(hidden // BLOCK):
                cols = slice(c * BLOCK, (c + 1) * BLOCK)
                up = mm(normed_s[...], expand_weight[layer, :, cols])
                for rows in row_blocks:
                    act, slope = gelu_parts(up[rows] + bias_up[:, cols])
                    act_s[layer, s, rows, cols] = act.astype(BF16)
                    slopes[layer][s, rows, cols] = slope.astype(BF16)
            end_forward(s, mm(act_s[layer, s], reduce_weight[layer]), bias_down)
            return 0

        if layer == 1:
            acc_s[...] = jnp.zeros_like(acc_s)
        lax.fori_loop(0, n_seq, feed, 0)

    for s in range(n_global):
        crop_s[:, s, :] = x_s[s, 0:glen, :]
    global_out[...] = crop_s[...].astype(BF16)
    for j in range(n_local):
        s, at = n_global + j // group, llen * (j % group)
        alive = (count > j).astype(F32)
        local_out[j] = (x_s[s, at : at + llen, :] * alive).astype(BF16)

    def put_vector(at, value):
        for c in range(0, value.shape[1], BLOCK):
            piece = value[:, c : c + BLOCK]
            vec_s[at + c // BLOCK : at + c // BLOCK + 1, 0 : piece.shape[1]] = piece

    def put_tile(layer, top, m, part):
        at = top + (m // 3) * (width + fold)
        side = m % 3 * LANES
        part = part.astype(BF16)
        if m % 3 < 2:
            sums[layer, at : at + width, side : side + LANES] = part
        else:
            at = at + width
            sums[layer, at : at + fold, 0:LANES] = part[:fold]
            sums[layer, at : at + fold, LANES:] = part[fold:]

    blocks = hidden // BLOCK
    fold = width // 2
    tops = dims.tops
    net.wait_greeting()
    for layer in (1, 0):
        vec_s[...] = jnp.zeros_like(vec_s)
        gain2, gain = row(feed_gain, layer), row(attend_gain, layer)
        put_vector(dims.at["reduce_bias"], jnp.sum(acc_s[2], 0, keepdims=True))

        for c in range(blocks):
            total = product(grad_t, act_s.at[layer], slice(c * BLOCK, (c + 1) * BLOCK))
            at = tops[0] + c * width
            sums[layer, at : at + width, :] = total.astype(BF16)
            flow.ready(layer, at + width)
            flow.tick(0.45)

        def feed_back(s, _):
            for c in range(blocks):
                cols = slice(c * BLOCK, (c + 1) * BLOCK)
                dact = mm_nt(grad_low[s], reduce_weight[layer, cols, :])
                for rows in row_blocks:
                    dup_s[s, rows, cols] = (dact[rows] * slopes[layer][s, rows, cols].astype(F32)).astype(BF16)
            end_back(s, 2 * layer + 1, gain2, mm_nt(dup_s[s], expand_weight[layer]))
            flow.ticks(s, n_seq, 1.3)
            return 0

        acc_s[0:2] = jnp.zeros((2, 8, width), F32)
        lax.fori_loop(0, n_seq, feed_back, 0)
        put_vector(dims.at["feed_gain"], jnp.sum(acc_s[0], 0, keepdims=True))
        put_vector(dims.at["feed_shift"], jnp.sum(acc_s[1], 0, keepdims=True))

        for c in range(blocks):
            total = product(norm_t.at[2 * layer + 1], dup_s, slice(c * BLOCK, (c + 1) * BLOCK))
            at = tops[1] + c * width
            sums[layer, at : at + width, :] = total[:width].astype(BF16)
            at_bias = dims.at["expand_bias"] + c
            vec_s[at_bias : at_bias + 1, :] = total[width : width + 1]
            flow.ready(layer, at + width)
            flow.tick(0.45)

        bias_parts = []
        for c in range(0, width, BLOCK):
            size = min(BLOCK, width - c)
            total = product(mixed_t.at[layer], grad_low, slice(c, c + size))
            for k in range(0, size, LANES):
                put_tile(layer, tops[2], (c + k) // LANES, total[:width, k : k + LANES])
                bias_parts.append(total[width : width + 1, k : k + LANES])
        put_vector(dims.at["output_bias"], jnp.concatenate(bias_parts, 1))
        flow.ready(layer, tops[3])
        flow.tick(0.8)

        def attend_back(s, _):
            dmixed = mm_nt(grad_low[s], output_weight[layer])
            for rows in row_blocks:
                dm_s[rows, :] = dmixed[rows].astype(BF16)
                inner_s[rows, :] = -(dmixed[rows] * mixed_s[layer, s, rows, :].astype(F32)).astype(BF16)
            key_t = packed_s[layer, s, :, width : 2 * width].T
            for p in range(pairs):
                at = p * LANES
                query = packed_s[layer, s, :, at : at + LANES]
                value = packed_s[layer, s, :, 2 * width + at : 2 * width + at + LANES]
                dm, inner = dm_s[:, at : at + LANES], inner_s[:, at : at + LANES]
                wide_value = jnp.concatenate([value, jnp.ones_like(value)], 1)
                dk = dv = None
                for h, half in enumerate((low_half, high_half)):
                    dm_half = dm * half
                    slope = mm_nt(wide_value, jnp.concatenate([dm_half, inner * half], 1))
                    ds = []
                    for rows in row_blocks:
                        ds.append((power_s[layer, s, 2 * p + h, rows, :].astype(F32) * slope[rows]).astype(BF16))
                    ds = jnp.concatenate(ds, 0)
                    head = slice(at + h * HEAD, at + (h + 1) * HEAD)
                    dqt_s[head, :] = (mm(key_t[head], ds) * score_scale).astype(BF16)
                    dk = add_to(dk, mm(ds, query * half))
                    dv = add_to(dv, mm(power_s[layer, s, 2 * p + h], dm_half))
                dup_s[s, :, width + at : width + at + LANES] = (dk * score_scale).astype(BF16)
                dup_s[s, :, 2 * width + at : 2 * width + at + LANES] = dv.astype(BF16)
            dup_s[s, :, 0:width] = dqt_s[...].T
            end_back(s, 2 * layer, gain, mm_nt(dup_s[s, :, 0 : 3 * width], mixer_weight[layer]))
            if layer == 1:
                start_back(s)
            flow.ticks(s, n_seq, 2.3)
            return 0

        acc_s[...] = jnp.zeros_like(acc_s)
        lax.fori_loop(0, n_seq, attend_back, 0)
        put_vector(dims.at["attend_gain"], jnp.sum(acc_s[0], 0, keepdims=True))
        put_vector(dims.at["attend_shift"], jnp.sum(acc_s[1], 0, keepdims=True))

        bias_parts = []
        for c in range(0, 3 * width, BLOCK):
            size = min(BLOCK, 3 * width - c)
            total = product(norm_t.at[2 * layer], dup_s, slice(c, c + size))
            for k in range(0, size, LANES):
                put_tile(layer, tops[3], (c + k) // LANES, total[:width, k : k + LANES])
                bias_parts.append(total[width : width + 1, k : k + LANES])
            flow.tick(0.5)
        each = width // LANES
        put_vector(
            dims.at["mixer_bias"],
            jnp.concatenate(bias_parts[:each] + bias_parts[2 * each :], 1),
        )
        sums[layer, tops[4] : tops[4] + dims.vec_rows, :] = vec_s[...].astype(BF16)
        rest = dims.rows - tops[4] - dims.vec_rows
        if rest:
            sums[layer, dims.rows - rest :, :] = jnp.zeros((rest, BLOCK), BF16)
        flow.ready(layer, dims.rows)

    for s in range(n_global):
        crop_s[:, s, :] = grad_s[s, 0:glen, :]
    global_back[...] = crop_s[...].astype(BF16)
    for j in range(n_local):
        s, at = n_global + j // group, llen * (j % group)
        local_back[j] = grad_s[s, at : at + llen, :].astype(BF16)
    flow.drain()


class Wire:
    def __init__(self, size, first, second):
        self.size, self.first, self.second = size, first, second


def wires_of(mesh):
    names = mesh.axis_names
    places = {}
    for axis, name in enumerate(names):
        line = [mesh.devices[tuple(i if a == axis else 0 for a in range(2))] for i in range(mesh.devices.shape[axis])]
        spots = [(d.core_on_chip,) + tuple(d.coords) for d in line]
        found, total = [], 1
        for k in range(4):
            values = sorted({p[k] for p in spots})
            if len(values) > 1:
                stride = next(i for i, p in enumerate(spots) if p[k] != spots[0][k])
                found.append((k, axis, stride, len(values)))
                total *= len(values)
        good = total == len(line)
        for k, _, stride, size in found:
            values = [p[k] for p in spots]
            good = good and all(v == values[i // stride % size * stride] for i, v in enumerate(values))
        if not good:
            found = [(4 + axis, axis, 1, len(line))]
        for k, axis, stride, size in found:
            places[k] = (axis, stride, size)
    wires = []
    if 0 in places:
        wires.append(Wire(places[0][2], places[0], places[0]))
    if 0 in places and 1 in places and 2 in places and places[1][2] == places[2][2]:
        wires.append(Wire(places[1][2], places[1], places[2]))
        wires.append(Wire(places[1][2], places[2], places[1]))
        order = [3, 4, 5]
    else:
        order = [1, 2, 3, 4, 5]
    for k in order:
        if k in places:
            wires.append(Wire(places[k][2], places[k], places[k]))
    return wires


class Net:
    def __init__(self, wires):
        self.axes = ("dp", "section")
        self.here = [lax.axis_index(a) for a in self.axes]
        self.wires = wires
        first = wires[0]
        odd = self.spot(first.first) % 2 if first.size == 2 else 0
        self.odd = odd
        self.at = []
        for w in wires:
            a, b = self.spot(w.first), self.spot(w.second)
            self.at.append(a if w.first == w.second else a + odd * (b - a))

    def spot(self, place):
        axis, stride, size = place
        return self.here[axis] // stride % size

    def peer(self, stage, k):
        w = self.wires[stage]
        place = (self.at[stage] + k) % w.size
        move = place - self.at[stage]
        target = list(self.here)
        if w.first == w.second:
            target[w.first[0]] = target[w.first[0]] + move * w.first[1]
        else:
            target[w.first[0]] = target[w.first[0]] + move * w.first[1] * (1 - self.odd)
            target[w.second[0]] = target[w.second[0]] + move * w.second[1] * self.odd
        return tuple(target), place

    def greet(self):
        barrier = pltpu.get_barrier_semaphore()
        for stage, w in enumerate(self.wires):
            for k in range(1, w.size):
                pl.semaphore_signal(barrier, inc=1, device_id=self.peer(stage, k)[0], device_id_type=pl.DeviceIdType.MESH)

    def wait_greeting(self):
        pl.semaphore_wait(pltpu.get_barrier_semaphore(), sum(w.size - 1 for w in self.wires))


class Chunk:
    def __init__(self, net, sums, out, landing, sems, turn, layer, end):
        self.net, self.sums, self.out, self.landing = net, sums, out, landing
        self.send, self.recv, self.local, self.sent, self.free = sems
        self.turn = turn
        self.layer, self.end = layer, end
        self.due = None
        size, start = sums.shape[0], 0
        self.unit = size
        for w in net.wires:
            self.unit //= w.size
        self.size, self.start = [], []
        for stage, w in enumerate(net.wires):
            size //= w.size
            self.size.append(size)
            self.start.append((start, size))
            start = start + net.at[stage] * size
        self.own = start
        self.stages = len(net.wires)
        self.step = 0
        self.sem_at, at = {}, 0
        for phase in range(2):
            for stage, w in enumerate(net.wires):
                for k in range(1, w.size):
                    self.sem_at[phase, stage, k] = at
                    at += 1

    def rows(self, stage, place):
        start, size = self.start[stage]
        return pl.ds(pl.multiple_of(start + place * size, TILE), size)

    def copy(self, phase, stage, k):
        target, place = self.net.peer(stage, k)
        at = self.sem_at[phase, stage, k]
        if phase == 0:
            source, to = self.sums.at[self.rows(stage, place)], self.landing[stage].at[k - 1]
        else:
            rows = self.rows(stage, self.net.at[stage])
            source = to = self.sums.at[rows]
        return pltpu.make_async_remote_copy(
            src_ref=source,
            dst_ref=to,
            send_sem=self.send.at[at],
            recv_sem=self.recv.at[at],
            device_id=target,
            device_id_type=pl.DeviceIdType.MESH,
        )

    def arrival(self, stage, k):
        target, place = self.net.peer(stage, self.net.wires[stage].size - k)
        at = self.sem_at[1, stage, k]
        landed = self.sums.at[self.rows(stage, place)]
        return pltpu.make_async_remote_copy(
            src_ref=landed,
            dst_ref=landed,
            send_sem=self.send.at[at],
            recv_sem=self.recv.at[at],
            device_id=target,
            device_id_type=pl.DeviceIdType.MESH,
        )

    def start_stage(self, phase, stage):
        if phase == 0 and self.turn == 1:
            pl.semaphore_wait(self.free.at[stage], self.net.wires[stage].size - 1)
        if phase == 1:
            pl.semaphore_wait(self.sent.at[stage], self.net.wires[stage].size - 1)
        for k in range(1, self.net.wires[stage].size):
            self.copy(phase, stage, k).start()

    def load(self):
        last = self.stages - 1
        stage = self.step if self.step <= last else 2 * self.stages - 1 - self.step
        peers = self.net.wires[stage].size - 1
        row = BLOCK * 2
        if stage == 0:
            return 0, self.size[0] * row / 4
        if stage == last:
            return 2, self.size[stage] * (peers + 1) ** 2 / 2 * row
        return 1, self.size[stage] * peers * row

    def begin(self):
        self.start_stage(0, 0)

    def out_copy(self):
        return pltpu.make_async_copy(self.sums, self.out, self.local.at[0])

    def advance(self):
        step = self.step
        self.step += 1
        if step < self.stages:
            peers = range(1, self.net.wires[step].size)
            for k in peers:
                self.copy(0, step, k).wait_recv()
            base = self.start[step][0] + self.net.at[step] * self.size[step]
            landing = self.landing[step]

            def add(i, _):
                at = pl.ds(pl.multiple_of(base + i * self.unit, TILE), self.unit)
                total = self.sums[at, :].astype(F32)
                for k in peers:
                    total = total + landing[k - 1, pl.ds(pl.multiple_of(i * self.unit, TILE), self.unit), :].astype(F32)
                self.sums[at, :] = total.astype(BF16)
                return 0

            lax.fori_loop(0, self.size[step] // self.unit, add, 0)
            for k in peers:
                self.copy(0, step, k).wait_send()
                target = self.net.peer(step, k)[0]
                pl.semaphore_signal(self.sent.at[step], inc=1, device_id=target, device_id_type=pl.DeviceIdType.MESH)
                if self.turn == 0:
                    pl.semaphore_signal(self.free.at[step], inc=1, device_id=target, device_id_type=pl.DeviceIdType.MESH)
            if step + 1 < self.stages:
                self.start_stage(0, step + 1)
            else:
                self.start_stage(1, step)
        else:
            stage = 2 * self.stages - 1 - step
            for k in range(1, self.net.wires[stage].size):
                self.arrival(stage, k).wait_recv()
            if stage > 0:
                self.start_stage(1, stage - 1)
            else:
                self.out_copy().start()

    def finish(self):
        for phase, stage, k in self.sem_at:
            if phase == 1:
                self.copy(phase, stage, k).wait_send()
        self.out_copy().wait()


LATENCY = 2.0
RATE = 80e3
STEP = 0.4


class Flow:
    def __init__(self, net):
        self.chunks, self.now, self.waiting, self.free = [], 0.0, 0, [0.0] * 3

    def book(self, chunk):
        kind, size = chunk.load()
        self.free[kind] = max(self.now, self.free[kind]) + size / RATE
        chunk.due = self.free[kind] + LATENCY

    def ready(self, layer, rows):
        while self.waiting < len(self.chunks):
            chunk = self.chunks[self.waiting]
            if chunk.layer != layer or chunk.end > rows:
                return
            chunk.begin()
            self.book(chunk)
            self.waiting += 1

    def due(self):
        return sorted((c for c in self.chunks if c.due is not None and c.due <= self.now), key=lambda c: c.due)

    def take(self):
        while self.due():
            chunk = self.due()[0]
            chunk.advance()
            self.now += STEP
            if chunk.step < 2 * chunk.stages:
                self.book(chunk)
            else:
                chunk.due = None

    def tick(self, time):
        self.now += time
        self.take()

    def ticks(self, s, count, time):
        for i in range(count):
            self.now += time
            if self.due():
                pl.when(s == i)(self.take)

    def drain(self):
        while any(c.due is not None for c in self.chunks):
            self.now = max(self.now, min(c.due for c in self.chunks if c.due is not None))
            self.take()
        for chunk in self.chunks:
            chunk.finish()


class Dims:
    def __init__(self, global_crops, local_crops, hidden, wires):
        self.wires = wires
        self.glen, self.n_global, self.width = global_crops.shape
        self.n_local, self.llen, _ = local_crops.shape
        self.hidden = hidden
        self.seq = up_to(self.glen, TILE)
        self.group = self.seq // self.llen
        while self.n_local % self.group:
            self.group -= 1
        self.n_seq = self.n_global + self.n_local // self.group
        sizes = (
            ("attend_gain", self.width),
            ("attend_shift", self.width),
            ("mixer_bias", 2 * self.width),
            ("output_bias", self.width),
            ("feed_gain", self.width),
            ("feed_shift", self.width),
            ("expand_bias", hidden),
            ("reduce_bias", self.width),
        )
        self.names, self.sizes = [name for name, _ in sizes], dict(sizes)
        self.at, row = {}, 0
        for name, size in sizes:
            self.at[name] = row
            row += -(-size // BLOCK)
        self.vec_rows = 2 * TILE
        assert row <= self.vec_rows and self.width * hidden % self.vec_rows == 0
        step = TILE
        for w in wires:
            step *= w.size
        ff = self.width * hidden // BLOCK
        square = self.width * self.width // BLOCK
        self.tops = (0, ff, 2 * ff, 2 * ff + square, 2 * ff + 4 * square)
        self.rows = up_to(self.tops[4] + self.vec_rows, step)
        parts = self.rows // step
        cuts = ((0, 4, 7, 10, 12, 14), (0, 4, 10, 14))
        self.bounds = [[c * step for c in sorted({parts * k // 14 for k in layer})] for layer in cuts]
        self.landing_sets = [len(b) - 1 for b in self.bounds[::-1]]
        if self.bounds[0] == self.bounds[1]:
            self.landing_sets = self.landing_sets[:1]
        self.n_chunk = sum(len(b) - 1 for b in self.bounds)


def run_kernel(counts, arrays, dims):
    d = dims
    n, seq, width, hidden = d.n_seq, d.seq, d.width, d.hidden
    crops = [jax.ShapeDtypeStruct(a.shape, BF16) for a in arrays[:2]]
    outs = crops + crops
    outs += [jax.ShapeDtypeStruct((2, d.rows, BLOCK), BF16)]
    scratch = [
        pltpu.VMEM((2, d.rows, BLOCK), BF16),
        pltpu.VMEM((d.glen, d.n_global, width), F32),
        pltpu.VMEM((n, seq, width), F32),
        pltpu.VMEM((4, n, seq, width), BF16),
        pltpu.VMEM((4, n, seq, 1), F32),
        pltpu.VMEM((4, n, width + TILE, seq), BF16),
        pltpu.VMEM((2, n, seq, 3 * width), BF16),
        pltpu.VMEM((2, n, HEADS, seq, seq), BF16),
        pltpu.VMEM((2, n, seq, width), BF16),
        pltpu.VMEM((2, n, width + TILE, seq), BF16),
        pltpu.VMEM((2, n, seq, hidden), BF16),
        pltpu.VMEM((2, n, seq, hidden), BF16),
        pltpu.VMEM((n, seq, width), F32),
        pltpu.VMEM((n, seq, width), BF16),
        pltpu.VMEM((n, width, seq), BF16),
        pltpu.VMEM((n, seq, hidden), BF16),
        pltpu.VMEM((2, seq, seq), F32),
        pltpu.VMEM((seq, width), BF16),
        pltpu.VMEM((seq, width), BF16),
        pltpu.VMEM((seq, width), BF16),
        pltpu.VMEM((width, seq), BF16),
        pltpu.VMEM((d.vec_rows, BLOCK), F32),
        pltpu.VMEM((3, 8, width), F32),
    ]
    for layer in (1, 0)[: len(d.landing_sets)]:
        for first, end in zip(d.bounds[layer], d.bounds[layer][1:]):
            rows = end - first
            for w in d.wires:
                rows //= w.size
                scratch.append(pltpu.VMEM((w.size - 1, rows, BLOCK), BF16))
    peers = 2 * sum(w.size - 1 for w in d.wires)
    scratch += [
        pltpu.SemaphoreType.DMA((d.n_chunk, peers)),
        pltpu.SemaphoreType.DMA((d.n_chunk, peers)),
        pltpu.SemaphoreType.DMA((d.n_chunk, 1)),
        pltpu.SemaphoreType.REGULAR((d.n_chunk, len(d.wires))),
        pltpu.SemaphoreType.REGULAR((d.n_chunk, len(d.wires))),
    ]
    vmem = pl.BlockSpec(memory_space=pltpu.VMEM)
    anywhere = pl.BlockSpec(memory_space=pl.ANY)
    return pl.pallas_call(
        functools.partial(kernel, d),
        out_shape=outs,
        in_specs=[pl.BlockSpec(memory_space=pltpu.SMEM)] + [vmem] * len(arrays),
        out_specs=[vmem] * 4 + [anywhere],
        scratch_shapes=scratch,
        compiler_params=pltpu.CompilerParams(
            vmem_limit_bytes=63 * 1024 * 1024, collective_id=0, has_side_effects=True
        ),
    )(counts, *arrays)


THIRDS = 3


def cast_kernel(dims, reduce, expand, output, mixer, vectors, *rest):
    crops, outs, held, sems = rest[:4], rest[4:-9], rest[-5:-1], rest[-1]
    step = pl.program_id(0) * THIRDS + pl.program_id(1)
    loads = [pltpu.make_async_copy(a, b, sems.at[0, i]) for i, (a, b) in enumerate(zip(crops, held, strict=True))]
    stores = [pltpu.make_async_copy(a, b, sems.at[1, i]) for i, (a, b) in enumerate(zip(held, rest[-9:-5], strict=True))]

    @pl.when(step == 0)
    def _():
        for copy in loads:
            copy.start()

    @pl.when(step == 1)
    def _():
        for load, store in zip(loads, stores, strict=True):
            load.wait()
            store.start()

    mixer_grad, output_grad, expand_grad, reduce_grad = outs[:4]
    width = dims.width
    fold = width // 2
    for b in range(2):
        rows = slice(b * width, (b + 1) * width)
        cols = slice(b * BLOCK, (b + 1) * BLOCK)
        expand_grad[0, :, cols] = expand[0, rows, :].astype(F32)
        reduce_grad[0, cols, :] = reduce[0, rows, :].T.astype(F32)
    for source, target in ((mixer, mixer_grad), (output, output_grad)):
        target[0, :, 0:BLOCK] = source[0, 0:width, :].astype(F32)
        target[0, 0:fold, BLOCK:] = source[0, width:, 0:LANES].astype(F32)
        target[0, fold:, BLOCK:] = source[0, width:, LANES:].astype(F32)

    @pl.when(step == 2 * THIRDS - 1)
    def _():
        for ref, name in zip(outs[4:], dims.names, strict=True):
            size = ref.shape[1]
            for c in range(0, size, BLOCK):
                at = dims.at[name] + c // BLOCK
                piece = min(BLOCK, size - c)
                for layer in range(2):
                    ref[layer : layer + 1, c : c + piece] = vectors[layer].astype(F32)[at : at + 1, 0:piece]
        for store in stores:
            store.wait()


def run_cast(sums, crops, dims):
    d = dims
    width, hidden = d.width, d.hidden
    part = (1, 2 * width, BLOCK)
    square = (1, width * width // BLOCK, BLOCK)
    grads = [(width, 3 * width), (width, width), (width, hidden), (hidden, width)]
    shapes = [jax.ShapeDtypeStruct((2,) + g, F32) for g in grads]
    specs = [
        pl.BlockSpec((1, width, 3 * width // THIRDS), lambda l, t: (l, 0, t)),
        pl.BlockSpec((1, width, width), lambda l, t: (l, 0, 0)),
        pl.BlockSpec((1, width, hidden // THIRDS), lambda l, t: (l, 0, t)),
        pl.BlockSpec((1, hidden // THIRDS, width), lambda l, t: (l, t, 0)),
    ]
    for name in d.names:
        shapes.append(jax.ShapeDtypeStruct((2, d.sizes[name]), F32))
        specs.append(pl.BlockSpec((2, d.sizes[name]), lambda l, t: (0, 0)))
    for crop in crops:
        shapes.append(jax.ShapeDtypeStruct(crop.shape, crop.dtype))
        specs.append(pl.BlockSpec(memory_space=pl.ANY))
    return pl.pallas_call(
        functools.partial(cast_kernel, d),
        grid=(2, THIRDS),
        out_shape=shapes,
        in_specs=[
            pl.BlockSpec(part, lambda l, t: (l, t, 0)),
            pl.BlockSpec(part, lambda l, t: (l, THIRDS + t, 0)),
            pl.BlockSpec(square, lambda l, t: (l, d.tops[2] // square[1], 0)),
            pl.BlockSpec(square, lambda l, t: (l, d.tops[3] // square[1] + t, 0)),
            pl.BlockSpec((2, d.vec_rows, BLOCK), lambda l, t: (0, d.tops[4] // d.vec_rows, 0)),
        ]
        + [pl.BlockSpec(memory_space=pl.ANY)] * 4,
        out_specs=specs,
        scratch_shapes=[pltpu.VMEM(c.shape, c.dtype) for c in crops] + [pltpu.SemaphoreType.DMA((2, 4))],
        compiler_params=pltpu.CompilerParams(vmem_limit_bytes=62 * 1024 * 1024),
    )(sums, sums, sums, sums, sums, *crops)


def shards(wires, global_crops, local_crops, local_count, global_cotangent, local_cotangent, *weights):
    global_crops, global_cotangent = global_crops.transpose(1, 0, 2), global_cotangent.transpose(1, 0, 2)
    dims = Dims(global_crops, local_crops, weights[8].shape[2], wires)
    outs = run_kernel(
        local_count, (global_crops, local_crops, global_cotangent, local_cotangent) + weights, dims
    )
    mixer, output, expand, reduce, *rest = run_cast(outs[4], outs[:4], dims)
    vectors, crops = rest[:-4], rest[-4:]
    v = dict(zip(dims.names, vectors, strict=True))
    return (
        crops[0].transpose(1, 0, 2),
        crops[1],
        crops[2].transpose(1, 0, 2),
        crops[3],
        v["attend_gain"],
        v["attend_shift"],
        mixer,
        v["mixer_bias"],
        output,
        v["output_bias"],
        v["feed_gain"],
        v["feed_shift"],
        expand,
        v["expand_bias"],
        reduce,
        v["reduce_bias"],
    )


def solution(mesh):
    crops = P(("dp", "section"), None, None)
    return jax.shard_map(
        functools.partial(shards, wires_of(mesh)),
        mesh=mesh,
        in_specs=(crops, crops, P("dp"), crops, crops) + (P(),) * 12,
        out_specs=(crops,) * 4 + (P(),) * 12,
        check_vma=False,
    )
```

```python
import functools

import jax
import jax.numpy as jnp
from jax import lax
from jax.experimental import pallas as pl
from jax.experimental.pallas import tpu as pltpu
from jax.sharding import PartitionSpec as P

HEADS = 6
HEAD = 64
EPS = 1e-06
TILE = 16
LANES = 128
BLOCK = 256
LOG2E = 1.4426950408889634
F32 = jnp.float32
BF16 = jnp.bfloat16


def up_to(value, step):
    return -(-value // step) * step


def mm(left, right):
    return lax.dot_general(left, right, (((1,), (0,)), ((), ())), preferred_element_type=F32)


def mm_nt(left, right):
    return lax.dot_general(left, right, (((1,), (1,)), ((), ())), preferred_element_type=F32)


def mm_tn(left, right):
    return lax.dot_general(left, right, (((0,), (0,)), ((), ())), preferred_element_type=F32)


def norm(rows):
    centred = rows - jnp.mean(rows, -1, keepdims=True)
    scale = lax.rsqrt(jnp.mean(centred * centred, -1, keepdims=True) + EPS)
    return centred * scale, scale


def norm_back(grad, unit, scale, gain):
    slope = grad * gain
    first = jnp.mean(slope, -1, keepdims=True)
    second = jnp.mean(slope * unit, -1, keepdims=True)
    return scale * (slope - first - unit * second)


def gelu_parts(u):
    size = jnp.abs(u)
    d = 1.0 + (0.3275911 * 0.7071067811865476) * size
    t = pl.reciprocal(d, approx=True)
    t = t * (2.0 - d * t)
    poly = 0.5 * 1.061405429
    for a in (-1.453152027, 1.421413741, -0.284496736, 0.254829592):
        poly = poly * t + 0.5 * a
    bell = jnp.exp2((u * u) * (-0.5 * LOG2E))
    tail = poly * t * bell
    phi = jnp.where(u < 0.0, tail, 1.0 - tail)
    return u * phi, phi + (u * bell) * 0.3989422804014327


def fold8(value):
    rows, width = value.shape
    return jnp.sum(value.reshape(rows // 8, 8, width), 0)


def kernel(
    dims,
    counts,
    global_in,
    local_in,
    global_cot,
    local_cot,
    attend_gain,
    attend_shift,
    mixer_weight,
    mixer_bias,
    output_weight,
    output_bias,
    feed_gain,
    feed_shift,
    expand_weight,
    expand_bias,
    reduce_weight,
    reduce_bias,
    global_out,
    local_out,
    global_back,
    local_back,
    sums_out,
    sums,
    crop_s,
    x_s,
    unit_s,
    scale_s,
    norm_t,
    packed_s,
    power_s,
    inverse_s,
    mixed_s,
    mixed_t,
    act_s,
    slope_s,
    grad_s,
    grad_low,
    grad_t,
    dup_s,
    mask_s,
    normed_s,
    inner_s,
    vec_s,
    acc_s,
    *wires,
):
    seq, group, width = dims.seq, dims.group, dims.width
    glen, llen = dims.glen, dims.llen
    n_global, n_local, n_seq = dims.n_global, dims.n_local, dims.n_seq
    hidden = dims.hidden
    count = counts[lax.axis_index("section")]
    pairs = HEADS // 2
    lane = lax.broadcasted_iota(jnp.int32, (1, LANES), 1)
    low_half = (lane < HEAD).astype(F32).astype(BF16)
    high_half = (lane >= HEAD).astype(F32).astype(BF16)
    score_scale = HEAD ** (-0.5)

    net = Net(dims.wires)
    net.greet()
    n_stage = len(dims.wires)
    sets = dims.landing_sets
    landings, sems = wires[: n_stage * sum(sets)], wires[n_stage * sum(sets) :]
    flow = Flow(net)
    number = 0
    for layer in (1, 0):
        bounds = dims.bounds[layer]
        for i in range(len(bounds) - 1):
            shared = len(sets) == 1
            at = (i if shared else number) * n_stage
            own = [w.at[number] for w in sems[:4]] + [sems[4].at[i]]
            rows = pl.ds(bounds[i], bounds[i + 1] - bounds[i])
            turn = (1 - layer) if shared else None
            flow.chunks.append(
                Chunk(net, sums.at[layer, rows], sums_out.at[layer, rows], landings[at : at + n_stage], own, turn, layer, bounds[i + 1])
            )
            number += 1

    for s in range(n_seq):
        x_s[(s + 1) * seq - 32 : (s + 1) * seq, :] = jnp.zeros((32, width), F32)
        grad_s[(s + 1) * seq - 32 : (s + 1) * seq, :] = jnp.zeros((32, width), F32)
    row_id = lax.broadcasted_iota(jnp.int32, (seq, seq), 0)
    col_id = lax.broadcasted_iota(jnp.int32, (seq, seq), 1)
    row_crop = sum((row_id >= llen * j).astype(jnp.int32) for j in range(1, group + 1))
    col_crop = sum((col_id >= llen * j).astype(jnp.int32) for j in range(1, group + 1))
    far = jnp.float32(-1e30)
    mask_s[0] = jnp.where(col_id < glen, jnp.float32(0), far).astype(BF16)
    mask_s[1] = jnp.where(row_crop == col_crop, jnp.float32(0), far).astype(BF16)
    one_row = (lax.broadcasted_iota(jnp.int32, (TILE, seq), 0) == 0).astype(F32).astype(BF16)
    for s in range(n_seq):
        for i in range(4):
            norm_t[i, s, width:, :] = one_row
        for i in range(2):
            mixed_t[i, s, width:, :] = one_row

    def local_at(j):
        return (n_global + j // group) * seq + llen * (j % group)

    def rows_of(s):
        return pl.ds(pl.multiple_of(s * seq, TILE), seq)

    def live_rows(g):
        rows = lax.broadcasted_iota(jnp.int32, (seq, 1), 0)
        return (rows < llen * jnp.clip(count - g * group, 0, group)).astype(F32)

    for source, target in ((global_in, x_s), (global_cot, grad_s)):
        crop_s[...] = source[...].astype(F32)
        for s in range(n_global):
            target[s * seq : s * seq + glen, :] = crop_s[:, s, :]
    for j in range(n_local):
        at = local_at(j)
        x_s[at : at + llen, :] = local_in[j].astype(F32)
        grad_s[at : at + llen, :] = local_cot[j].astype(F32)
    for s in range(n_global, n_seq):
        at = slice(s * seq, (s + 1) * seq)
        grad_s[at, :] = grad_s[at, :] * live_rows(s - n_global)

    def row(ref, layer):
        return ref[...].astype(F32)[layer : layer + 1]

    slopes = (slope_s, dup_s)

    halves = [slice(c, min(c + BLOCK, width)) for c in range(0, width, BLOCK)]

    def start_back(s):
        grad = grad_s[rows_of(s), :]
        acc_s[2] = acc_s[2] + fold8(grad)
        grad = grad.astype(BF16)
        grad_low[rows_of(s), :] = grad
        grad_t[s] = grad.T

    def end_back(s, place, gain):
        rows = rows_of(s)
        dh, unit, scale = x_s[rows, :], unit_s[place, rows, :].astype(F32), scale_s[place, rows, :]
        acc_s[0] = acc_s[0] + fold8(dh * unit)
        acc_s[1] = acc_s[1] + fold8(dh)
        grad = (grad_s[rows, :] + norm_back(dh, unit, scale, gain)).astype(BF16)
        grad_low[rows, :] = grad
        grad_s[rows, :] = grad.astype(F32)

    def norms(place, gain, shift, with_grad=False):
        def one(s, _):
            rows = rows_of(s)
            unit, scale = norm(x_s[rows, :])
            unit_s[place, rows, :] = unit.astype(BF16)
            scale_s[place, rows, :] = scale
            normed = (unit * gain + shift).astype(BF16)
            normed_s[rows, :] = normed
            norm_t[place, s, 0:width, :] = normed.T
            if with_grad:
                start_back(s)
            return 0

        lax.fori_loop(0, n_seq, one, 0)

    def onto_stream(left, weight, bias):
        for cols in halves:
            branch = mm(left[...], weight[:, cols]) + bias[:, cols]
            x_s[:, cols] = (x_s[:, cols] + branch).astype(BF16).astype(F32)

    def product(left, right, cols):
        total = mm(left[0], right[0:seq, cols])
        for s in range(1, n_seq):
            total = total + mm(left[s], right[s * seq : (s + 1) * seq, cols])
        return total

    for layer in range(2):
        gain, shift = row(attend_gain, layer), row(attend_shift, layer)
        bias = row(mixer_bias, layer)
        bias = jnp.concatenate([bias[:, :width], jnp.zeros((1, width), F32), bias[:, width:]], 1)
        out_bias = row(output_bias, layer)
        gain2, shift2 = row(feed_gain, layer), row(feed_shift, layer)
        bias_down = row(reduce_bias, layer)

        norms(2 * layer, gain, shift)
        for c in range(0, 3 * width, BLOCK):
            cols = slice(c, min(c + BLOCK, 3 * width))
            packed = mm(normed_s[...], mixer_weight[layer, :, cols]) + bias[:, cols]
            packed_s[layer, :, cols] = packed.astype(BF16)

        def attend(s, _):
            rows = rows_of(s)
            mask = mask_s[jnp.where(s < n_global, 0, 1)].astype(F32)
            mixed = []
            for p in range(pairs):
                at = p * LANES
                query = packed_s[layer, rows, at : at + LANES]
                key = packed_s[layer, rows, width + at : width + at + LANES]
                value = packed_s[layer, rows, 2 * width + at : 2 * width + at + LANES]
                total = None
                for h, half in enumerate((low_half, high_half)):
                    scores = mm_nt(query * half, key) * (score_scale * LOG2E) + mask
                    power = jnp.exp2(scores - jnp.max(scores, -1, keepdims=True)).astype(BF16)
                    power_s[layer, s, 2 * p + h] = power
                    spread = jnp.broadcast_to(half, (seq, LANES))
                    term = mm(power, jnp.concatenate([value * half, spread], 1))
                    total = term if total is None else total + term
                inverse = 1.0 / total[:, LANES:]
                inverse_s[layer, rows, at : at + LANES] = inverse
                mixed.append((total[:, :LANES] * inverse).astype(BF16))
            mixed = jnp.concatenate(mixed, 1)
            mixed_s[layer, rows, :] = mixed
            mixed_t[layer, s, 0:width, :] = mixed.T
            return 0

        lax.fori_loop(0, n_seq, attend, 0)

        onto_stream(mixed_s.at[layer], output_weight.at[layer], out_bias)
        if layer == 1:
            acc_s[...] = jnp.zeros_like(acc_s)
        norms(2 * layer + 1, gain2, shift2, layer == 1)

        def feed(c, _):
            cols = pl.ds(pl.multiple_of(c * BLOCK, BLOCK), BLOCK)
            bias_up = expand_bias[:, cols].astype(F32)[layer : layer + 1]
            act, slope = gelu_parts(mm(normed_s[...], expand_weight[layer, :, cols]) + bias_up)
            act_s[layer, :, cols] = act.astype(BF16)
            slopes[layer][:, cols] = slope.astype(BF16)
            return 0

        lax.fori_loop(0, hidden // BLOCK, feed, 0)
        onto_stream(act_s.at[layer], reduce_weight.at[layer], bias_down)

    for s in range(n_global):
        crop_s[:, s, :] = x_s[s * seq : s * seq + glen, :]
    global_out[...] = crop_s[...].astype(BF16)
    for j in range(n_local):
        at = local_at(j)
        alive = (count > j).astype(F32)
        local_out[j] = (x_s[at : at + llen, :] * alive).astype(BF16)

    def put_vector(at, value):
        for c in range(0, value.shape[1], BLOCK):
            piece = value[:, c : c + BLOCK]
            vec_s[at + c // BLOCK : at + c // BLOCK + 1, 0 : piece.shape[1]] = piece

    def put_tile(layer, top, m, part):
        at = top + (m // 3) * (width + fold)
        side = m % 3 * LANES
        part = part.astype(BF16)
        if m % 3 < 2:
            sums[layer, at : at + width, side : side + LANES] = part
        else:
            at = at + width
            sums[layer, at : at + fold, 0:LANES] = part[:fold]
            sums[layer, at : at + fold, LANES:] = part[fold:]

    blocks = hidden // BLOCK
    fold = width // 2
    tops = dims.tops
    net.wait_greeting()
    for layer in (1, 0):
        vec_s[...] = jnp.zeros_like(vec_s)
        gain2, gain = row(feed_gain, layer), row(attend_gain, layer)
        put_vector(dims.at["reduce_bias"], jnp.sum(acc_s[2], 0, keepdims=True))

        for c in range(blocks):
            total = product(grad_t, act_s.at[layer], slice(c * BLOCK, (c + 1) * BLOCK))
            at = tops[0] + c * width
            sums[layer, at : at + width, :] = total.astype(BF16)
            flow.ready(layer, at + width)
            flow.tick(0.45)

        def feed_back(c, _):
            cols = pl.ds(pl.multiple_of(c * BLOCK, BLOCK), BLOCK)
            dact = mm_nt(grad_low[...], reduce_weight[layer, cols, :])
            dup_s[:, cols] = (dact * slopes[layer][:, cols].astype(F32)).astype(BF16)
            flow.ticks(c, blocks, 0.4)
            return 0

        lax.fori_loop(0, blocks, feed_back, 0)
        for cols in halves:
            x_s[:, cols] = mm_nt(dup_s[...], expand_weight[layer, cols, :])
            flow.tick(0.8)
        acc_s[0:2] = jnp.zeros((2, 8, width), F32)

        def feed_norm_back(s, _):
            end_back(s, 2 * layer + 1, gain2)
            flow.ticks(s, n_seq, 0.3)
            return 0

        lax.fori_loop(0, n_seq, feed_norm_back, 0)
        put_vector(dims.at["feed_gain"], jnp.sum(acc_s[0], 0, keepdims=True))
        put_vector(dims.at["feed_shift"], jnp.sum(acc_s[1], 0, keepdims=True))

        for c in range(blocks):
            total = product(norm_t.at[2 * layer + 1], dup_s, slice(c * BLOCK, (c + 1) * BLOCK))
            at = tops[1] + c * width
            sums[layer, at : at + width, :] = total[:width].astype(BF16)
            at_bias = dims.at["expand_bias"] + c
            vec_s[at_bias : at_bias + 1, :] = total[width : width + 1]
            flow.ready(layer, at + width)
            flow.tick(0.45)

        bias_parts = []
        for c in range(0, width, BLOCK):
            size = min(BLOCK, width - c)
            total = product(mixed_t.at[layer], grad_low, slice(c, c + size))
            for k in range(0, size, LANES):
                put_tile(layer, tops[2], (c + k) // LANES, total[:width, k : k + LANES])
                bias_parts.append(total[width : width + 1, k : k + LANES])
        put_vector(dims.at["output_bias"], jnp.concatenate(bias_parts, 1))
        flow.ready(layer, tops[3])
        flow.tick(0.8)

        for cols in halves:
            dm = mm_nt(grad_low[...], output_weight[layer, cols, :]) * inverse_s[layer, :, cols]
            inner_s[:, cols] = -(dm * mixed_s[layer, :, cols].astype(F32)).astype(BF16)
            normed_s[:, cols] = dm.astype(BF16)
        flow.tick(0.8)

        def attend_back(s, _):
            rows = rows_of(s)
            for p in range(pairs):
                at = p * LANES
                query = packed_s[layer, rows, at : at + LANES]
                key = packed_s[layer, rows, width + at : width + at + LANES]
                value = packed_s[layer, rows, 2 * width + at : 2 * width + at + LANES]
                dm, inner = normed_s[rows, at : at + LANES], inner_s[rows, at : at + LANES]
                wide_value = jnp.concatenate([value, jnp.ones_like(value)], 1)
                dq = dk = dv = None
                for h, half in enumerate((low_half, high_half)):
                    power = power_s[layer, s, 2 * p + h]
                    dm_half = dm * half
                    left = jnp.concatenate([dm_half, inner * half], 1)
                    ds = (power.astype(F32) * mm_nt(left, wide_value)).astype(BF16)
                    terms = (mm(ds, key * half), mm_tn(ds, query * half), mm_tn(power, dm_half))
                    dq = terms[0] if dq is None else dq + terms[0]
                    dk = terms[1] if dk is None else dk + terms[1]
                    dv = terms[2] if dv is None else dv + terms[2]
                dup_s[rows, at : at + LANES] = (dq * score_scale).astype(BF16)
                dup_s[rows, width + at : width + at + LANES] = (dk * score_scale).astype(BF16)
                dup_s[rows, 2 * width + at : 2 * width + at + LANES] = dv.astype(BF16)
            flow.ticks(s, n_seq, 1.5)
            return 0

        lax.fori_loop(0, n_seq, attend_back, 0)
        for cols in halves:
            x_s[:, cols] = mm_nt(dup_s[:, 0 : 3 * width], mixer_weight[layer, cols, :])
            flow.tick(0.6)
        acc_s[...] = jnp.zeros_like(acc_s)

        def attend_norm_back(s, _):
            end_back(s, 2 * layer, gain)
            if layer == 1:
                start_back(s)
            flow.ticks(s, n_seq, 0.4)
            return 0

        lax.fori_loop(0, n_seq, attend_norm_back, 0)
        put_vector(dims.at["attend_gain"], jnp.sum(acc_s[0], 0, keepdims=True))
        put_vector(dims.at["attend_shift"], jnp.sum(acc_s[1], 0, keepdims=True))

        bias_parts = []
        for c in range(0, 3 * width, BLOCK):
            size = min(BLOCK, 3 * width - c)
            total = product(norm_t.at[2 * layer], dup_s, slice(c, c + size))
            for k in range(0, size, LANES):
                put_tile(layer, tops[3], (c + k) // LANES, total[:width, k : k + LANES])
                bias_parts.append(total[width : width + 1, k : k + LANES])
            flow.tick(0.5)
        each = width // LANES
        put_vector(
            dims.at["mixer_bias"],
            jnp.concatenate(bias_parts[:each] + bias_parts[2 * each :], 1),
        )
        sums[layer, tops[4] : tops[4] + dims.vec_rows, :] = vec_s[...].astype(BF16)
        rest = dims.rows - tops[4] - dims.vec_rows
        if rest:
            sums[layer, dims.rows - rest :, :] = jnp.zeros((rest, BLOCK), BF16)
        flow.ready(layer, dims.rows)

    for s in range(n_global):
        crop_s[:, s, :] = grad_s[s * seq : s * seq + glen, :]
    global_back[...] = crop_s[...].astype(BF16)
    for j in range(n_local):
        at = local_at(j)
        local_back[j] = grad_s[at : at + llen, :].astype(BF16)
    flow.drain()


class Wire:
    def __init__(self, size, first, second):
        self.size, self.first, self.second = size, first, second


def wires_of(mesh):
    names = mesh.axis_names
    places = {}
    for axis, name in enumerate(names):
        line = [mesh.devices[tuple(i if a == axis else 0 for a in range(2))] for i in range(mesh.devices.shape[axis])]
        spots = [(d.core_on_chip,) + tuple(d.coords) for d in line]
        found, total = [], 1
        for k in range(4):
            values = sorted({p[k] for p in spots})
            if len(values) > 1:
                stride = next(i for i, p in enumerate(spots) if p[k] != spots[0][k])
                found.append((k, axis, stride, len(values)))
                total *= len(values)
        good = total == len(line)
        for k, _, stride, size in found:
            values = [p[k] for p in spots]
            good = good and all(v == values[i // stride % size * stride] for i, v in enumerate(values))
        if not good:
            found = [(4 + axis, axis, 1, len(line))]
        for k, axis, stride, size in found:
            places[k] = (axis, stride, size)
    wires = []
    if 0 in places:
        wires.append(Wire(places[0][2], places[0], places[0]))
    if 0 in places and 1 in places and 2 in places and places[1][2] == places[2][2]:
        wires.append(Wire(places[1][2], places[1], places[2]))
        wires.append(Wire(places[1][2], places[2], places[1]))
        order = [3, 4, 5]
    else:
        order = [1, 2, 3, 4, 5]
    for k in order:
        if k in places:
            wires.append(Wire(places[k][2], places[k], places[k]))
    return wires


class Net:
    def __init__(self, wires):
        self.axes = ("dp", "section")
        self.here = [lax.axis_index(a) for a in self.axes]
        self.wires = wires
        first = wires[0]
        odd = self.spot(first.first) % 2 if first.size == 2 else 0
        self.odd = odd
        self.at = []
        for w in wires:
            a, b = self.spot(w.first), self.spot(w.second)
            self.at.append(a if w.first == w.second else a + odd * (b - a))

    def spot(self, place):
        axis, stride, size = place
        return self.here[axis] // stride % size

    def peer(self, stage, k):
        w = self.wires[stage]
        place = (self.at[stage] + k) % w.size
        move = place - self.at[stage]
        target = list(self.here)
        if w.first == w.second:
            target[w.first[0]] = target[w.first[0]] + move * w.first[1]
        else:
            target[w.first[0]] = target[w.first[0]] + move * w.first[1] * (1 - self.odd)
            target[w.second[0]] = target[w.second[0]] + move * w.second[1] * self.odd
        return tuple(target), place

    def greet(self):
        barrier = pltpu.get_barrier_semaphore()
        for stage, w in enumerate(self.wires):
            for k in range(1, w.size):
                pl.semaphore_signal(barrier, inc=1, device_id=self.peer(stage, k)[0], device_id_type=pl.DeviceIdType.MESH)

    def wait_greeting(self):
        pl.semaphore_wait(pltpu.get_barrier_semaphore(), sum(w.size - 1 for w in self.wires))


class Chunk:
    def __init__(self, net, sums, out, landing, sems, turn, layer, end):
        self.net, self.sums, self.out, self.landing = net, sums, out, landing
        self.send, self.recv, self.local, self.sent, self.free = sems
        self.turn = turn
        self.layer, self.end = layer, end
        self.due = None
        size, start = sums.shape[0], 0
        self.unit = size
        for w in net.wires:
            self.unit //= w.size
        self.size, self.start = [], []
        for stage, w in enumerate(net.wires):
            size //= w.size
            self.size.append(size)
            self.start.append((start, size))
            start = start + net.at[stage] * size
        self.own = start
        self.stages = len(net.wires)
        self.step = 0
        self.sem_at, at = {}, 0
        for phase in range(2):
            for stage, w in enumerate(net.wires):
                for k in range(1, w.size):
                    self.sem_at[phase, stage, k] = at
                    at += 1

    def rows(self, stage, place):
        start, size = self.start[stage]
        return pl.ds(pl.multiple_of(start + place * size, TILE), size)

    def copy(self, phase, stage, k):
        target, place = self.net.peer(stage, k)
        at = self.sem_at[phase, stage, k]
        if phase == 0:
            source, to = self.sums.at[self.rows(stage, place)], self.landing[stage].at[k - 1]
        else:
            rows = self.rows(stage, self.net.at[stage])
            source = to = self.sums.at[rows]
        return pltpu.make_async_remote_copy(
            src_ref=source,
            dst_ref=to,
            send_sem=self.send.at[at],
            recv_sem=self.recv.at[at],
            device_id=target,
            device_id_type=pl.DeviceIdType.MESH,
        )

    def arrival(self, stage, k):
        target, place = self.net.peer(stage, self.net.wires[stage].size - k)
        at = self.sem_at[1, stage, k]
        landed = self.sums.at[self.rows(stage, place)]
        return pltpu.make_async_remote_copy(
            src_ref=landed,
            dst_ref=landed,
            send_sem=self.send.at[at],
            recv_sem=self.recv.at[at],
            device_id=target,
            device_id_type=pl.DeviceIdType.MESH,
        )

    def start_stage(self, phase, stage):
        if phase == 0 and self.turn == 1:
            pl.semaphore_wait(self.free.at[stage], self.net.wires[stage].size - 1)
        if phase == 1:
            pl.semaphore_wait(self.sent.at[stage], self.net.wires[stage].size - 1)
        for k in range(1, self.net.wires[stage].size):
            self.copy(phase, stage, k).start()

    def load(self):
        last = self.stages - 1
        stage = self.step if self.step <= last else 2 * self.stages - 1 - self.step
        peers = self.net.wires[stage].size - 1
        row = BLOCK * 2
        if stage == 0:
            return 0, self.size[0] * row / 4
        if stage == last:
            return 2, self.size[stage] * (peers + 1) ** 2 / 2 * row
        return 1, self.size[stage] * peers * row

    def begin(self):
        self.start_stage(0, 0)

    def out_copy(self):
        return pltpu.make_async_copy(self.sums, self.out, self.local.at[0])

    def advance(self):
        step = self.step
        self.step += 1
        if step < self.stages:
            peers = range(1, self.net.wires[step].size)
            for k in peers:
                self.copy(0, step, k).wait_recv()
            base = self.start[step][0] + self.net.at[step] * self.size[step]
            landing = self.landing[step]

            def add(i, _):
                at = pl.ds(pl.multiple_of(base + i * self.unit, TILE), self.unit)
                total = self.sums[at, :].astype(F32)
                for k in peers:
                    total = total + landing[k - 1, pl.ds(pl.multiple_of(i * self.unit, TILE), self.unit), :].astype(F32)
                self.sums[at, :] = total.astype(BF16)
                return 0

            lax.fori_loop(0, self.size[step] // self.unit, add, 0)
            for k in peers:
                self.copy(0, step, k).wait_send()
                target = self.net.peer(step, k)[0]
                pl.semaphore_signal(self.sent.at[step], inc=1, device_id=target, device_id_type=pl.DeviceIdType.MESH)
                if self.turn == 0:
                    pl.semaphore_signal(self.free.at[step], inc=1, device_id=target, device_id_type=pl.DeviceIdType.MESH)
            if step + 1 < self.stages:
                self.start_stage(0, step + 1)
            else:
                self.start_stage(1, step)
        else:
            stage = 2 * self.stages - 1 - step
            for k in range(1, self.net.wires[stage].size):
                self.arrival(stage, k).wait_recv()
            if stage > 0:
                self.start_stage(1, stage - 1)
            else:
                self.out_copy().start()

    def finish(self):
        for phase, stage, k in self.sem_at:
            if phase == 1:
                self.copy(phase, stage, k).wait_send()
        self.out_copy().wait()


LATENCY = 2.0
RATE = 80e3
STEP = 0.4


class Flow:
    def __init__(self, net):
        self.chunks, self.now, self.waiting, self.free = [], 0.0, 0, [0.0] * 3

    def book(self, chunk):
        kind, size = chunk.load()
        self.free[kind] = max(self.now, self.free[kind]) + size / RATE
        chunk.due = self.free[kind] + LATENCY

    def ready(self, layer, rows):
        while self.waiting < len(self.chunks):
            chunk = self.chunks[self.waiting]
            if chunk.layer != layer or chunk.end > rows:
                return
            chunk.begin()
            self.book(chunk)
            self.waiting += 1

    def due(self):
        return sorted((c for c in self.chunks if c.due is not None and c.due <= self.now), key=lambda c: c.due)

    def take(self):
        while self.due():
            chunk = self.due()[0]
            chunk.advance()
            self.now += STEP
            if chunk.step < 2 * chunk.stages:
                self.book(chunk)
            else:
                chunk.due = None

    def tick(self, time):
        self.now += time
        self.take()

    def ticks(self, s, count, time):
        for i in range(count):
            self.now += time
            if self.due():
                pl.when(s == i)(self.take)

    def drain(self):
        while any(c.due is not None for c in self.chunks):
            self.now = max(self.now, min(c.due for c in self.chunks if c.due is not None))
            self.take()
        for chunk in self.chunks:
            chunk.finish()


class Dims:
    def __init__(self, global_crops, local_crops, hidden, wires):
        self.wires = wires
        self.glen, self.n_global, self.width = global_crops.shape
        self.n_local, self.llen, _ = local_crops.shape
        self.hidden = hidden
        self.seq = up_to(self.glen, TILE)
        self.group = self.seq // self.llen
        while self.n_local % self.group:
            self.group -= 1
        self.n_seq = self.n_global + self.n_local // self.group
        sizes = (
            ("attend_gain", self.width),
            ("attend_shift", self.width),
            ("mixer_bias", 2 * self.width),
            ("output_bias", self.width),
            ("feed_gain", self.width),
            ("feed_shift", self.width),
            ("expand_bias", hidden),
            ("reduce_bias", self.width),
        )
        self.names, self.sizes = [name for name, _ in sizes], dict(sizes)
        self.at, row = {}, 0
        for name, size in sizes:
            self.at[name] = row
            row += -(-size // BLOCK)
        self.vec_rows = 2 * TILE
        assert row <= self.vec_rows and self.width * hidden % self.vec_rows == 0
        step = TILE
        for w in wires:
            step *= w.size
        ff = self.width * hidden // BLOCK
        square = self.width * self.width // BLOCK
        self.tops = (0, ff, 2 * ff, 2 * ff + square, 2 * ff + 4 * square)
        self.rows = up_to(self.tops[4] + self.vec_rows, step)
        parts = self.rows // step
        cuts = ((0, 4, 7, 10, 12, 14), (0, 4, 10, 14))
        self.bounds = [[c * step for c in sorted({parts * k // 14 for k in layer})] for layer in cuts]
        self.landing_sets = [len(b) - 1 for b in self.bounds[::-1]]
        if self.bounds[0] == self.bounds[1]:
            self.landing_sets = self.landing_sets[:1]
        self.n_chunk = sum(len(b) - 1 for b in self.bounds)


def run_kernel(counts, arrays, dims):
    d = dims
    n, seq, width, hidden = d.n_seq, d.seq, d.width, d.hidden
    crops = [jax.ShapeDtypeStruct(a.shape, BF16) for a in arrays[:2]]
    outs = crops + crops
    outs += [jax.ShapeDtypeStruct((2, d.rows, BLOCK), BF16)]
    scratch = [
        pltpu.VMEM((2, d.rows, BLOCK), BF16),
        pltpu.VMEM((d.glen, d.n_global, width), F32),
        pltpu.VMEM((n * seq, width), F32),
        pltpu.VMEM((4, n * seq, width), BF16),
        pltpu.VMEM((4, n * seq, 1), F32),
        pltpu.VMEM((4, n, width + TILE, seq), BF16),
        pltpu.VMEM((2, n * seq, 3 * width), BF16),
        pltpu.VMEM((2, n, HEADS, seq, seq), BF16),
        pltpu.VMEM((2, n * seq, width), F32),
        pltpu.VMEM((2, n * seq, width), BF16),
        pltpu.VMEM((2, n, width + TILE, seq), BF16),
        pltpu.VMEM((2, n * seq, hidden), BF16),
        pltpu.VMEM((n * seq, hidden), BF16),
        pltpu.VMEM((n * seq, width), F32),
        pltpu.VMEM((n * seq, width), BF16),
        pltpu.VMEM((n, width, seq), BF16),
        pltpu.VMEM((n * seq, hidden), BF16),
        pltpu.VMEM((2, seq, seq), BF16),
        pltpu.VMEM((n * seq, width), BF16),
        pltpu.VMEM((n * seq, width), BF16),
        pltpu.VMEM((d.vec_rows, BLOCK), F32),
        pltpu.VMEM((3, 8, width), F32),
    ]
    for layer in (1, 0)[: len(d.landing_sets)]:
        for first, end in zip(d.bounds[layer], d.bounds[layer][1:]):
            rows = end - first
            for w in d.wires:
                rows //= w.size
                scratch.append(pltpu.VMEM((w.size - 1, rows, BLOCK), BF16))
    peers = 2 * sum(w.size - 1 for w in d.wires)
    scratch += [
        pltpu.SemaphoreType.DMA((d.n_chunk, peers)),
        pltpu.SemaphoreType.DMA((d.n_chunk, peers)),
        pltpu.SemaphoreType.DMA((d.n_chunk, 1)),
        pltpu.SemaphoreType.REGULAR((d.n_chunk, len(d.wires))),
        pltpu.SemaphoreType.REGULAR((d.n_chunk, len(d.wires))),
    ]
    vmem = pl.BlockSpec(memory_space=pltpu.VMEM)
    anywhere = pl.BlockSpec(memory_space=pl.ANY)
    return pl.pallas_call(
        functools.partial(kernel, d),
        out_shape=outs,
        in_specs=[pl.BlockSpec(memory_space=pltpu.SMEM)] + [vmem] * len(arrays),
        out_specs=[vmem] * 4 + [anywhere],
        scratch_shapes=scratch,
        compiler_params=pltpu.CompilerParams(
            vmem_limit_bytes=63 * 1024 * 1024, collective_id=0, has_side_effects=True
        ),
    )(counts, *arrays)


THIRDS = 3


def cast_kernel(dims, reduce, expand, output, mixer, vectors, *rest):
    crops, outs, held, sems = rest[:4], rest[4:-9], rest[-5:-1], rest[-1]
    step = pl.program_id(0) * THIRDS + pl.program_id(1)
    loads = [pltpu.make_async_copy(a, b, sems.at[0, i]) for i, (a, b) in enumerate(zip(crops, held, strict=True))]
    stores = [pltpu.make_async_copy(a, b, sems.at[1, i]) for i, (a, b) in enumerate(zip(held, rest[-9:-5], strict=True))]

    @pl.when(step == 0)
    def _():
        for copy in loads:
            copy.start()

    @pl.when(step == 1)
    def _():
        for load, store in zip(loads, stores, strict=True):
            load.wait()
            store.start()

    mixer_grad, output_grad, expand_grad, reduce_grad = outs[:4]
    width = dims.width
    fold = width // 2
    for b in range(2):
        rows = slice(b * width, (b + 1) * width)
        cols = slice(b * BLOCK, (b + 1) * BLOCK)
        expand_grad[0, :, cols] = expand[0, rows, :].astype(F32)
        reduce_grad[0, cols, :] = reduce[0, rows, :].T.astype(F32)
    for source, target in ((mixer, mixer_grad), (output, output_grad)):
        target[0, :, 0:BLOCK] = source[0, 0:width, :].astype(F32)
        target[0, 0:fold, BLOCK:] = source[0, width:, 0:LANES].astype(F32)
        target[0, fold:, BLOCK:] = source[0, width:, LANES:].astype(F32)

    @pl.when(step == 2 * THIRDS - 1)
    def _():
        for ref, name in zip(outs[4:], dims.names, strict=True):
            size = ref.shape[1]
            for c in range(0, size, BLOCK):
                at = dims.at[name] + c // BLOCK
                piece = min(BLOCK, size - c)
                for layer in range(2):
                    ref[layer : layer + 1, c : c + piece] = vectors[layer].astype(F32)[at : at + 1, 0:piece]
        for store in stores:
            store.wait()


def run_cast(sums, crops, dims):
    d = dims
    width, hidden = d.width, d.hidden
    part = (1, 2 * width, BLOCK)
    square = (1, width * width // BLOCK, BLOCK)
    grads = [(width, 3 * width), (width, width), (width, hidden), (hidden, width)]
    shapes = [jax.ShapeDtypeStruct((2,) + g, F32) for g in grads]
    specs = [
        pl.BlockSpec((1, width, 3 * width // THIRDS), lambda l, t: (l, 0, t)),
        pl.BlockSpec((1, width, width), lambda l, t: (l, 0, 0)),
        pl.BlockSpec((1, width, hidden // THIRDS), lambda l, t: (l, 0, t)),
        pl.BlockSpec((1, hidden // THIRDS, width), lambda l, t: (l, t, 0)),
    ]
    for name in d.names:
        shapes.append(jax.ShapeDtypeStruct((2, d.sizes[name]), F32))
        specs.append(pl.BlockSpec((2, d.sizes[name]), lambda l, t: (0, 0)))
    for crop in crops:
        shapes.append(jax.ShapeDtypeStruct(crop.shape, crop.dtype))
        specs.append(pl.BlockSpec(memory_space=pl.ANY))
    return pl.pallas_call(
        functools.partial(cast_kernel, d),
        grid=(2, THIRDS),
        out_shape=shapes,
        in_specs=[
            pl.BlockSpec(part, lambda l, t: (l, t, 0)),
            pl.BlockSpec(part, lambda l, t: (l, THIRDS + t, 0)),
            pl.BlockSpec(square, lambda l, t: (l, d.tops[2] // square[1], 0)),
            pl.BlockSpec(square, lambda l, t: (l, d.tops[3] // square[1] + t, 0)),
            pl.BlockSpec((2, d.vec_rows, BLOCK), lambda l, t: (0, d.tops[4] // d.vec_rows, 0)),
        ]
        + [pl.BlockSpec(memory_space=pl.ANY)] * 4,
        out_specs=specs,
        scratch_shapes=[pltpu.VMEM(c.shape, c.dtype) for c in crops] + [pltpu.SemaphoreType.DMA((2, 4))],
        compiler_params=pltpu.CompilerParams(vmem_limit_bytes=62 * 1024 * 1024),
    )(sums, sums, sums, sums, sums, *crops)


def shards(wires, global_crops, local_crops, local_count, global_cotangent, local_cotangent, *weights):
    global_crops, global_cotangent = global_crops.transpose(1, 0, 2), global_cotangent.transpose(1, 0, 2)
    dims = Dims(global_crops, local_crops, weights[8].shape[2], wires)
    outs = run_kernel(
        local_count, (global_crops, local_crops, global_cotangent, local_cotangent) + weights, dims
    )
    mixer, output, expand, reduce, *rest = run_cast(outs[4], outs[:4], dims)
    vectors, crops = rest[:-4], rest[-4:]
    v = dict(zip(dims.names, vectors, strict=True))
    return (
        crops[0].transpose(1, 0, 2),
        crops[1],
        crops[2].transpose(1, 0, 2),
        crops[3],
        v["attend_gain"],
        v["attend_shift"],
        mixer,
        v["mixer_bias"],
        output,
        v["output_bias"],
        v["feed_gain"],
        v["feed_shift"],
        expand,
        v["expand_bias"],
        reduce,
        v["reduce_bias"],
    )


def solution(mesh):
    crops = P(("dp", "section"), None, None)
    return jax.shard_map(
        functools.partial(shards, wires_of(mesh)),
        mesh=mesh,
        in_specs=(crops, crops, P("dp"), crops, crops) + (P(),) * 12,
        out_specs=(crops,) * 4 + (P(),) * 12,
        check_vma=False,
    )
```

```python
import functools

import jax
import jax.numpy as jnp
from jax import lax
from jax.experimental import pallas as pl
from jax.experimental.pallas import tpu as pltpu
from jax.sharding import PartitionSpec as P

HEADS = 6
HEAD = 64
EPS = 1e-06
TILE = 16
LANES = 128
BLOCK = 256
LOG2E = 1.4426950408889634
F32 = jnp.float32
BF16 = jnp.bfloat16


def up_to(value, step):
    return -(-value // step) * step


def mm(left, right):
    return lax.dot_general(left, right, (((1,), (0,)), ((), ())), preferred_element_type=F32)


def mm_nt(left, right):
    return lax.dot_general(left, right, (((1,), (1,)), ((), ())), preferred_element_type=F32)


def mm_tn(left, right):
    return lax.dot_general(left, right, (((0,), (0,)), ((), ())), preferred_element_type=F32)


def norm(rows):
    centred = rows - jnp.mean(rows, -1, keepdims=True)
    scale = lax.rsqrt(jnp.mean(centred * centred, -1, keepdims=True) + EPS)
    return centred * scale, scale


def norm_back(grad, unit, scale, gain):
    slope = grad * gain
    first = jnp.mean(slope, -1, keepdims=True)
    second = jnp.mean(slope * unit, -1, keepdims=True)
    return scale * (slope - first - unit * second)


def gelu_parts(u):
    size = jnp.abs(u)
    d = 1.0 + (0.3275911 * 0.7071067811865476) * size
    t = pl.reciprocal(d, approx=True)
    t = t * (2.0 - d * t)
    poly = 0.5 * 1.061405429
    for a in (-1.453152027, 1.421413741, -0.284496736, 0.254829592):
        poly = poly * t + 0.5 * a
    bell = jnp.exp2((u * u) * (-0.5 * LOG2E))
    tail = poly * t * bell
    phi = jnp.where(u < 0.0, tail, 1.0 - tail)
    return u * phi, phi + (u * bell) * 0.3989422804014327


def fold8(value):
    rows, width = value.shape
    return jnp.sum(value.reshape(rows // 8, 8, width), 0)


def kernel(
    dims,
    counts,
    global_in_hbm,
    local_in_hbm,
    global_cot_hbm,
    local_cot_hbm,
    attend_gain,
    attend_shift,
    mixer_hbm,
    mixer_bias,
    output_hbm,
    output_bias,
    feed_gain,
    feed_shift,
    expand_hbm,
    expand_bias,
    reduce_hbm,
    reduce_bias,
    global_out_hbm,
    local_out_hbm,
    global_back_hbm,
    local_back_hbm,
    sums_out,
    global_in,
    local_in,
    global_cot,
    local_cot,
    global_out,
    local_out,
    global_back,
    local_back,
    mixer_weight,
    output_weight,
    expand_weight,
    reduce_weight,
    io_sem,
    sums,
    crop_s,
    x_s,
    unit_s,
    scale_s,
    norm_t,
    packed_s,
    power_s,
    inverse_s,
    mixed_s,
    mixed_t,
    act_s,
    slope_s,
    grad_s,
    grad_low,
    grad_t,
    dup_s,
    mask_s,
    vec_s,
    acc_s,
    *wires,
):
    seq, group, width = dims.seq, dims.group, dims.width
    glen, llen = dims.glen, dims.llen
    n_global, n_local, n_seq = dims.n_global, dims.n_local, dims.n_seq
    hidden = dims.hidden
    count = counts[lax.axis_index("section")]
    pairs = HEADS // 2
    lane = lax.broadcasted_iota(jnp.int32, (1, LANES), 1)
    low_half = (lane < HEAD).astype(F32).astype(BF16)
    high_half = (lane >= HEAD).astype(F32).astype(BF16)
    score_scale = HEAD ** (-0.5)

    moves = [pltpu.make_async_copy(global_in_hbm, global_in, io_sem.at[0]), pltpu.make_async_copy(local_in_hbm, local_in, io_sem.at[1])]
    weights = ((mixer_hbm, mixer_weight), (output_hbm, output_weight), (expand_hbm, expand_weight), (reduce_hbm, reduce_weight))
    for layer in range(2):
        for source, target in weights:
            moves.append(pltpu.make_async_copy(source.at[layer], target.at[layer], io_sem.at[len(moves)]))
    moves += [
        pltpu.make_async_copy(global_cot_hbm, global_cot, io_sem.at[10]),
        pltpu.make_async_copy(local_cot_hbm, local_cot, io_sem.at[11]),
    ]
    outward = [
        pltpu.make_async_copy(global_out, global_out_hbm, io_sem.at[12]),
        pltpu.make_async_copy(local_out, local_out_hbm, io_sem.at[13]),
        pltpu.make_async_copy(global_back, global_back_hbm, io_sem.at[14]),
        pltpu.make_async_copy(local_back, local_back_hbm, io_sem.at[15]),
    ]
    for move in moves:
        move.start()

    net = Net(dims.wires)
    net.greet()
    n_stage = len(dims.wires)
    sets = dims.landing_sets
    landings, sems = wires[: n_stage * sum(sets)], wires[n_stage * sum(sets) :]
    flow = Flow(net)
    number = 0
    for layer in (1, 0):
        bounds = dims.bounds[layer]
        for i in range(len(bounds) - 1):
            shared = len(sets) == 1
            at = (i if shared else number) * n_stage
            own = [w.at[number] for w in sems[:4]] + [sems[4].at[i]]
            rows = pl.ds(bounds[i], bounds[i + 1] - bounds[i])
            turn = (1 - layer) if shared else None
            flow.chunks.append(
                Chunk(net, sums.at[layer, rows], sums_out.at[layer, rows], landings[at : at + n_stage], own, turn, layer, bounds[i + 1])
            )
            number += 1

    for s in range(n_seq):
        x_s[s, seq - 32 :, :] = jnp.zeros((32, width), F32)
        grad_s[s, seq - 32 :, :] = jnp.zeros((32, width), F32)
    row_id = lax.broadcasted_iota(jnp.int32, (seq, seq), 0)
    col_id = lax.broadcasted_iota(jnp.int32, (seq, seq), 1)
    row_crop = sum((row_id >= llen * j).astype(jnp.int32) for j in range(1, group + 1))
    col_crop = sum((col_id >= llen * j).astype(jnp.int32) for j in range(1, group + 1))
    far = jnp.float32(-1e30)
    mask_s[0] = jnp.where(col_id < glen, jnp.float32(0), far).astype(BF16)
    mask_s[1] = jnp.where(row_crop == col_crop, jnp.float32(0), far).astype(BF16)
    one_row = (lax.broadcasted_iota(jnp.int32, (TILE, seq), 0) == 0).astype(F32).astype(BF16)
    for s in range(n_seq):
        for i in range(4):
            norm_t[i, s, width:, :] = one_row
        for i in range(2):
            mixed_t[i, s, width:, :] = one_row

    def live_rows(g):
        rows = lax.broadcasted_iota(jnp.int32, (seq, 1), 0)
        return (rows < llen * jnp.clip(count - g * group, 0, group)).astype(F32)

    def take_crops(crops, locals_, target):
        crop_s[...] = crops[...].astype(F32)
        for s in range(n_global):
            target[s, 0:glen, :] = crop_s[:, s, :]
        for j in range(n_local):
            s, at = n_global + j // group, llen * (j % group)
            target[s, at : at + llen, :] = locals_[j].astype(F32)

    def take_cotangents():
        moves[10].wait()
        moves[11].wait()
        take_crops(global_cot, local_cot, grad_s)
        for s in range(n_global, n_seq):
            grad_s[s] = grad_s[s] * live_rows(s - n_global)

    moves[0].wait()
    moves[1].wait()
    take_crops(global_in, local_in, x_s)

    def row(ref, layer):
        return ref[...].astype(F32)[layer : layer + 1]

    slopes = (slope_s, dup_s)

    def start_back(s, grad):
        grad_t[s] = grad.astype(BF16).T
        acc_s[2] = acc_s[2] + fold8(grad)

    def end_back(s, grad, unit, scale, gain, dh):
        unit = unit.astype(F32)
        acc_s[0] = acc_s[0] + fold8(dh * unit)
        acc_s[1] = acc_s[1] + fold8(dh)
        grad = (grad + norm_back(dh, unit, scale, gain)).astype(BF16)
        grad_low[s] = grad
        grad_s[s] = grad.astype(F32)

    def product(left, right, cols):
        total = mm(left[0], right[0, :, cols])
        for s in range(1, n_seq):
            total = total + mm(left[s], right[s, :, cols])
        return total

    for layer in range(2):
        gain, shift = row(attend_gain, layer), row(attend_shift, layer)
        bias = row(mixer_bias, layer)
        bias = jnp.concatenate([bias[:, :width], jnp.zeros((1, width), F32), bias[:, width:]], 1)
        out_bias = row(output_bias, layer)
        gain2, shift2 = row(feed_gain, layer), row(feed_shift, layer)
        bias_up, bias_down = row(expand_bias, layer), row(reduce_bias, layer)

        def attend(s, _):
            x = x_s[s]
            unit, scale = norm(x)
            unit_s[2 * layer, s] = unit.astype(BF16)
            scale_s[2 * layer, s] = scale
            normed = (unit * gain + shift).astype(BF16)
            norm_t[2 * layer, s, 0:width, :] = normed.T
            packed = (mm(normed, mixer_weight[layer]) + bias).astype(BF16)
            packed_s[layer, s] = packed
            mask = mask_s[jnp.where(s < n_global, 0, 1)].astype(F32)
            mixed = []
            for p in range(pairs):
                at = p * LANES
                query = packed[:, at : at + LANES]
                key = packed[:, width + at : width + at + LANES]
                value = packed[:, 2 * width + at : 2 * width + at + LANES]
                total = None
                for h, half in enumerate((low_half, high_half)):
                    scores = mm_nt(query * half, key) * (score_scale * LOG2E) + mask
                    power = jnp.exp2(scores - jnp.max(scores, -1, keepdims=True)).astype(BF16)
                    power_s[layer, s, 2 * p + h] = power
                    spread = jnp.broadcast_to(half, (seq, LANES))
                    term = mm(power, jnp.concatenate([value * half, spread], 1))
                    total = term if total is None else total + term
                inverse = 1.0 / total[:, LANES:]
                inverse_s[layer, s, :, at : at + LANES] = inverse
                mixed.append((total[:, :LANES] * inverse).astype(BF16))
            mixed = jnp.concatenate(mixed, 1)
            mixed_s[layer, s] = mixed
            mixed_t[layer, s, 0:width, :] = mixed.T
            x = x + mm(mixed, output_weight[layer]) + out_bias
            x_s[s] = x.astype(BF16).astype(F32)
            return 0

        moves[2 + 4 * layer].wait()
        moves[3 + 4 * layer].wait()
        lax.fori_loop(0, n_seq, attend, 0)

        def feed(s, _):
            x = x_s[s]
            unit, scale = norm(x)
            normed = (unit * gain2 + shift2).astype(BF16)
            norm_t[2 * layer + 1, s, 0:width, :] = normed.T
            unit_s[2 * layer + 1, s] = unit.astype(BF16)
            scale_s[2 * layer + 1, s] = scale
            if layer == 1:
                start_back(s, grad_s[s])
            for c in range(hidden // BLOCK):
                cols = slice(c * BLOCK, (c + 1) * BLOCK)
                up = mm(normed, expand_weight[layer, :, cols]) + bias_up[:, cols]
                act, slope = gelu_parts(up)
                act_s[layer, s, :, cols] = act.astype(BF16)
                slopes[layer][s, :, cols] = slope.astype(BF16)
            x = x + mm(act_s[layer, s], reduce_weight[layer]) + bias_down
            x_s[s] = x.astype(BF16).astype(F32)
            return 0

        moves[4 + 4 * layer].wait()
        moves[5 + 4 * layer].wait()
        if layer == 1:
            take_cotangents()
            acc_s[...] = jnp.zeros_like(acc_s)
        lax.fori_loop(0, n_seq, feed, 0)

    for s in range(n_global):
        crop_s[:, s, :] = x_s[s, 0:glen, :]
    global_out[...] = crop_s[...].astype(BF16)
    for j in range(n_local):
        s, at = n_global + j // group, llen * (j % group)
        alive = (count > j).astype(F32)
        local_out[j] = (x_s[s, at : at + llen, :] * alive).astype(BF16)
    outward[0].start()
    outward[1].start()

    def put_vector(at, value):
        for c in range(0, value.shape[1], BLOCK):
            piece = value[:, c : c + BLOCK]
            vec_s[at + c // BLOCK : at + c // BLOCK + 1, 0 : piece.shape[1]] = piece

    def put_tile(layer, top, m, part):
        at = top + (m // 3) * (width + fold)
        side = m % 3 * LANES
        part = part.astype(BF16)
        if m % 3 < 2:
            sums[layer, at : at + width, side : side + LANES] = part
        else:
            at = at + width
            sums[layer, at : at + fold, 0:LANES] = part[:fold]
            sums[layer, at : at + fold, LANES:] = part[fold:]

    blocks = hidden // BLOCK
    fold = width // 2
    tops = dims.tops
    net.wait_greeting()
    for layer, used in ((1, tops[4]), (0, tops[4] + 2 * dims.vec_rows)):
        if dims.rows > used:
            sums[layer, used:, :] = jnp.zeros((dims.rows - used, BLOCK), BF16)
    for layer in (1, 0):
        vec_s[...] = jnp.zeros_like(vec_s)
        gain2, gain = row(feed_gain, layer), row(attend_gain, layer)
        put_vector(dims.at["reduce_bias"], jnp.sum(acc_s[2], 0, keepdims=True))

        for c in range(blocks):
            total = product(grad_t, act_s.at[layer], slice(c * BLOCK, (c + 1) * BLOCK))
            at = tops[0] + c * width
            sums[layer, at : at + width, :] = total.astype(BF16)
            flow.ready(layer, at + width)
            flow.tick(0.45)

        def feed_back(s, _):
            grad_in = grad_s[s].astype(BF16)
            for c in range(blocks):
                cols = slice(c * BLOCK, (c + 1) * BLOCK)
                dact = mm_nt(grad_in, reduce_weight[layer, cols, :])
                dup_s[s, :, cols] = (dact * slopes[layer][s, :, cols].astype(F32)).astype(BF16)
            flow.ticks(s, n_seq, 0.6)
            return 0

        lax.fori_loop(0, n_seq, feed_back, 0)

        for c in range(blocks):
            total = product(norm_t.at[2 * layer + 1], dup_s, slice(c * BLOCK, (c + 1) * BLOCK))
            at = tops[1] + c * width
            sums[layer, at : at + width, :] = total[:width].astype(BF16)
            at_bias = dims.at["expand_bias"] + c
            vec_s[at_bias : at_bias + 1, :] = total[width : width + 1]
            flow.ready(layer, at + width)
            flow.tick(0.45)

        def feed_norm_back(s, _):
            dh = mm_nt(dup_s[s], expand_weight[layer])
            end_back(s, grad_s[s], unit_s[2 * layer + 1, s], scale_s[2 * layer + 1, s], gain2, dh)
            flow.ticks(s, n_seq, 0.7)
            return 0

        acc_s[0:2] = jnp.zeros((2, 8, width), F32)
        lax.fori_loop(0, n_seq, feed_norm_back, 0)
        put_vector(dims.at["feed_gain"], jnp.sum(acc_s[0], 0, keepdims=True))
        put_vector(dims.at["feed_shift"], jnp.sum(acc_s[1], 0, keepdims=True))

        bias_parts = []
        for c in range(0, width, BLOCK):
            size = min(BLOCK, width - c)
            total = product(mixed_t.at[layer], grad_low, slice(c, c + size))
            for k in range(0, size, LANES):
                put_tile(layer, tops[2], (c + k) // LANES, total[:width, k : k + LANES])
                bias_parts.append(total[width : width + 1, k : k + LANES])
        put_vector(dims.at["output_bias"], jnp.concatenate(bias_parts, 1))
        flow.ready(layer, tops[3])
        flow.tick(0.8)

        def attend_back(s, _):
            dmixed = mm_nt(grad_low[s], output_weight[layer])
            parts = [None] * (3 * pairs)
            for p in range(pairs):
                at = p * LANES
                query = packed_s[layer, s, :, at : at + LANES]
                key = packed_s[layer, s, :, width + at : width + at + LANES]
                value = packed_s[layer, s, :, 2 * width + at : 2 * width + at + LANES]
                dm = dmixed[:, at : at + LANES] * inverse_s[layer, s, :, at : at + LANES]
                inner = -(dm * mixed_s[layer, s, :, at : at + LANES].astype(F32)).astype(BF16)
                dm = dm.astype(BF16)
                wide_value = jnp.concatenate([value, jnp.ones_like(value)], 1)
                dq = dk = dv = None
                for h, half in enumerate((low_half, high_half)):
                    power = power_s[layer, s, 2 * p + h]
                    dm_half = dm * half
                    left = jnp.concatenate([dm_half, inner * half], 1)
                    ds = (power.astype(F32) * mm_nt(left, wide_value)).astype(BF16)
                    terms = (mm(ds, key * half), mm_tn(ds, query * half), mm_tn(power, dm_half))
                    dq = terms[0] if dq is None else dq + terms[0]
                    dk = terms[1] if dk is None else dk + terms[1]
                    dv = terms[2] if dv is None else dv + terms[2]
                parts[p] = (dq * score_scale).astype(BF16)
                parts[pairs + p] = (dk * score_scale).astype(BF16)
                parts[2 * pairs + p] = dv.astype(BF16)
            dup_s[s, :, 0 : 3 * width] = jnp.concatenate(parts, 1)
            flow.ticks(s, n_seq, 1.7)
            return 0

        lax.fori_loop(0, n_seq, attend_back, 0)

        bias_parts = []
        for c in range(0, 3 * width, BLOCK):
            size = min(BLOCK, 3 * width - c)
            total = product(norm_t.at[2 * layer], dup_s, slice(c, c + size))
            for k in range(0, size, LANES):
                put_tile(layer, tops[3], (c + k) // LANES, total[:width, k : k + LANES])
                bias_parts.append(total[width : width + 1, k : k + LANES])
            flow.tick(0.5)
        each = width // LANES
        put_vector(
            dims.at["mixer_bias"],
            jnp.concatenate(bias_parts[:each] + bias_parts[2 * each :], 1),
        )
        flow.ready(layer, dims.rows if layer == 1 else tops[4])

        def attend_norm_back(s, _):
            dh = mm_nt(dup_s[s, :, 0 : 3 * width], mixer_weight[layer])
            end_back(s, grad_s[s], unit_s[2 * layer, s], scale_s[2 * layer, s], gain, dh)
            if layer == 1:
                start_back(s, grad_s[s])
            flow.ticks(s, n_seq, 0.6)
            return 0

        acc_s[...] = jnp.zeros_like(acc_s)
        lax.fori_loop(0, n_seq, attend_norm_back, 0)
        put_vector(dims.at["attend_gain"], jnp.sum(acc_s[0], 0, keepdims=True))
        put_vector(dims.at["attend_shift"], jnp.sum(acc_s[1], 0, keepdims=True))
        at = tops[4] + layer * dims.vec_rows
        sums[0, at : at + dims.vec_rows, :] = vec_s[...].astype(BF16)
        if layer == 0:
            flow.ready(0, dims.rows)

    for s in range(n_global):
        crop_s[:, s, :] = grad_s[s, 0:glen, :]
    global_back[...] = crop_s[...].astype(BF16)
    for j in range(n_local):
        s, at = n_global + j // group, llen * (j % group)
        local_back[j] = grad_s[s, at : at + llen, :].astype(BF16)
    outward[2].start()
    outward[3].start()
    flow.drain()
    for move in outward:
        move.wait()


class Wire:
    def __init__(self, size, first, second):
        self.size, self.first, self.second = size, first, second


def wires_of(mesh):
    names = mesh.axis_names
    places = {}
    for axis, name in enumerate(names):
        line = [mesh.devices[tuple(i if a == axis else 0 for a in range(2))] for i in range(mesh.devices.shape[axis])]
        spots = [(d.core_on_chip,) + tuple(d.coords) for d in line]
        found, total = [], 1
        for k in range(4):
            values = sorted({p[k] for p in spots})
            if len(values) > 1:
                stride = next(i for i, p in enumerate(spots) if p[k] != spots[0][k])
                found.append((k, axis, stride, len(values)))
                total *= len(values)
        good = total == len(line)
        for k, _, stride, size in found:
            values = [p[k] for p in spots]
            good = good and all(v == values[i // stride % size * stride] for i, v in enumerate(values))
        if not good:
            found = [(4 + axis, axis, 1, len(line))]
        for k, axis, stride, size in found:
            places[k] = (axis, stride, size)
    wires = []
    if 0 in places:
        wires.append(Wire(places[0][2], places[0], places[0]))
    if 0 in places and 1 in places and 2 in places and places[1][2] == places[2][2]:
        wires.append(Wire(places[1][2], places[1], places[2]))
        wires.append(Wire(places[1][2], places[2], places[1]))
        order = [3, 4, 5]
    else:
        order = [1, 2, 3, 4, 5]
    for k in order:
        if k in places:
            wires.append(Wire(places[k][2], places[k], places[k]))
    return wires


class Net:
    def __init__(self, wires):
        self.axes = ("dp", "section")
        self.here = [lax.axis_index(a) for a in self.axes]
        self.wires = wires
        first = wires[0]
        odd = self.spot(first.first) % 2 if first.size == 2 else 0
        self.odd = odd
        self.at = []
        for w in wires:
            a, b = self.spot(w.first), self.spot(w.second)
            self.at.append(a if w.first == w.second else a + odd * (b - a))

    def spot(self, place):
        axis, stride, size = place
        return self.here[axis] // stride % size

    def peer(self, stage, k):
        w = self.wires[stage]
        place = (self.at[stage] + k) % w.size
        move = place - self.at[stage]
        target = list(self.here)
        if w.first == w.second:
            target[w.first[0]] = target[w.first[0]] + move * w.first[1]
        else:
            target[w.first[0]] = target[w.first[0]] + move * w.first[1] * (1 - self.odd)
            target[w.second[0]] = target[w.second[0]] + move * w.second[1] * self.odd
        return tuple(target), place

    def greet(self):
        barrier = pltpu.get_barrier_semaphore()
        for stage, w in enumerate(self.wires):
            for k in range(1, w.size):
                pl.semaphore_signal(barrier, inc=1, device_id=self.peer(stage, k)[0], device_id_type=pl.DeviceIdType.MESH)

    def wait_greeting(self):
        pl.semaphore_wait(pltpu.get_barrier_semaphore(), sum(w.size - 1 for w in self.wires))


class Chunk:
    def __init__(self, net, sums, out, landing, sems, turn, layer, end):
        self.net, self.sums, self.out, self.landing = net, sums, out, landing
        self.send, self.recv, self.local, self.sent, self.free = sems
        self.turn = turn
        self.layer, self.end = layer, end
        self.due = None
        size, start = sums.shape[0], 0
        self.unit = size
        for w in net.wires:
            self.unit //= w.size
        self.size, self.start = [], []
        for stage, w in enumerate(net.wires):
            size //= w.size
            self.size.append(size)
            self.start.append((start, size))
            start = start + net.at[stage] * size
        self.own = start
        self.stages = len(net.wires)
        self.step = 0
        self.sem_at, at = {}, 0
        for phase in range(2):
            for stage, w in enumerate(net.wires):
                for k in range(1, w.size):
                    self.sem_at[phase, stage, k] = at
                    at += 1

    def rows(self, stage, place):
        start, size = self.start[stage]
        return pl.ds(pl.multiple_of(start + place * size, TILE), size)

    def copy(self, phase, stage, k):
        target, place = self.net.peer(stage, k)
        at = self.sem_at[phase, stage, k]
        if phase == 0:
            source, to = self.sums.at[self.rows(stage, place)], self.landing[stage].at[k - 1]
        else:
            rows = self.rows(stage, self.net.at[stage])
            source = to = self.sums.at[rows]
        return pltpu.make_async_remote_copy(
            src_ref=source,
            dst_ref=to,
            send_sem=self.send.at[at],
            recv_sem=self.recv.at[at],
            device_id=target,
            device_id_type=pl.DeviceIdType.MESH,
        )

    def arrival(self, stage, k):
        target, place = self.net.peer(stage, self.net.wires[stage].size - k)
        at = self.sem_at[1, stage, k]
        landed = self.sums.at[self.rows(stage, place)]
        return pltpu.make_async_remote_copy(
            src_ref=landed,
            dst_ref=landed,
            send_sem=self.send.at[at],
            recv_sem=self.recv.at[at],
            device_id=target,
            device_id_type=pl.DeviceIdType.MESH,
        )

    def start_stage(self, phase, stage):
        if phase == 0 and self.turn == 1:
            pl.semaphore_wait(self.free.at[stage], self.net.wires[stage].size - 1)
        if phase == 1:
            pl.semaphore_wait(self.sent.at[stage], self.net.wires[stage].size - 1)
        for k in range(1, self.net.wires[stage].size):
            self.copy(phase, stage, k).start()

    def load(self):
        last = self.stages - 1
        stage = self.step if self.step <= last else 2 * self.stages - 1 - self.step
        peers = self.net.wires[stage].size - 1
        row = BLOCK * 2
        if stage == 0:
            return 0, self.size[0] * row / 4
        if stage == last:
            return 2, self.size[stage] * (peers + 1) ** 2 / 2 * row
        return 1, self.size[stage] * peers * row

    def begin(self):
        self.start_stage(0, 0)

    def out_copy(self):
        return pltpu.make_async_copy(self.sums, self.out, self.local.at[0])

    def advance(self):
        step = self.step
        self.step += 1
        if step < self.stages:
            peers = range(1, self.net.wires[step].size)
            for k in peers:
                self.copy(0, step, k).wait_recv()
            base = self.start[step][0] + self.net.at[step] * self.size[step]
            landing = self.landing[step]

            count = self.size[step] // self.unit
            while count % 2 == 0 and self.size[step] // count < 128:
                count //= 2
            size = self.size[step] // count

            def add(i, _):
                at = pl.ds(pl.multiple_of(base + i * size, TILE), size)
                here = [landing[k - 1, pl.ds(pl.multiple_of(i * size, TILE), size), :] for k in peers]
                if len(here) == 1:
                    self.sums[at, :] = self.sums[at, :] + here[0]
                else:
                    total = self.sums[at, :].astype(F32)
                    for part in here:
                        total = total + part.astype(F32)
                    self.sums[at, :] = total.astype(BF16)
                return 0

            lax.fori_loop(0, count, add, 0)
            for k in peers:
                self.copy(0, step, k).wait_send()
                target = self.net.peer(step, k)[0]
                pl.semaphore_signal(self.sent.at[step], inc=1, device_id=target, device_id_type=pl.DeviceIdType.MESH)
                if self.turn == 0:
                    pl.semaphore_signal(self.free.at[step], inc=1, device_id=target, device_id_type=pl.DeviceIdType.MESH)
            if step + 1 < self.stages:
                self.start_stage(0, step + 1)
            else:
                self.start_stage(1, step)
        else:
            stage = 2 * self.stages - 1 - step
            for k in range(1, self.net.wires[stage].size):
                self.arrival(stage, k).wait_recv()
            if stage > 0:
                self.start_stage(1, stage - 1)
            else:
                self.out_copy().start()

    def finish(self):
        for phase, stage, k in self.sem_at:
            if phase == 1:
                self.copy(phase, stage, k).wait_send()
        self.out_copy().wait()


LATENCY = 2.0
RATE = 80e3
STEP = 0.4


class Flow:
    def __init__(self, net):
        self.chunks, self.now, self.waiting, self.free = [], 0.0, 0, [0.0] * 3

    def book(self, chunk):
        kind, size = chunk.load()
        self.free[kind] = max(self.now, self.free[kind]) + size / RATE
        chunk.due = self.free[kind] + LATENCY

    def ready(self, layer, rows):
        while self.waiting < len(self.chunks):
            chunk = self.chunks[self.waiting]
            if chunk.layer != layer or chunk.end > rows:
                return
            chunk.begin()
            self.book(chunk)
            self.waiting += 1

    def due(self):
        return sorted((c for c in self.chunks if c.due is not None and c.due <= self.now), key=lambda c: c.due)

    def take(self):
        while self.due():
            chunk = self.due()[0]
            chunk.advance()
            self.now += STEP
            if chunk.step < 2 * chunk.stages:
                self.book(chunk)
            else:
                chunk.due = None

    def tick(self, time):
        self.now += time
        self.take()

    def ticks(self, s, count, time):
        for i in range(count):
            self.now += time
            if self.due():
                pl.when(s == i)(self.take)

    def drain(self):
        while any(c.due is not None for c in self.chunks):
            self.now = max(self.now, min(c.due for c in self.chunks if c.due is not None))
            self.take()
        for chunk in self.chunks:
            chunk.finish()


class Dims:
    def __init__(self, global_crops, local_crops, hidden, wires):
        self.wires = wires
        self.glen, self.n_global, self.width = global_crops.shape
        self.n_local, self.llen, _ = local_crops.shape
        self.hidden = hidden
        self.seq = up_to(self.glen, TILE)
        self.group = self.seq // self.llen
        while self.n_local % self.group:
            self.group -= 1
        self.n_seq = self.n_global + self.n_local // self.group
        sizes = (
            ("attend_gain", self.width),
            ("attend_shift", self.width),
            ("mixer_bias", 2 * self.width),
            ("output_bias", self.width),
            ("feed_gain", self.width),
            ("feed_shift", self.width),
            ("expand_bias", hidden),
            ("reduce_bias", self.width),
        )
        self.names, self.sizes = [name for name, _ in sizes], dict(sizes)
        self.at, row = {}, 0
        for name, size in sizes:
            self.at[name] = row
            row += -(-size // BLOCK)
        self.vec_rows = 2 * TILE
        assert row <= self.vec_rows and self.width * hidden % self.vec_rows == 0
        step = TILE
        for w in wires:
            step *= w.size
        ff = self.width * hidden // BLOCK
        square = self.width * self.width // BLOCK
        self.tops = (0, ff, 2 * ff, 2 * ff + square, 2 * ff + 4 * square)
        self.rows = up_to(self.tops[4] + 2 * self.vec_rows, step)
        parts = self.rows // step
        cuts = ((0, 4, 7, 10, 13, 14), (0, 4, 10, 14))
        self.bounds = [[c * step for c in sorted({parts * k // 14 for k in layer})] for layer in cuts]
        self.landing_sets = [len(b) - 1 for b in self.bounds[::-1]]
        if self.bounds[0] == self.bounds[1]:
            self.landing_sets = self.landing_sets[:1]
        self.n_chunk = sum(len(b) - 1 for b in self.bounds)


HEAVY = (6, 8, 12, 14)


def run_kernel(counts, arrays, dims):
    d = dims
    n, seq, width, hidden = d.n_seq, d.seq, d.width, d.hidden
    crops = [jax.ShapeDtypeStruct(a.shape, BF16) for a in arrays[:2]]
    outs = crops + crops
    outs += [jax.ShapeDtypeStruct((2, d.rows, BLOCK), BF16)]
    scratch = [pltpu.VMEM(a.shape, BF16) for a in tuple(arrays[:4]) * 2]
    scratch += [pltpu.VMEM(arrays[i].shape, BF16) for i in HEAVY]
    scratch += [
        pltpu.SemaphoreType.DMA((16,)),
        pltpu.VMEM((2, d.rows, BLOCK), BF16),
        pltpu.VMEM((d.glen, d.n_global, width), F32),
        pltpu.VMEM((n, seq, width), F32),
        pltpu.VMEM((4, n, seq, width), BF16),
        pltpu.VMEM((4, n, seq, 1), F32),
        pltpu.VMEM((4, n, width + TILE, seq), BF16),
        pltpu.VMEM((2, n, seq, 3 * width), BF16),
        pltpu.VMEM((2, n, HEADS, seq, seq), BF16),
        pltpu.VMEM((2, n, seq, width), F32),
        pltpu.VMEM((2, n, seq, width), BF16),
        pltpu.VMEM((2, n, width + TILE, seq), BF16),
        pltpu.VMEM((2, n, seq, hidden), BF16),
        pltpu.VMEM((n, seq, hidden), BF16),
        pltpu.VMEM((n, seq, width), F32),
        pltpu.VMEM((n, seq, width), BF16),
        pltpu.VMEM((n, width, seq), BF16),
        pltpu.VMEM((n, seq, hidden), BF16),
        pltpu.VMEM((2, seq, seq), BF16),
        pltpu.VMEM((d.vec_rows, BLOCK), F32),
        pltpu.VMEM((3, 8, width), F32),
    ]
    for layer in (1, 0)[: len(d.landing_sets)]:
        for first, end in zip(d.bounds[layer], d.bounds[layer][1:]):
            rows = end - first
            for w in d.wires:
                rows //= w.size
                scratch.append(pltpu.VMEM((w.size - 1, rows, BLOCK), BF16))
    peers = 2 * sum(w.size - 1 for w in d.wires)
    scratch += [
        pltpu.SemaphoreType.DMA((d.n_chunk, peers)),
        pltpu.SemaphoreType.DMA((d.n_chunk, peers)),
        pltpu.SemaphoreType.DMA((d.n_chunk, 1)),
        pltpu.SemaphoreType.REGULAR((d.n_chunk, len(d.wires))),
        pltpu.SemaphoreType.REGULAR((d.n_chunk, len(d.wires))),
    ]
    vmem = pl.BlockSpec(memory_space=pltpu.VMEM)
    anywhere = pl.BlockSpec(memory_space=pl.ANY)
    return pl.pallas_call(
        functools.partial(kernel, d),
        out_shape=outs,
        in_specs=[pl.BlockSpec(memory_space=pltpu.SMEM)]
        + [anywhere if i < 4 or i in HEAVY else vmem for i in range(len(arrays))],
        out_specs=[anywhere] * len(outs),
        scratch_shapes=scratch,
        compiler_params=pltpu.CompilerParams(
            vmem_limit_bytes=63 * 1024 * 1024, collective_id=0, has_side_effects=True
        ),
    )(counts, *arrays)


THIRDS = 3


def cast_kernel(dims, reduce, expand, output, mixer, vectors, *rest):
    crops, outs, held, sems = rest[:4], rest[4:-9], rest[-5:-1], rest[-1]
    step = pl.program_id(0) * THIRDS + pl.program_id(1)
    loads = [pltpu.make_async_copy(a, b, sems.at[0, i]) for i, (a, b) in enumerate(zip(crops, held, strict=True))]
    stores = [pltpu.make_async_copy(a, b, sems.at[1, i]) for i, (a, b) in enumerate(zip(held, rest[-9:-5], strict=True))]

    @pl.when(step == 0)
    def _():
        for copy in loads:
            copy.start()

    @pl.when(step == 1)
    def _():
        for load, store in zip(loads, stores, strict=True):
            load.wait()
            store.start()

    mixer_grad, output_grad, expand_grad, reduce_grad = outs[:4]
    width = dims.width
    fold = width // 2
    for b in range(2):
        rows = slice(b * width, (b + 1) * width)
        cols = slice(b * BLOCK, (b + 1) * BLOCK)
        expand_grad[0, :, cols] = expand[0, rows, :].astype(F32)
        reduce_grad[0, cols, :] = reduce[0, rows, :].T.astype(F32)
    for source, target in ((mixer, mixer_grad), (output, output_grad)):
        target[0, :, 0:BLOCK] = source[0, 0:width, :].astype(F32)
        target[0, 0:fold, BLOCK:] = source[0, width:, 0:LANES].astype(F32)
        target[0, fold:, BLOCK:] = source[0, width:, LANES:].astype(F32)

    @pl.when(step == 2 * THIRDS - 1)
    def _():
        for ref, name in zip(outs[4:], dims.names, strict=True):
            size = ref.shape[1]
            for c in range(0, size, BLOCK):
                at = dims.at[name] + c // BLOCK
                piece = min(BLOCK, size - c)
                for layer in range(2):
                    ref[layer : layer + 1, c : c + piece] = vectors[0].astype(F32)[at + layer * dims.vec_rows :][:1, 0:piece]
        for store in stores:
            store.wait()


def run_cast(sums, crops, dims):
    d = dims
    width, hidden = d.width, d.hidden
    part = (1, 2 * width, BLOCK)
    square = (1, width * width // BLOCK, BLOCK)
    grads = [(width, 3 * width), (width, width), (width, hidden), (hidden, width)]
    shapes = [jax.ShapeDtypeStruct((2,) + g, F32) for g in grads]
    specs = [
        pl.BlockSpec((1, width, 3 * width // THIRDS), lambda l, t: (l, 0, t)),
        pl.BlockSpec((1, width, width), lambda l, t: (l, 0, 0)),
        pl.BlockSpec((1, width, hidden // THIRDS), lambda l, t: (l, 0, t)),
        pl.BlockSpec((1, hidden // THIRDS, width), lambda l, t: (l, t, 0)),
    ]
    for name in d.names:
        shapes.append(jax.ShapeDtypeStruct((2, d.sizes[name]), F32))
        specs.append(pl.BlockSpec((2, d.sizes[name]), lambda l, t: (0, 0)))
    for crop in crops:
        shapes.append(jax.ShapeDtypeStruct(crop.shape, crop.dtype))
        specs.append(pl.BlockSpec(memory_space=pl.ANY))
    return pl.pallas_call(
        functools.partial(cast_kernel, d),
        grid=(2, THIRDS),
        out_shape=shapes,
        in_specs=[
            pl.BlockSpec(part, lambda l, t: (l, t, 0)),
            pl.BlockSpec(part, lambda l, t: (l, THIRDS + t, 0)),
            pl.BlockSpec(square, lambda l, t: (l, d.tops[2] // square[1], 0)),
            pl.BlockSpec(square, lambda l, t: (l, d.tops[3] // square[1] + t, 0)),
            pl.BlockSpec((1, 2 * d.vec_rows, BLOCK), lambda l, t: (0, d.tops[4] // (2 * d.vec_rows), 0)),
        ]
        + [pl.BlockSpec(memory_space=pl.ANY)] * 4,
        out_specs=specs,
        scratch_shapes=[pltpu.VMEM(c.shape, c.dtype) for c in crops] + [pltpu.SemaphoreType.DMA((2, 4))],
        compiler_params=pltpu.CompilerParams(vmem_limit_bytes=62 * 1024 * 1024),
    )(sums, sums, sums, sums, sums, *crops)


def shards(wires, global_crops, local_crops, local_count, global_cotangent, local_cotangent, *weights):
    global_crops, global_cotangent = global_crops.transpose(1, 0, 2), global_cotangent.transpose(1, 0, 2)
    dims = Dims(global_crops, local_crops, weights[8].shape[2], wires)
    outs = run_kernel(
        local_count, (global_crops, local_crops, global_cotangent, local_cotangent) + weights, dims
    )
    mixer, output, expand, reduce, *rest = run_cast(outs[4], outs[:4], dims)
    vectors, crops = rest[:-4], rest[-4:]
    v = dict(zip(dims.names, vectors, strict=True))
    return (
        crops[0].transpose(1, 0, 2),
        crops[1],
        crops[2].transpose(1, 0, 2),
        crops[3],
        v["attend_gain"],
        v["attend_shift"],
        mixer,
        v["mixer_bias"],
        output,
        v["output_bias"],
        v["feed_gain"],
        v["feed_shift"],
        expand,
        v["expand_bias"],
        reduce,
        v["reduce_bias"],
    )


def solution(mesh):
    crops = P(("dp", "section"), None, None)
    return jax.shard_map(
        functools.partial(shards, wires_of(mesh)),
        mesh=mesh,
        in_specs=(crops, crops, P("dp"), crops, crops) + (P(),) * 12,
        out_specs=(crops,) * 4 + (P(),) * 12,
        check_vma=False,
    )
```

```python
import functools

import jax
import jax.numpy as jnp
from jax import lax
from jax.experimental import pallas as pl
from jax.experimental.pallas import tpu as pltpu
from jax.sharding import PartitionSpec as P

HEADS = 6
HEAD = 64
EPS = 1e-06
TILE = 16
LANES = 128
BLOCK = 256
LOG2E = 1.4426950408889634
F32 = jnp.float32
BF16 = jnp.bfloat16


def up_to(value, step):
    return -(-value // step) * step


def mm(left, right):
    return lax.dot_general(left, right, (((1,), (0,)), ((), ())), preferred_element_type=F32)


def mm_nt(left, right):
    return lax.dot_general(left, right, (((1,), (1,)), ((), ())), preferred_element_type=F32)


def mm_tn(left, right):
    return lax.dot_general(left, right, (((0,), (0,)), ((), ())), preferred_element_type=F32)


def norm(rows):
    centred = rows - jnp.mean(rows, -1, keepdims=True)
    scale = lax.rsqrt(jnp.mean(centred * centred, -1, keepdims=True) + EPS)
    return centred * scale, scale


def norm_back(grad, unit, scale, gain):
    slope = grad * gain
    first = jnp.mean(slope, -1, keepdims=True)
    second = jnp.mean(slope * unit, -1, keepdims=True)
    return scale * (slope - first - unit * second)


def gelu_parts(u):
    size = jnp.abs(u)
    d = 1.0 + (0.3275911 * 0.7071067811865476) * size
    t = pl.reciprocal(d, approx=True)
    t = t * (2.0 - d * t)
    poly = 0.5 * 1.061405429
    for a in (-1.453152027, 1.421413741, -0.284496736, 0.254829592):
        poly = poly * t + 0.5 * a
    bell = jnp.exp2((u * u) * (-0.5 * LOG2E))
    tail = poly * t * bell
    phi = jnp.where(u < 0.0, tail, 1.0 - tail)
    return u * phi, phi + (u * bell) * 0.3989422804014327


def fold8(value):
    rows, width = value.shape
    return jnp.sum(value.reshape(rows // 8, 8, width), 0)


def kernel(
    dims,
    counts,
    global_in_hbm,
    local_in_hbm,
    global_cot_hbm,
    local_cot_hbm,
    attend_gain,
    attend_shift,
    mixer_hbm,
    mixer_bias,
    output_hbm,
    output_bias,
    feed_gain,
    feed_shift,
    expand_hbm,
    expand_bias,
    reduce_hbm,
    reduce_bias,
    global_out_hbm,
    local_out_hbm,
    global_back_hbm,
    local_back_hbm,
    sums_out,
    global_in,
    local_in,
    global_cot,
    local_cot,
    global_out,
    local_out,
    global_back,
    local_back,
    mixer_weight,
    output_weight,
    expand_weight,
    reduce_weight,
    io_sem,
    sums,
    crop_s,
    x_s,
    unit_s,
    scale_s,
    norm_n,
    packed_s,
    power_s,
    inverse_s,
    mixed_s,
    act_s,
    slope_s,
    grad_s,
    grad_low,
    dup_s,
    aug_s,
    vec_s,
    acc_s,
    *wires,
):
    seq, group, width = dims.seq, dims.group, dims.width
    glen, llen = dims.glen, dims.llen
    n_global, n_local, n_seq = dims.n_global, dims.n_local, dims.n_seq
    hidden = dims.hidden
    count = counts[lax.axis_index("section")]
    pairs = HEADS // 2
    lane = lax.broadcasted_iota(jnp.int32, (1, LANES), 1)
    low_half = (lane < HEAD).astype(F32).astype(BF16)
    high_half = (lane >= HEAD).astype(F32).astype(BF16)
    score_scale = HEAD ** (-0.5)

    moves = [pltpu.make_async_copy(global_in_hbm, global_in, io_sem.at[0]), pltpu.make_async_copy(local_in_hbm, local_in, io_sem.at[1])]
    weights = ((mixer_hbm, mixer_weight), (output_hbm, output_weight), (expand_hbm, expand_weight), (reduce_hbm, reduce_weight))
    for layer in range(2):
        for source, target in weights:
            moves.append(pltpu.make_async_copy(source.at[layer], target.at[layer], io_sem.at[len(moves)]))
    moves += [
        pltpu.make_async_copy(global_cot_hbm, global_cot, io_sem.at[10]),
        pltpu.make_async_copy(local_cot_hbm, local_cot, io_sem.at[11]),
    ]
    outward = [
        pltpu.make_async_copy(global_out, global_out_hbm, io_sem.at[12]),
        pltpu.make_async_copy(local_out, local_out_hbm, io_sem.at[13]),
        pltpu.make_async_copy(global_back, global_back_hbm, io_sem.at[14]),
        pltpu.make_async_copy(local_back, local_back_hbm, io_sem.at[15]),
    ]
    for move in moves:
        move.start()

    net = Net(dims.wires)
    net.greet()
    n_stage = len(dims.wires)
    sets = dims.landing_sets
    landings, sems = wires[: n_stage * sum(sets)], wires[n_stage * sum(sets) :]
    flow = Flow(net)
    number = 0
    for layer in (1, 0):
        bounds = dims.bounds[layer]
        for i in range(len(bounds) - 1):
            shared = len(sets) == 1
            at = (i if shared else number) * n_stage
            own = [w.at[number] for w in sems[:4]] + [sems[4].at[i]]
            rows = pl.ds(bounds[i], bounds[i + 1] - bounds[i])
            turn = (1 - layer) if shared else None
            flow.chunks.append(
                Chunk(net, sums.at[layer, rows], sums_out.at[layer, rows], landings[at : at + n_stage], own, turn, layer, bounds[i + 1])
            )
            number += 1

    for s in range(n_seq):
        x_s[s, seq - 32 :, :] = jnp.zeros((32, width), F32)
        grad_s[s, seq - 32 :, :] = jnp.zeros((32, width), F32)
    row_id = lax.broadcasted_iota(jnp.int32, (seq, LANES), 0)
    col_id = lax.broadcasted_iota(jnp.int32, (seq, LANES), 1)
    row_crop = sum((row_id >= llen * j).astype(jnp.int32) for j in range(1, group + 1))
    far = jnp.float32(-1e30)
    zero = jnp.float32(0)
    for h in range(2):
        place = col_id - (1 - h) * HEAD
        used = (place >= 0) & (place <= group)
        aug_s[0, h, 0] = jnp.where(place == 0, jnp.float32(1), zero).astype(BF16)
        aug_s[0, h, 1] = jnp.where((place == 0) & (row_id >= glen), far, zero).astype(BF16)
        aug_s[1, h, 0] = jnp.where(place == row_crop, jnp.float32(1), zero).astype(BF16)
        aug_s[1, h, 1] = jnp.where(used & (place != row_crop), far, zero).astype(BF16)
    one_column = (lax.broadcasted_iota(jnp.int32, (seq, LANES), 1) == 0).astype(F32).astype(BF16)
    for s in range(n_seq):
        for i in range(4):
            norm_n[i, s, :, width:] = one_column
        for i in range(2):
            mixed_s[i, s, :, width:] = one_column

    def live_rows(g):
        rows = lax.broadcasted_iota(jnp.int32, (seq, 1), 0)
        return (rows < llen * jnp.clip(count - g * group, 0, group)).astype(F32)

    def take_crops(crops, locals_, target):
        crop_s[...] = crops[...].astype(F32)
        for s in range(n_global):
            target[s, 0:glen, :] = crop_s[:, s, :]
        for j in range(n_local):
            s, at = n_global + j // group, llen * (j % group)
            target[s, at : at + llen, :] = locals_[j].astype(F32)

    def take_cotangents():
        moves[10].wait()
        moves[11].wait()
        take_crops(global_cot, local_cot, grad_s)
        for s in range(n_global, n_seq):
            grad_s[s] = grad_s[s] * live_rows(s - n_global)

    moves[0].wait()
    moves[1].wait()
    take_crops(global_in, local_in, x_s)

    def row(ref, layer):
        return ref[...].astype(F32)[layer : layer + 1]

    slopes = (slope_s, dup_s)

    def start_back(s, grad):
        grad_low[s] = grad.astype(BF16)
        acc_s[2] = acc_s[2] + fold8(grad)

    def end_back(s, grad, unit, scale, gain, dh):
        unit = unit.astype(F32)
        acc_s[0] = acc_s[0] + fold8(dh * unit)
        acc_s[1] = acc_s[1] + fold8(dh)
        grad = (grad + norm_back(dh, unit, scale, gain)).astype(BF16)
        grad_low[s] = grad
        grad_s[s] = grad.astype(F32)

    def product(left, right, cols, first):
        total = None
        for s in range(n_seq):
            term = mm_tn(left[s, :, 0:first], right[s, :, cols])
            total = term if total is None else total + term
        return total

    for layer in range(2):
        gain, shift = row(attend_gain, layer), row(attend_shift, layer)
        bias = row(mixer_bias, layer)
        bias = jnp.concatenate([bias[:, :width], jnp.zeros((1, width), F32), bias[:, width:]], 1)
        out_bias = row(output_bias, layer)
        gain2, shift2 = row(feed_gain, layer), row(feed_shift, layer)
        bias_up, bias_down = row(expand_bias, layer), row(reduce_bias, layer)

        def attend(s, _):
            x = x_s[s]
            unit, scale = norm(x)
            unit_s[2 * layer, s] = unit.astype(BF16)
            scale_s[2 * layer, s] = scale
            normed = (unit * gain + shift).astype(BF16)
            norm_n[2 * layer, s, :, 0:width] = normed
            packed = (mm(normed, mixer_weight[layer]) + bias).astype(BF16)
            packed_s[layer, s] = packed
            kind = jnp.where(s < n_global, 0, 1)
            mixed = []
            for p in range(pairs):
                at = p * LANES
                query = packed[:, at : at + LANES]
                key = packed[:, width + at : width + at + LANES]
                value = packed[:, 2 * width + at : 2 * width + at + LANES]
                total = None
                for h, half in enumerate((low_half, high_half)):
                    scores = mm_nt(query * half + aug_s[kind, h, 0], key * half + aug_s[kind, h, 1]) * (score_scale * LOG2E)
                    power = jnp.exp2(scores - jnp.max(scores, -1, keepdims=True)).astype(BF16)
                    power_s[layer, s, 2 * p + h] = power
                    spread = jnp.broadcast_to(half, (seq, LANES))
                    term = mm(power, jnp.concatenate([value * half, spread], 1))
                    total = term if total is None else total + term
                inverse = 1.0 / total[:, LANES:]
                inverse_s[layer, s, :, at : at + LANES] = inverse
                mixed.append((total[:, :LANES] * inverse).astype(BF16))
            mixed = jnp.concatenate(mixed, 1)
            mixed_s[layer, s, :, 0:width] = mixed
            x = x + mm(mixed, output_weight[layer]) + out_bias
            x_s[s] = x.astype(BF16).astype(F32)
            return 0

        moves[2 + 4 * layer].wait()
        moves[3 + 4 * layer].wait()
        lax.fori_loop(0, n_seq, attend, 0)

        def feed(s, _):
            x = x_s[s]
            unit, scale = norm(x)
            normed = (unit * gain2 + shift2).astype(BF16)
            norm_n[2 * layer + 1, s, :, 0:width] = normed
            unit_s[2 * layer + 1, s] = unit.astype(BF16)
            scale_s[2 * layer + 1, s] = scale
            if layer == 1:
                start_back(s, grad_s[s])
            for c in range(hidden // BLOCK):
                cols = slice(c * BLOCK, (c + 1) * BLOCK)
                up = mm(normed, expand_weight[layer, :, cols]) + bias_up[:, cols]
                act, slope = gelu_parts(up)
                act_s[layer, s, :, cols] = act.astype(BF16)
                slopes[layer][s, :, cols] = slope.astype(BF16)
            x = x + mm(act_s[layer, s], reduce_weight[layer]) + bias_down
            x_s[s] = x.astype(BF16).astype(F32)
            return 0

        moves[4 + 4 * layer].wait()
        moves[5 + 4 * layer].wait()
        if layer == 1:
            take_cotangents()
            acc_s[...] = jnp.zeros_like(acc_s)
        lax.fori_loop(0, n_seq, feed, 0)

    for s in range(n_global):
        crop_s[:, s, :] = x_s[s, 0:glen, :]
    global_out[...] = crop_s[...].astype(BF16)
    for j in range(n_local):
        s, at = n_global + j // group, llen * (j % group)
        alive = (count > j).astype(F32)
        local_out[j] = (x_s[s, at : at + llen, :] * alive).astype(BF16)
    outward[0].start()
    outward[1].start()

    def put_vector(at, value):
        for c in range(0, value.shape[1], BLOCK):
            piece = value[:, c : c + BLOCK]
            vec_s[at + c // BLOCK : at + c // BLOCK + 1, 0 : piece.shape[1]] = piece

    def put_tile(layer, top, m, part):
        at = top + (m // 3) * (width + fold)
        side = m % 3 * LANES
        part = part.astype(BF16)
        if m % 3 < 2:
            sums[layer, at : at + width, side : side + LANES] = part
        else:
            at = at + width
            sums[layer, at : at + fold, 0:LANES] = part[:fold]
            sums[layer, at : at + fold, LANES:] = part[fold:]

    blocks = hidden // BLOCK
    fold = width // 2
    tops = dims.tops
    net.wait_greeting()
    for layer, used in ((1, tops[4]), (0, tops[4] + 2 * dims.vec_rows)):
        if dims.rows > used:
            sums[layer, used:, :] = jnp.zeros((dims.rows - used, BLOCK), BF16)
    for layer in (1, 0):
        vec_s[...] = jnp.zeros_like(vec_s)
        gain2, gain = row(feed_gain, layer), row(attend_gain, layer)
        put_vector(dims.at["reduce_bias"], jnp.sum(acc_s[2], 0, keepdims=True))

        for c in range(blocks):
            total = product(grad_low, act_s.at[layer], slice(c * BLOCK, (c + 1) * BLOCK), width)
            at = tops[0] + c * width
            sums[layer, at : at + width, :] = total.astype(BF16)
            flow.ready(layer, at + width)
            flow.tick(0.45)

        def feed_back(s, _):
            grad_in = grad_s[s].astype(BF16)
            for c in range(blocks):
                cols = slice(c * BLOCK, (c + 1) * BLOCK)
                dact = mm_nt(grad_in, reduce_weight[layer, cols, :])
                dup_s[s, :, cols] = (dact * slopes[layer][s, :, cols].astype(F32)).astype(BF16)
            flow.ticks(s, n_seq, 0.6)
            return 0

        lax.fori_loop(0, n_seq, feed_back, 0)

        for c in range(blocks):
            total = product(norm_n.at[2 * layer + 1], dup_s, slice(c * BLOCK, (c + 1) * BLOCK), width + TILE)
            at = tops[1] + c * width
            sums[layer, at : at + width, :] = total[:width].astype(BF16)
            at_bias = dims.at["expand_bias"] + c
            vec_s[at_bias : at_bias + 1, :] = total[width : width + 1]
            flow.ready(layer, at + width)
            flow.tick(0.45)

        def feed_norm_back(s, _):
            dh = mm_nt(dup_s[s], expand_weight[layer])
            end_back(s, grad_s[s], unit_s[2 * layer + 1, s], scale_s[2 * layer + 1, s], gain2, dh)
            flow.ticks(s, n_seq, 0.7)
            return 0

        acc_s[0:2] = jnp.zeros((2, 8, width), F32)
        lax.fori_loop(0, n_seq, feed_norm_back, 0)
        put_vector(dims.at["feed_gain"], jnp.sum(acc_s[0], 0, keepdims=True))
        put_vector(dims.at["feed_shift"], jnp.sum(acc_s[1], 0, keepdims=True))

        bias_parts = []
        for c in range(0, width, BLOCK):
            size = min(BLOCK, width - c)
            total = product(mixed_s.at[layer], grad_low, slice(c, c + size), width + TILE)
            for k in range(0, size, LANES):
                put_tile(layer, tops[2], (c + k) // LANES, total[:width, k : k + LANES])
                bias_parts.append(total[width : width + 1, k : k + LANES])
        put_vector(dims.at["output_bias"], jnp.concatenate(bias_parts, 1))
        flow.ready(layer, tops[3])
        flow.tick(0.8)

        def attend_back(s, _):
            dmixed = mm_nt(grad_low[s], output_weight[layer])
            parts = [None] * (3 * pairs)
            for p in range(pairs):
                at = p * LANES
                query = packed_s[layer, s, :, at : at + LANES]
                key = packed_s[layer, s, :, width + at : width + at + LANES]
                value = packed_s[layer, s, :, 2 * width + at : 2 * width + at + LANES]
                dm = dmixed[:, at : at + LANES] * inverse_s[layer, s, :, at : at + LANES]
                inner = -(dm * mixed_s[layer, s, :, at : at + LANES].astype(F32)).astype(BF16)
                dm = dm.astype(BF16)
                wide_value = jnp.concatenate([value, jnp.ones_like(value)], 1)
                dq = dk = dv = None
                for h, half in enumerate((low_half, high_half)):
                    power = power_s[layer, s, 2 * p + h]
                    dm_half = dm * half
                    left = jnp.concatenate([dm_half, inner * half], 1)
                    ds = (power.astype(F32) * mm_nt(left, wide_value)).astype(BF16)
                    terms = (mm(ds, key * half), mm_tn(ds, query * half), mm_tn(power, dm_half))
                    dq = terms[0] if dq is None else dq + terms[0]
                    dk = terms[1] if dk is None else dk + terms[1]
                    dv = terms[2] if dv is None else dv + terms[2]
                parts[p] = (dq * score_scale).astype(BF16)
                parts[pairs + p] = (dk * score_scale).astype(BF16)
                parts[2 * pairs + p] = dv.astype(BF16)
            dup_s[s, :, 0 : 3 * width] = jnp.concatenate(parts, 1)
            flow.ticks(s, n_seq, 1.7)
            return 0

        lax.fori_loop(0, n_seq, attend_back, 0)

        bias_parts = []
        for c in range(0, 3 * width, BLOCK):
            size = min(BLOCK, 3 * width - c)
            total = product(norm_n.at[2 * layer], dup_s, slice(c, c + size), width + TILE)
            for k in range(0, size, LANES):
                put_tile(layer, tops[3], (c + k) // LANES, total[:width, k : k + LANES])
                bias_parts.append(total[width : width + 1, k : k + LANES])
            flow.tick(0.5)
        each = width // LANES
        put_vector(
            dims.at["mixer_bias"],
            jnp.concatenate(bias_parts[:each] + bias_parts[2 * each :], 1),
        )
        flow.ready(layer, dims.rows if layer == 1 else tops[4])

        def attend_norm_back(s, _):
            dh = mm_nt(dup_s[s, :, 0 : 3 * width], mixer_weight[layer])
            end_back(s, grad_s[s], unit_s[2 * layer, s], scale_s[2 * layer, s], gain, dh)
            if layer == 1:
                start_back(s, grad_s[s])
            flow.ticks(s, n_seq, 0.6)
            return 0

        acc_s[...] = jnp.zeros_like(acc_s)
        lax.fori_loop(0, n_seq, attend_norm_back, 0)
        put_vector(dims.at["attend_gain"], jnp.sum(acc_s[0], 0, keepdims=True))
        put_vector(dims.at["attend_shift"], jnp.sum(acc_s[1], 0, keepdims=True))
        at = tops[4] + layer * dims.vec_rows
        sums[0, at : at + dims.vec_rows, :] = vec_s[...].astype(BF16)
        if layer == 0:
            flow.ready(0, dims.rows)

    for s in range(n_global):
        crop_s[:, s, :] = grad_s[s, 0:glen, :]
    global_back[...] = crop_s[...].astype(BF16)
    for j in range(n_local):
        s, at = n_global + j // group, llen * (j % group)
        local_back[j] = grad_s[s, at : at + llen, :].astype(BF16)
    outward[2].start()
    outward[3].start()
    flow.drain()
    for move in outward:
        move.wait()


class Wire:
    def __init__(self, size, first, second):
        self.size, self.first, self.second = size, first, second


def wires_of(mesh):
    names = mesh.axis_names
    places = {}
    for axis, name in enumerate(names):
        line = [mesh.devices[tuple(i if a == axis else 0 for a in range(2))] for i in range(mesh.devices.shape[axis])]
        spots = [(d.core_on_chip,) + tuple(d.coords) for d in line]
        found, total = [], 1
        for k in range(4):
            values = sorted({p[k] for p in spots})
            if len(values) > 1:
                stride = next(i for i, p in enumerate(spots) if p[k] != spots[0][k])
                found.append((k, axis, stride, len(values)))
                total *= len(values)
        good = total == len(line)
        for k, _, stride, size in found:
            values = [p[k] for p in spots]
            good = good and all(v == values[i // stride % size * stride] for i, v in enumerate(values))
        if not good:
            found = [(4 + axis, axis, 1, len(line))]
        for k, axis, stride, size in found:
            places[k] = (axis, stride, size)
    wires = []
    if 0 in places:
        wires.append(Wire(places[0][2], places[0], places[0]))
    if 0 in places and 1 in places and 2 in places and places[1][2] == places[2][2]:
        wires.append(Wire(places[1][2], places[1], places[2]))
        wires.append(Wire(places[1][2], places[2], places[1]))
        order = [3, 4, 5]
    else:
        order = [1, 2, 3, 4, 5]
    for k in order:
        if k in places:
            wires.append(Wire(places[k][2], places[k], places[k]))
    return wires


class Net:
    def __init__(self, wires):
        self.axes = ("dp", "section")
        self.here = [lax.axis_index(a) for a in self.axes]
        self.wires = wires
        first = wires[0]
        odd = self.spot(first.first) % 2 if first.size == 2 else 0
        self.odd = odd
        self.at = []
        for w in wires:
            a, b = self.spot(w.first), self.spot(w.second)
            self.at.append(a if w.first == w.second else a + odd * (b - a))

    def spot(self, place):
        axis, stride, size = place
        return self.here[axis] // stride % size

    def peer(self, stage, k):
        w = self.wires[stage]
        place = (self.at[stage] + k) % w.size
        move = place - self.at[stage]
        target = list(self.here)
        if w.first == w.second:
            target[w.first[0]] = target[w.first[0]] + move * w.first[1]
        else:
            target[w.first[0]] = target[w.first[0]] + move * w.first[1] * (1 - self.odd)
            target[w.second[0]] = target[w.second[0]] + move * w.second[1] * self.odd
        return tuple(target), place

    def greet(self):
        barrier = pltpu.get_barrier_semaphore()
        for stage, w in enumerate(self.wires):
            for k in range(1, w.size):
                pl.semaphore_signal(barrier, inc=1, device_id=self.peer(stage, k)[0], device_id_type=pl.DeviceIdType.MESH)

    def wait_greeting(self):
        pl.semaphore_wait(pltpu.get_barrier_semaphore(), sum(w.size - 1 for w in self.wires))


class Chunk:
    def __init__(self, net, sums, out, landing, sems, turn, layer, end):
        self.net, self.sums, self.out, self.landing = net, sums, out, landing
        self.send, self.recv, self.local, self.sent, self.free = sems
        self.turn = turn
        self.layer, self.end = layer, end
        self.due = None
        size, start = sums.shape[0], 0
        self.unit = size
        for w in net.wires:
            self.unit //= w.size
        self.size, self.start = [], []
        for stage, w in enumerate(net.wires):
            size //= w.size
            self.size.append(size)
            self.start.append((start, size))
            start = start + net.at[stage] * size
        self.own = start
        self.stages = len(net.wires)
        self.step = 0
        self.sem_at, at = {}, 0
        for phase in range(2):
            for stage, w in enumerate(net.wires):
                for k in range(1, w.size):
                    self.sem_at[phase, stage, k] = at
                    at += 1

    def rows(self, stage, place):
        start, size = self.start[stage]
        return pl.ds(pl.multiple_of(start + place * size, TILE), size)

    def copy(self, phase, stage, k):
        target, place = self.net.peer(stage, k)
        at = self.sem_at[phase, stage, k]
        if phase == 0:
            source, to = self.sums.at[self.rows(stage, place)], self.landing[stage].at[k - 1]
        else:
            rows = self.rows(stage, self.net.at[stage])
            source = to = self.sums.at[rows]
        return pltpu.make_async_remote_copy(
            src_ref=source,
            dst_ref=to,
            send_sem=self.send.at[at],
            recv_sem=self.recv.at[at],
            device_id=target,
            device_id_type=pl.DeviceIdType.MESH,
        )

    def arrival(self, stage, k):
        target, place = self.net.peer(stage, self.net.wires[stage].size - k)
        at = self.sem_at[1, stage, k]
        landed = self.sums.at[self.rows(stage, place)]
        return pltpu.make_async_remote_copy(
            src_ref=landed,
            dst_ref=landed,
            send_sem=self.send.at[at],
            recv_sem=self.recv.at[at],
            device_id=target,
            device_id_type=pl.DeviceIdType.MESH,
        )

    def start_stage(self, phase, stage):
        if phase == 0 and self.turn == 1:
            pl.semaphore_wait(self.free.at[stage], self.net.wires[stage].size - 1)
        if phase == 1:
            pl.semaphore_wait(self.sent.at[stage], self.net.wires[stage].size - 1)
        for k in range(1, self.net.wires[stage].size):
            self.copy(phase, stage, k).start()

    def load(self):
        last = self.stages - 1
        stage = self.step if self.step <= last else 2 * self.stages - 1 - self.step
        peers = self.net.wires[stage].size - 1
        row = BLOCK * 2
        if stage == 0:
            return 0, self.size[0] * row / 4
        if stage == last:
            return 2, self.size[stage] * (peers + 1) ** 2 / 2 * row
        return 1, self.size[stage] * peers * row

    def begin(self):
        self.start_stage(0, 0)

    def out_copy(self):
        return pltpu.make_async_copy(self.sums, self.out, self.local.at[0])

    def advance(self):
        step = self.step
        self.step += 1
        if step < self.stages:
            peers = range(1, self.net.wires[step].size)
            for k in peers:
                self.copy(0, step, k).wait_recv()
            base = self.start[step][0] + self.net.at[step] * self.size[step]
            landing = self.landing[step]

            count = self.size[step] // self.unit
            while count % 2 == 0 and self.size[step] // count < 128:
                count //= 2
            size = self.size[step] // count

            def add(i, _):
                at = pl.ds(pl.multiple_of(base + i * size, TILE), size)
                here = [landing[k - 1, pl.ds(pl.multiple_of(i * size, TILE), size), :] for k in peers]
                if len(here) == 1:
                    self.sums[at, :] = self.sums[at, :] + here[0]
                else:
                    total = self.sums[at, :].astype(F32)
                    for part in here:
                        total = total + part.astype(F32)
                    self.sums[at, :] = total.astype(BF16)
                return 0

            lax.fori_loop(0, count, add, 0)
            for k in peers:
                self.copy(0, step, k).wait_send()
                target = self.net.peer(step, k)[0]
                pl.semaphore_signal(self.sent.at[step], inc=1, device_id=target, device_id_type=pl.DeviceIdType.MESH)
                if self.turn == 0:
                    pl.semaphore_signal(self.free.at[step], inc=1, device_id=target, device_id_type=pl.DeviceIdType.MESH)
            if step + 1 < self.stages:
                self.start_stage(0, step + 1)
            else:
                self.start_stage(1, step)
        else:
            stage = 2 * self.stages - 1 - step
            for k in range(1, self.net.wires[stage].size):
                self.arrival(stage, k).wait_recv()
            if stage > 0:
                self.start_stage(1, stage - 1)
            else:
                self.out_copy().start()

    def finish(self):
        for phase, stage, k in self.sem_at:
            if phase == 1:
                self.copy(phase, stage, k).wait_send()
        self.out_copy().wait()


LATENCY = 2.0
RATE = 80e3
STEP = 0.4


class Flow:
    def __init__(self, net):
        self.chunks, self.now, self.waiting, self.free = [], 0.0, 0, [0.0] * 3

    def book(self, chunk):
        kind, size = chunk.load()
        self.free[kind] = max(self.now, self.free[kind]) + size / RATE
        chunk.due = self.free[kind] + LATENCY

    def ready(self, layer, rows):
        while self.waiting < len(self.chunks):
            chunk = self.chunks[self.waiting]
            if chunk.layer != layer or chunk.end > rows:
                return
            chunk.begin()
            self.book(chunk)
            self.waiting += 1

    def due(self):
        return sorted((c for c in self.chunks if c.due is not None and c.due <= self.now), key=lambda c: c.due)

    def take(self):
        while self.due():
            chunk = self.due()[0]
            chunk.advance()
            self.now += STEP
            if chunk.step < 2 * chunk.stages:
                self.book(chunk)
            else:
                chunk.due = None

    def tick(self, time):
        self.now += time
        self.take()

    def ticks(self, s, count, time):
        for i in range(count):
            self.now += time
            if self.due():
                pl.when(s == i)(self.take)

    def drain(self):
        while any(c.due is not None for c in self.chunks):
            self.now = max(self.now, min(c.due for c in self.chunks if c.due is not None))
            self.take()
        for chunk in self.chunks:
            chunk.finish()


class Dims:
    def __init__(self, global_crops, local_crops, hidden, wires):
        self.wires = wires
        self.glen, self.n_global, self.width = global_crops.shape
        self.n_local, self.llen, _ = local_crops.shape
        self.hidden = hidden
        self.seq = up_to(self.glen, TILE)
        self.group = self.seq // self.llen
        while self.n_local % self.group:
            self.group -= 1
        self.n_seq = self.n_global + self.n_local // self.group
        sizes = (
            ("attend_gain", self.width),
            ("attend_shift", self.width),
            ("mixer_bias", 2 * self.width),
            ("output_bias", self.width),
            ("feed_gain", self.width),
            ("feed_shift", self.width),
            ("expand_bias", hidden),
            ("reduce_bias", self.width),
        )
        self.names, self.sizes = [name for name, _ in sizes], dict(sizes)
        self.at, row = {}, 0
        for name, size in sizes:
            self.at[name] = row
            row += -(-size // BLOCK)
        self.vec_rows = 2 * TILE
        assert row <= self.vec_rows and self.width * hidden % self.vec_rows == 0
        step = TILE
        for w in wires:
            step *= w.size
        ff = self.width * hidden // BLOCK
        square = self.width * self.width // BLOCK
        self.tops = (0, ff, 2 * ff, 2 * ff + square, 2 * ff + 4 * square)
        self.rows = up_to(self.tops[4] + 2 * self.vec_rows, step)
        parts = self.rows // step
        cuts = ((0, 4, 7, 10, 13, 14), (0, 4, 10, 14))
        self.bounds = [[c * step for c in sorted({parts * k // 14 for k in layer})] for layer in cuts]
        self.landing_sets = [len(b) - 1 for b in self.bounds[::-1]]
        if self.bounds[0] == self.bounds[1]:
            self.landing_sets = self.landing_sets[:1]
        self.n_chunk = sum(len(b) - 1 for b in self.bounds)


HEAVY = (6, 8, 12, 14)


def run_kernel(counts, arrays, dims):
    d = dims
    n, seq, width, hidden = d.n_seq, d.seq, d.width, d.hidden
    crops = [jax.ShapeDtypeStruct(a.shape, BF16) for a in arrays[:2]]
    outs = crops + crops
    outs += [jax.ShapeDtypeStruct((2, d.rows, BLOCK), BF16)]
    scratch = [pltpu.VMEM(a.shape, BF16) for a in tuple(arrays[:4]) * 2]
    scratch += [pltpu.VMEM(arrays[i].shape, BF16) for i in HEAVY]
    scratch += [
        pltpu.SemaphoreType.DMA((16,)),
        pltpu.VMEM((2, d.rows, BLOCK), BF16),
        pltpu.VMEM((d.glen, d.n_global, width), F32),
        pltpu.VMEM((n, seq, width), F32),
        pltpu.VMEM((4, n, seq, width), BF16),
        pltpu.VMEM((4, n, seq, 1), F32),
        pltpu.VMEM((4, n, seq, width + LANES), BF16),
        pltpu.VMEM((2, n, seq, 3 * width), BF16),
        pltpu.VMEM((2, n, HEADS, seq, seq), BF16),
        pltpu.VMEM((2, n, seq, width), F32),
        pltpu.VMEM((2, n, seq, width + LANES), BF16),
        pltpu.VMEM((2, n, seq, hidden), BF16),
        pltpu.VMEM((n, seq, hidden), BF16),
        pltpu.VMEM((n, seq, width), F32),
        pltpu.VMEM((n, seq, width), BF16),
        pltpu.VMEM((n, seq, hidden), BF16),
        pltpu.VMEM((2, 2, 2, seq, LANES), BF16),
        pltpu.VMEM((d.vec_rows, BLOCK), F32),
        pltpu.VMEM((3, 8, width), F32),
    ]
    for layer in (1, 0)[: len(d.landing_sets)]:
        for first, end in zip(d.bounds[layer], d.bounds[layer][1:]):
            rows = end - first
            for w in d.wires:
                rows //= w.size
                scratch.append(pltpu.VMEM((w.size - 1, rows, BLOCK), BF16))
    peers = 2 * sum(w.size - 1 for w in d.wires)
    scratch += [
        pltpu.SemaphoreType.DMA((d.n_chunk, peers)),
        pltpu.SemaphoreType.DMA((d.n_chunk, peers)),
        pltpu.SemaphoreType.DMA((d.n_chunk, 1)),
        pltpu.SemaphoreType.REGULAR((d.n_chunk, len(d.wires))),
        pltpu.SemaphoreType.REGULAR((d.n_chunk, len(d.wires))),
    ]
    vmem = pl.BlockSpec(memory_space=pltpu.VMEM)
    anywhere = pl.BlockSpec(memory_space=pl.ANY)
    return pl.pallas_call(
        functools.partial(kernel, d),
        out_shape=outs,
        in_specs=[pl.BlockSpec(memory_space=pltpu.SMEM)]
        + [anywhere if i < 4 or i in HEAVY else vmem for i in range(len(arrays))],
        out_specs=[anywhere] * len(outs),
        scratch_shapes=scratch,
        compiler_params=pltpu.CompilerParams(
            vmem_limit_bytes=63 * 1024 * 1024, collective_id=0, has_side_effects=True
        ),
    )(counts, *arrays)


THIRDS = 3


def cast_kernel(dims, reduce, expand, output, mixer, vectors, *rest):
    crops, outs, held, sems = rest[:4], rest[4:-9], rest[-5:-1], rest[-1]
    step = pl.program_id(0) * THIRDS + pl.program_id(1)
    loads = [pltpu.make_async_copy(a, b, sems.at[0, i]) for i, (a, b) in enumerate(zip(crops, held, strict=True))]
    stores = [pltpu.make_async_copy(a, b, sems.at[1, i]) for i, (a, b) in enumerate(zip(held, rest[-9:-5], strict=True))]

    @pl.when(step == 0)
    def _():
        for copy in loads:
            copy.start()

    @pl.when(step == 1)
    def _():
        for load, store in zip(loads, stores, strict=True):
            load.wait()
            store.start()

    mixer_grad, output_grad, expand_grad, reduce_grad = outs[:4]
    width = dims.width
    fold = width // 2
    for b in range(2):
        rows = slice(b * width, (b + 1) * width)
        cols = slice(b * BLOCK, (b + 1) * BLOCK)
        expand_grad[0, :, cols] = expand[0, rows, :].astype(F32)
        reduce_grad[0, cols, :] = reduce[0, rows, :].T.astype(F32)
    for source, target in ((mixer, mixer_grad), (output, output_grad)):
        target[0, :, 0:BLOCK] = source[0, 0:width, :].astype(F32)
        target[0, 0:fold, BLOCK:] = source[0, width:, 0:LANES].astype(F32)
        target[0, fold:, BLOCK:] = source[0, width:, LANES:].astype(F32)

    @pl.when(step == 2 * THIRDS - 1)
    def _():
        for ref, name in zip(outs[4:], dims.names, strict=True):
            size = ref.shape[1]
            for c in range(0, size, BLOCK):
                at = dims.at[name] + c // BLOCK
                piece = min(BLOCK, size - c)
                for layer in range(2):
                    ref[layer : layer + 1, c : c + piece] = vectors[0].astype(F32)[at + layer * dims.vec_rows :][:1, 0:piece]
        for store in stores:
            store.wait()


def run_cast(sums, crops, dims):
    d = dims
    width, hidden = d.width, d.hidden
    part = (1, 2 * width, BLOCK)
    square = (1, width * width // BLOCK, BLOCK)
    grads = [(width, 3 * width), (width, width), (width, hidden), (hidden, width)]
    shapes = [jax.ShapeDtypeStruct((2,) + g, F32) for g in grads]
    specs = [
        pl.BlockSpec((1, width, 3 * width // THIRDS), lambda l, t: (l, 0, t)),
        pl.BlockSpec((1, width, width), lambda l, t: (l, 0, 0)),
        pl.BlockSpec((1, width, hidden // THIRDS), lambda l, t: (l, 0, t)),
        pl.BlockSpec((1, hidden // THIRDS, width), lambda l, t: (l, t, 0)),
    ]
    for name in d.names:
        shapes.append(jax.ShapeDtypeStruct((2, d.sizes[name]), F32))
        specs.append(pl.BlockSpec((2, d.sizes[name]), lambda l, t: (0, 0)))
    for crop in crops:
        shapes.append(jax.ShapeDtypeStruct(crop.shape, crop.dtype))
        specs.append(pl.BlockSpec(memory_space=pl.ANY))
    return pl.pallas_call(
        functools.partial(cast_kernel, d),
        grid=(2, THIRDS),
        out_shape=shapes,
        in_specs=[
            pl.BlockSpec(part, lambda l, t: (l, t, 0)),
            pl.BlockSpec(part, lambda l, t: (l, THIRDS + t, 0)),
            pl.BlockSpec(square, lambda l, t: (l, d.tops[2] // square[1], 0)),
            pl.BlockSpec(square, lambda l, t: (l, d.tops[3] // square[1] + t, 0)),
            pl.BlockSpec((1, 2 * d.vec_rows, BLOCK), lambda l, t: (0, d.tops[4] // (2 * d.vec_rows), 0)),
        ]
        + [pl.BlockSpec(memory_space=pl.ANY)] * 4,
        out_specs=specs,
        scratch_shapes=[pltpu.VMEM(c.shape, c.dtype) for c in crops] + [pltpu.SemaphoreType.DMA((2, 4))],
        compiler_params=pltpu.CompilerParams(vmem_limit_bytes=62 * 1024 * 1024),
    )(sums, sums, sums, sums, sums, *crops)


def shards(wires, global_crops, local_crops, local_count, global_cotangent, local_cotangent, *weights):
    global_crops, global_cotangent = global_crops.transpose(1, 0, 2), global_cotangent.transpose(1, 0, 2)
    dims = Dims(global_crops, local_crops, weights[8].shape[2], wires)
    outs = run_kernel(
        local_count, (global_crops, local_crops, global_cotangent, local_cotangent) + weights, dims
    )
    mixer, output, expand, reduce, *rest = run_cast(outs[4], outs[:4], dims)
    vectors, crops = rest[:-4], rest[-4:]
    v = dict(zip(dims.names, vectors, strict=True))
    return (
        crops[0].transpose(1, 0, 2),
        crops[1],
        crops[2].transpose(1, 0, 2),
        crops[3],
        v["attend_gain"],
        v["attend_shift"],
        mixer,
        v["mixer_bias"],
        output,
        v["output_bias"],
        v["feed_gain"],
        v["feed_shift"],
        expand,
        v["expand_bias"],
        reduce,
        v["reduce_bias"],
    )


def solution(mesh):
    crops = P(("dp", "section"), None, None)
    return jax.shard_map(
        functools.partial(shards, wires_of(mesh)),
        mesh=mesh,
        in_specs=(crops, crops, P("dp"), crops, crops) + (P(),) * 12,
        out_specs=(crops,) * 4 + (P(),) * 12,
        check_vma=False,
    )
```

```python
import functools

import jax
import jax.numpy as jnp
from jax import lax
from jax.experimental import pallas as pl
from jax.experimental.pallas import tpu as pltpu
from jax.sharding import PartitionSpec as P

HEADS = 6
HEAD = 64
EPS = 1e-06
TILE = 16
LANES = 128
BLOCK = 256
LOG2E = 1.4426950408889634
F32 = jnp.float32
BF16 = jnp.bfloat16


def up_to(value, step):
    return -(-value // step) * step


def mm(left, right):
    return lax.dot_general(left, right, (((1,), (0,)), ((), ())), preferred_element_type=F32)


def mm_nt(left, right):
    return lax.dot_general(left, right, (((1,), (1,)), ((), ())), preferred_element_type=F32)


def mm_tn(left, right):
    return lax.dot_general(left, right, (((0,), (0,)), ((), ())), preferred_element_type=F32)


def norm(rows):
    centred = rows - jnp.mean(rows, -1, keepdims=True)
    scale = lax.rsqrt(jnp.mean(centred * centred, -1, keepdims=True) + EPS)
    return centred * scale, scale


def norm_back(grad, unit, scale, gain):
    slope = grad * gain
    first = jnp.mean(slope, -1, keepdims=True)
    second = jnp.mean(slope * unit, -1, keepdims=True)
    return scale * (slope - first - unit * second)


def gelu_parts(u):
    size = jnp.abs(u)
    d = 1.0 + (0.3275911 * 0.7071067811865476) * size
    t = pl.reciprocal(d, approx=True)
    t = t * (2.0 - d * t)
    poly = 0.5 * 1.061405429
    for a in (-1.453152027, 1.421413741, -0.284496736, 0.254829592):
        poly = poly * t + 0.5 * a
    bell = jnp.exp2((u * u) * (-0.5 * LOG2E))
    tail = poly * t * bell
    phi = jnp.where(u < 0.0, tail, 1.0 - tail)
    return u * phi, phi + (u * bell) * 0.3989422804014327


def fold8(value):
    rows, width = value.shape
    return jnp.sum(value.reshape(rows // 8, 8, width), 0)


def kernel(
    dims,
    counts,
    global_in_hbm,
    local_in_hbm,
    global_cot_hbm,
    local_cot_hbm,
    attend_gain,
    attend_shift,
    mixer_hbm,
    mixer_bias,
    output_hbm,
    output_bias,
    feed_gain,
    feed_shift,
    expand_hbm,
    expand_bias,
    reduce_hbm,
    reduce_bias,
    global_out_hbm,
    local_out_hbm,
    global_back_hbm,
    local_back_hbm,
    sums_out,
    global_in,
    local_in,
    global_cot,
    local_cot,
    global_out,
    local_out,
    global_back,
    local_back,
    mixer_weight,
    output_weight,
    expand_weight,
    reduce_weight,
    io_sem,
    sums,
    crop_s,
    x_s,
    unit_s,
    scale_s,
    norm_n,
    packed_s,
    power_s,
    inverse_s,
    mixed_s,
    act_s,
    slope_s,
    grad_s,
    grad_low,
    dup_s,
    aug_s,
    vec_s,
    side_s,
    acc_s,
    *wires,
):
    seq, group, width = dims.seq, dims.group, dims.width
    glen, llen = dims.glen, dims.llen
    n_global, n_local, n_seq = dims.n_global, dims.n_local, dims.n_seq
    hidden = dims.hidden
    count = counts[lax.axis_index("section")]
    pairs = HEADS // 2
    lane = lax.broadcasted_iota(jnp.int32, (1, LANES), 1)
    low_half = (lane < HEAD).astype(F32).astype(BF16)
    high_half = (lane >= HEAD).astype(F32).astype(BF16)
    score_scale = HEAD ** (-0.5)

    moves = [pltpu.make_async_copy(global_in_hbm, global_in, io_sem.at[0]), pltpu.make_async_copy(local_in_hbm, local_in, io_sem.at[1])]
    weights = ((mixer_hbm, mixer_weight), (output_hbm, output_weight), (expand_hbm, expand_weight), (reduce_hbm, reduce_weight))
    for layer in range(2):
        for source, target in weights:
            moves.append(pltpu.make_async_copy(source.at[layer], target.at[layer], io_sem.at[len(moves)]))
    moves += [
        pltpu.make_async_copy(global_cot_hbm, global_cot, io_sem.at[10]),
        pltpu.make_async_copy(local_cot_hbm, local_cot, io_sem.at[11]),
    ]
    outward = [
        pltpu.make_async_copy(global_out, global_out_hbm, io_sem.at[12]),
        pltpu.make_async_copy(local_out, local_out_hbm, io_sem.at[13]),
        pltpu.make_async_copy(global_back, global_back_hbm, io_sem.at[14]),
        pltpu.make_async_copy(local_back, local_back_hbm, io_sem.at[15]),
    ]
    for move in moves:
        move.start()

    net = Net(dims.wires)
    net.greet()
    n_stage = len(dims.wires)
    sets = dims.landing_sets
    landings, sems = wires[: n_stage * sum(sets)], wires[n_stage * sum(sets) :]
    flow = Flow(net)
    number = 0
    for layer in (1, 0):
        bounds = dims.bounds[layer]
        for i in range(len(bounds) - 1):
            shared = len(sets) == 1
            at = (i if shared else number) * n_stage
            own = [w.at[number] for w in sems[:4]] + [sems[4].at[i]]
            rows = pl.ds(bounds[i], bounds[i + 1] - bounds[i])
            turn = (1 - layer) if shared else None
            flow.chunks.append(
                Chunk(net, sums.at[layer, rows], sums_out.at[layer, rows], landings[at : at + n_stage], own, turn, layer, bounds[i + 1])
            )
            number += 1

    for s in range(n_seq):
        x_s[s, seq - 32 :, :] = jnp.zeros((32, width), F32)
        grad_s[s, seq - 32 :, :] = jnp.zeros((32, width), F32)
    row_id = lax.broadcasted_iota(jnp.int32, (seq, LANES), 0)
    col_id = lax.broadcasted_iota(jnp.int32, (seq, LANES), 1)
    row_crop = sum((row_id >= llen * j).astype(jnp.int32) for j in range(1, group + 1))
    far = jnp.float32(-1e30)
    zero = jnp.float32(0)
    for h in range(2):
        place = col_id - (1 - h) * HEAD
        used = (place >= 0) & (place <= group)
        aug_s[0, h, 0] = jnp.where(place == 0, jnp.float32(1), zero).astype(BF16)
        aug_s[0, h, 1] = jnp.where((place == 0) & (row_id >= glen), far, zero).astype(BF16)
        aug_s[1, h, 0] = jnp.where(place == row_crop, jnp.float32(1), zero).astype(BF16)
        aug_s[1, h, 1] = jnp.where(used & (place != row_crop), far, zero).astype(BF16)
    one_column = (lax.broadcasted_iota(jnp.int32, (seq, LANES), 1) == 0).astype(F32).astype(BF16)
    for s in range(n_seq):
        for i in range(4):
            norm_n[i, s, :, width:] = one_column
        for i in range(2):
            mixed_s[i, s, :, width:] = one_column

    def live_rows(g):
        rows = lax.broadcasted_iota(jnp.int32, (seq, 1), 0)
        return (rows < llen * jnp.clip(count - g * group, 0, group)).astype(F32)

    def take_crops(crops, locals_, target):
        crop_s[...] = crops[...].astype(F32)
        for s in range(n_global):
            target[s, 0:glen, :] = crop_s[:, s, :]
        for j in range(n_local):
            s, at = n_global + j // group, llen * (j % group)
            target[s, at : at + llen, :] = locals_[j].astype(F32)

    def take_cotangents():
        moves[10].wait()
        moves[11].wait()
        take_crops(global_cot, local_cot, grad_s)
        for s in range(n_global, n_seq):
            grad_s[s] = grad_s[s] * live_rows(s - n_global)

    moves[0].wait()
    moves[1].wait()
    take_crops(global_in, local_in, x_s)

    def row(ref, layer):
        return ref[...].astype(F32)[layer : layer + 1]

    slopes = (slope_s, dup_s)

    def start_back(s, grad):
        grad_low[s] = grad.astype(BF16)
        acc_s[2] = acc_s[2] + fold8(grad)

    def end_back(s, grad, unit, scale, gain, dh):
        unit = unit.astype(F32)
        acc_s[0] = acc_s[0] + fold8(dh * unit)
        acc_s[1] = acc_s[1] + fold8(dh)
        grad = (grad + norm_back(dh, unit, scale, gain)).astype(BF16)
        grad_low[s] = grad
        grad_s[s] = grad.astype(F32)

    def block_of(c, size=BLOCK):
        return pl.ds(pl.multiple_of(c * size, LANES), size)

    def product(left, right, cols, first):
        total = None
        for s in range(n_seq):
            term = mm_tn(left[s, :, 0:first], right[s, :, cols])
            total = term if total is None else total + term
        return total

    for layer in range(2):
        gain, shift = row(attend_gain, layer), row(attend_shift, layer)
        bias = row(mixer_bias, layer)
        bias = jnp.concatenate([bias[:, :width], jnp.zeros((1, width), F32), bias[:, width:]], 1)
        out_bias = row(output_bias, layer)
        gain2, shift2 = row(feed_gain, layer), row(feed_shift, layer)
        bias_down = row(reduce_bias, layer)

        def attend(s, _):
            x = x_s[s]
            unit, scale = norm(x)
            unit_s[2 * layer, s] = unit.astype(BF16)
            scale_s[2 * layer, s] = scale
            normed = (unit * gain + shift).astype(BF16)
            norm_n[2 * layer, s, :, 0:width] = normed
            packed = (mm(normed, mixer_weight[layer]) + bias).astype(BF16)
            packed_s[layer, s] = packed
            kind = jnp.where(s < n_global, 0, 1)
            mixed = []
            for p in range(pairs):
                at = p * LANES
                query = packed[:, at : at + LANES]
                key = packed[:, width + at : width + at + LANES]
                value = packed[:, 2 * width + at : 2 * width + at + LANES]
                total = None
                for h, half in enumerate((low_half, high_half)):
                    scores = mm_nt(query * half + aug_s[kind, h, 0], key * half + aug_s[kind, h, 1]) * (score_scale * LOG2E)
                    power = jnp.exp2(scores - jnp.max(scores, -1, keepdims=True)).astype(BF16)
                    power_s[layer, s, 2 * p + h] = power
                    spread = jnp.broadcast_to(half, (seq, LANES))
                    term = mm(power, jnp.concatenate([value * half, spread], 1))
                    total = term if total is None else total + term
                inverse = 1.0 / total[:, LANES:]
                inverse_s[layer, s, :, at : at + LANES] = inverse
                mixed.append((total[:, :LANES] * inverse).astype(BF16))
            mixed = jnp.concatenate(mixed, 1)
            mixed_s[layer, s, :, 0:width] = mixed
            x = x + mm(mixed, output_weight[layer]) + out_bias
            x_s[s] = x.astype(BF16).astype(F32)
            return 0

        moves[2 + 4 * layer].wait()
        moves[3 + 4 * layer].wait()
        lax.fori_loop(0, n_seq, attend, 0)

        def feed(s, _):
            x = x_s[s]
            unit, scale = norm(x)
            normed = (unit * gain2 + shift2).astype(BF16)
            norm_n[2 * layer + 1, s, :, 0:width] = normed
            unit_s[2 * layer + 1, s] = unit.astype(BF16)
            scale_s[2 * layer + 1, s] = scale
            if layer == 1:
                start_back(s, grad_s[s])

            def up_block(c, _):
                cols = block_of(c)
                up = mm(norm_n[2 * layer + 1, s, :, 0:width], expand_weight[layer, :, cols])
                act, slope = gelu_parts(up + expand_bias[:, cols].astype(F32)[layer : layer + 1])
                act_s[layer, s, :, cols] = act.astype(BF16)
                slopes[layer][s, :, cols] = slope.astype(BF16)
                return 0

            lax.fori_loop(0, hidden // BLOCK, up_block, 0)
            x = x_s[s] + mm(act_s[layer, s], reduce_weight[layer]) + bias_down
            x_s[s] = x.astype(BF16).astype(F32)
            return 0

        moves[4 + 4 * layer].wait()
        moves[5 + 4 * layer].wait()
        if layer == 1:
            take_cotangents()
            acc_s[...] = jnp.zeros_like(acc_s)
        lax.fori_loop(0, n_seq, feed, 0)

    for s in range(n_global):
        crop_s[:, s, :] = x_s[s, 0:glen, :]
    global_out[...] = crop_s[...].astype(BF16)
    for j in range(n_local):
        s, at = n_global + j // group, llen * (j % group)
        alive = (count > j).astype(F32)
        local_out[j] = (x_s[s, at : at + llen, :] * alive).astype(BF16)
    outward[0].start()
    outward[1].start()

    def put_vector(at, value):
        for c in range(0, value.shape[1], BLOCK):
            piece = value[:, c : c + BLOCK]
            vec_s[at + c // BLOCK : at + c // BLOCK + 1, 0 : piece.shape[1]] = piece

    def put_third(layer, top, t, total):
        at = pl.multiple_of(top + t * (width + fold), TILE)
        sums[layer, pl.ds(at, width), :] = total[:width, :BLOCK].astype(BF16)
        at = pl.ds(pl.multiple_of(at + width, TILE), fold)
        sums[layer, at, 0:LANES] = total[:fold, BLOCK:].astype(BF16)
        sums[layer, at, LANES:] = total[fold:width, BLOCK:].astype(BF16)
        side_s[t] = total[width : width + 8]

    blocks = hidden // BLOCK
    fold = width // 2
    tops = dims.tops
    net.wait_greeting()
    for layer, used in ((1, tops[4]), (0, tops[4] + 2 * dims.vec_rows)):
        if dims.rows > used:
            sums[layer, used:, :] = jnp.zeros((dims.rows - used, BLOCK), BF16)
    for layer in (1, 0):
        vec_s[...] = jnp.zeros_like(vec_s)
        gain2, gain = row(feed_gain, layer), row(attend_gain, layer)
        put_vector(dims.at["reduce_bias"], jnp.sum(acc_s[2], 0, keepdims=True))

        def reduce_block(c, _):
            total = product(grad_low, act_s.at[layer], block_of(c), width)
            sums[layer, pl.ds(pl.multiple_of(tops[0] + c * width, TILE), width), :] = total.astype(BF16)
            flow.ticks(c, blocks, 0.45, layer, [tops[0] + (i + 1) * width for i in range(blocks)])
            return 0

        lax.fori_loop(0, blocks, reduce_block, 0)

        def feed_back(s, _):
            def dup_block(c, _):
                cols = block_of(c)
                dact = mm_nt(grad_low[s], reduce_weight[layer, cols, :])
                dup_s[s, :, cols] = (dact * slopes[layer][s, :, cols].astype(F32)).astype(BF16)
                return 0

            lax.fori_loop(0, blocks, dup_block, 0)
            flow.ticks(s, n_seq, 0.6)
            return 0

        lax.fori_loop(0, n_seq, feed_back, 0)

        def expand_block(c, _):
            total = product(norm_n.at[2 * layer + 1], dup_s, block_of(c), width + TILE)
            sums[layer, pl.ds(pl.multiple_of(tops[1] + c * width, TILE), width), :] = total[:width].astype(BF16)
            side_s[c, :, 0:BLOCK] = total[width : width + 8]
            flow.ticks(c, blocks, 0.45, layer, [tops[1] + (i + 1) * width for i in range(blocks)])
            return 0

        lax.fori_loop(0, blocks, expand_block, 0)
        for c in range(blocks):
            at = dims.at["expand_bias"] + c
            vec_s[at : at + 1, :] = side_s[c, 0:1, 0:BLOCK]

        def feed_norm_back(s, _):
            dh = mm_nt(dup_s[s], expand_weight[layer])
            end_back(s, grad_s[s], unit_s[2 * layer + 1, s], scale_s[2 * layer + 1, s], gain2, dh)
            flow.ticks(s, n_seq, 0.7)
            return 0

        acc_s[0:2] = jnp.zeros((2, 8, width), F32)
        lax.fori_loop(0, n_seq, feed_norm_back, 0)
        put_vector(dims.at["feed_gain"], jnp.sum(acc_s[0], 0, keepdims=True))
        put_vector(dims.at["feed_shift"], jnp.sum(acc_s[1], 0, keepdims=True))

        put_third(layer, tops[2], 0, product(mixed_s.at[layer], grad_low, slice(0, width), width + TILE))
        put_vector(dims.at["output_bias"], side_s[0, 0:1, :])
        flow.ready(layer, tops[3])
        flow.tick(0.8)

        def attend_back(s, _):
            dmixed = mm_nt(grad_low[s], output_weight[layer])
            parts = [None] * (3 * pairs)
            for p in range(pairs):
                at = p * LANES
                query = packed_s[layer, s, :, at : at + LANES]
                key = packed_s[layer, s, :, width + at : width + at + LANES]
                value = packed_s[layer, s, :, 2 * width + at : 2 * width + at + LANES]
                dm = dmixed[:, at : at + LANES] * inverse_s[layer, s, :, at : at + LANES]
                inner = -(dm * mixed_s[layer, s, :, at : at + LANES].astype(F32)).astype(BF16)
                dm = dm.astype(BF16)
                wide_value = jnp.concatenate([value, jnp.ones_like(value)], 1)
                dq = dk = dv = None
                for h, half in enumerate((low_half, high_half)):
                    power = power_s[layer, s, 2 * p + h]
                    dm_half = dm * half
                    left = jnp.concatenate([dm_half, inner * half], 1)
                    ds = (power.astype(F32) * mm_nt(left, wide_value)).astype(BF16)
                    terms = (mm(ds, key * half), mm_tn(ds, query * half), mm_tn(power, dm_half))
                    dq = terms[0] if dq is None else dq + terms[0]
                    dk = terms[1] if dk is None else dk + terms[1]
                    dv = terms[2] if dv is None else dv + terms[2]
                parts[p] = (dq * score_scale).astype(BF16)
                parts[pairs + p] = (dk * score_scale).astype(BF16)
                parts[2 * pairs + p] = dv.astype(BF16)
            dup_s[s, :, 0 : 3 * width] = jnp.concatenate(parts, 1)
            flow.ticks(s, n_seq, 1.7)
            return 0

        lax.fori_loop(0, n_seq, attend_back, 0)

        def mixer_third(t, _):
            total = product(norm_n.at[2 * layer], dup_s, block_of(t, width), width + TILE)
            put_third(layer, tops[3], t, total)
            flow.ticks(t, 3, 0.8, layer, [tops[3] + (i + 1) * (width + fold) for i in range(3)])
            return 0

        lax.fori_loop(0, 3, mixer_third, 0)
        put_vector(dims.at["mixer_bias"], jnp.concatenate([side_s[0, 0:1, :], side_s[2, 0:1, :]], 1))
        flow.ready(layer, dims.rows if layer == 1 else tops[4])

        def attend_norm_back(s, _):
            dh = mm_nt(dup_s[s, :, 0 : 3 * width], mixer_weight[layer])
            end_back(s, grad_s[s], unit_s[2 * layer, s], scale_s[2 * layer, s], gain, dh)
            if layer == 1:
                start_back(s, grad_s[s])
            flow.ticks(s, n_seq, 0.6)
            return 0

        acc_s[...] = jnp.zeros_like(acc_s)
        lax.fori_loop(0, n_seq, attend_norm_back, 0)
        put_vector(dims.at["attend_gain"], jnp.sum(acc_s[0], 0, keepdims=True))
        put_vector(dims.at["attend_shift"], jnp.sum(acc_s[1], 0, keepdims=True))
        at = tops[4] + layer * dims.vec_rows
        sums[0, at : at + dims.vec_rows, :] = vec_s[...].astype(BF16)
        if layer == 0:
            flow.ready(0, dims.rows)

    for s in range(n_global):
        crop_s[:, s, :] = grad_s[s, 0:glen, :]
    global_back[...] = crop_s[...].astype(BF16)
    for j in range(n_local):
        s, at = n_global + j // group, llen * (j % group)
        local_back[j] = grad_s[s, at : at + llen, :].astype(BF16)
    outward[2].start()
    outward[3].start()
    flow.drain()
    for move in outward:
        move.wait()


class Wire:
    def __init__(self, size, first, second):
        self.size, self.first, self.second = size, first, second


def wires_of(mesh):
    names = mesh.axis_names
    places = {}
    for axis, name in enumerate(names):
        line = [mesh.devices[tuple(i if a == axis else 0 for a in range(2))] for i in range(mesh.devices.shape[axis])]
        spots = [(d.core_on_chip,) + tuple(d.coords) for d in line]
        found, total = [], 1
        for k in range(4):
            values = sorted({p[k] for p in spots})
            if len(values) > 1:
                stride = next(i for i, p in enumerate(spots) if p[k] != spots[0][k])
                found.append((k, axis, stride, len(values)))
                total *= len(values)
        good = total == len(line)
        for k, _, stride, size in found:
            values = [p[k] for p in spots]
            good = good and all(v == values[i // stride % size * stride] for i, v in enumerate(values))
        if not good:
            found = [(4 + axis, axis, 1, len(line))]
        for k, axis, stride, size in found:
            places[k] = (axis, stride, size)
    wires = []
    if 0 in places:
        wires.append(Wire(places[0][2], places[0], places[0]))
    if 0 in places and 1 in places and 2 in places and places[1][2] == places[2][2]:
        wires.append(Wire(places[1][2], places[1], places[2]))
        wires.append(Wire(places[1][2], places[2], places[1]))
        order = [3, 4, 5]
    else:
        order = [1, 2, 3, 4, 5]
    for k in order:
        if k in places:
            wires.append(Wire(places[k][2], places[k], places[k]))
    return wires


class Net:
    def __init__(self, wires):
        self.axes = ("dp", "section")
        self.here = [lax.axis_index(a) for a in self.axes]
        self.wires = wires
        first = wires[0]
        odd = self.spot(first.first) % 2 if first.size == 2 else 0
        self.odd = odd
        self.at = []
        for w in wires:
            a, b = self.spot(w.first), self.spot(w.second)
            self.at.append(a if w.first == w.second else a + odd * (b - a))

    def spot(self, place):
        axis, stride, size = place
        return self.here[axis] // stride % size

    def peer(self, stage, k):
        w = self.wires[stage]
        place = (self.at[stage] + k) % w.size
        move = place - self.at[stage]
        target = list(self.here)
        if w.first == w.second:
            target[w.first[0]] = target[w.first[0]] + move * w.first[1]
        else:
            target[w.first[0]] = target[w.first[0]] + move * w.first[1] * (1 - self.odd)
            target[w.second[0]] = target[w.second[0]] + move * w.second[1] * self.odd
        return tuple(target), place

    def greet(self):
        barrier = pltpu.get_barrier_semaphore()
        for stage, w in enumerate(self.wires):
            for k in range(1, w.size):
                pl.semaphore_signal(barrier, inc=1, device_id=self.peer(stage, k)[0], device_id_type=pl.DeviceIdType.MESH)

    def wait_greeting(self):
        pl.semaphore_wait(pltpu.get_barrier_semaphore(), sum(w.size - 1 for w in self.wires))


class Chunk:
    def __init__(self, net, sums, out, landing, sems, turn, layer, end):
        self.net, self.sums, self.out, self.landing = net, sums, out, landing
        self.send, self.recv, self.local, self.sent, self.free = sems
        self.turn = turn
        self.layer, self.end = layer, end
        self.due = None
        size, start = sums.shape[0], 0
        self.unit = size
        for w in net.wires:
            self.unit //= w.size
        self.size, self.start = [], []
        for stage, w in enumerate(net.wires):
            size //= w.size
            self.size.append(size)
            self.start.append((start, size))
            start = start + net.at[stage] * size
        self.own = start
        self.stages = len(net.wires)
        self.step = 0
        self.sem_at, at = {}, 0
        for phase in range(2):
            for stage, w in enumerate(net.wires):
                for k in range(1, w.size):
                    self.sem_at[phase, stage, k] = at
                    at += 1

    def rows(self, stage, place):
        start, size = self.start[stage]
        return pl.ds(pl.multiple_of(start + place * size, TILE), size)

    def copy(self, phase, stage, k):
        target, place = self.net.peer(stage, k)
        at = self.sem_at[phase, stage, k]
        if phase == 0:
            source, to = self.sums.at[self.rows(stage, place)], self.landing[stage].at[k - 1]
        else:
            rows = self.rows(stage, self.net.at[stage])
            source = to = self.sums.at[rows]
        return pltpu.make_async_remote_copy(
            src_ref=source,
            dst_ref=to,
            send_sem=self.send.at[at],
            recv_sem=self.recv.at[at],
            device_id=target,
            device_id_type=pl.DeviceIdType.MESH,
        )

    def arrival(self, stage, k):
        target, place = self.net.peer(stage, self.net.wires[stage].size - k)
        at = self.sem_at[1, stage, k]
        landed = self.sums.at[self.rows(stage, place)]
        return pltpu.make_async_remote_copy(
            src_ref=landed,
            dst_ref=landed,
            send_sem=self.send.at[at],
            recv_sem=self.recv.at[at],
            device_id=target,
            device_id_type=pl.DeviceIdType.MESH,
        )

    def start_stage(self, phase, stage):
        if phase == 0 and self.turn == 1:
            pl.semaphore_wait(self.free.at[stage], self.net.wires[stage].size - 1)
        if phase == 1:
            pl.semaphore_wait(self.sent.at[stage], self.net.wires[stage].size - 1)
        for k in range(1, self.net.wires[stage].size):
            self.copy(phase, stage, k).start()

    def load(self):
        last = self.stages - 1
        stage = self.step if self.step <= last else 2 * self.stages - 1 - self.step
        peers = self.net.wires[stage].size - 1
        row = BLOCK * 2
        if stage == 0:
            return 0, self.size[0] * row / 4
        if stage == last:
            return 2, self.size[stage] * (peers + 1) ** 2 / 2 * row
        return 1, self.size[stage] * peers * row

    def begin(self):
        self.start_stage(0, 0)

    def out_copy(self):
        return pltpu.make_async_copy(self.sums, self.out, self.local.at[0])

    def advance(self):
        step = self.step
        self.step += 1
        if step < self.stages:
            peers = range(1, self.net.wires[step].size)
            for k in peers:
                self.copy(0, step, k).wait_recv()
            base = self.start[step][0] + self.net.at[step] * self.size[step]
            landing = self.landing[step]

            count = self.size[step] // self.unit
            while count % 2 == 0 and self.size[step] // count < 128:
                count //= 2
            size = self.size[step] // count

            def add(i, _):
                at = pl.ds(pl.multiple_of(base + i * size, TILE), size)
                here = [landing[k - 1, pl.ds(pl.multiple_of(i * size, TILE), size), :] for k in peers]
                if len(here) == 1:
                    self.sums[at, :] = self.sums[at, :] + here[0]
                else:
                    total = self.sums[at, :].astype(F32)
                    for part in here:
                        total = total + part.astype(F32)
                    self.sums[at, :] = total.astype(BF16)
                return 0

            lax.fori_loop(0, count, add, 0)
            for k in peers:
                self.copy(0, step, k).wait_send()
                target = self.net.peer(step, k)[0]
                pl.semaphore_signal(self.sent.at[step], inc=1, device_id=target, device_id_type=pl.DeviceIdType.MESH)
                if self.turn == 0:
                    pl.semaphore_signal(self.free.at[step], inc=1, device_id=target, device_id_type=pl.DeviceIdType.MESH)
            if step + 1 < self.stages:
                self.start_stage(0, step + 1)
            else:
                self.start_stage(1, step)
        else:
            stage = 2 * self.stages - 1 - step
            for k in range(1, self.net.wires[stage].size):
                self.arrival(stage, k).wait_recv()
            if stage > 0:
                self.start_stage(1, stage - 1)
            else:
                self.out_copy().start()

    def finish(self):
        for phase, stage, k in self.sem_at:
            if phase == 1:
                self.copy(phase, stage, k).wait_send()
        self.out_copy().wait()


LATENCY = 2.0
RATE = 80e3
STEP = 0.4


class Flow:
    def __init__(self, net):
        self.chunks, self.now, self.waiting, self.free = [], 0.0, 0, [0.0] * 3

    def book(self, chunk):
        kind, size = chunk.load()
        self.free[kind] = max(self.now, self.free[kind]) + size / RATE
        chunk.due = self.free[kind] + LATENCY

    def startable(self, layer, rows):
        found = []
        while self.waiting < len(self.chunks):
            chunk = self.chunks[self.waiting]
            if chunk.layer != layer or chunk.end > rows:
                break
            found.append(chunk)
            self.waiting += 1
        return found

    def begin(self, chunks):
        for chunk in chunks:
            chunk.begin()
            self.book(chunk)

    def ready(self, layer, rows):
        self.begin(self.startable(layer, rows))

    def due(self):
        return sorted((c for c in self.chunks if c.due is not None and c.due <= self.now), key=lambda c: c.due)

    def take(self):
        while self.due():
            chunk = self.due()[0]
            chunk.advance()
            self.now += STEP
            if chunk.step < 2 * chunk.stages:
                self.book(chunk)
            else:
                chunk.due = None

    def tick(self, time):
        self.now += time
        self.take()

    def ticks(self, s, count, time, layer=None, ends=None):
        for i in range(count):
            self.now += time
            chunks = self.startable(layer, ends[i]) if ends else []
            if chunks or self.due():

                @pl.when(s == i)
                def _():
                    self.begin(chunks)
                    self.take()

    def drain(self):
        while any(c.due is not None for c in self.chunks):
            self.now = max(self.now, min(c.due for c in self.chunks if c.due is not None))
            self.take()
        for chunk in self.chunks:
            chunk.finish()


class Dims:
    def __init__(self, global_crops, local_crops, hidden, wires):
        self.wires = wires
        self.glen, self.n_global, self.width = global_crops.shape
        self.n_local, self.llen, _ = local_crops.shape
        self.hidden = hidden
        self.seq = up_to(self.glen, TILE)
        self.group = self.seq // self.llen
        while self.n_local % self.group:
            self.group -= 1
        self.n_seq = self.n_global + self.n_local // self.group
        sizes = (
            ("attend_gain", self.width),
            ("attend_shift", self.width),
            ("mixer_bias", 2 * self.width),
            ("output_bias", self.width),
            ("feed_gain", self.width),
            ("feed_shift", self.width),
            ("expand_bias", hidden),
            ("reduce_bias", self.width),
        )
        self.names, self.sizes = [name for name, _ in sizes], dict(sizes)
        self.at, row = {}, 0
        for name, size in sizes:
            self.at[name] = row
            row += -(-size // BLOCK)
        self.vec_rows = 2 * TILE
        assert row <= self.vec_rows and self.width * hidden % self.vec_rows == 0
        step = TILE
        for w in wires:
            step *= w.size
        ff = self.width * hidden // BLOCK
        square = self.width * self.width // BLOCK
        self.tops = (0, ff, 2 * ff, 2 * ff + square, 2 * ff + 4 * square)
        self.rows = up_to(self.tops[4] + 2 * self.vec_rows, step)
        parts = self.rows // step
        cuts = ((0, 4, 7, 10, 12, 14), (0, 4, 10, 14))
        self.bounds = [[c * step for c in sorted({parts * k // 14 for k in layer})] for layer in cuts]
        self.landing_sets = [len(b) - 1 for b in self.bounds[::-1]]
        if self.bounds[0] == self.bounds[1]:
            self.landing_sets = self.landing_sets[:1]
        self.n_chunk = sum(len(b) - 1 for b in self.bounds)


HEAVY = (6, 8, 12, 14)


def run_kernel(counts, arrays, dims):
    d = dims
    n, seq, width, hidden = d.n_seq, d.seq, d.width, d.hidden
    crops = [jax.ShapeDtypeStruct(a.shape, BF16) for a in arrays[:2]]
    outs = crops + crops
    outs += [jax.ShapeDtypeStruct((2, d.rows, BLOCK), BF16)]
    scratch = [pltpu.VMEM(a.shape, BF16) for a in tuple(arrays[:4]) * 2]
    scratch += [pltpu.VMEM(arrays[i].shape, BF16) for i in HEAVY]
    scratch += [
        pltpu.SemaphoreType.DMA((16,)),
        pltpu.VMEM((2, d.rows, BLOCK), BF16),
        pltpu.VMEM((d.glen, d.n_global, width), F32),
        pltpu.VMEM((n, seq, width), F32),
        pltpu.VMEM((4, n, seq, width), BF16),
        pltpu.VMEM((4, n, seq, 1), F32),
        pltpu.VMEM((4, n, seq, width + LANES), BF16),
        pltpu.VMEM((2, n, seq, 3 * width), BF16),
        pltpu.VMEM((2, n, HEADS, seq, seq), BF16),
        pltpu.VMEM((2, n, seq, width), F32),
        pltpu.VMEM((2, n, seq, width + LANES), BF16),
        pltpu.VMEM((2, n, seq, hidden), BF16),
        pltpu.VMEM((n, seq, hidden), BF16),
        pltpu.VMEM((n, seq, width), F32),
        pltpu.VMEM((n, seq, width), BF16),
        pltpu.VMEM((n, seq, hidden), BF16),
        pltpu.VMEM((2, 2, 2, seq, LANES), BF16),
        pltpu.VMEM((d.vec_rows, BLOCK), F32),
        pltpu.VMEM((hidden // BLOCK, 8, width), F32),
        pltpu.VMEM((3, 8, width), F32),
    ]
    for layer in (1, 0)[: len(d.landing_sets)]:
        for first, end in zip(d.bounds[layer], d.bounds[layer][1:]):
            rows = end - first
            for w in d.wires:
                rows //= w.size
                scratch.append(pltpu.VMEM((w.size - 1, rows, BLOCK), BF16))
    peers = 2 * sum(w.size - 1 for w in d.wires)
    scratch += [
        pltpu.SemaphoreType.DMA((d.n_chunk, peers)),
        pltpu.SemaphoreType.DMA((d.n_chunk, peers)),
        pltpu.SemaphoreType.DMA((d.n_chunk, 1)),
        pltpu.SemaphoreType.REGULAR((d.n_chunk, len(d.wires))),
        pltpu.SemaphoreType.REGULAR((d.n_chunk, len(d.wires))),
    ]
    vmem = pl.BlockSpec(memory_space=pltpu.VMEM)
    anywhere = pl.BlockSpec(memory_space=pl.ANY)
    return pl.pallas_call(
        functools.partial(kernel, d),
        out_shape=outs,
        in_specs=[pl.BlockSpec(memory_space=pltpu.SMEM)]
        + [anywhere if i < 4 or i in HEAVY else vmem for i in range(len(arrays))],
        out_specs=[anywhere] * len(outs),
        scratch_shapes=scratch,
        compiler_params=pltpu.CompilerParams(
            vmem_limit_bytes=63 * 1024 * 1024, collective_id=0, has_side_effects=True
        ),
    )(counts, *arrays)


THIRDS = 3


def cast_kernel(dims, reduce, expand, output, mixer, vectors, *rest):
    crops, outs, held, sems = rest[:4], rest[4:-9], rest[-5:-1], rest[-1]
    step = pl.program_id(0) * THIRDS + pl.program_id(1)
    loads = [pltpu.make_async_copy(a, b, sems.at[0, i]) for i, (a, b) in enumerate(zip(crops, held, strict=True))]
    stores = [pltpu.make_async_copy(a, b, sems.at[1, i]) for i, (a, b) in enumerate(zip(held, rest[-9:-5], strict=True))]

    @pl.when(step == 0)
    def _():
        for copy in loads:
            copy.start()

    @pl.when(step == 1)
    def _():
        for load, store in zip(loads, stores, strict=True):
            load.wait()
            store.start()

    mixer_grad, output_grad, expand_grad, reduce_grad = outs[:4]
    width = dims.width
    fold = width // 2
    for b in range(2):
        rows = slice(b * width, (b + 1) * width)
        cols = slice(b * BLOCK, (b + 1) * BLOCK)
        expand_grad[0, :, cols] = expand[0, rows, :].astype(F32)
        reduce_grad[0, cols, :] = reduce[0, rows, :].T.astype(F32)
    for source, target in ((mixer, mixer_grad), (output, output_grad)):
        target[0, :, 0:BLOCK] = source[0, 0:width, :].astype(F32)
        target[0, 0:fold, BLOCK:] = source[0, width:, 0:LANES].astype(F32)
        target[0, fold:, BLOCK:] = source[0, width:, LANES:].astype(F32)

    @pl.when(step == 2 * THIRDS - 1)
    def _():
        for ref, name in zip(outs[4:], dims.names, strict=True):
            size = ref.shape[1]
            for c in range(0, size, BLOCK):
                at = dims.at[name] + c // BLOCK
                piece = min(BLOCK, size - c)
                for layer in range(2):
                    ref[layer : layer + 1, c : c + piece] = vectors[0].astype(F32)[at + layer * dims.vec_rows :][:1, 0:piece]
        for store in stores:
            store.wait()


def run_cast(sums, crops, dims):
    d = dims
    width, hidden = d.width, d.hidden
    part = (1, 2 * width, BLOCK)
    square = (1, width * width // BLOCK, BLOCK)
    grads = [(width, 3 * width), (width, width), (width, hidden), (hidden, width)]
    shapes = [jax.ShapeDtypeStruct((2,) + g, F32) for g in grads]
    specs = [
        pl.BlockSpec((1, width, 3 * width // THIRDS), lambda l, t: (l, 0, t)),
        pl.BlockSpec((1, width, width), lambda l, t: (l, 0, 0)),
        pl.BlockSpec((1, width, hidden // THIRDS), lambda l, t: (l, 0, t)),
        pl.BlockSpec((1, hidden // THIRDS, width), lambda l, t: (l, t, 0)),
    ]
    for name in d.names:
        shapes.append(jax.ShapeDtypeStruct((2, d.sizes[name]), F32))
        specs.append(pl.BlockSpec((2, d.sizes[name]), lambda l, t: (0, 0)))
    for crop in crops:
        shapes.append(jax.ShapeDtypeStruct(crop.shape, crop.dtype))
        specs.append(pl.BlockSpec(memory_space=pl.ANY))
    return pl.pallas_call(
        functools.partial(cast_kernel, d),
        grid=(2, THIRDS),
        out_shape=shapes,
        in_specs=[
            pl.BlockSpec(part, lambda l, t: (l, t, 0)),
            pl.BlockSpec(part, lambda l, t: (l, THIRDS + t, 0)),
            pl.BlockSpec(square, lambda l, t: (l, d.tops[2] // square[1], 0)),
            pl.BlockSpec(square, lambda l, t: (l, d.tops[3] // square[1] + t, 0)),
            pl.BlockSpec((1, 2 * d.vec_rows, BLOCK), lambda l, t: (0, d.tops[4] // (2 * d.vec_rows), 0)),
        ]
        + [pl.BlockSpec(memory_space=pl.ANY)] * 4,
        out_specs=specs,
        scratch_shapes=[pltpu.VMEM(c.shape, c.dtype) for c in crops] + [pltpu.SemaphoreType.DMA((2, 4))],
        compiler_params=pltpu.CompilerParams(vmem_limit_bytes=62 * 1024 * 1024),
    )(sums, sums, sums, sums, sums, *crops)


def shards(wires, global_crops, local_crops, local_count, global_cotangent, local_cotangent, *weights):
    global_crops, global_cotangent = global_crops.transpose(1, 0, 2), global_cotangent.transpose(1, 0, 2)
    dims = Dims(global_crops, local_crops, weights[8].shape[2], wires)
    outs = run_kernel(
        local_count, (global_crops, local_crops, global_cotangent, local_cotangent) + weights, dims
    )
    mixer, output, expand, reduce, *rest = run_cast(outs[4], outs[:4], dims)
    vectors, crops = rest[:-4], rest[-4:]
    v = dict(zip(dims.names, vectors, strict=True))
    return (
        crops[0].transpose(1, 0, 2),
        crops[1],
        crops[2].transpose(1, 0, 2),
        crops[3],
        v["attend_gain"],
        v["attend_shift"],
        mixer,
        v["mixer_bias"],
        output,
        v["output_bias"],
        v["feed_gain"],
        v["feed_shift"],
        expand,
        v["expand_bias"],
        reduce,
        v["reduce_bias"],
    )


def solution(mesh):
    crops = P(("dp", "section"), None, None)
    return jax.shard_map(
        functools.partial(shards, wires_of(mesh)),
        mesh=mesh,
        in_specs=(crops, crops, P("dp"), crops, crops) + (P(),) * 12,
        out_specs=(crops,) * 4 + (P(),) * 12,
        check_vma=False,
    )
```

```python
import functools

import jax
import jax.numpy as jnp
from jax import lax
from jax.experimental import pallas as pl
from jax.experimental.pallas import tpu as pltpu
from jax.sharding import PartitionSpec as P

HEADS = 6
HEAD = 64
EPS = 1e-06
TILE = 16
LANES = 128
BLOCK = 256
LOG2E = 1.4426950408889634
F32 = jnp.float32
BF16 = jnp.bfloat16


def up_to(value, step):
    return -(-value // step) * step


def mm(left, right):
    return lax.dot_general(left, right, (((1,), (0,)), ((), ())), preferred_element_type=F32)


def mm_nt(left, right):
    return lax.dot_general(left, right, (((1,), (1,)), ((), ())), preferred_element_type=F32)


def mm_tn(left, right):
    return lax.dot_general(left, right, (((0,), (0,)), ((), ())), preferred_element_type=F32)


def norm(rows):
    centred = rows - jnp.mean(rows, -1, keepdims=True)
    scale = lax.rsqrt(jnp.mean(centred * centred, -1, keepdims=True) + EPS)
    return centred * scale, scale


def norm_back(grad, unit, scale, gain):
    slope = grad * gain
    first = jnp.mean(slope, -1, keepdims=True)
    second = jnp.mean(slope * unit, -1, keepdims=True)
    return scale * (slope - first - unit * second)


def gelu_parts(u):
    size = jnp.abs(u)
    d = 1.0 + (0.3275911 * 0.7071067811865476) * size
    t = pl.reciprocal(d, approx=True)
    t = t * (2.0 - d * t)
    poly = 0.5 * 1.061405429
    for a in (-1.453152027, 1.421413741, -0.284496736, 0.254829592):
        poly = poly * t + 0.5 * a
    bell = jnp.exp2((u * u) * (-0.5 * LOG2E))
    tail = poly * t * bell
    phi = jnp.where(u < 0.0, tail, 1.0 - tail)
    return u * phi, phi + (u * bell) * 0.3989422804014327


def add_to(total, value):
    return value if total is None else total + value


def fold8(value):
    rows, width = value.shape
    return jnp.sum(value.reshape(rows // 8, 8, width), 0)


def kernel(
    dims,
    counts,
    global_in_hbm,
    local_in_hbm,
    global_cot_hbm,
    local_cot_hbm,
    attend_gain,
    attend_shift,
    mixer_hbm,
    mixer_bias,
    output_hbm,
    output_bias,
    feed_gain,
    feed_shift,
    expand_hbm,
    expand_bias,
    reduce_hbm,
    reduce_bias,
    global_out_hbm,
    local_out_hbm,
    global_back_hbm,
    local_back_hbm,
    sums_out,
    global_in,
    local_in,
    global_cot,
    local_cot,
    global_out,
    local_out,
    global_back,
    local_back,
    mixer_weight,
    output_weight,
    expand_weight,
    reduce_weight,
    io_sem,
    sums,
    crop_s,
    x_s,
    unit_s,
    scale_s,
    norm_n,
    packed_s,
    power_s,
    inverse_s,
    mixed_s,
    act_s,
    slope_s,
    grad_s,
    grad_low,
    dup_s,
    aug_s,
    vec_s,
    acc_s,
    *wires,
):
    seq, group, width = dims.seq, dims.group, dims.width
    glen, llen = dims.glen, dims.llen
    n_global, n_local, n_seq = dims.n_global, dims.n_local, dims.n_seq
    hidden = dims.hidden
    count = counts[lax.axis_index("section")]
    pairs = HEADS // 2
    lane = lax.broadcasted_iota(jnp.int32, (1, LANES), 1)
    low_half = (lane < HEAD).astype(F32).astype(BF16)
    high_half = (lane >= HEAD).astype(F32).astype(BF16)
    score_scale = HEAD ** (-0.5)

    moves = [pltpu.make_async_copy(global_in_hbm, global_in, io_sem.at[0]), pltpu.make_async_copy(local_in_hbm, local_in, io_sem.at[1])]
    weights = ((mixer_hbm, mixer_weight), (output_hbm, output_weight), (expand_hbm, expand_weight), (reduce_hbm, reduce_weight))
    for layer in range(2):
        for source, target in weights:
            moves.append(pltpu.make_async_copy(source.at[layer], target.at[layer], io_sem.at[len(moves)]))
    moves += [
        pltpu.make_async_copy(global_cot_hbm, global_cot, io_sem.at[10]),
        pltpu.make_async_copy(local_cot_hbm, local_cot, io_sem.at[11]),
    ]
    outward = [
        pltpu.make_async_copy(global_out, global_out_hbm, io_sem.at[12]),
        pltpu.make_async_copy(local_out, local_out_hbm, io_sem.at[13]),
        pltpu.make_async_copy(global_back, global_back_hbm, io_sem.at[14]),
        pltpu.make_async_copy(local_back, local_back_hbm, io_sem.at[15]),
    ]
    for move in moves:
        move.start()

    net = Net(dims.wires)
    net.greet()
    n_stage = len(dims.wires)
    sets = dims.landing_sets
    landings, sems = wires[: n_stage * sum(sets)], wires[n_stage * sum(sets) :]
    flow = Flow(net)
    number = 0
    for layer in (1, 0):
        bounds = dims.bounds[layer]
        for i in range(len(bounds) - 1):
            shared = len(sets) == 1
            at = (i if shared else number) * n_stage
            own = [w.at[number] for w in sems[:4]] + [sems[4].at[i]]
            rows = pl.ds(bounds[i], bounds[i + 1] - bounds[i])
            turn = (1 - layer) if shared else None
            flow.chunks.append(
                Chunk(net, sums.at[layer, rows], sums_out.at[layer, rows], landings[at : at + n_stage], own, turn, layer, bounds[i + 1])
            )
            number += 1

    for s in range(n_seq):
        x_s[s, seq - 32 :, :] = jnp.zeros((32, width), F32)
        grad_s[s, seq - 32 :, :] = jnp.zeros((32, width), F32)
    row_id = lax.broadcasted_iota(jnp.int32, (seq, LANES), 0)
    col_id = lax.broadcasted_iota(jnp.int32, (seq, LANES), 1)
    row_crop = sum((row_id >= llen * j).astype(jnp.int32) for j in range(1, group + 1))
    far = jnp.float32(-1e30)
    zero = jnp.float32(0)
    for h in range(2):
        place = col_id - (1 - h) * HEAD
        used = (place >= 0) & (place <= group)
        aug_s[0, h, 0] = jnp.where(place == 0, jnp.float32(1), zero).astype(BF16)
        aug_s[0, h, 1] = jnp.where((place == 0) & (row_id >= glen), far, zero).astype(BF16)
        aug_s[1, h, 0] = jnp.where(place == row_crop, jnp.float32(1), zero).astype(BF16)
        aug_s[1, h, 1] = jnp.where(used & (place != row_crop), far, zero).astype(BF16)
    one_column = (lax.broadcasted_iota(jnp.int32, (seq, LANES), 1) == 0).astype(F32).astype(BF16)
    for s in range(n_seq):
        for i in range(4):
            norm_n[i, s, :, width:] = one_column
        for i in range(2):
            mixed_s[i, s, :, width:] = one_column

    def live_rows(g):
        rows = lax.broadcasted_iota(jnp.int32, (seq, 1), 0)
        return (rows < llen * jnp.clip(count - g * group, 0, group)).astype(F32)

    def take_crops(crops, locals_, target):
        crop_s[...] = crops[...].astype(F32)
        for s in range(n_global):
            target[s, 0:glen, :] = crop_s[:, s, :]
        for j in range(n_local):
            s, at = n_global + j // group, llen * (j % group)
            target[s, at : at + llen, :] = locals_[j].astype(F32)

    def take_cotangents():
        moves[10].wait()
        moves[11].wait()
        take_crops(global_cot, local_cot, grad_s)
        for s in range(n_global, n_seq):
            grad_s[s] = grad_s[s] * live_rows(s - n_global)

    moves[0].wait()
    moves[1].wait()
    take_crops(global_in, local_in, x_s)

    def row(ref, layer):
        return ref[...].astype(F32)[layer : layer + 1]

    slopes = (slope_s, dup_s)

    def start_back(s, grad):
        grad_low[s] = grad.astype(BF16)
        acc_s[2] = acc_s[2] + fold8(grad)

    def end_back(s, grad, unit, scale, gain, dh):
        unit = unit.astype(F32)
        acc_s[0] = acc_s[0] + fold8(dh * unit)
        acc_s[1] = acc_s[1] + fold8(dh)
        grad = (grad + norm_back(dh, unit, scale, gain)).astype(BF16)
        grad_low[s] = grad
        grad_s[s] = grad.astype(F32)

    def pair_of(i):
        return (2 * i, 2 * i + 1)

    def start_norm(s, place, gain, shift):
        x = x_s[s]
        unit, scale = norm(x)
        unit_s[place, s] = unit.astype(BF16)
        scale_s[place, s] = scale
        normed = (unit * gain + shift).astype(BF16)
        norm_n[place, s, :, 0:width] = normed
        return normed

    def product(left, right, cols, first):
        total = None
        for s in range(n_seq):
            term = mm_tn(left[s, :, 0:first], right[s, :, cols])
            total = term if total is None else total + term
        return total

    for layer in range(2):
        gain, shift = row(attend_gain, layer), row(attend_shift, layer)
        bias = row(mixer_bias, layer)
        bias = jnp.concatenate([bias[:, :width], jnp.zeros((1, width), F32), bias[:, width:]], 1)
        out_bias = row(output_bias, layer)
        gain2, shift2 = row(feed_gain, layer), row(feed_shift, layer)
        bias_up, bias_down = row(expand_bias, layer), row(reduce_bias, layer)

        def attend(i, _):
            two = pair_of(i)
            normed = [start_norm(s, 2 * layer, gain, shift) for s in two]
            for c in range(0, 3 * width, BLOCK):
                cols = slice(c, min(c + BLOCK, 3 * width))
                for n, s in zip(normed, two, strict=True):
                    packed_s[layer, s, :, cols] = (mm(n, mixer_weight[layer, :, cols]) + bias[:, cols]).astype(BF16)
            kind = jnp.where(two[0] < n_global, 0, 1)
            for p in range(pairs):
                at = p * LANES
                totals = [None, None]
                for h, half in enumerate((low_half, high_half)):
                    for k, s in enumerate(two):
                        query = packed_s[layer, s, :, at : at + LANES]
                        key = packed_s[layer, s, :, width + at : width + at + LANES]
                        value = packed_s[layer, s, :, 2 * width + at : 2 * width + at + LANES]
                        scores = mm_nt(query * half + aug_s[kind, h, 0], key * half + aug_s[kind, h, 1]) * (score_scale * LOG2E)
                        power = jnp.exp2(scores - jnp.max(scores, -1, keepdims=True)).astype(BF16)
                        power_s[layer, s, 2 * p + h] = power
                        spread = jnp.broadcast_to(half, (seq, LANES))
                        term = mm(power, jnp.concatenate([value * half, spread], 1))
                        totals[k] = term if totals[k] is None else totals[k] + term
                for total, s in zip(totals, two, strict=True):
                    inverse = 1.0 / total[:, LANES:]
                    inverse_s[layer, s, :, at : at + LANES] = inverse
                    mixed_s[layer, s, :, at : at + LANES] = (total[:, :LANES] * inverse).astype(BF16)
            for s in two:
                x = x_s[s] + mm(mixed_s[layer, s, :, 0:width], output_weight[layer]) + out_bias
                x_s[s] = x.astype(BF16).astype(F32)
            return 0

        moves[2 + 4 * layer].wait()
        moves[3 + 4 * layer].wait()
        lax.fori_loop(0, n_seq // 2, attend, 0)

        def feed(i, _):
            two = pair_of(i)
            normed = [start_norm(s, 2 * layer + 1, gain2, shift2) for s in two]
            if layer == 1:
                for s in two:
                    start_back(s, grad_s[s])
            for c in range(hidden // BLOCK):
                cols = slice(c * BLOCK, (c + 1) * BLOCK)
                for n, s in zip(normed, two, strict=True):
                    act, slope = gelu_parts(mm(n, expand_weight[layer, :, cols]) + bias_up[:, cols])
                    act_s[layer, s, :, cols] = act.astype(BF16)
                    slopes[layer][s, :, cols] = slope.astype(BF16)
            for s in two:
                x = x_s[s] + mm(act_s[layer, s], reduce_weight[layer]) + bias_down
                x_s[s] = x.astype(BF16).astype(F32)
            return 0

        moves[4 + 4 * layer].wait()
        moves[5 + 4 * layer].wait()
        if layer == 1:
            take_cotangents()
            acc_s[...] = jnp.zeros_like(acc_s)
        lax.fori_loop(0, n_seq // 2, feed, 0)

    for s in range(n_global):
        crop_s[:, s, :] = x_s[s, 0:glen, :]
    global_out[...] = crop_s[...].astype(BF16)
    for j in range(n_local):
        s, at = n_global + j // group, llen * (j % group)
        alive = (count > j).astype(F32)
        local_out[j] = (x_s[s, at : at + llen, :] * alive).astype(BF16)
    outward[0].start()
    outward[1].start()

    def put_vector(at, value):
        for c in range(0, value.shape[1], BLOCK):
            piece = value[:, c : c + BLOCK]
            vec_s[at + c // BLOCK : at + c // BLOCK + 1, 0 : piece.shape[1]] = piece

    def put_tile(layer, top, m, part):
        at = top + (m // 3) * (width + fold)
        side = m % 3 * LANES
        part = part.astype(BF16)
        if m % 3 < 2:
            sums[layer, at : at + width, side : side + LANES] = part
        else:
            at = at + width
            sums[layer, at : at + fold, 0:LANES] = part[:fold]
            sums[layer, at : at + fold, LANES:] = part[fold:]

    blocks = hidden // BLOCK
    fold = width // 2
    tops = dims.tops
    net.wait_greeting()
    for layer, used in ((1, tops[4]), (0, tops[4] + 2 * dims.vec_rows)):
        if dims.rows > used:
            sums[layer, used:, :] = jnp.zeros((dims.rows - used, BLOCK), BF16)
    for layer in (1, 0):
        vec_s[...] = jnp.zeros_like(vec_s)
        gain2, gain = row(feed_gain, layer), row(attend_gain, layer)
        put_vector(dims.at["reduce_bias"], jnp.sum(acc_s[2], 0, keepdims=True))

        for c in range(blocks):
            total = product(grad_low, act_s.at[layer], slice(c * BLOCK, (c + 1) * BLOCK), width)
            at = tops[0] + c * width
            sums[layer, at : at + width, :] = total.astype(BF16)
            flow.ready(layer, at + width)
            flow.tick(0.45)

        def feed_back(i, _):
            two = pair_of(i)
            grads = [grad_s[s].astype(BF16) for s in two]
            for c in range(blocks):
                cols = slice(c * BLOCK, (c + 1) * BLOCK)
                for g, s in zip(grads, two, strict=True):
                    dact = mm_nt(g, reduce_weight[layer, cols, :])
                    dup_s[s, :, cols] = (dact * slopes[layer][s, :, cols].astype(F32)).astype(BF16)
            flow.ticks(i, n_seq // 2, 1.2)
            return 0

        lax.fori_loop(0, n_seq // 2, feed_back, 0)

        for c in range(blocks):
            total = product(norm_n.at[2 * layer + 1], dup_s, slice(c * BLOCK, (c + 1) * BLOCK), width + TILE)
            at = tops[1] + c * width
            sums[layer, at : at + width, :] = total[:width].astype(BF16)
            at_bias = dims.at["expand_bias"] + c
            vec_s[at_bias : at_bias + 1, :] = total[width : width + 1]
            flow.ready(layer, at + width)
            flow.tick(0.45)

        def feed_norm_back(i, _):
            two = pair_of(i)
            dhs = [mm_nt(dup_s[s], expand_weight[layer]) for s in two]
            for dh, s in zip(dhs, two, strict=True):
                end_back(s, grad_s[s], unit_s[2 * layer + 1, s], scale_s[2 * layer + 1, s], gain2, dh)
            flow.ticks(i, n_seq // 2, 1.4)
            return 0

        acc_s[0:2] = jnp.zeros((2, 8, width), F32)
        lax.fori_loop(0, n_seq // 2, feed_norm_back, 0)
        put_vector(dims.at["feed_gain"], jnp.sum(acc_s[0], 0, keepdims=True))
        put_vector(dims.at["feed_shift"], jnp.sum(acc_s[1], 0, keepdims=True))

        bias_parts = []
        for c in range(0, width, BLOCK):
            size = min(BLOCK, width - c)
            total = product(mixed_s.at[layer], grad_low, slice(c, c + size), width + TILE)
            for k in range(0, size, LANES):
                put_tile(layer, tops[2], (c + k) // LANES, total[:width, k : k + LANES])
                bias_parts.append(total[width : width + 1, k : k + LANES])
        put_vector(dims.at["output_bias"], jnp.concatenate(bias_parts, 1))
        flow.ready(layer, tops[3])
        flow.tick(0.8)

        def attend_back(i, _):
            two = pair_of(i)
            dmixed = [mm_nt(grad_low[s], output_weight[layer]) for s in two]
            for p in range(pairs):
                at = p * LANES
                dqs, dks, dvs, dms, inners = [None] * 2, [None] * 2, [None] * 2, [], []
                for d, s in zip(dmixed, two, strict=True):
                    dm = d[:, at : at + LANES] * inverse_s[layer, s, :, at : at + LANES]
                    inners.append(-(dm * mixed_s[layer, s, :, at : at + LANES].astype(F32)).astype(BF16))
                    dms.append(dm.astype(BF16))
                for h, half in enumerate((low_half, high_half)):
                    for k, s in enumerate(two):
                        query = packed_s[layer, s, :, at : at + LANES]
                        key = packed_s[layer, s, :, width + at : width + at + LANES]
                        value = packed_s[layer, s, :, 2 * width + at : 2 * width + at + LANES]
                        power = power_s[layer, s, 2 * p + h]
                        dm_half = dms[k] * half
                        left = jnp.concatenate([dm_half, inners[k] * half], 1)
                        wide_value = jnp.concatenate([value, jnp.ones_like(value)], 1)
                        ds = (power.astype(F32) * mm_nt(left, wide_value)).astype(BF16)
                        dqs[k] = add_to(dqs[k], mm(ds, key * half))
                        dks[k] = add_to(dks[k], mm_tn(ds, query * half))
                        dvs[k] = add_to(dvs[k], mm_tn(power, dm_half))
                for k, s in enumerate(two):
                    dup_s[s, :, at : at + LANES] = (dqs[k] * score_scale).astype(BF16)
                    dup_s[s, :, width + at : width + at + LANES] = (dks[k] * score_scale).astype(BF16)
                    dup_s[s, :, 2 * width + at : 2 * width + at + LANES] = dvs[k].astype(BF16)
            flow.ticks(i, n_seq // 2, 3.4)
            return 0

        lax.fori_loop(0, n_seq // 2, attend_back, 0)

        bias_parts = []
        for c in range(0, 3 * width, BLOCK):
            size = min(BLOCK, 3 * width - c)
            total = product(norm_n.at[2 * layer], dup_s, slice(c, c + size), width + TILE)
            for k in range(0, size, LANES):
                put_tile(layer, tops[3], (c + k) // LANES, total[:width, k : k + LANES])
                bias_parts.append(total[width : width + 1, k : k + LANES])
            flow.tick(0.5)
        each = width // LANES
        put_vector(
            dims.at["mixer_bias"],
            jnp.concatenate(bias_parts[:each] + bias_parts[2 * each :], 1),
        )
        flow.ready(layer, dims.rows if layer == 1 else tops[4])

        def attend_norm_back(i, _):
            two = pair_of(i)
            dhs = [mm_nt(dup_s[s, :, 0 : 3 * width], mixer_weight[layer]) for s in two]
            for dh, s in zip(dhs, two, strict=True):
                end_back(s, grad_s[s], unit_s[2 * layer, s], scale_s[2 * layer, s], gain, dh)
                if layer == 1:
                    start_back(s, grad_s[s])
            flow.ticks(i, n_seq // 2, 1.2)
            return 0

        acc_s[...] = jnp.zeros_like(acc_s)
        lax.fori_loop(0, n_seq // 2, attend_norm_back, 0)
        put_vector(dims.at["attend_gain"], jnp.sum(acc_s[0], 0, keepdims=True))
        put_vector(dims.at["attend_shift"], jnp.sum(acc_s[1], 0, keepdims=True))
        at = tops[4] + layer * dims.vec_rows
        sums[0, at : at + dims.vec_rows, :] = vec_s[...].astype(BF16)
        if layer == 0:
            flow.ready(0, dims.rows)

    for s in range(n_global):
        crop_s[:, s, :] = grad_s[s, 0:glen, :]
    global_back[...] = crop_s[...].astype(BF16)
    for j in range(n_local):
        s, at = n_global + j // group, llen * (j % group)
        local_back[j] = grad_s[s, at : at + llen, :].astype(BF16)
    outward[2].start()
    outward[3].start()
    flow.drain()
    for move in outward:
        move.wait()


class Wire:
    def __init__(self, size, first, second):
        self.size, self.first, self.second = size, first, second


def wires_of(mesh):
    names = mesh.axis_names
    places = {}
    for axis, name in enumerate(names):
        line = [mesh.devices[tuple(i if a == axis else 0 for a in range(2))] for i in range(mesh.devices.shape[axis])]
        spots = [(d.core_on_chip,) + tuple(d.coords) for d in line]
        found, total = [], 1
        for k in range(4):
            values = sorted({p[k] for p in spots})
            if len(values) > 1:
                stride = next(i for i, p in enumerate(spots) if p[k] != spots[0][k])
                found.append((k, axis, stride, len(values)))
                total *= len(values)
        good = total == len(line)
        for k, _, stride, size in found:
            values = [p[k] for p in spots]
            good = good and all(v == values[i // stride % size * stride] for i, v in enumerate(values))
        if not good:
            found = [(4 + axis, axis, 1, len(line))]
        for k, axis, stride, size in found:
            places[k] = (axis, stride, size)
    wires = []
    if 0 in places:
        wires.append(Wire(places[0][2], places[0], places[0]))
    if 0 in places and 1 in places and 2 in places and places[1][2] == places[2][2]:
        wires.append(Wire(places[1][2], places[1], places[2]))
        wires.append(Wire(places[1][2], places[2], places[1]))
        order = [3, 4, 5]
    else:
        order = [1, 2, 3, 4, 5]
    for k in order:
        if k in places:
            wires.append(Wire(places[k][2], places[k], places[k]))
    return wires


class Net:
    def __init__(self, wires):
        self.axes = ("dp", "section")
        self.here = [lax.axis_index(a) for a in self.axes]
        self.wires = wires
        first = wires[0]
        odd = self.spot(first.first) % 2 if first.size == 2 else 0
        self.odd = odd
        self.at = []
        for w in wires:
            a, b = self.spot(w.first), self.spot(w.second)
            self.at.append(a if w.first == w.second else a + odd * (b - a))

    def spot(self, place):
        axis, stride, size = place
        return self.here[axis] // stride % size

    def peer(self, stage, k):
        w = self.wires[stage]
        place = (self.at[stage] + k) % w.size
        move = place - self.at[stage]
        target = list(self.here)
        if w.first == w.second:
            target[w.first[0]] = target[w.first[0]] + move * w.first[1]
        else:
            target[w.first[0]] = target[w.first[0]] + move * w.first[1] * (1 - self.odd)
            target[w.second[0]] = target[w.second[0]] + move * w.second[1] * self.odd
        return tuple(target), place

    def greet(self):
        barrier = pltpu.get_barrier_semaphore()
        for stage, w in enumerate(self.wires):
            for k in range(1, w.size):
                pl.semaphore_signal(barrier, inc=1, device_id=self.peer(stage, k)[0], device_id_type=pl.DeviceIdType.MESH)

    def wait_greeting(self):
        pl.semaphore_wait(pltpu.get_barrier_semaphore(), sum(w.size - 1 for w in self.wires))


class Chunk:
    def __init__(self, net, sums, out, landing, sems, turn, layer, end):
        self.net, self.sums, self.out, self.landing = net, sums, out, landing
        self.send, self.recv, self.local, self.sent, self.free = sems
        self.turn = turn
        self.layer, self.end = layer, end
        self.due = None
        size, start = sums.shape[0], 0
        self.unit = size
        for w in net.wires:
            self.unit //= w.size
        self.size, self.start = [], []
        for stage, w in enumerate(net.wires):
            size //= w.size
            self.size.append(size)
            self.start.append((start, size))
            start = start + net.at[stage] * size
        self.own = start
        self.stages = len(net.wires)
        self.step = 0
        self.sem_at, at = {}, 0
        for phase in range(2):
            for stage, w in enumerate(net.wires):
                for k in range(1, w.size):
                    self.sem_at[phase, stage, k] = at
                    at += 1

    def rows(self, stage, place):
        start, size = self.start[stage]
        return pl.ds(pl.multiple_of(start + place * size, TILE), size)

    def copy(self, phase, stage, k):
        target, place = self.net.peer(stage, k)
        at = self.sem_at[phase, stage, k]
        if phase == 0:
            source, to = self.sums.at[self.rows(stage, place)], self.landing[stage].at[k - 1]
        else:
            rows = self.rows(stage, self.net.at[stage])
            source = to = self.sums.at[rows]
        return pltpu.make_async_remote_copy(
            src_ref=source,
            dst_ref=to,
            send_sem=self.send.at[at],
            recv_sem=self.recv.at[at],
            device_id=target,
            device_id_type=pl.DeviceIdType.MESH,
        )

    def arrival(self, stage, k):
        target, place = self.net.peer(stage, self.net.wires[stage].size - k)
        at = self.sem_at[1, stage, k]
        landed = self.sums.at[self.rows(stage, place)]
        return pltpu.make_async_remote_copy(
            src_ref=landed,
            dst_ref=landed,
            send_sem=self.send.at[at],
            recv_sem=self.recv.at[at],
            device_id=target,
            device_id_type=pl.DeviceIdType.MESH,
        )

    def start_stage(self, phase, stage):
        if phase == 0 and self.turn == 1:
            pl.semaphore_wait(self.free.at[stage], self.net.wires[stage].size - 1)
        if phase == 1:
            pl.semaphore_wait(self.sent.at[stage], self.net.wires[stage].size - 1)
        for k in range(1, self.net.wires[stage].size):
            self.copy(phase, stage, k).start()

    def load(self):
        last = self.stages - 1
        stage = self.step if self.step <= last else 2 * self.stages - 1 - self.step
        peers = self.net.wires[stage].size - 1
        row = BLOCK * 2
        if stage == 0:
            return 0, self.size[0] * row / 4
        if stage == last:
            return 2, self.size[stage] * (peers + 1) ** 2 / 2 * row
        return 1, self.size[stage] * peers * row

    def begin(self):
        self.start_stage(0, 0)

    def out_copy(self):
        return pltpu.make_async_copy(self.sums, self.out, self.local.at[0])

    def advance(self):
        step = self.step
        self.step += 1
        if step < self.stages:
            peers = range(1, self.net.wires[step].size)
            for k in peers:
                self.copy(0, step, k).wait_recv()
            base = self.start[step][0] + self.net.at[step] * self.size[step]
            landing = self.landing[step]

            count = self.size[step] // self.unit
            while count % 2 == 0 and self.size[step] // count < 128:
                count //= 2
            size = self.size[step] // count

            def add(i, _):
                at = pl.ds(pl.multiple_of(base + i * size, TILE), size)
                here = [landing[k - 1, pl.ds(pl.multiple_of(i * size, TILE), size), :] for k in peers]
                if len(here) == 1:
                    self.sums[at, :] = self.sums[at, :] + here[0]
                else:
                    total = self.sums[at, :].astype(F32)
                    for part in here:
                        total = total + part.astype(F32)
                    self.sums[at, :] = total.astype(BF16)
                return 0

            lax.fori_loop(0, count, add, 0)
            for k in peers:
                self.copy(0, step, k).wait_send()
                target = self.net.peer(step, k)[0]
                pl.semaphore_signal(self.sent.at[step], inc=1, device_id=target, device_id_type=pl.DeviceIdType.MESH)
                if self.turn == 0:
                    pl.semaphore_signal(self.free.at[step], inc=1, device_id=target, device_id_type=pl.DeviceIdType.MESH)
            if step + 1 < self.stages:
                self.start_stage(0, step + 1)
            else:
                self.start_stage(1, step)
        else:
            stage = 2 * self.stages - 1 - step
            for k in range(1, self.net.wires[stage].size):
                self.arrival(stage, k).wait_recv()
            if stage > 0:
                self.start_stage(1, stage - 1)
            else:
                self.out_copy().start()

    def finish(self):
        for phase, stage, k in self.sem_at:
            if phase == 1:
                self.copy(phase, stage, k).wait_send()
        self.out_copy().wait()


LATENCY = 2.0
RATE = 80e3
STEP = 0.4


class Flow:
    def __init__(self, net):
        self.chunks, self.now, self.waiting, self.free = [], 0.0, 0, [0.0] * 3

    def book(self, chunk):
        kind, size = chunk.load()
        self.free[kind] = max(self.now, self.free[kind]) + size / RATE
        chunk.due = self.free[kind] + LATENCY

    def ready(self, layer, rows):
        while self.waiting < len(self.chunks):
            chunk = self.chunks[self.waiting]
            if chunk.layer != layer or chunk.end > rows:
                return
            chunk.begin()
            self.book(chunk)
            self.waiting += 1

    def due(self):
        return sorted((c for c in self.chunks if c.due is not None and c.due <= self.now), key=lambda c: c.due)

    def take(self):
        while self.due():
            chunk = self.due()[0]
            chunk.advance()
            self.now += STEP
            if chunk.step < 2 * chunk.stages:
                self.book(chunk)
            else:
                chunk.due = None

    def tick(self, time):
        self.now += time
        self.take()

    def ticks(self, s, count, time):
        for i in range(count):
            self.now += time
            if self.due():
                pl.when(s == i)(self.take)

    def drain(self):
        while any(c.due is not None for c in self.chunks):
            self.now = max(self.now, min(c.due for c in self.chunks if c.due is not None))
            self.take()
        for chunk in self.chunks:
            chunk.finish()


class Dims:
    def __init__(self, global_crops, local_crops, hidden, wires):
        self.wires = wires
        self.glen, self.n_global, self.width = global_crops.shape
        self.n_local, self.llen, _ = local_crops.shape
        self.hidden = hidden
        self.seq = up_to(self.glen, TILE)
        self.group = self.seq // self.llen
        while self.n_local % self.group:
            self.group -= 1
        self.n_seq = self.n_global + self.n_local // self.group
        assert self.n_seq % 2 == self.n_global % 2 == 0
        sizes = (
            ("attend_gain", self.width),
            ("attend_shift", self.width),
            ("mixer_bias", 2 * self.width),
            ("output_bias", self.width),
            ("feed_gain", self.width),
            ("feed_shift", self.width),
            ("expand_bias", hidden),
            ("reduce_bias", self.width),
        )
        self.names, self.sizes = [name for name, _ in sizes], dict(sizes)
        self.at, row = {}, 0
        for name, size in sizes:
            self.at[name] = row
            row += -(-size // BLOCK)
        self.vec_rows = 2 * TILE
        assert row <= self.vec_rows and self.width * hidden % self.vec_rows == 0
        step = TILE
        for w in wires:
            step *= w.size
        ff = self.width * hidden // BLOCK
        square = self.width * self.width // BLOCK
        self.tops = (0, ff, 2 * ff, 2 * ff + square, 2 * ff + 4 * square)
        self.rows = up_to(self.tops[4] + 2 * self.vec_rows, step)
        parts = self.rows // step
        cuts = ((0, 4, 7, 10, 12, 14), (0, 4, 10, 14))
        self.bounds = [[c * step for c in sorted({parts * k // 14 for k in layer})] for layer in cuts]
        self.landing_sets = [len(b) - 1 for b in self.bounds[::-1]]
        if self.bounds[0] == self.bounds[1]:
            self.landing_sets = self.landing_sets[:1]
        self.n_chunk = sum(len(b) - 1 for b in self.bounds)


HEAVY = (6, 8, 12, 14)


def run_kernel(counts, arrays, dims):
    d = dims
    n, seq, width, hidden = d.n_seq, d.seq, d.width, d.hidden
    crops = [jax.ShapeDtypeStruct(a.shape, BF16) for a in arrays[:2]]
    outs = crops + crops
    outs += [jax.ShapeDtypeStruct((2, d.rows, BLOCK), BF16)]
    scratch = [pltpu.VMEM(a.shape, BF16) for a in tuple(arrays[:4]) * 2]
    scratch += [pltpu.VMEM(arrays[i].shape, BF16) for i in HEAVY]
    scratch += [
        pltpu.SemaphoreType.DMA((16,)),
        pltpu.VMEM((2, d.rows, BLOCK), BF16),
        pltpu.VMEM((d.glen, d.n_global, width), F32),
        pltpu.VMEM((n, seq, width), F32),
        pltpu.VMEM((4, n, seq, width), BF16),
        pltpu.VMEM((4, n, seq, 1), F32),
        pltpu.VMEM((4, n, seq, width + LANES), BF16),
        pltpu.VMEM((2, n, seq, 3 * width), BF16),
        pltpu.VMEM((2, n, HEADS, seq, seq), BF16),
        pltpu.VMEM((2, n, seq, width), F32),
        pltpu.VMEM((2, n, seq, width + LANES), BF16),
        pltpu.VMEM((2, n, seq, hidden), BF16),
        pltpu.VMEM((n, seq, hidden), BF16),
        pltpu.VMEM((n, seq, width), F32),
        pltpu.VMEM((n, seq, width), BF16),
        pltpu.VMEM((n, seq, hidden), BF16),
        pltpu.VMEM((2, 2, 2, seq, LANES), BF16),
        pltpu.VMEM((d.vec_rows, BLOCK), F32),
        pltpu.VMEM((3, 8, width), F32),
    ]
    for layer in (1, 0)[: len(d.landing_sets)]:
        for first, end in zip(d.bounds[layer], d.bounds[layer][1:]):
            rows = end - first
            for w in d.wires:
                rows //= w.size
                scratch.append(pltpu.VMEM((w.size - 1, rows, BLOCK), BF16))
    peers = 2 * sum(w.size - 1 for w in d.wires)
    scratch += [
        pltpu.SemaphoreType.DMA((d.n_chunk, peers)),
        pltpu.SemaphoreType.DMA((d.n_chunk, peers)),
        pltpu.SemaphoreType.DMA((d.n_chunk, 1)),
        pltpu.SemaphoreType.REGULAR((d.n_chunk, len(d.wires))),
        pltpu.SemaphoreType.REGULAR((d.n_chunk, len(d.wires))),
    ]
    vmem = pl.BlockSpec(memory_space=pltpu.VMEM)
    anywhere = pl.BlockSpec(memory_space=pl.ANY)
    return pl.pallas_call(
        functools.partial(kernel, d),
        out_shape=outs,
        in_specs=[pl.BlockSpec(memory_space=pltpu.SMEM)]
        + [anywhere if i < 4 or i in HEAVY else vmem for i in range(len(arrays))],
        out_specs=[anywhere] * len(outs),
        scratch_shapes=scratch,
        compiler_params=pltpu.CompilerParams(
            vmem_limit_bytes=63 * 1024 * 1024, collective_id=0, has_side_effects=True
        ),
    )(counts, *arrays)


THIRDS = 3


def cast_kernel(dims, reduce, expand, output, mixer, vectors, *rest):
    crops, outs, held, sems = rest[:4], rest[4:-9], rest[-5:-1], rest[-1]
    step = pl.program_id(0) * THIRDS + pl.program_id(1)
    loads = [pltpu.make_async_copy(a, b, sems.at[0, i]) for i, (a, b) in enumerate(zip(crops, held, strict=True))]
    stores = [pltpu.make_async_copy(a, b, sems.at[1, i]) for i, (a, b) in enumerate(zip(held, rest[-9:-5], strict=True))]

    @pl.when(step == 0)
    def _():
        for copy in loads:
            copy.start()

    @pl.when(step == 1)
    def _():
        for load, store in zip(loads, stores, strict=True):
            load.wait()
            store.start()

    mixer_grad, output_grad, expand_grad, reduce_grad = outs[:4]
    width = dims.width
    fold = width // 2
    for b in range(2):
        rows = slice(b * width, (b + 1) * width)
        cols = slice(b * BLOCK, (b + 1) * BLOCK)
        expand_grad[0, :, cols] = expand[0, rows, :].astype(F32)
        reduce_grad[0, cols, :] = reduce[0, rows, :].T.astype(F32)
    for source, target in ((mixer, mixer_grad), (output, output_grad)):
        target[0, :, 0:BLOCK] = source[0, 0:width, :].astype(F32)
        target[0, 0:fold, BLOCK:] = source[0, width:, 0:LANES].astype(F32)
        target[0, fold:, BLOCK:] = source[0, width:, LANES:].astype(F32)

    @pl.when(step == 2 * THIRDS - 1)
    def _():
        for ref, name in zip(outs[4:], dims.names, strict=True):
            size = ref.shape[1]
            for c in range(0, size, BLOCK):
                at = dims.at[name] + c // BLOCK
                piece = min(BLOCK, size - c)
                for layer in range(2):
                    ref[layer : layer + 1, c : c + piece] = vectors[0].astype(F32)[at + layer * dims.vec_rows :][:1, 0:piece]
        for store in stores:
            store.wait()


def run_cast(sums, crops, dims):
    d = dims
    width, hidden = d.width, d.hidden
    part = (1, 2 * width, BLOCK)
    square = (1, width * width // BLOCK, BLOCK)
    grads = [(width, 3 * width), (width, width), (width, hidden), (hidden, width)]
    shapes = [jax.ShapeDtypeStruct((2,) + g, F32) for g in grads]
    specs = [
        pl.BlockSpec((1, width, 3 * width // THIRDS), lambda l, t: (l, 0, t)),
        pl.BlockSpec((1, width, width), lambda l, t: (l, 0, 0)),
        pl.BlockSpec((1, width, hidden // THIRDS), lambda l, t: (l, 0, t)),
        pl.BlockSpec((1, hidden // THIRDS, width), lambda l, t: (l, t, 0)),
    ]
    for name in d.names:
        shapes.append(jax.ShapeDtypeStruct((2, d.sizes[name]), F32))
        specs.append(pl.BlockSpec((2, d.sizes[name]), lambda l, t: (0, 0)))
    for crop in crops:
        shapes.append(jax.ShapeDtypeStruct(crop.shape, crop.dtype))
        specs.append(pl.BlockSpec(memory_space=pl.ANY))
    return pl.pallas_call(
        functools.partial(cast_kernel, d),
        grid=(2, THIRDS),
        out_shape=shapes,
        in_specs=[
            pl.BlockSpec(part, lambda l, t: (l, t, 0)),
            pl.BlockSpec(part, lambda l, t: (l, THIRDS + t, 0)),
            pl.BlockSpec(square, lambda l, t: (l, d.tops[2] // square[1], 0)),
            pl.BlockSpec(square, lambda l, t: (l, d.tops[3] // square[1] + t, 0)),
            pl.BlockSpec((1, 2 * d.vec_rows, BLOCK), lambda l, t: (0, d.tops[4] // (2 * d.vec_rows), 0)),
        ]
        + [pl.BlockSpec(memory_space=pl.ANY)] * 4,
        out_specs=specs,
        scratch_shapes=[pltpu.VMEM(c.shape, c.dtype) for c in crops] + [pltpu.SemaphoreType.DMA((2, 4))],
        compiler_params=pltpu.CompilerParams(vmem_limit_bytes=62 * 1024 * 1024),
    )(sums, sums, sums, sums, sums, *crops)


def shards(wires, global_crops, local_crops, local_count, global_cotangent, local_cotangent, *weights):
    global_crops, global_cotangent = global_crops.transpose(1, 0, 2), global_cotangent.transpose(1, 0, 2)
    dims = Dims(global_crops, local_crops, weights[8].shape[2], wires)
    outs = run_kernel(
        local_count, (global_crops, local_crops, global_cotangent, local_cotangent) + weights, dims
    )
    mixer, output, expand, reduce, *rest = run_cast(outs[4], outs[:4], dims)
    vectors, crops = rest[:-4], rest[-4:]
    v = dict(zip(dims.names, vectors, strict=True))
    return (
        crops[0].transpose(1, 0, 2),
        crops[1],
        crops[2].transpose(1, 0, 2),
        crops[3],
        v["attend_gain"],
        v["attend_shift"],
        mixer,
        v["mixer_bias"],
        output,
        v["output_bias"],
        v["feed_gain"],
        v["feed_shift"],
        expand,
        v["expand_bias"],
        reduce,
        v["reduce_bias"],
    )


def solution(mesh):
    crops = P(("dp", "section"), None, None)
    return jax.shard_map(
        functools.partial(shards, wires_of(mesh)),
        mesh=mesh,
        in_specs=(crops, crops, P("dp"), crops, crops) + (P(),) * 12,
        out_specs=(crops,) * 4 + (P(),) * 12,
        check_vma=False,
    )
```

```python
import functools

import jax
import jax.numpy as jnp
from jax import lax
from jax.experimental import pallas as pl
from jax.experimental.pallas import tpu as pltpu
from jax.sharding import PartitionSpec as P

HEADS = 6
HEAD = 64
EPS = 1e-06
TILE = 16
LANES = 128
BLOCK = 256
LOG2E = 1.4426950408889634
F32 = jnp.float32
BF16 = jnp.bfloat16


def up_to(value, step):
    return -(-value // step) * step


def mm(left, right):
    return lax.dot_general(left, right, (((1,), (0,)), ((), ())), preferred_element_type=F32)


def mm_nt(left, right):
    return lax.dot_general(left, right, (((1,), (1,)), ((), ())), preferred_element_type=F32)


def mm_tn(left, right):
    return lax.dot_general(left, right, (((0,), (0,)), ((), ())), preferred_element_type=F32)


def norm(rows):
    centred = rows - jnp.mean(rows, -1, keepdims=True)
    scale = lax.rsqrt(jnp.mean(centred * centred, -1, keepdims=True) + EPS)
    return centred * scale, scale


def norm_back(grad, unit, scale, gain):
    slope = grad * gain
    first = jnp.mean(slope, -1, keepdims=True)
    second = jnp.mean(slope * unit, -1, keepdims=True)
    return scale * (slope - first - unit * second)


def gelu_parts(u):
    size = jnp.abs(u)
    d = 1.0 + (0.3275911 * 0.7071067811865476) * size
    t = pl.reciprocal(d, approx=True)
    t = t * (2.0 - d * t)
    poly = 0.5 * 1.061405429
    for a in (-1.453152027, 1.421413741, -0.284496736, 0.254829592):
        poly = poly * t + 0.5 * a
    bell = jnp.exp2((u * u) * (-0.5 * LOG2E))
    tail = poly * t * bell
    phi = jnp.where(u < 0.0, tail, 1.0 - tail)
    return u * phi, phi + (u * bell) * 0.3989422804014327


def add_to(total, value):
    return value if total is None else total + value


def fold8(value):
    rows, width = value.shape
    return jnp.sum(value.reshape(rows // 8, 8, width), 0)


def kernel(
    dims,
    counts,
    global_in_hbm,
    local_in_hbm,
    global_cot_hbm,
    local_cot_hbm,
    attend_gain,
    attend_shift,
    mixer_hbm,
    mixer_bias,
    output_hbm,
    output_bias,
    feed_gain,
    feed_shift,
    expand_hbm,
    expand_bias,
    reduce_hbm,
    reduce_bias,
    global_out_hbm,
    local_out_hbm,
    global_back_hbm,
    local_back_hbm,
    sums_out,
    global_in,
    local_in,
    global_cot,
    local_cot,
    global_out,
    local_out,
    global_back,
    local_back,
    mixer_weight,
    output_weight,
    expand_weight,
    reduce_weight,
    io_sem,
    sums,
    crop_s,
    x_s,
    unit_s,
    scale_s,
    norm_n,
    packed_s,
    power_s,
    inverse_s,
    mixed_s,
    act_s,
    slope_s,
    grad_s,
    grad_low,
    dup_s,
    aug_s,
    vec_s,
    acc_s,
    *wires,
):
    seq, group, width = dims.seq, dims.group, dims.width
    glen, llen = dims.glen, dims.llen
    n_global, n_local, n_seq = dims.n_global, dims.n_local, dims.n_seq
    hidden = dims.hidden
    count = counts[lax.axis_index("section")]
    pairs = HEADS // 2
    lane = lax.broadcasted_iota(jnp.int32, (1, LANES), 1)
    low_half = (lane < HEAD).astype(F32).astype(BF16)
    high_half = (lane >= HEAD).astype(F32).astype(BF16)
    score_scale = HEAD ** (-0.5)

    moves = [pltpu.make_async_copy(global_in_hbm, global_in, io_sem.at[0]), pltpu.make_async_copy(local_in_hbm, local_in, io_sem.at[1])]
    weights = ((mixer_hbm, mixer_weight), (output_hbm, output_weight), (expand_hbm, expand_weight), (reduce_hbm, reduce_weight))
    for layer in range(2):
        for source, target in weights:
            moves.append(pltpu.make_async_copy(source.at[layer], target.at[layer], io_sem.at[len(moves)]))
    moves += [
        pltpu.make_async_copy(global_cot_hbm, global_cot, io_sem.at[10]),
        pltpu.make_async_copy(local_cot_hbm, local_cot, io_sem.at[11]),
    ]
    outward = [
        pltpu.make_async_copy(global_out, global_out_hbm, io_sem.at[12]),
        pltpu.make_async_copy(local_out, local_out_hbm, io_sem.at[13]),
        pltpu.make_async_copy(global_back, global_back_hbm, io_sem.at[14]),
        pltpu.make_async_copy(local_back, local_back_hbm, io_sem.at[15]),
    ]
    for move in moves:
        move.start()

    net = Net(dims.wires)
    net.greet()
    n_stage = len(dims.wires)
    sets = dims.landing_sets
    landings, sems = wires[: n_stage * sum(sets)], wires[n_stage * sum(sets) :]
    flow = Flow(net)
    number = 0
    for layer in (1, 0):
        bounds = dims.bounds[layer]
        for i in range(len(bounds) - 1):
            shared = len(sets) == 1
            at = (i if shared else number) * n_stage
            own = [w.at[number] for w in sems[:4]] + [sems[4].at[i]]
            rows = pl.ds(bounds[i], bounds[i + 1] - bounds[i])
            turn = (1 - layer) if shared else None
            flow.chunks.append(
                Chunk(net, sums.at[layer, rows], sums_out.at[layer, rows], landings[at : at + n_stage], own, turn, layer, bounds[i + 1])
            )
            number += 1

    for s in range(n_seq):
        x_s[s, seq - 32 :, :] = jnp.zeros((32, width), F32)
        grad_s[s, seq - 32 :, :] = jnp.zeros((32, width), F32)
    row_id = lax.broadcasted_iota(jnp.int32, (seq, LANES), 0)
    col_id = lax.broadcasted_iota(jnp.int32, (seq, LANES), 1)
    row_crop = sum((row_id >= llen * j).astype(jnp.int32) for j in range(1, group + 1))
    far = jnp.float32(-1e30)
    zero = jnp.float32(0)
    for h in range(2):
        place = col_id - (1 - h) * HEAD
        used = (place >= 0) & (place <= group)
        aug_s[0, h, 0] = jnp.where(place == 0, jnp.float32(1), zero).astype(BF16)
        aug_s[0, h, 1] = jnp.where((place == 0) & (row_id >= glen), far, zero).astype(BF16)
        aug_s[1, h, 0] = jnp.where(place == row_crop, jnp.float32(1), zero).astype(BF16)
        aug_s[1, h, 1] = jnp.where(used & (place != row_crop), far, zero).astype(BF16)
    one_column = (lax.broadcasted_iota(jnp.int32, (seq, LANES), 1) == 0).astype(F32).astype(BF16)
    for s in range(n_seq):
        for i in range(4):
            norm_n[i, s, :, width:] = one_column
        for i in range(2):
            mixed_s[i, s, :, width:] = one_column

    def live_rows(g):
        rows = lax.broadcasted_iota(jnp.int32, (seq, 1), 0)
        return (rows < llen * jnp.clip(count - g * group, 0, group)).astype(F32)

    def take_crops(crops, locals_, target):
        crop_s[...] = crops[...].astype(F32)
        for s in range(n_global):
            target[s, 0:glen, :] = crop_s[:, s, :]
        for j in range(n_local):
            s, at = n_global + j // group, llen * (j % group)
            target[s, at : at + llen, :] = locals_[j].astype(F32)

    def take_cotangents():
        moves[10].wait()
        moves[11].wait()
        take_crops(global_cot, local_cot, grad_s)
        for s in range(n_global, n_seq):
            grad_s[s] = grad_s[s] * live_rows(s - n_global)

    moves[0].wait()
    moves[1].wait()
    take_crops(global_in, local_in, x_s)

    def row(ref, layer):
        return ref[...].astype(F32)[layer : layer + 1]

    slopes = (slope_s, dup_s)

    def start_back(s, grad):
        grad_low[s] = grad.astype(BF16)
        acc_s[2] = acc_s[2] + fold8(grad)

    def end_back(s, grad, unit, scale, gain, dh):
        unit = unit.astype(F32)
        acc_s[0] = acc_s[0] + fold8(dh * unit)
        acc_s[1] = acc_s[1] + fold8(dh)
        grad = (grad + norm_back(dh, unit, scale, gain)).astype(BF16)
        grad_low[s] = grad
        grad_s[s] = grad.astype(F32)

    def pair_of(i):
        return (2 * i, 2 * i + 1)

    def start_norm(s, place, gain, shift):
        x = x_s[s]
        unit, scale = norm(x)
        unit_s[place, s] = unit.astype(BF16)
        scale_s[place, s] = scale
        normed = (unit * gain + shift).astype(BF16)
        norm_n[place, s, :, 0:width] = normed
        return normed

    def product(left, right, cols, first):
        total = None
        for s in range(n_seq):
            term = mm_tn(left[s, :, 0:first], right[s, :, cols])
            total = term if total is None else total + term
        return total

    for layer in range(2):
        gain, shift = row(attend_gain, layer), row(attend_shift, layer)
        bias = row(mixer_bias, layer)
        bias = jnp.concatenate([bias[:, :width], jnp.zeros((1, width), F32), bias[:, width:]], 1)
        out_bias = row(output_bias, layer)
        gain2, shift2 = row(feed_gain, layer), row(feed_shift, layer)
        bias_up, bias_down = row(expand_bias, layer), row(reduce_bias, layer)

        def attend(i, _):
            two = pair_of(i)
            normed = [start_norm(s, 2 * layer, gain, shift) for s in two]
            for c in range(0, 3 * width, BLOCK):
                cols = slice(c, min(c + BLOCK, 3 * width))
                for n, s in zip(normed, two, strict=True):
                    packed_s[layer, s, :, cols] = (mm(n, mixer_weight[layer, :, cols]) + bias[:, cols]).astype(BF16)
            kind = jnp.where(two[0] < n_global, 0, 1)
            for p in range(pairs):
                at = p * LANES
                totals = [None, None]
                for h, half in enumerate((low_half, high_half)):
                    for k, s in enumerate(two):
                        query = packed_s[layer, s, :, at : at + LANES]
                        key = packed_s[layer, s, :, width + at : width + at + LANES]
                        value = packed_s[layer, s, :, 2 * width + at : 2 * width + at + LANES]
                        scores = mm_nt(query * half + aug_s[kind, h, 0], key * half + aug_s[kind, h, 1]) * (score_scale * LOG2E)
                        power = jnp.exp2(scores - jnp.max(scores, -1, keepdims=True)).astype(BF16)
                        power_s[layer, s, 2 * p + h] = power
                        spread = jnp.broadcast_to(half, (seq, LANES))
                        term = mm(power, jnp.concatenate([value * half, spread], 1))
                        totals[k] = term if totals[k] is None else totals[k] + term
                for total, s in zip(totals, two, strict=True):
                    inverse = 1.0 / total[:, LANES:]
                    inverse_s[layer, s, :, at : at + LANES] = inverse
                    mixed_s[layer, s, :, at : at + LANES] = (total[:, :LANES] * inverse).astype(BF16)
            for s in two:
                x = x_s[s] + mm(mixed_s[layer, s, :, 0:width], output_weight[layer]) + out_bias
                x_s[s] = x.astype(BF16).astype(F32)
            return 0

        moves[2 + 4 * layer].wait()
        moves[3 + 4 * layer].wait()
        lax.fori_loop(0, n_seq // 2, attend, 0)

        def feed(i, _):
            two = pair_of(i)
            normed = [start_norm(s, 2 * layer + 1, gain2, shift2) for s in two]
            if layer == 1:
                for s in two:
                    start_back(s, grad_s[s])
            for c in range(hidden // BLOCK):
                cols = slice(c * BLOCK, (c + 1) * BLOCK)
                for n, s in zip(normed, two, strict=True):
                    act, slope = gelu_parts(mm(n, expand_weight[layer, :, cols]) + bias_up[:, cols])
                    act_s[layer, s, :, cols] = act.astype(BF16)
                    slopes[layer][s, :, cols] = slope.astype(BF16)
            for s in two:
                x = x_s[s] + mm(act_s[layer, s], reduce_weight[layer]) + bias_down
                x_s[s] = x.astype(BF16).astype(F32)
            return 0

        moves[4 + 4 * layer].wait()
        moves[5 + 4 * layer].wait()
        if layer == 1:
            take_cotangents()
            acc_s[...] = jnp.zeros_like(acc_s)
        lax.fori_loop(0, n_seq // 2, feed, 0)

    for s in range(n_global):
        crop_s[:, s, :] = x_s[s, 0:glen, :]
    global_out[...] = crop_s[...].astype(BF16)
    for j in range(n_local):
        s, at = n_global + j // group, llen * (j % group)
        alive = (count > j).astype(F32)
        local_out[j] = (x_s[s, at : at + llen, :] * alive).astype(BF16)
    outward[0].start()
    outward[1].start()

    def put_vector(at, value):
        for c in range(0, value.shape[1], BLOCK):
            piece = value[:, c : c + BLOCK]
            vec_s[at + c // BLOCK : at + c // BLOCK + 1, 0 : piece.shape[1]] = piece

    def put_tile(layer, top, m, part):
        at = top + (m // 3) * (width + fold)
        side = m % 3 * LANES
        part = part.astype(BF16)
        if m % 3 < 2:
            sums[layer, at : at + width, side : side + LANES] = part
        else:
            at = at + width
            sums[layer, at : at + fold, 0:LANES] = part[:fold]
            sums[layer, at : at + fold, LANES:] = part[fold:]

    blocks = hidden // BLOCK
    fold = width // 2
    tops = dims.tops
    net.wait_greeting()
    for layer, used in ((1, tops[4]), (0, tops[4] + 2 * dims.vec_rows)):
        if dims.rows > used:
            sums[layer, used:, :] = jnp.zeros((dims.rows - used, BLOCK), BF16)
    for layer in (1, 0):
        vec_s[...] = jnp.zeros_like(vec_s)
        gain2, gain = row(feed_gain, layer), row(attend_gain, layer)
        put_vector(dims.at["reduce_bias"], jnp.sum(acc_s[2], 0, keepdims=True))

        for c in range(blocks):
            total = product(grad_low, act_s.at[layer], slice(c * BLOCK, (c + 1) * BLOCK), width)
            at = tops[0] + c * width
            sums[layer, at : at + width, :] = total.astype(BF16)
            flow.ready(layer, at + width)
            flow.tick(0.45)

        def feed_back(i):
            two = pair_of(i)
            grads = [grad_s[s].astype(BF16) for s in two]
            for c in range(blocks):
                cols = slice(c * BLOCK, (c + 1) * BLOCK)
                for g, s in zip(grads, two, strict=True):
                    dact = mm_nt(g, reduce_weight[layer, cols, :])
                    dup_s[s, :, cols] = (dact * slopes[layer][s, :, cols].astype(F32)).astype(BF16)
            flow.tick(1.2)

        for i in range(n_seq // 2):
            feed_back(i)

        for c in range(blocks):
            total = product(norm_n.at[2 * layer + 1], dup_s, slice(c * BLOCK, (c + 1) * BLOCK), width + TILE)
            at = tops[1] + c * width
            sums[layer, at : at + width, :] = total[:width].astype(BF16)
            at_bias = dims.at["expand_bias"] + c
            vec_s[at_bias : at_bias + 1, :] = total[width : width + 1]
            flow.ready(layer, at + width)
            flow.tick(0.45)

        def feed_norm_back(i):
            two = pair_of(i)
            dhs = [mm_nt(dup_s[s], expand_weight[layer]) for s in two]
            for dh, s in zip(dhs, two, strict=True):
                end_back(s, grad_s[s], unit_s[2 * layer + 1, s], scale_s[2 * layer + 1, s], gain2, dh)
            flow.tick(1.4)

        acc_s[0:2] = jnp.zeros((2, 8, width), F32)
        for i in range(n_seq // 2):
            feed_norm_back(i)
        put_vector(dims.at["feed_gain"], jnp.sum(acc_s[0], 0, keepdims=True))
        put_vector(dims.at["feed_shift"], jnp.sum(acc_s[1], 0, keepdims=True))

        bias_parts = []
        for c in range(0, width, BLOCK):
            size = min(BLOCK, width - c)
            total = product(mixed_s.at[layer], grad_low, slice(c, c + size), width + TILE)
            for k in range(0, size, LANES):
                put_tile(layer, tops[2], (c + k) // LANES, total[:width, k : k + LANES])
                bias_parts.append(total[width : width + 1, k : k + LANES])
        put_vector(dims.at["output_bias"], jnp.concatenate(bias_parts, 1))
        flow.ready(layer, tops[3])
        flow.tick(0.8)

        def attend_back(i):
            two = pair_of(i)
            dmixed = [mm_nt(grad_low[s], output_weight[layer]) for s in two]
            for p in range(pairs):
                at = p * LANES
                dqs, dks, dvs, dms, inners = [None] * 2, [None] * 2, [None] * 2, [], []
                for d, s in zip(dmixed, two, strict=True):
                    dm = d[:, at : at + LANES] * inverse_s[layer, s, :, at : at + LANES]
                    inners.append(-(dm * mixed_s[layer, s, :, at : at + LANES].astype(F32)).astype(BF16))
                    dms.append(dm.astype(BF16))
                for h, half in enumerate((low_half, high_half)):
                    for k, s in enumerate(two):
                        query = packed_s[layer, s, :, at : at + LANES]
                        key = packed_s[layer, s, :, width + at : width + at + LANES]
                        value = packed_s[layer, s, :, 2 * width + at : 2 * width + at + LANES]
                        power = power_s[layer, s, 2 * p + h]
                        dm_half = dms[k] * half
                        left = jnp.concatenate([dm_half, inners[k] * half], 1)
                        wide_value = jnp.concatenate([value, jnp.ones_like(value)], 1)
                        ds = (power.astype(F32) * mm_nt(left, wide_value)).astype(BF16)
                        dqs[k] = add_to(dqs[k], mm(ds, key * half))
                        dks[k] = add_to(dks[k], mm_tn(ds, query * half))
                        dvs[k] = add_to(dvs[k], mm_tn(power, dm_half))
                for k, s in enumerate(two):
                    dup_s[s, :, at : at + LANES] = (dqs[k] * score_scale).astype(BF16)
                    dup_s[s, :, width + at : width + at + LANES] = (dks[k] * score_scale).astype(BF16)
                    dup_s[s, :, 2 * width + at : 2 * width + at + LANES] = dvs[k].astype(BF16)
                flow.tick(1.1)

        for i in range(n_seq // 2):
            attend_back(i)

        bias_parts = []
        for c in range(0, 3 * width, BLOCK):
            size = min(BLOCK, 3 * width - c)
            total = product(norm_n.at[2 * layer], dup_s, slice(c, c + size), width + TILE)
            for k in range(0, size, LANES):
                put_tile(layer, tops[3], (c + k) // LANES, total[:width, k : k + LANES])
                bias_parts.append(total[width : width + 1, k : k + LANES])
            flow.tick(0.5)
        each = width // LANES
        put_vector(
            dims.at["mixer_bias"],
            jnp.concatenate(bias_parts[:each] + bias_parts[2 * each :], 1),
        )
        flow.ready(layer, dims.rows if layer == 1 else tops[4])

        def attend_norm_back(i):
            two = pair_of(i)
            dhs = [mm_nt(dup_s[s, :, 0 : 3 * width], mixer_weight[layer]) for s in two]
            for dh, s in zip(dhs, two, strict=True):
                end_back(s, grad_s[s], unit_s[2 * layer, s], scale_s[2 * layer, s], gain, dh)
                if layer == 1:
                    start_back(s, grad_s[s])
            flow.tick(1.2)

        acc_s[...] = jnp.zeros_like(acc_s)
        for i in range(n_seq // 2):
            attend_norm_back(i)
        put_vector(dims.at["attend_gain"], jnp.sum(acc_s[0], 0, keepdims=True))
        put_vector(dims.at["attend_shift"], jnp.sum(acc_s[1], 0, keepdims=True))
        at = tops[4] + layer * dims.vec_rows
        sums[0, at : at + dims.vec_rows, :] = vec_s[...].astype(BF16)
        if layer == 0:
            flow.ready(0, dims.rows)

    for s in range(n_global):
        crop_s[:, s, :] = grad_s[s, 0:glen, :]
    global_back[...] = crop_s[...].astype(BF16)
    for j in range(n_local):
        s, at = n_global + j // group, llen * (j % group)
        local_back[j] = grad_s[s, at : at + llen, :].astype(BF16)
    outward[2].start()
    outward[3].start()
    flow.drain()
    for move in outward:
        move.wait()


class Wire:
    def __init__(self, size, first, second):
        self.size, self.first, self.second = size, first, second


def wires_of(mesh):
    names = mesh.axis_names
    places = {}
    for axis, name in enumerate(names):
        line = [mesh.devices[tuple(i if a == axis else 0 for a in range(2))] for i in range(mesh.devices.shape[axis])]
        spots = [(d.core_on_chip,) + tuple(d.coords) for d in line]
        found, total = [], 1
        for k in range(4):
            values = sorted({p[k] for p in spots})
            if len(values) > 1:
                stride = next(i for i, p in enumerate(spots) if p[k] != spots[0][k])
                found.append((k, axis, stride, len(values)))
                total *= len(values)
        good = total == len(line)
        for k, _, stride, size in found:
            values = [p[k] for p in spots]
            good = good and all(v == values[i // stride % size * stride] for i, v in enumerate(values))
        if not good:
            found = [(4 + axis, axis, 1, len(line))]
        for k, axis, stride, size in found:
            places[k] = (axis, stride, size)
    wires = []
    if 0 in places:
        wires.append(Wire(places[0][2], places[0], places[0]))
    if 0 in places and 1 in places and 2 in places and places[1][2] == places[2][2]:
        wires.append(Wire(places[1][2], places[1], places[2]))
        wires.append(Wire(places[1][2], places[2], places[1]))
        order = [3, 4, 5]
    else:
        order = [1, 2, 3, 4, 5]
    for k in order:
        if k in places:
            wires.append(Wire(places[k][2], places[k], places[k]))
    return wires


class Net:
    def __init__(self, wires):
        self.axes = ("dp", "section")
        self.here = [lax.axis_index(a) for a in self.axes]
        self.wires = wires
        first = wires[0]
        odd = self.spot(first.first) % 2 if first.size == 2 else 0
        self.odd = odd
        self.at = []
        for w in wires:
            a, b = self.spot(w.first), self.spot(w.second)
            self.at.append(a if w.first == w.second else a + odd * (b - a))

    def spot(self, place):
        axis, stride, size = place
        return self.here[axis] // stride % size

    def peer(self, stage, k):
        w = self.wires[stage]
        place = (self.at[stage] + k) % w.size
        move = place - self.at[stage]
        target = list(self.here)
        if w.first == w.second:
            target[w.first[0]] = target[w.first[0]] + move * w.first[1]
        else:
            target[w.first[0]] = target[w.first[0]] + move * w.first[1] * (1 - self.odd)
            target[w.second[0]] = target[w.second[0]] + move * w.second[1] * self.odd
        return tuple(target), place

    def greet(self):
        barrier = pltpu.get_barrier_semaphore()
        for stage, w in enumerate(self.wires):
            for k in range(1, w.size):
                pl.semaphore_signal(barrier, inc=1, device_id=self.peer(stage, k)[0], device_id_type=pl.DeviceIdType.MESH)

    def wait_greeting(self):
        pl.semaphore_wait(pltpu.get_barrier_semaphore(), sum(w.size - 1 for w in self.wires))


class Chunk:
    def __init__(self, net, sums, out, landing, sems, turn, layer, end):
        self.net, self.sums, self.out, self.landing = net, sums, out, landing
        self.send, self.recv, self.local, self.sent, self.free = sems
        self.turn = turn
        self.layer, self.end = layer, end
        self.due = None
        size, start = sums.shape[0], 0
        self.unit = size
        for w in net.wires:
            self.unit //= w.size
        self.size, self.start = [], []
        for stage, w in enumerate(net.wires):
            size //= w.size
            self.size.append(size)
            self.start.append((start, size))
            start = start + net.at[stage] * size
        self.own = start
        self.stages = len(net.wires)
        self.step = 0
        self.sem_at, at = {}, 0
        for phase in range(2):
            for stage, w in enumerate(net.wires):
                for k in range(1, w.size):
                    self.sem_at[phase, stage, k] = at
                    at += 1

    def rows(self, stage, place):
        start, size = self.start[stage]
        return pl.ds(pl.multiple_of(start + place * size, TILE), size)

    def copy(self, phase, stage, k):
        target, place = self.net.peer(stage, k)
        at = self.sem_at[phase, stage, k]
        if phase == 0:
            source, to = self.sums.at[self.rows(stage, place)], self.landing[stage].at[k - 1]
        else:
            rows = self.rows(stage, self.net.at[stage])
            source = to = self.sums.at[rows]
        return pltpu.make_async_remote_copy(
            src_ref=source,
            dst_ref=to,
            send_sem=self.send.at[at],
            recv_sem=self.recv.at[at],
            device_id=target,
            device_id_type=pl.DeviceIdType.MESH,
        )

    def arrival(self, stage, k):
        target, place = self.net.peer(stage, self.net.wires[stage].size - k)
        at = self.sem_at[1, stage, k]
        landed = self.sums.at[self.rows(stage, place)]
        return pltpu.make_async_remote_copy(
            src_ref=landed,
            dst_ref=landed,
            send_sem=self.send.at[at],
            recv_sem=self.recv.at[at],
            device_id=target,
            device_id_type=pl.DeviceIdType.MESH,
        )

    def start_stage(self, phase, stage):
        if phase == 0 and self.turn == 1:
            pl.semaphore_wait(self.free.at[stage], self.net.wires[stage].size - 1)
        if phase == 1:
            pl.semaphore_wait(self.sent.at[stage], self.net.wires[stage].size - 1)
        for k in range(1, self.net.wires[stage].size):
            self.copy(phase, stage, k).start()

    def load(self):
        last = self.stages - 1
        stage = self.step if self.step <= last else 2 * self.stages - 1 - self.step
        peers = self.net.wires[stage].size - 1
        row = BLOCK * 2
        if stage == 0:
            return 0, self.size[0] * row / 4
        if stage == last:
            return 2, self.size[stage] * (peers + 1) ** 2 / 2 * row
        return 1, self.size[stage] * peers * row

    def begin(self):
        self.start_stage(0, 0)

    def out_copy(self):
        return pltpu.make_async_copy(self.sums, self.out, self.local.at[0])

    def advance(self):
        step = self.step
        self.step += 1
        if step < self.stages:
            peers = range(1, self.net.wires[step].size)
            for k in peers:
                self.copy(0, step, k).wait_recv()
            base = self.start[step][0] + self.net.at[step] * self.size[step]
            landing = self.landing[step]

            count = self.size[step] // self.unit
            while count % 2 == 0 and self.size[step] // count < 128:
                count //= 2
            size = self.size[step] // count

            def add(i, _):
                at = pl.ds(pl.multiple_of(base + i * size, TILE), size)
                here = [landing[k - 1, pl.ds(pl.multiple_of(i * size, TILE), size), :] for k in peers]
                if len(here) == 1:
                    self.sums[at, :] = self.sums[at, :] + here[0]
                else:
                    total = self.sums[at, :].astype(F32)
                    for part in here:
                        total = total + part.astype(F32)
                    self.sums[at, :] = total.astype(BF16)
                return 0

            lax.fori_loop(0, count, add, 0)
            for k in peers:
                self.copy(0, step, k).wait_send()
                target = self.net.peer(step, k)[0]
                pl.semaphore_signal(self.sent.at[step], inc=1, device_id=target, device_id_type=pl.DeviceIdType.MESH)
                if self.turn == 0:
                    pl.semaphore_signal(self.free.at[step], inc=1, device_id=target, device_id_type=pl.DeviceIdType.MESH)
            if step + 1 < self.stages:
                self.start_stage(0, step + 1)
            else:
                self.start_stage(1, step)
        else:
            stage = 2 * self.stages - 1 - step
            for k in range(1, self.net.wires[stage].size):
                self.arrival(stage, k).wait_recv()
            if stage > 0:
                self.start_stage(1, stage - 1)
            else:
                self.out_copy().start()

    def finish(self):
        for phase, stage, k in self.sem_at:
            if phase == 1:
                self.copy(phase, stage, k).wait_send()
        self.out_copy().wait()


LATENCY = 1.5
RATE = 70e3
STEP = 0.4


class Flow:
    def __init__(self, net):
        self.chunks, self.now, self.waiting, self.free = [], 0.0, 0, [0.0] * 3

    def book(self, chunk):
        kind, size = chunk.load()
        self.free[kind] = max(self.now, self.free[kind]) + size / RATE
        chunk.due = self.free[kind] + LATENCY

    def ready(self, layer, rows):
        while self.waiting < len(self.chunks):
            chunk = self.chunks[self.waiting]
            if chunk.layer != layer or chunk.end > rows:
                return
            chunk.begin()
            self.book(chunk)
            self.waiting += 1

    def due(self):
        return sorted((c for c in self.chunks if c.due is not None and c.due <= self.now), key=lambda c: c.due)

    def take(self):
        while self.due():
            chunk = self.due()[0]
            chunk.advance()
            self.now += STEP
            if chunk.step < 2 * chunk.stages:
                self.book(chunk)
            else:
                chunk.due = None

    def tick(self, time):
        self.now += time
        self.take()

    def drain(self):
        while any(c.due is not None for c in self.chunks):
            self.now = max(self.now, min(c.due for c in self.chunks if c.due is not None))
            self.take()
        for chunk in self.chunks:
            chunk.finish()


class Dims:
    def __init__(self, global_crops, local_crops, hidden, wires):
        self.wires = wires
        self.glen, self.n_global, self.width = global_crops.shape
        self.n_local, self.llen, _ = local_crops.shape
        self.hidden = hidden
        self.seq = up_to(self.glen, TILE)
        self.group = self.seq // self.llen
        while self.n_local % self.group:
            self.group -= 1
        self.n_seq = self.n_global + self.n_local // self.group
        assert self.n_seq % 2 == self.n_global % 2 == 0
        sizes = (
            ("attend_gain", self.width),
            ("attend_shift", self.width),
            ("mixer_bias", 2 * self.width),
            ("output_bias", self.width),
            ("feed_gain", self.width),
            ("feed_shift", self.width),
            ("expand_bias", hidden),
            ("reduce_bias", self.width),
        )
        self.names, self.sizes = [name for name, _ in sizes], dict(sizes)
        self.at, row = {}, 0
        for name, size in sizes:
            self.at[name] = row
            row += -(-size // BLOCK)
        self.vec_rows = 2 * TILE
        assert row <= self.vec_rows and self.width * hidden % self.vec_rows == 0
        step = TILE
        for w in wires:
            step *= w.size
        ff = self.width * hidden // BLOCK
        square = self.width * self.width // BLOCK
        self.tops = (0, ff, 2 * ff, 2 * ff + square, 2 * ff + 4 * square)
        self.rows = up_to(self.tops[4] + 2 * self.vec_rows, step)
        parts = self.rows // step
        cuts = ((0, 4, 7, 10, 12, 14), (0, 4, 10, 14))
        self.bounds = [[c * step for c in sorted({parts * k // 14 for k in layer})] for layer in cuts]
        self.landing_sets = [len(b) - 1 for b in self.bounds[::-1]]
        if self.bounds[0] == self.bounds[1]:
            self.landing_sets = self.landing_sets[:1]
        self.n_chunk = sum(len(b) - 1 for b in self.bounds)


HEAVY = (6, 8, 12, 14)


def run_kernel(counts, arrays, dims):
    d = dims
    n, seq, width, hidden = d.n_seq, d.seq, d.width, d.hidden
    crops = [jax.ShapeDtypeStruct(a.shape, BF16) for a in arrays[:2]]
    outs = crops + crops
    outs += [jax.ShapeDtypeStruct((2, d.rows, BLOCK), BF16)]
    scratch = [pltpu.VMEM(a.shape, BF16) for a in tuple(arrays[:4]) * 2]
    scratch += [pltpu.VMEM(arrays[i].shape, BF16) for i in HEAVY]
    scratch += [
        pltpu.SemaphoreType.DMA((16,)),
        pltpu.VMEM((2, d.rows, BLOCK), BF16),
        pltpu.VMEM((d.glen, d.n_global, width), F32),
        pltpu.VMEM((n, seq, width), F32),
        pltpu.VMEM((4, n, seq, width), BF16),
        pltpu.VMEM((4, n, seq, 1), F32),
        pltpu.VMEM((4, n, seq, width + LANES), BF16),
        pltpu.VMEM((2, n, seq, 3 * width), BF16),
        pltpu.VMEM((2, n, HEADS, seq, seq), BF16),
        pltpu.VMEM((2, n, seq, width), F32),
        pltpu.VMEM((2, n, seq, width + LANES), BF16),
        pltpu.VMEM((2, n, seq, hidden), BF16),
        pltpu.VMEM((n, seq, hidden), BF16),
        pltpu.VMEM((n, seq, width), F32),
        pltpu.VMEM((n, seq, width), BF16),
        pltpu.VMEM((n, seq, hidden), BF16),
        pltpu.VMEM((2, 2, 2, seq, LANES), BF16),
        pltpu.VMEM((d.vec_rows, BLOCK), F32),
        pltpu.VMEM((3, 8, width), F32),
    ]
    for layer in (1, 0)[: len(d.landing_sets)]:
        for first, end in zip(d.bounds[layer], d.bounds[layer][1:]):
            rows = end - first
            for w in d.wires:
                rows //= w.size
                scratch.append(pltpu.VMEM((w.size - 1, rows, BLOCK), BF16))
    peers = 2 * sum(w.size - 1 for w in d.wires)
    scratch += [
        pltpu.SemaphoreType.DMA((d.n_chunk, peers)),
        pltpu.SemaphoreType.DMA((d.n_chunk, peers)),
        pltpu.SemaphoreType.DMA((d.n_chunk, 1)),
        pltpu.SemaphoreType.REGULAR((d.n_chunk, len(d.wires))),
        pltpu.SemaphoreType.REGULAR((d.n_chunk, len(d.wires))),
    ]
    vmem = pl.BlockSpec(memory_space=pltpu.VMEM)
    anywhere = pl.BlockSpec(memory_space=pl.ANY)
    return pl.pallas_call(
        functools.partial(kernel, d),
        out_shape=outs,
        in_specs=[pl.BlockSpec(memory_space=pltpu.SMEM)]
        + [anywhere if i < 4 or i in HEAVY else vmem for i in range(len(arrays))],
        out_specs=[anywhere] * len(outs),
        scratch_shapes=scratch,
        compiler_params=pltpu.CompilerParams(
            vmem_limit_bytes=63 * 1024 * 1024, collective_id=0, has_side_effects=True
        ),
    )(counts, *arrays)


THIRDS = 3


def cast_kernel(dims, reduce, expand, output, mixer, vectors, *rest):
    crops, outs, held, sems = rest[:4], rest[4:16], rest[20:24], rest[-1]
    tables = rest[24:-1]
    notes = [pltpu.make_async_copy(a, b, sems.at[2, i]) for i, (a, b) in enumerate(zip(tables, outs[4:], strict=True))]
    step = pl.program_id(0) * THIRDS + pl.program_id(1)
    loads = [pltpu.make_async_copy(a, b, sems.at[0, i]) for i, (a, b) in enumerate(zip(crops, held, strict=True))]
    stores = [pltpu.make_async_copy(a, b, sems.at[1, i]) for i, (a, b) in enumerate(zip(held, rest[16:20], strict=True))]

    @pl.when(step == 0)
    def _():
        for copy in loads:
            copy.start()
        for ref, name, note in zip(tables, dims.names, notes, strict=True):
            size = ref.shape[1]
            for c in range(0, size, BLOCK):
                at = dims.at[name] + c // BLOCK
                piece = min(BLOCK, size - c)
                for layer in range(2):
                    ref[layer : layer + 1, c : c + piece] = vectors[0].astype(F32)[at + layer * dims.vec_rows :][:1, 0:piece]
            note.start()

    @pl.when(step == 1)
    def _():
        for load, store in zip(loads, stores, strict=True):
            load.wait()
            store.start()

    mixer_grad, output_grad, expand_grad, reduce_grad = outs[:4]
    width = dims.width
    fold = width // 2
    for b in range(2):
        rows = slice(b * width, (b + 1) * width)
        cols = slice(b * BLOCK, (b + 1) * BLOCK)
        expand_grad[0, :, cols] = expand[0, rows, :].astype(F32)
        reduce_grad[0, cols, :] = reduce[0, rows, :].T.astype(F32)
    for source, target in ((mixer, mixer_grad), (output, output_grad)):
        target[0, :, 0:BLOCK] = source[0, 0:width, :].astype(F32)
        target[0, 0:fold, BLOCK:] = source[0, width:, 0:LANES].astype(F32)
        target[0, fold:, BLOCK:] = source[0, width:, LANES:].astype(F32)

    @pl.when(step == 2 * THIRDS - 1)
    def _():
        for note in notes:
            note.wait()
        for store in stores:
            store.wait()


def run_cast(sums, crops, dims):
    d = dims
    width, hidden = d.width, d.hidden
    part = (1, 2 * width, BLOCK)
    square = (1, width * width // BLOCK, BLOCK)
    grads = [(width, 3 * width), (width, width), (width, hidden), (hidden, width)]
    shapes = [jax.ShapeDtypeStruct((2,) + g, F32) for g in grads]
    specs = [
        pl.BlockSpec((1, width, 3 * width // THIRDS), lambda l, t: (l, 0, t)),
        pl.BlockSpec((1, width, width), lambda l, t: (l, 0, 0)),
        pl.BlockSpec((1, width, hidden // THIRDS), lambda l, t: (l, 0, t)),
        pl.BlockSpec((1, hidden // THIRDS, width), lambda l, t: (l, t, 0)),
    ]
    for name in d.names:
        shapes.append(jax.ShapeDtypeStruct((2, d.sizes[name]), F32))
        specs.append(pl.BlockSpec(memory_space=pl.ANY))
    for crop in crops:
        shapes.append(jax.ShapeDtypeStruct(crop.shape, crop.dtype))
        specs.append(pl.BlockSpec(memory_space=pl.ANY))
    return pl.pallas_call(
        functools.partial(cast_kernel, d),
        grid=(2, THIRDS),
        out_shape=shapes,
        in_specs=[
            pl.BlockSpec(part, lambda l, t: (l, t, 0)),
            pl.BlockSpec(part, lambda l, t: (l, THIRDS + t, 0)),
            pl.BlockSpec(square, lambda l, t: (l, d.tops[2] // square[1], 0)),
            pl.BlockSpec(square, lambda l, t: (l, d.tops[3] // square[1] + t, 0)),
            pl.BlockSpec((1, 2 * d.vec_rows, BLOCK), lambda l, t: (0, d.tops[4] // (2 * d.vec_rows), 0)),
        ]
        + [pl.BlockSpec(memory_space=pl.ANY)] * 4,
        out_specs=specs,
        scratch_shapes=[pltpu.VMEM(c.shape, c.dtype) for c in crops]
        + [pltpu.VMEM((2, d.sizes[name]), F32) for name in d.names]
        + [pltpu.SemaphoreType.DMA((3, 8))],
        compiler_params=pltpu.CompilerParams(vmem_limit_bytes=62 * 1024 * 1024),
    )(sums, sums, sums, sums, sums, *crops)


def shards(wires, global_crops, local_crops, local_count, global_cotangent, local_cotangent, *weights):
    global_crops, global_cotangent = global_crops.transpose(1, 0, 2), global_cotangent.transpose(1, 0, 2)
    dims = Dims(global_crops, local_crops, weights[8].shape[2], wires)
    outs = run_kernel(
        local_count, (global_crops, local_crops, global_cotangent, local_cotangent) + weights, dims
    )
    mixer, output, expand, reduce, *rest = run_cast(outs[4], outs[:4], dims)
    vectors, crops = rest[:-4], rest[-4:]
    v = dict(zip(dims.names, vectors, strict=True))
    return (
        crops[0].transpose(1, 0, 2),
        crops[1],
        crops[2].transpose(1, 0, 2),
        crops[3],
        v["attend_gain"],
        v["attend_shift"],
        mixer,
        v["mixer_bias"],
        output,
        v["output_bias"],
        v["feed_gain"],
        v["feed_shift"],
        expand,
        v["expand_bias"],
        reduce,
        v["reduce_bias"],
    )


def solution(mesh):
    crops = P(("dp", "section"), None, None)
    return jax.shard_map(
        functools.partial(shards, wires_of(mesh)),
        mesh=mesh,
        in_specs=(crops, crops, P("dp"), crops, crops) + (P(),) * 12,
        out_specs=(crops,) * 4 + (P(),) * 12,
        check_vma=False,
    )
```

```python
import functools

import jax
import jax.numpy as jnp
from jax import lax
from jax.experimental import pallas as pl
from jax.experimental.pallas import tpu as pltpu
from jax.sharding import PartitionSpec as P

HEADS = 6
HEAD = 64
EPS = 1e-06
TILE = 16
LANES = 128
BLOCK = 256
LOG2E = 1.4426950408889634
F32 = jnp.float32
BF16 = jnp.bfloat16


def up_to(value, step):
    return -(-value // step) * step


def mm(left, right):
    return lax.dot_general(left, right, (((1,), (0,)), ((), ())), preferred_element_type=F32)


def mm_nt(left, right):
    return lax.dot_general(left, right, (((1,), (1,)), ((), ())), preferred_element_type=F32)


def mm_tn(left, right):
    return lax.dot_general(left, right, (((0,), (0,)), ((), ())), preferred_element_type=F32)


def norm(rows):
    centred = rows - jnp.mean(rows, -1, keepdims=True)
    scale = lax.rsqrt(jnp.mean(centred * centred, -1, keepdims=True) + EPS)
    return centred * scale, scale


def norm_back(grad, unit, scale, gain):
    slope = grad * gain
    first = jnp.mean(slope, -1, keepdims=True)
    second = jnp.mean(slope * unit, -1, keepdims=True)
    return scale * (slope - first - unit * second)


def gelu_parts(u):
    size = jnp.abs(u)
    d = 1.0 + (0.3275911 * 0.7071067811865476) * size
    t = pl.reciprocal(d, approx=True)
    t = t * (2.0 - d * t)
    poly = 0.5 * 1.061405429
    for a in (-1.453152027, 1.421413741, -0.284496736, 0.254829592):
        poly = poly * t + 0.5 * a
    bell = jnp.exp2((u * u) * (-0.5 * LOG2E))
    tail = poly * t * bell
    phi = jnp.where(u < 0.0, tail, 1.0 - tail)
    return u * phi, phi + (u * bell) * 0.3989422804014327


def fold8(value):
    rows, width = value.shape
    return jnp.sum(value.reshape(rows // 8, 8, width), 0)


def kernel(
    dims,
    counts,
    global_in_hbm,
    local_in_hbm,
    global_cot_hbm,
    local_cot_hbm,
    attend_gain,
    attend_shift,
    mixer_hbm,
    mixer_bias,
    output_hbm,
    output_bias,
    feed_gain,
    feed_shift,
    expand_hbm,
    expand_bias,
    reduce_hbm,
    reduce_bias,
    global_out_hbm,
    local_out_hbm,
    global_back_hbm,
    local_back_hbm,
    sums_out,
    global_in,
    local_in,
    global_cot,
    local_cot,
    global_out,
    local_out,
    global_back,
    local_back,
    mixer_weight,
    output_weight,
    expand_weight,
    reduce_weight,
    io_sem,
    sums,
    crop_s,
    x_s,
    unit_s,
    scale_s,
    norm_n,
    packed_s,
    power_s,
    inverse_s,
    mixed_s,
    act_s,
    slope_s,
    grad_s,
    grad_low,
    dup_s,
    aug_s,
    vec_s,
    acc_s,
    *wires,
):
    seq, group, width = dims.seq, dims.group, dims.width
    glen, llen = dims.glen, dims.llen
    n_global, n_local, n_seq = dims.n_global, dims.n_local, dims.n_seq
    hidden = dims.hidden
    count = counts[lax.axis_index("section")]
    pairs = HEADS // 2
    lane = lax.broadcasted_iota(jnp.int32, (1, LANES), 1)
    low_half = (lane < HEAD).astype(F32).astype(BF16)
    high_half = (lane >= HEAD).astype(F32).astype(BF16)
    score_scale = HEAD ** (-0.5)

    moves = [pltpu.make_async_copy(global_in_hbm, global_in, io_sem.at[0]), pltpu.make_async_copy(local_in_hbm, local_in, io_sem.at[1])]
    weights = ((mixer_hbm, mixer_weight), (output_hbm, output_weight), (expand_hbm, expand_weight), (reduce_hbm, reduce_weight))
    for layer in range(2):
        for source, target in weights:
            moves.append(pltpu.make_async_copy(source.at[layer], target.at[layer], io_sem.at[len(moves)]))
    moves += [
        pltpu.make_async_copy(global_cot_hbm, global_cot, io_sem.at[10]),
        pltpu.make_async_copy(local_cot_hbm, local_cot, io_sem.at[11]),
    ]
    outward = [
        pltpu.make_async_copy(global_out, global_out_hbm, io_sem.at[12]),
        pltpu.make_async_copy(local_out, local_out_hbm, io_sem.at[13]),
        pltpu.make_async_copy(global_back, global_back_hbm, io_sem.at[14]),
        pltpu.make_async_copy(local_back, local_back_hbm, io_sem.at[15]),
    ]
    for move in moves:
        move.start()

    net = Net(dims.wires)
    net.greet()
    n_stage = len(dims.wires)
    sets = dims.landing_sets
    landings, sems = wires[: n_stage * sum(sets)], wires[n_stage * sum(sets) :]
    flow = Flow(net)
    number = 0
    for layer in (1, 0):
        bounds = dims.bounds[layer]
        for i in range(len(bounds) - 1):
            shared = len(sets) == 1
            at = (i if shared else number) * n_stage
            own = [w.at[number] for w in sems[:4]] + [sems[4].at[i]]
            rows = pl.ds(bounds[i], bounds[i + 1] - bounds[i])
            turn = (1 - layer) if shared else None
            flow.chunks.append(
                Chunk(net, dims.orders[layer][i], sums.at[layer, rows], sums_out.at[layer, rows], landings[at : at + n_stage], own, turn, layer, bounds[i + 1])
            )
            number += 1

    for s in range(n_seq):
        x_s[s, seq - 32 :, :] = jnp.zeros((32, width), F32)
        grad_s[s, seq - 32 :, :] = jnp.zeros((32, width), F32)
    row_id = lax.broadcasted_iota(jnp.int32, (seq, LANES), 0)
    col_id = lax.broadcasted_iota(jnp.int32, (seq, LANES), 1)
    row_crop = sum((row_id >= llen * j).astype(jnp.int32) for j in range(1, group + 1))
    far = jnp.float32(-1e30)
    zero = jnp.float32(0)
    for h in range(2):
        place = col_id - (1 - h) * HEAD
        used = (place >= 0) & (place <= group)
        aug_s[0, h, 0] = jnp.where(place == 0, jnp.float32(1), zero).astype(BF16)
        aug_s[0, h, 1] = jnp.where((place == 0) & (row_id >= glen), far, zero).astype(BF16)
        aug_s[1, h, 0] = jnp.where(place == row_crop, jnp.float32(1), zero).astype(BF16)
        aug_s[1, h, 1] = jnp.where(used & (place != row_crop), far, zero).astype(BF16)
    one_column = (lax.broadcasted_iota(jnp.int32, (seq, LANES), 1) == 0).astype(F32).astype(BF16)
    for s in range(n_seq):
        for i in range(4):
            norm_n[i, s, :, width:] = one_column
        for i in range(2):
            mixed_s[i, s, :, width:] = one_column

    def live_rows(g):
        rows = lax.broadcasted_iota(jnp.int32, (seq, 1), 0)
        return (rows < llen * jnp.clip(count - g * group, 0, group)).astype(F32)

    def take_crops(crops, locals_, target):
        crop_s[...] = crops[...].astype(F32)
        for s in range(n_global):
            target[s, 0:glen, :] = crop_s[:, s, :]
        for j in range(n_local):
            s, at = n_global + j // group, llen * (j % group)
            target[s, at : at + llen, :] = locals_[j].astype(F32)

    def take_cotangents():
        moves[10].wait()
        moves[11].wait()
        take_crops(global_cot, local_cot, grad_s)
        for s in range(n_global, n_seq):
            grad_s[s] = grad_s[s] * live_rows(s - n_global)

    moves[0].wait()
    moves[1].wait()
    take_crops(global_in, local_in, x_s)

    def row(ref, layer):
        return ref[...].astype(F32)[layer : layer + 1]

    slopes = (slope_s, dup_s)

    def start_back(s, grad):
        grad_low[s] = grad.astype(BF16)
        acc_s[2] = acc_s[2] + fold8(grad)

    def end_back(s, grad, unit, scale, gain, dh):
        unit = unit.astype(F32)
        acc_s[0] = acc_s[0] + fold8(dh * unit)
        acc_s[1] = acc_s[1] + fold8(dh)
        grad = (grad + norm_back(dh, unit, scale, gain)).astype(BF16)
        grad_low[s] = grad
        grad_s[s] = grad.astype(F32)

    def product(left, right, cols, first):
        total = None
        for s in range(n_seq):
            term = mm_tn(left[s, :, 0:first], right[s, :, cols])
            total = term if total is None else total + term
        return total

    for layer in range(2):
        gain, shift = row(attend_gain, layer), row(attend_shift, layer)
        bias = row(mixer_bias, layer)
        bias = jnp.concatenate([bias[:, :width], jnp.zeros((1, width), F32), bias[:, width:]], 1)
        out_bias = row(output_bias, layer)
        gain2, shift2 = row(feed_gain, layer), row(feed_shift, layer)
        bias_up, bias_down = row(expand_bias, layer), row(reduce_bias, layer)

        def attend(s, _):
            x = x_s[s]
            unit, scale = norm(x)
            unit_s[2 * layer, s] = unit.astype(BF16)
            scale_s[2 * layer, s] = scale
            normed = (unit * gain + shift).astype(BF16)
            norm_n[2 * layer, s, :, 0:width] = normed
            packed = (mm(normed, mixer_weight[layer]) + bias).astype(BF16)
            packed_s[layer, s] = packed
            kind = jnp.where(s < n_global, 0, 1)
            mixed = []
            for p in range(pairs):
                at = p * LANES
                query = packed[:, at : at + LANES]
                key = packed[:, width + at : width + at + LANES]
                value = packed[:, 2 * width + at : 2 * width + at + LANES]
                total = None
                for h, half in enumerate((low_half, high_half)):
                    scores = mm_nt(query * half + aug_s[kind, h, 0], key * half + aug_s[kind, h, 1]) * (score_scale * LOG2E)
                    power = jnp.exp2(scores - jnp.max(scores, -1, keepdims=True)).astype(BF16)
                    power_s[layer, s, 2 * p + h] = power
                    spread = jnp.broadcast_to(half, (seq, LANES))
                    term = mm(power, jnp.concatenate([value * half, spread], 1))
                    total = term if total is None else total + term
                inverse = 1.0 / total[:, LANES:]
                inverse_s[layer, s, :, at : at + LANES] = inverse
                mixed.append((total[:, :LANES] * inverse).astype(BF16))
            mixed = jnp.concatenate(mixed, 1)
            mixed_s[layer, s, :, 0:width] = mixed
            x = x + mm(mixed, output_weight[layer]) + out_bias
            x_s[s] = x.astype(BF16).astype(F32)
            return 0

        moves[2 + 4 * layer].wait()
        moves[3 + 4 * layer].wait()
        lax.fori_loop(0, n_seq, attend, 0)

        def feed(s, _):
            x = x_s[s]
            unit, scale = norm(x)
            normed = (unit * gain2 + shift2).astype(BF16)
            norm_n[2 * layer + 1, s, :, 0:width] = normed
            unit_s[2 * layer + 1, s] = unit.astype(BF16)
            scale_s[2 * layer + 1, s] = scale
            if layer == 1:
                start_back(s, grad_s[s])
            for c in range(hidden // BLOCK):
                cols = slice(c * BLOCK, (c + 1) * BLOCK)
                up = mm(normed, expand_weight[layer, :, cols]) + bias_up[:, cols]
                act, slope = gelu_parts(up)
                act_s[layer, s, :, cols] = act.astype(BF16)
                slopes[layer][s, :, cols] = slope.astype(BF16)
            x = x + mm(act_s[layer, s], reduce_weight[layer]) + bias_down
            x_s[s] = x.astype(BF16).astype(F32)
            return 0

        moves[4 + 4 * layer].wait()
        moves[5 + 4 * layer].wait()
        if layer == 1:
            take_cotangents()
            acc_s[...] = jnp.zeros_like(acc_s)
        lax.fori_loop(0, n_seq, feed, 0)

    for s in range(n_global):
        crop_s[:, s, :] = x_s[s, 0:glen, :]
    global_out[...] = crop_s[...].astype(BF16)
    for j in range(n_local):
        s, at = n_global + j // group, llen * (j % group)
        alive = (count > j).astype(F32)
        local_out[j] = (x_s[s, at : at + llen, :] * alive).astype(BF16)
    outward[0].start()
    outward[1].start()

    def put_vector(at, value):
        for c in range(0, value.shape[1], BLOCK):
            piece = value[:, c : c + BLOCK]
            vec_s[at + c // BLOCK : at + c // BLOCK + 1, 0 : piece.shape[1]] = piece

    def put_tile(layer, top, m, part):
        at = top + (m // 3) * (width + fold)
        side = m % 3 * LANES
        part = part.astype(BF16)
        if m % 3 < 2:
            sums[layer, at : at + width, side : side + LANES] = part
        else:
            at = at + width
            sums[layer, at : at + fold, 0:LANES] = part[:fold]
            sums[layer, at : at + fold, LANES:] = part[fold:]

    blocks = hidden // BLOCK
    fold = width // 2
    tops = dims.tops
    net.wait_greeting()
    for layer, used in ((1, tops[4]), (0, tops[4] + 2 * dims.vec_rows)):
        if dims.rows > used:
            sums[layer, used:, :] = jnp.zeros((dims.rows - used, BLOCK), BF16)
    for layer in (1, 0):
        vec_s[...] = jnp.zeros_like(vec_s)
        gain2, gain = row(feed_gain, layer), row(attend_gain, layer)
        put_vector(dims.at["reduce_bias"], jnp.sum(acc_s[2], 0, keepdims=True))

        for c in range(blocks):
            total = product(grad_low, act_s.at[layer], slice(c * BLOCK, (c + 1) * BLOCK), width)
            at = tops[0] + c * width
            sums[layer, at : at + width, :] = total.astype(BF16)
            flow.ready(layer, at + width)
            flow.tick(0.45)

        def feed_back(s, _):
            grad_in = grad_s[s].astype(BF16)
            for c in range(blocks):
                cols = slice(c * BLOCK, (c + 1) * BLOCK)
                dact = mm_nt(grad_in, reduce_weight[layer, cols, :])
                dup_s[s, :, cols] = (dact * slopes[layer][s, :, cols].astype(F32)).astype(BF16)
            flow.ticks(s, n_seq, 0.6)
            return 0

        lax.fori_loop(0, n_seq, feed_back, 0)

        for c in range(blocks):
            total = product(norm_n.at[2 * layer + 1], dup_s, slice(c * BLOCK, (c + 1) * BLOCK), width + TILE)
            at = tops[1] + c * width
            sums[layer, at : at + width, :] = total[:width].astype(BF16)
            at_bias = dims.at["expand_bias"] + c
            vec_s[at_bias : at_bias + 1, :] = total[width : width + 1]
            flow.ready(layer, at + width)
            flow.tick(0.45)

        def feed_norm_back(s, _):
            dh = mm_nt(dup_s[s], expand_weight[layer])
            end_back(s, grad_s[s], unit_s[2 * layer + 1, s], scale_s[2 * layer + 1, s], gain2, dh)
            flow.ticks(s, n_seq, 0.7)
            return 0

        acc_s[0:2] = jnp.zeros((2, 8, width), F32)
        lax.fori_loop(0, n_seq, feed_norm_back, 0)
        put_vector(dims.at["feed_gain"], jnp.sum(acc_s[0], 0, keepdims=True))
        put_vector(dims.at["feed_shift"], jnp.sum(acc_s[1], 0, keepdims=True))

        bias_parts = []
        for c in range(0, width, BLOCK):
            size = min(BLOCK, width - c)
            total = product(mixed_s.at[layer], grad_low, slice(c, c + size), width + TILE)
            for k in range(0, size, LANES):
                put_tile(layer, tops[2], (c + k) // LANES, total[:width, k : k + LANES])
                bias_parts.append(total[width : width + 1, k : k + LANES])
        put_vector(dims.at["output_bias"], jnp.concatenate(bias_parts, 1))
        flow.ready(layer, tops[3])
        flow.tick(0.8)

        def attend_back(s, _):
            dmixed = mm_nt(grad_low[s], output_weight[layer])
            parts = [None] * (3 * pairs)
            for p in range(pairs):
                at = p * LANES
                query = packed_s[layer, s, :, at : at + LANES]
                key = packed_s[layer, s, :, width + at : width + at + LANES]
                value = packed_s[layer, s, :, 2 * width + at : 2 * width + at + LANES]
                dm = dmixed[:, at : at + LANES] * inverse_s[layer, s, :, at : at + LANES]
                inner = -(dm * mixed_s[layer, s, :, at : at + LANES].astype(F32)).astype(BF16)
                dm = dm.astype(BF16)
                wide_value = jnp.concatenate([value, jnp.ones_like(value)], 1)
                dq = dk = dv = None
                for h, half in enumerate((low_half, high_half)):
                    power = power_s[layer, s, 2 * p + h]
                    dm_half = dm * half
                    left = jnp.concatenate([dm_half, inner * half], 1)
                    ds = (power.astype(F32) * mm_nt(left, wide_value)).astype(BF16)
                    terms = (mm(ds, key * half), mm_tn(ds, query * half), mm_tn(power, dm_half))
                    dq = terms[0] if dq is None else dq + terms[0]
                    dk = terms[1] if dk is None else dk + terms[1]
                    dv = terms[2] if dv is None else dv + terms[2]
                parts[p] = (dq * score_scale).astype(BF16)
                parts[pairs + p] = (dk * score_scale).astype(BF16)
                parts[2 * pairs + p] = dv.astype(BF16)
            dup_s[s, :, 0 : 3 * width] = jnp.concatenate(parts, 1)
            flow.ticks(s, n_seq, 1.7)
            return 0

        lax.fori_loop(0, n_seq, attend_back, 0)

        bias_parts = []
        for c in range(0, 3 * width, BLOCK):
            size = min(BLOCK, 3 * width - c)
            total = product(norm_n.at[2 * layer], dup_s, slice(c, c + size), width + TILE)
            for k in range(0, size, LANES):
                put_tile(layer, tops[3], (c + k) // LANES, total[:width, k : k + LANES])
                bias_parts.append(total[width : width + 1, k : k + LANES])
            flow.tick(0.5)
        each = width // LANES
        put_vector(
            dims.at["mixer_bias"],
            jnp.concatenate(bias_parts[:each] + bias_parts[2 * each :], 1),
        )
        flow.ready(layer, dims.rows if layer == 1 else tops[4])

        def attend_norm_back(s, _):
            dh = mm_nt(dup_s[s, :, 0 : 3 * width], mixer_weight[layer])
            end_back(s, grad_s[s], unit_s[2 * layer, s], scale_s[2 * layer, s], gain, dh)
            if layer == 1:
                start_back(s, grad_s[s])
            flow.ticks(s, n_seq, 0.6)
            return 0

        acc_s[...] = jnp.zeros_like(acc_s)
        lax.fori_loop(0, n_seq, attend_norm_back, 0)
        put_vector(dims.at["attend_gain"], jnp.sum(acc_s[0], 0, keepdims=True))
        put_vector(dims.at["attend_shift"], jnp.sum(acc_s[1], 0, keepdims=True))
        at = tops[4] + layer * dims.vec_rows
        sums[0, at : at + dims.vec_rows, :] = vec_s[...].astype(BF16)
        if layer == 0:
            flow.ready(0, dims.rows)

    for s in range(n_global):
        crop_s[:, s, :] = grad_s[s, 0:glen, :]
    global_back[...] = crop_s[...].astype(BF16)
    for j in range(n_local):
        s, at = n_global + j // group, llen * (j % group)
        local_back[j] = grad_s[s, at : at + llen, :].astype(BF16)
    outward[2].start()
    outward[3].start()
    flow.drain()
    for move in outward:
        move.wait()


class Wire:
    def __init__(self, size, first, second):
        self.size, self.first, self.second = size, first, second


def wires_of(mesh):
    names = mesh.axis_names
    places = {}
    for axis, name in enumerate(names):
        line = [mesh.devices[tuple(i if a == axis else 0 for a in range(2))] for i in range(mesh.devices.shape[axis])]
        spots = [(d.core_on_chip,) + tuple(d.coords) for d in line]
        found, total = [], 1
        for k in range(4):
            values = sorted({p[k] for p in spots})
            if len(values) > 1:
                stride = next(i for i, p in enumerate(spots) if p[k] != spots[0][k])
                found.append((k, axis, stride, len(values)))
                total *= len(values)
        good = total == len(line)
        for k, _, stride, size in found:
            values = [p[k] for p in spots]
            good = good and all(v == values[i // stride % size * stride] for i, v in enumerate(values))
        if not good:
            found = [(4 + axis, axis, 1, len(line))]
        for k, axis, stride, size in found:
            places[k] = (axis, stride, size)
    wires = []
    if 0 in places:
        wires.append(Wire(places[0][2], places[0], places[0]))
    if 0 in places and 1 in places and 2 in places and places[1][2] == places[2][2]:
        wires.append(Wire(places[1][2], places[1], places[2]))
        wires.append(Wire(places[1][2], places[2], places[1]))
        order = [3, 4, 5]
    else:
        order = [1, 2, 3, 4, 5]
    for k in order:
        if k in places:
            wires.append(Wire(places[k][2], places[k], places[k]))
    return wires


class Net:
    def __init__(self, wires):
        self.axes = ("dp", "section")
        self.here = [lax.axis_index(a) for a in self.axes]
        self.wires = wires
        first = wires[0]
        odd = self.spot(first.first) % 2 if first.size == 2 else 0
        self.odd = odd
        self.at = []
        for w in wires:
            a, b = self.spot(w.first), self.spot(w.second)
            self.at.append(a if w.first == w.second else a + odd * (b - a))

    def spot(self, place):
        axis, stride, size = place
        return self.here[axis] // stride % size

    def peer(self, stage, k):
        w = self.wires[stage]
        place = (self.at[stage] + k) % w.size
        move = place - self.at[stage]
        target = list(self.here)
        if w.first == w.second:
            target[w.first[0]] = target[w.first[0]] + move * w.first[1]
        else:
            target[w.first[0]] = target[w.first[0]] + move * w.first[1] * (1 - self.odd)
            target[w.second[0]] = target[w.second[0]] + move * w.second[1] * self.odd
        return tuple(target), place

    def greet(self):
        barrier = pltpu.get_barrier_semaphore()
        for stage, w in enumerate(self.wires):
            for k in range(1, w.size):
                pl.semaphore_signal(barrier, inc=1, device_id=self.peer(stage, k)[0], device_id_type=pl.DeviceIdType.MESH)

    def wait_greeting(self):
        pl.semaphore_wait(pltpu.get_barrier_semaphore(), sum(w.size - 1 for w in self.wires))


class Chunk:
    def __init__(self, net, order, sums, out, landing, sems, turn, layer, end):
        self.order = order
        self.wires = [net.wires[i] for i in order]
        self.net, self.sums, self.out, self.landing = net, sums, out, landing
        self.send, self.recv, self.local, self.sent, self.free = sems
        self.turn = turn
        self.layer, self.end = layer, end
        self.due = None
        size, start = sums.shape[0], 0
        self.unit = size
        for w in self.wires:
            self.unit //= w.size
        self.size, self.start = [], []
        for stage, w in enumerate(self.wires):
            size //= w.size
            self.size.append(size)
            self.start.append((start, size))
            start = start + net.at[order[stage]] * size
        self.own = start
        self.stages = len(self.wires)
        self.step = 0
        self.sem_at, at = {}, 0
        for phase in range(2):
            for stage, w in enumerate(self.wires):
                for k in range(1, w.size):
                    self.sem_at[phase, stage, k] = at
                    at += 1

    def rows(self, stage, place):
        start, size = self.start[stage]
        return pl.ds(pl.multiple_of(start + place * size, TILE), size)

    def copy(self, phase, stage, k):
        target, place = self.net.peer(self.order[stage], k)
        at = self.sem_at[phase, stage, k]
        if phase == 0:
            source, to = self.sums.at[self.rows(stage, place)], self.landing[stage].at[k - 1]
        else:
            rows = self.rows(stage, self.net.at[self.order[stage]])
            source = to = self.sums.at[rows]
        return pltpu.make_async_remote_copy(
            src_ref=source,
            dst_ref=to,
            send_sem=self.send.at[at],
            recv_sem=self.recv.at[at],
            device_id=target,
            device_id_type=pl.DeviceIdType.MESH,
        )

    def arrival(self, stage, k):
        target, place = self.net.peer(self.order[stage], self.wires[stage].size - k)
        at = self.sem_at[1, stage, k]
        landed = self.sums.at[self.rows(stage, place)]
        return pltpu.make_async_remote_copy(
            src_ref=landed,
            dst_ref=landed,
            send_sem=self.send.at[at],
            recv_sem=self.recv.at[at],
            device_id=target,
            device_id_type=pl.DeviceIdType.MESH,
        )

    def start_stage(self, phase, stage):
        if phase == 0 and self.turn == 1:
            pl.semaphore_wait(self.free.at[stage], self.wires[stage].size - 1)
        if phase == 1:
            pl.semaphore_wait(self.sent.at[stage], self.wires[stage].size - 1)
        for k in range(1, self.wires[stage].size):
            self.copy(phase, stage, k).start()

    def load(self):
        last = self.stages - 1
        stage = self.step if self.step <= last else 2 * self.stages - 1 - self.step
        peers = self.wires[stage].size - 1
        row = BLOCK * 2
        if stage == 0:
            return 0, self.size[0] * row / 4
        if self.order[stage] == last:
            return 2, self.size[stage] * (peers + 1) ** 2 / 2 * row
        return 1, self.size[stage] * peers * row

    def begin(self):
        self.start_stage(0, 0)

    def out_copy(self):
        return pltpu.make_async_copy(self.sums, self.out, self.local.at[0])

    def advance(self):
        step = self.step
        self.step += 1
        if step < self.stages:
            peers = range(1, self.wires[step].size)
            for k in peers:
                self.copy(0, step, k).wait_recv()
            base = self.start[step][0] + self.net.at[self.order[step]] * self.size[step]
            landing = self.landing[step]

            count = self.size[step] // self.unit
            while count % 2 == 0 and self.size[step] // count < 128:
                count //= 2
            size = self.size[step] // count

            def add(i, _):
                at = pl.ds(pl.multiple_of(base + i * size, TILE), size)
                here = [landing[k - 1, pl.ds(pl.multiple_of(i * size, TILE), size), :] for k in peers]
                if len(here) == 1:
                    self.sums[at, :] = self.sums[at, :] + here[0]
                else:
                    total = self.sums[at, :].astype(F32)
                    for part in here:
                        total = total + part.astype(F32)
                    self.sums[at, :] = total.astype(BF16)
                return 0

            lax.fori_loop(0, count, add, 0)
            for k in peers:
                self.copy(0, step, k).wait_send()
                target = self.net.peer(self.order[step], k)[0]
                pl.semaphore_signal(self.sent.at[step], inc=1, device_id=target, device_id_type=pl.DeviceIdType.MESH)
                if self.turn == 0:
                    pl.semaphore_signal(self.free.at[step], inc=1, device_id=target, device_id_type=pl.DeviceIdType.MESH)
            if step + 1 < self.stages:
                self.start_stage(0, step + 1)
            else:
                self.start_stage(1, step)
        else:
            stage = 2 * self.stages - 1 - step
            for k in range(1, self.wires[stage].size):
                self.arrival(stage, k).wait_recv()
            if stage > 0:
                self.start_stage(1, stage - 1)
            else:
                self.out_copy().start()

    def finish(self):
        for phase, stage, k in self.sem_at:
            if phase == 1:
                self.copy(phase, stage, k).wait_send()
        self.out_copy().wait()


LATENCY = 1.5
RATE = 65e3
STEP = 0.4


class Flow:
    def __init__(self, net):
        self.chunks, self.now, self.waiting, self.free = [], 0.0, 0, [0.0] * 3

    def book(self, chunk):
        kind, size = chunk.load()
        self.free[kind] = max(self.now, self.free[kind]) + size / RATE
        chunk.due = self.free[kind] + LATENCY

    def ready(self, layer, rows):
        while self.waiting < len(self.chunks):
            chunk = self.chunks[self.waiting]
            if chunk.layer != layer or chunk.end > rows:
                return
            chunk.begin()
            self.book(chunk)
            self.waiting += 1

    def due(self):
        return sorted((c for c in self.chunks if c.due is not None and c.due <= self.now), key=lambda c: c.due)

    def take(self):
        while self.due():
            chunk = self.due()[0]
            chunk.advance()
            self.now += STEP
            if chunk.step < 2 * chunk.stages:
                self.book(chunk)
            else:
                chunk.due = None

    def tick(self, time):
        self.now += time
        self.take()

    def ticks(self, s, count, time):
        for i in range(count):
            self.now += time
            if self.due():
                pl.when(s == i)(self.take)

    def drain(self):
        while any(c.due is not None for c in self.chunks):
            self.now = max(self.now, min(c.due for c in self.chunks if c.due is not None))
            self.take()
        for chunk in self.chunks:
            chunk.finish()


class Dims:
    def __init__(self, global_crops, local_crops, hidden, wires):
        self.wires = wires
        self.glen, self.n_global, self.width = global_crops.shape
        self.n_local, self.llen, _ = local_crops.shape
        self.hidden = hidden
        self.seq = up_to(self.glen, TILE)
        self.group = self.seq // self.llen
        while self.n_local % self.group:
            self.group -= 1
        self.n_seq = self.n_global + self.n_local // self.group
        sizes = (
            ("attend_gain", self.width),
            ("attend_shift", self.width),
            ("mixer_bias", 2 * self.width),
            ("output_bias", self.width),
            ("feed_gain", self.width),
            ("feed_shift", self.width),
            ("expand_bias", hidden),
            ("reduce_bias", self.width),
        )
        self.names, self.sizes = [name for name, _ in sizes], dict(sizes)
        self.at, row = {}, 0
        for name, size in sizes:
            self.at[name] = row
            row += -(-size // BLOCK)
        self.vec_rows = 2 * TILE
        assert row <= self.vec_rows and self.width * hidden % self.vec_rows == 0
        step = TILE
        for w in wires:
            step *= w.size
        ff = self.width * hidden // BLOCK
        square = self.width * self.width // BLOCK
        self.tops = (0, ff, 2 * ff, 2 * ff + square, 2 * ff + 4 * square)
        self.rows = up_to(self.tops[4] + 2 * self.vec_rows, step)
        parts = self.rows // step
        cuts = ((0, 4, 7, 10, 12, 14), (0, 4, 10, 14))
        self.bounds = [[c * step for c in sorted({parts * k // 14 for k in layer})] for layer in cuts]
        stages = list(range(len(wires)))
        turned = stages[:-2] + stages[:-3:-1] if len(wires) > 2 else stages
        self.orders = [[turned if i == 1 and len(b) > 3 else stages for i in range(len(b) - 1)] for b in self.bounds]
        self.landing_sets = [len(b) - 1 for b in self.bounds[::-1]]
        if self.bounds[0] == self.bounds[1]:
            self.landing_sets = self.landing_sets[:1]
        self.n_chunk = sum(len(b) - 1 for b in self.bounds)


HEAVY = (6, 8, 12, 14)


def run_kernel(counts, arrays, dims):
    d = dims
    n, seq, width, hidden = d.n_seq, d.seq, d.width, d.hidden
    crops = [jax.ShapeDtypeStruct(a.shape, BF16) for a in arrays[:2]]
    outs = crops + crops
    outs += [jax.ShapeDtypeStruct((2, d.rows, BLOCK), BF16)]
    scratch = [pltpu.VMEM(a.shape, BF16) for a in tuple(arrays[:4]) * 2]
    scratch += [pltpu.VMEM(arrays[i].shape, BF16) for i in HEAVY]
    scratch += [
        pltpu.SemaphoreType.DMA((16,)),
        pltpu.VMEM((2, d.rows, BLOCK), BF16),
        pltpu.VMEM((d.glen, d.n_global, width), F32),
        pltpu.VMEM((n, seq, width), F32),
        pltpu.VMEM((4, n, seq, width), BF16),
        pltpu.VMEM((4, n, seq, 1), F32),
        pltpu.VMEM((4, n, seq, width + LANES), BF16),
        pltpu.VMEM((2, n, seq, 3 * width), BF16),
        pltpu.VMEM((2, n, HEADS, seq, seq), BF16),
        pltpu.VMEM((2, n, seq, width), F32),
        pltpu.VMEM((2, n, seq, width + LANES), BF16),
        pltpu.VMEM((2, n, seq, hidden), BF16),
        pltpu.VMEM((n, seq, hidden), BF16),
        pltpu.VMEM((n, seq, width), F32),
        pltpu.VMEM((n, seq, width), BF16),
        pltpu.VMEM((n, seq, hidden), BF16),
        pltpu.VMEM((2, 2, 2, seq, LANES), BF16),
        pltpu.VMEM((d.vec_rows, BLOCK), F32),
        pltpu.VMEM((3, 8, width), F32),
    ]
    for layer in (1, 0)[: len(d.landing_sets)]:
        for first, end, order in zip(d.bounds[layer], d.bounds[layer][1:], d.orders[layer]):
            rows = end - first
            for w in [d.wires[i] for i in order]:
                rows //= w.size
                scratch.append(pltpu.VMEM((w.size - 1, rows, BLOCK), BF16))
    peers = 2 * sum(w.size - 1 for w in d.wires)
    scratch += [
        pltpu.SemaphoreType.DMA((d.n_chunk, peers)),
        pltpu.SemaphoreType.DMA((d.n_chunk, peers)),
        pltpu.SemaphoreType.DMA((d.n_chunk, 1)),
        pltpu.SemaphoreType.REGULAR((d.n_chunk, len(d.wires))),
        pltpu.SemaphoreType.REGULAR((d.n_chunk, len(d.wires))),
    ]
    vmem = pl.BlockSpec(memory_space=pltpu.VMEM)
    anywhere = pl.BlockSpec(memory_space=pl.ANY)
    return pl.pallas_call(
        functools.partial(kernel, d),
        out_shape=outs,
        in_specs=[pl.BlockSpec(memory_space=pltpu.SMEM)]
        + [anywhere if i < 4 or i in HEAVY else vmem for i in range(len(arrays))],
        out_specs=[anywhere] * len(outs),
        scratch_shapes=scratch,
        compiler_params=pltpu.CompilerParams(
            vmem_limit_bytes=63 * 1024 * 1024, collective_id=0, has_side_effects=True
        ),
    )(counts, *arrays)


THIRDS = 3


def cast_kernel(dims, reduce, expand, output, mixer, vectors, *rest):
    crops, outs, held, sems = rest[:4], rest[4:-9], rest[-5:-1], rest[-1]
    step = pl.program_id(0) * THIRDS + pl.program_id(1)
    loads = [pltpu.make_async_copy(a, b, sems.at[0, i]) for i, (a, b) in enumerate(zip(crops, held, strict=True))]
    stores = [pltpu.make_async_copy(a, b, sems.at[1, i]) for i, (a, b) in enumerate(zip(held, rest[-9:-5], strict=True))]

    @pl.when(step == 0)
    def _():
        for copy in loads:
            copy.start()

    @pl.when(step == 1)
    def _():
        for load, store in zip(loads, stores, strict=True):
            load.wait()
            store.start()

    mixer_grad, output_grad, expand_grad, reduce_grad = outs[:4]
    width = dims.width
    fold = width // 2
    for b in range(2):
        rows = slice(b * width, (b + 1) * width)
        cols = slice(b * BLOCK, (b + 1) * BLOCK)
        expand_grad[0, :, cols] = expand[0, rows, :].astype(F32)
        reduce_grad[0, cols, :] = reduce[0, rows, :].T.astype(F32)
    for source, target in ((mixer, mixer_grad), (output, output_grad)):
        target[0, :, 0:BLOCK] = source[0, 0:width, :].astype(F32)
        target[0, 0:fold, BLOCK:] = source[0, width:, 0:LANES].astype(F32)
        target[0, fold:, BLOCK:] = source[0, width:, LANES:].astype(F32)

    @pl.when(step == 2 * THIRDS - 1)
    def _():
        for ref, name in zip(outs[4:], dims.names, strict=True):
            size = ref.shape[1]
            for c in range(0, size, BLOCK):
                at = dims.at[name] + c // BLOCK
                piece = min(BLOCK, size - c)
                for layer in range(2):
                    ref[layer : layer + 1, c : c + piece] = vectors[0].astype(F32)[at + layer * dims.vec_rows :][:1, 0:piece]
        for store in stores:
            store.wait()


def run_cast(sums, crops, dims):
    d = dims
    width, hidden = d.width, d.hidden
    part = (1, 2 * width, BLOCK)
    square = (1, width * width // BLOCK, BLOCK)
    grads = [(width, 3 * width), (width, width), (width, hidden), (hidden, width)]
    shapes = [jax.ShapeDtypeStruct((2,) + g, F32) for g in grads]
    specs = [
        pl.BlockSpec((1, width, 3 * width // THIRDS), lambda l, t: (l, 0, t)),
        pl.BlockSpec((1, width, width), lambda l, t: (l, 0, 0)),
        pl.BlockSpec((1, width, hidden // THIRDS), lambda l, t: (l, 0, t)),
        pl.BlockSpec((1, hidden // THIRDS, width), lambda l, t: (l, t, 0)),
    ]
    for name in d.names:
        shapes.append(jax.ShapeDtypeStruct((2, d.sizes[name]), F32))
        specs.append(pl.BlockSpec((2, d.sizes[name]), lambda l, t: (0, 0)))
    for crop in crops:
        shapes.append(jax.ShapeDtypeStruct(crop.shape, crop.dtype))
        specs.append(pl.BlockSpec(memory_space=pl.ANY))
    return pl.pallas_call(
        functools.partial(cast_kernel, d),
        grid=(2, THIRDS),
        out_shape=shapes,
        in_specs=[
            pl.BlockSpec(part, lambda l, t: (l, t, 0)),
            pl.BlockSpec(part, lambda l, t: (l, THIRDS + t, 0)),
            pl.BlockSpec(square, lambda l, t: (l, d.tops[2] // square[1], 0)),
            pl.BlockSpec(square, lambda l, t: (l, d.tops[3] // square[1] + t, 0)),
            pl.BlockSpec((1, 2 * d.vec_rows, BLOCK), lambda l, t: (0, d.tops[4] // (2 * d.vec_rows), 0)),
        ]
        + [pl.BlockSpec(memory_space=pl.ANY)] * 4,
        out_specs=specs,
        scratch_shapes=[pltpu.VMEM(c.shape, c.dtype) for c in crops] + [pltpu.SemaphoreType.DMA((2, 4))],
        compiler_params=pltpu.CompilerParams(vmem_limit_bytes=62 * 1024 * 1024),
    )(sums, sums, sums, sums, sums, *crops)


def shards(wires, global_crops, local_crops, local_count, global_cotangent, local_cotangent, *weights):
    global_crops, global_cotangent = global_crops.transpose(1, 0, 2), global_cotangent.transpose(1, 0, 2)
    dims = Dims(global_crops, local_crops, weights[8].shape[2], wires)
    outs = run_kernel(
        local_count, (global_crops, local_crops, global_cotangent, local_cotangent) + weights, dims
    )
    mixer, output, expand, reduce, *rest = run_cast(outs[4], outs[:4], dims)
    vectors, crops = rest[:-4], rest[-4:]
    v = dict(zip(dims.names, vectors, strict=True))
    return (
        crops[0].transpose(1, 0, 2),
        crops[1],
        crops[2].transpose(1, 0, 2),
        crops[3],
        v["attend_gain"],
        v["attend_shift"],
        mixer,
        v["mixer_bias"],
        output,
        v["output_bias"],
        v["feed_gain"],
        v["feed_shift"],
        expand,
        v["expand_bias"],
        reduce,
        v["reduce_bias"],
    )


def solution(mesh):
    crops = P(("dp", "section"), None, None)
    return jax.shard_map(
        functools.partial(shards, wires_of(mesh)),
        mesh=mesh,
        in_specs=(crops, crops, P("dp"), crops, crops) + (P(),) * 12,
        out_specs=(crops,) * 4 + (P(),) * 12,
        check_vma=False,
    )
```
